32 devices in a mesh: section: 2 (over core), group: 4 (over y, x), replica: 4 (over z).
Axes of the slice: x: 2, y: 2, z: 4, core: 2. Of those that a mesh axis runs over, the one named last changes fastest.
Arguments:
- block_input: bfloat16 [8192, 640], P(('group', 'replica')), may hold values from -6 to 6
- cotangent: bfloat16 [8192, 640], P(('group', 'replica')), may hold values from -6 to 6
- crop_count: int32 [16], P(('group', 'replica')), may hold values from 1 to 2, as said below
- mask_count: int32 [32], P(('group', 'replica')), may hold values from 12 to 75
- qkv_weight: bfloat16 [2, 640, 1920], P('section'), may hold values from -0.25 to 0.25
- qkv_bias: float32 [2, 1920], P('section'), may hold values from -1.5 to 1.5
- out_weight: bfloat16 [2, 640, 640], P('section'), may hold values from -2 to 2
- out_bias: float32 [2, 640], P('section'), may hold values from -1.5 to 1.5
- up_weight: bfloat16 [2, 640, 2560], P('section'), may hold values from -0.25 to 0.25
- up_bias: float32 [2, 2560], P('section'), may hold values from -1.5 to 1.5
- down_weight: bfloat16 [2, 2560, 640], P('section'), may hold values from -0.125 to 0.125
- down_bias: float32 [2, 640], P('section'), may hold values from -1.5 to 1.5
- norm_gain: float32 [2, 2, 640], P('section'), may hold values from 0.4 to 1.6
- norm_shift: float32 [2, 2, 640], P('section'), may hold values from -1.5 to 1.5
Outputs:
- activations: bfloat16 [2, 8192, 640], P('section', ('group', 'replica'))
- input_grads: bfloat16 [2, 8192, 640], P('section', ('group', 'replica'))
- grad_qkv_weight: float32 [2, 640, 1920], P('section', 'group')
- grad_qkv_bias: float32 [2, 1920], P('section', 'group')
- grad_out_weight: float32 [2, 640, 640], P('section', 'group')
- grad_out_bias: float32 [2, 640], P('section', 'group')
- grad_up_weight: float32 [2, 640, 2560], P('section', 'group')
- grad_up_bias: float32 [2, 2560], P('section', 'group')
- grad_down_weight: float32 [2, 2560, 640], P('section', 'group')
- grad_down_bias: float32 [2, 640], P('section', 'group')
- grad_norm_gain: float32 [2, 2, 640], P('section', None, 'group')
- grad_norm_shift: float32 [2, 2, 640], P('section', None, 'group')
The draws below stay inside these ranges and needn't reach their ends.
Inputs may be any that keep to these rules, and one draw needn't show every extreme that they name: The live crops of a data rank fill its first crop_count slots; some rank fills all 2.
All inputs are finite; a program needn't handle non-finite values.
Results may differ from the reference program's by a relative error of at most 0.017.
Values may be sent and summed in bfloat16 or wider, within the bound.
No kernel may reach another device: no remote copies, remote signals or barrier semaphores. Data moves between devices by JAX's collectives and lax.ppermute only.
A program may use at most 256 MiB of HBM per device.

```python
import math
import jax
import jax.numpy as jnp
from jax import lax

D = 640
HEADS = 20
HEAD_DIM = 32
FF = 2560
LEN = 256
MASK_MEAN = 38
CROP_DEV = 2
RANKS = 16
CROPS = 32
TOKENS = 8192


def draw_crop_count(key, part):
    key = jax.random.fold_in(key, 11)
    base_key, pick_key = jax.random.split(key)
    counts = jax.random.randint(base_key, (RANKS,), 1, CROP_DEV + 1)
    chosen = jax.random.randint(pick_key, (), 0, RANKS)
    return jnp.where(jnp.arange(RANKS) == chosen, CROP_DEV, counts).astype(jnp.int32)


def set_ends(drawn, rng, least, top_value):
    longest = drawn.shape.index(max(drawn.shape))
    spots = []
    for shift in (0, 1):
        where = [jax.random.randint(jax.random.fold_in(rng, axis), (), 0, length) for axis, length in enumerate(drawn.shape)]
        where[longest] = (where[longest] + shift) % drawn.shape[longest]
        spots.append(tuple(where))
    return drawn.at[spots[0]].set(least).at[spots[1]].set(top_value)


def block_levels(key, extent, cuts, smallest, largest):
    loudness, own = 1.0, jax.random.fold_in(key, 6)
    for dim, parts in cuts:
        heights = jnp.exp(jax.random.uniform(jax.random.fold_in(own, dim), (parts,), jnp.float32, smallest / len(cuts), largest / len(cuts)))
        loudness = loudness * jnp.repeat(heights, extent[dim] // parts).reshape([-1 if axis == dim else 1 for axis in range(len(extent))])
    return loudness


def scatter_about(stream_key, extent, spread, bound, cuts=(), kind=jnp.bfloat16):
    result = spread * jax.random.normal(stream_key, extent, jnp.float32)
    if cuts:
        result = result * block_levels(stream_key, extent, cuts, -0.22, 0.18)
    return jnp.clip(result, -bound, bound).astype(kind)


def setup_inputs(seed: int = 0) -> dict:
    arg_keys = jax.random.split(jax.random.key(seed), 15)
    return {
        "block_input": scatter_about(arg_keys[0], (TOKENS, D), 1.0, 6.0, ((0, 16),)),
        "cotangent": scatter_about(arg_keys[1], (TOKENS, D), 1.0, 6.0, ((0, 16),)),
        "crop_count": draw_crop_count(jax.random.fold_in(arg_keys[14], 71), 0),
        "mask_count": set_ends(jax.random.randint(arg_keys[3], (CROPS,), MASK_MEAN // 3, 2 * MASK_MEAN), jax.random.fold_in(arg_keys[3], 1), MASK_MEAN // 3, (2 * MASK_MEAN) - 1).astype(jnp.int32),
        "qkv_weight": scatter_about(arg_keys[4], (2, D, 3 * D), D ** -0.5, 0.25, ((0, 2),)),
        "qkv_bias": scatter_about(arg_keys[5], (2, 3 * D), 0.3, 1.5, ((0, 2),), jnp.float32),
        "out_weight": scatter_about(arg_keys[6], (2, D, D), (D // 64) ** -0.5, 2.0, ((0, 2),)),
        "out_bias": scatter_about(arg_keys[7], (2, D), 0.3, 1.5, ((0, 2),), jnp.float32),
        "up_weight": scatter_about(arg_keys[8], (2, D, FF), D ** -0.5, 0.25, ((0, 2),)),
        "up_bias": scatter_about(arg_keys[9], (2, FF), 0.3, 1.5, ((0, 2),), jnp.float32),
        "down_weight": scatter_about(arg_keys[10], (2, FF, D), FF ** -0.5, 0.125, ((0, 2),)),
        "down_bias": scatter_about(arg_keys[11], (2, D), 0.3, 1.5, ((0, 2),), jnp.float32),
        "norm_gain": jnp.clip(1.0 + 0.12 * jax.random.normal(arg_keys[12], (2, 2, D), jnp.float32), 0.4, 1.6),
        "norm_shift": scatter_about(arg_keys[13], (2, 2, D), 0.3, 1.5, ((0, 2),), jnp.float32),
    }


EPSILON = 1e-05
ROTARY_BASE = 10000.0

@jax.custom_vjp
def low(v):
    return lax.optimization_barrier(v.astype(jnp.bfloat16)).astype(jnp.float32)

@jax.custom_vjp
def low_back(v):
    return v

def low_keep(v):
    return (low(v), None)

def low_pass(kept, grad):
    return (grad,)

def back_keep(v):
    return (v, None)

def back_low(kept, grad):
    return (low(grad),)
low.defvjp(low_keep, low_pass)
low_back.defvjp(back_keep, back_low)

def exact_dot(left, right):
    return jnp.dot(left, right, precision=lax.Precision.HIGHEST)

def layer_norm(values, norm_gain, norm_bias):
    row_mean = lax.optimization_barrier(jnp.mean(values, axis=-1, keepdims=True))
    centred = values - row_mean
    row_var = lax.optimization_barrier(jnp.mean(centred * centred, axis=-1, keepdims=True))
    return centred * lax.rsqrt(row_var + EPSILON) * norm_gain + norm_bias

def rotary_tables():
    half_dim = HEAD_DIM // 2
    inverse_freq = ROTARY_BASE ** (-jnp.arange(half_dim, dtype=jnp.float32) * (2.0 / HEAD_DIM))
    angles = jnp.arange(LEN, dtype=jnp.float32)[:, None] * inverse_freq[None, :]
    return (jnp.cos(angles)[None, :, None, :], jnp.sin(angles)[None, :, None, :])

def rotate(tensor, cosine, sine_table):
    half_dim = tensor.shape[-1] // 2
    lower_half = tensor[..., :half_dim]
    upper_half = tensor[..., half_dim:]
    return jnp.concatenate([lower_half * cosine - upper_half * sine_table, upper_half * cosine + lower_half * sine_table], axis=-1)

def layer_apply(params, layer_in):
    qkv_weight, qkv_bias, out_weight, out_bias, up_weight, up_bias, down_weight, down_bias, norm_gain, norm_shift = params
    crop_total = layer_in.shape[0] // LEN
    normed_one = low(layer_norm(layer_in, norm_gain[0], norm_shift[0]))
    qkv_rows = low_back(exact_dot(normed_one, qkv_weight) + qkv_bias)
    qkv_heads = qkv_rows.reshape(crop_total, LEN, 3, HEADS, HEAD_DIM)
    cosine, sine_table = rotary_tables()
    queries = low(rotate(qkv_heads[:, :, 0], cosine, sine_table) * HEAD_DIM ** (-0.5))
    keys_rot = low(rotate(qkv_heads[:, :, 1], cosine, sine_table))
    values = low(qkv_heads[:, :, 2])
    scores = low_back(jnp.einsum('cqhd,ckhd->chqk', queries, keys_rot, precision=lax.Precision.HIGHEST))
    attention = low(jax.nn.softmax(scores, axis=-1))
    mixed_heads = jnp.einsum('chqk,ckhd->cqhd', attention, values, precision=lax.Precision.HIGHEST)
    mixed_heads = low(low_back(mixed_heads.reshape(layer_in.shape[0], D)))
    branch = low_back(exact_dot(mixed_heads, out_weight) + out_bias)
    middle = layer_in + branch
    normed_two = low(layer_norm(middle, norm_gain[1], norm_shift[1]))
    up_rows = low_back(exact_dot(normed_two, up_weight) + up_bias)
    hidden_act = low(jax.nn.gelu(up_rows, approximate=False))
    down_rows = low_back(exact_dot(hidden_act, down_weight) + down_bias)
    return middle + down_rows

def two_layers(params_zero, params_one, layer_in, nudge):
    sent_rows = low(layer_apply(params_zero, layer_in))
    passed = low_back(sent_rows + nudge)
    return (sent_rows, layer_apply(params_one, passed))

def reference(block_input, cotangent, crop_count, mask_count, qkv_weight, qkv_bias, out_weight, out_bias, up_weight, up_bias, down_weight, down_bias, norm_gain, norm_shift):
    stacked = [arr.astype(jnp.float32) for arr in (qkv_weight, qkv_bias, out_weight, out_bias, up_weight, up_bias, down_weight, down_bias, norm_gain, norm_shift)]
    params_zero = tuple((arr[0] for arr in stacked))
    params_one = tuple((arr[1] for arr in stacked))
    crop_index = jnp.arange(CROPS, dtype=jnp.int32)
    rank_index = crop_index // CROP_DEV
    slot_index = crop_index % CROP_DEV
    live_crops = (slot_index < crop_count[rank_index]).astype(jnp.float32)
    loss_weight = live_crops * mask_count.astype(jnp.float32) / MASK_MEAN
    block_crops = math.gcd(CROPS, 16)
    block_total = CROPS // block_crops
    block_rows = block_crops * LEN
    input_blocks = block_input.astype(jnp.float32).reshape(block_total, block_rows, D)
    cotan_blocks = cotangent.astype(jnp.float32).reshape(block_total, block_rows, D)
    weight_blocks = jnp.repeat(loss_weight, LEN).reshape(block_total, block_rows, 1)
    live_blocks = jnp.repeat(live_crops, LEN).reshape(block_total, block_rows, 1)

    def one_block(totals, element):
        layer_in, cotan_rows, weight_rows, live_rows = element
        results, pullback = jax.vjp(two_layers, params_zero, params_one, layer_in, jnp.zeros_like(layer_in))
        sent_rows, final_rows = results
        grad_zero, grad_one, grad_input, grad_passed = pullback((jnp.zeros_like(sent_rows), cotan_rows * weight_rows))
        totals = jax.tree.map(jnp.add, totals, (grad_zero, grad_one))
        outputs = jnp.stack([(sent_rows * live_rows).astype(jnp.bfloat16), (final_rows * live_rows).astype(jnp.bfloat16)])
        backs = jnp.stack([grad_input.astype(jnp.bfloat16), grad_passed.astype(jnp.bfloat16)])
        return (totals, (outputs, backs))
    start = jax.tree.map(jnp.zeros_like, (params_zero, params_one))
    totals, (outputs, backs) = lax.scan(one_block, start, (input_blocks, cotan_blocks, weight_blocks, live_blocks))
    activations = jnp.moveaxis(outputs, 1, 0).reshape(2, TOKENS, D)
    input_grads = jnp.moveaxis(backs, 1, 0).reshape(2, TOKENS, D)
    grads = [jnp.stack([totals[0][index], totals[1][index]]) for index in range(10)]
    return (activations, input_grads, grads[0], grads[1], grads[2], grads[3], grads[4], grads[5], grads[6], grads[7], grads[8], grads[9])
```

```python
import jax
import jax.numpy as jnp
import numpy as np
from jax import lax
from jax.experimental import pallas as pl
from jax.experimental.pallas import tpu as pltpu
from jax.sharding import PartitionSpec as P

HEADS = 20
HEAD_DIM = 32
LEN = 256
MASK_MEAN = 38
CROP_DEV = 2
EPSILON = 1e-05
ROTARY_BASE = 10000.0

BF = jnp.bfloat16
F32 = jnp.float32
NN = (((1,), (0,)), ((), ()))
NT = (((1,), (1,)), ((), ()))
TN = (((0,), (0,)), ((), ()))

VMEM_LIMIT = 60 << 20
PAD = 16
ROW_QKV, ROW_OUT, ROW_UP, ROW_DOWN, ROW_GAIN, ROW_SHIFT = 0, 3, 4, 8, 9, 11

HBM = pl.BlockSpec(memory_space=pltpu.HBM)
SMEM = pl.BlockSpec(memory_space=pltpu.SMEM)


def shape(dims, dtype):
    return jax.ShapeDtypeStruct(dims, dtype)


def mm(left, right, dims=NN):
    return lax.dot_general(left, right, dims, preferred_element_type=F32)


def unit_rows_of(values):
    centred = values - jnp.mean(values, axis=-1, keepdims=True)
    inverse = lax.rsqrt(jnp.mean(centred * centred, axis=-1, keepdims=True) + EPSILON)
    return centred * inverse, inverse


def norm_back(grad, unit, inverse, gain):
    scaled = grad * gain
    return inverse * (
        scaled
        - jnp.mean(scaled, axis=-1, keepdims=True)
        - unit * jnp.mean(scaled * unit, axis=-1, keepdims=True)
    )


def rotary_tables():
    lane = np.arange(128) % HEAD_DIM
    half = HEAD_DIM // 2
    freq = ROTARY_BASE ** (-(lane % half).astype(np.float64) * (2.0 / HEAD_DIM))
    angles = np.arange(LEN)[:, None] * freq[None, :]
    sign = np.where(lane < half, -1.0, 1.0)[None, :]
    return np.stack([np.cos(angles), np.sin(angles) * sign]).astype(np.float32)


def swap_halves(values):
    lane = lax.broadcasted_iota(jnp.int32, values.shape, 1) % HEAD_DIM
    half = HEAD_DIM // 2
    return jnp.where(
        lane < half,
        pltpu.roll(values, 128 - half, axis=1),
        pltpu.roll(values, half, axis=1),
    )


def head_stack(block, per):
    head = lax.broadcasted_iota(jnp.int32, block.shape, 1) // HEAD_DIM
    return jnp.concatenate(
        [jnp.where(head == h, block, jnp.zeros_like(block)) for h in range(per)], axis=0
    )


class Copies:
    def __init__(self, sems):
        self.sems = sems
        self.used = 0
        self.open = []

    def start(self, src, dst):
        copy = pltpu.make_async_copy(src, dst, self.sems.at[self.used])
        self.used += 1
        copy.start()
        return copy

    def save(self, src, dst):
        self.open.append(self.start(src, dst))

    def finish(self):
        for copy in self.open:
            copy.wait()


def call(kernel, outs, ins, scratch, sems, aliases, name):
    return pl.pallas_call(
        kernel,
        out_shape=outs,
        in_specs=[SMEM if a.ndim == 1 else HBM for a in ins],
        out_specs=[HBM] * len(outs),
        scratch_shapes=scratch + [pltpu.SemaphoreType.DMA((sems,))],
        input_output_aliases=aliases,
        compiler_params=pltpu.CompilerParams(vmem_limit_bytes=VMEM_LIMIT),
        name=name,
    )(*ins)


def vmem_like(arr):
    return pltpu.VMEM(arr.shape, arr.dtype)


def forward_kernel(*refs, fresh):
    info, x_h, qkvb_h, outb_h, upb_h, downb_h, gain_h, shift_h, tab_h = refs[:9]
    qkvw_h, outw_h, upw_h, downw_h = refs[9:13]
    refs = refs[13 if fresh else 20 :]
    y_h, qkv_h, prob_h, mixt_h, mid_h, gp_h, hid_h = refs[:7]
    x_s, qkvb, outb, upb, downb, gain, shift, tab, qkvw, outw, upw, downw = refs[7:19]
    y_s, qkv_s, prob_s, mixt_s, mid_s, gp_s, hid_s, vt_s, score_s, up_s, sems = refs[19:]
    rows, dim = x_s.shape
    blocks = dim // 128
    parts = upw.shape[1] // dim
    per = 128 // HEAD_DIM

    @pl.when(info[0] != 0)
    def _():
        copies = Copies(sems)
        small = [
            copies.start(h, s)
            for h, s in (
                (x_h, x_s),
                (gain_h, gain),
                (shift_h, shift),
                (qkvb_h, qkvb),
                (tab_h, tab),
                (outb_h, outb),
                (upb_h, upb),
                (downb_h, downb),
            )
        ]
        loads = [
            copies.start(h, s)
            for h, s in ((qkvw_h, qkvw), (outw_h, outw), (upw_h, upw), (downw_h, downw))
        ]
        for copy in small:
            copy.wait()
        x = x_s[...].astype(F32)
        unit, _ = unit_rows_of(x)
        normed = (unit * gain[0:1, :] + shift[0:1, :]).astype(BF)
        loads[0].wait()
        for part in range(3):
            cols = slice(part * dim, (part + 1) * dim)
            third = mm(normed, qkvw[:, cols]) + qkvb[:, cols]
            for c in range(rows // LEN):
                crop = slice(c * LEN, (c + 1) * LEN)
                if part == 2:
                    low = third[crop].astype(BF)
                    qkv_s[crop, cols] = low
                    vt_s[c] = low.T
                    continue
                for j in range(blocks):
                    b = third[crop, 128 * j : 128 * j + 128]
                    b = b * tab[0] + swap_halves(b) * tab[1]
                    if part == 0:
                        b = b * HEAD_DIM**-0.5
                    at = part * dim + 128 * j
                    qkv_s[crop, at : at + 128] = b.astype(BF)
        copies.save(qkv_s, qkv_h)
        for c in range(rows // LEN):
            crop = slice(c * LEN, (c + 1) * LEN)
            for j in range(blocks):
                q = qkv_s[crop, 128 * j : 128 * j + 128]
                k = qkv_s[crop, dim + 128 * j : dim + 128 * j + 128]
                score_s[per * LEN * j : per * LEN * (j + 1), :] = mm(head_stack(k, per), q, NT)

            def soft(h, _):
                s = score_s[pl.ds(pl.multiple_of(h * LEN, LEN), LEN), :]
                e = jnp.exp(s - jnp.max(s, axis=0, keepdims=True))
                prob_s[c * HEADS + h] = (e * (1.0 / jnp.sum(e, axis=0, keepdims=True))).astype(BF)
                return 0

            lax.fori_loop(0, HEADS, soft, 0, unroll=2)
            copies.save(
                prob_s.at[pl.ds(c * HEADS, HEADS)], prob_h.at[pl.ds(c * HEADS, HEADS)]
            )
            for h in range(HEADS):
                at = slice(HEAD_DIM * h, HEAD_DIM * (h + 1))
                mixt_s[at, crop] = mm(vt_s[c, at, :], prob_s[c * HEADS + h]).astype(BF)
        copies.save(mixt_s, mixt_h)
        loads[1].wait()
        mid = x + mm(mixt_s[...], outw[...], TN) + outb[...]
        mid_s[...] = mid
        copies.save(mid_s, mid_h)
        unit, _ = unit_rows_of(mid)
        normed = (unit * gain[1:2, :] + shift[1:2, :]).astype(BF)
        loads[2].wait()
        for c in range(parts):
            cols = slice(c * dim, (c + 1) * dim)
            up_s[c] = mm(normed, upw[:, cols]) + upb[:, cols]
        for c in range(parts):
            u = up_s[c]
            cdf = 0.5 + 0.5 * lax.erf(u * 0.5**0.5)
            hid_s[c] = (u * cdf).astype(BF)
            gp_s[c] = (cdf + u * (jnp.exp(u * u * -0.5) * (2 * np.pi) ** -0.5)).astype(BF)
            copies.save(hid_s.at[c], hid_h.at[c])
            copies.save(gp_s.at[c], gp_h.at[c])
        loads[3].wait()
        out = mid + downb[...]
        for c in range(parts):
            out = out + mm(hid_s[c], downw[c * dim : (c + 1) * dim, :])
        y_s[...] = out.astype(BF)
        copies.save(y_s, y_h)
        copies.finish()


def forward(info, x, params, tab, before):
    qkvw, qkvb, outw, outb, upw, upb, downw, downb, gain, shift = params
    rows, dim = x.shape
    crops = rows // LEN
    parts = upw.shape[1] // dim
    outs = [
        shape((rows, dim), BF),
        shape((rows, 3 * dim), BF),
        shape((crops * HEADS, LEN, LEN), BF),
        shape((dim, rows), BF),
        shape((rows, dim), F32),
        shape((parts, rows, dim), BF),
        shape((parts, rows, dim), BF),
    ]
    ins = [x, qkvb, outb, upb, downb, gain, shift, tab, qkvw, outw, upw, downw]
    scratch = [vmem_like(a) for a in ins + outs]
    scratch += [
        pltpu.VMEM((crops, dim, LEN), BF),
        pltpu.VMEM((HEADS * LEN, LEN), F32),
        pltpu.VMEM((parts, rows, dim), F32),
    ]
    fresh = before is None
    ins = [info] + ins + ([] if fresh else list(before))

    def kernel(*refs):
        forward_kernel(*refs, fresh=fresh)

    aliases = {} if fresh else {13 + i: i for i in range(7)}
    return call(kernel, outs, ins, scratch, 48, aliases, "layer_forward")


def row_weights(info_w, rows):
    row = lax.broadcasted_iota(jnp.int32, (rows, 1), 0) // LEN
    weight = jnp.zeros((rows, 1), F32)
    for c in range(rows // LEN):
        weight = jnp.where(row == c, info_w[c], weight)
    return weight


def place(copies, info, block, pieces, bufs):
    send_a, keep_a, send_b, keep_b = bufs
    half_rows = send_b.shape[0] // 2
    waits = []
    for src_row, count, shard, half, at in pieces:
        x, y = shard % 2, shard // 2
        own, index, keep, send = (
            (info[1] == x, y, keep_a, send_a) if half == 0 else (info[2] == y, x, keep_b, send_b)
        )
        src = block.at[pl.ds(src_row, count)]
        dst = pl.ds(index * half_rows + at, count)
        sem = copies.sems.at[copies.used]
        copies.used += 1

        @pl.when(own)
        def _():
            pltpu.make_async_copy(src, keep.at[dst], sem).start()

        @pl.when(jnp.logical_not(own))
        def _():
            pltpu.make_async_copy(src, send.at[dst], sem).start()

        waits.append(pltpu.make_async_copy(src, keep.at[dst], sem))
    copies.open += waits


def buffer_shapes(dim):
    return [
        shape((dim + PAD, dim), BF),
        shape((dim + PAD, dim), BF),
        shape((dim, dim), BF),
        shape((dim, dim), BF),
    ]


def down_kernel(*refs, fresh):
    info, weights, g_h, hid_h = refs[:4]
    refs = refs[4 if fresh else 8 :]
    bufs = refs[:4]
    g_s, hid_s, block_s, sems = refs[4:]
    parts, rows, dim = hid_s.shape

    @pl.when(info[0] != 0)
    def _():
        copies = Copies(sems)
        load = copies.start(g_h, g_s)
        loads = [copies.start(hid_h.at[c], hid_s.at[c]) for c in range(parts)]
        load.wait()
        low = (g_s[...].astype(F32) * row_weights(weights, rows)).astype(BF)
        for c in range(parts):
            loads[c].wait()
            block_s[c] = mm(hid_s[c], low, TN).astype(BF)
            half = dim // 2
            place(copies, info, block_s.at[c], [(0, half, c, 0, 0), (half, half, c, 1, 0)], bufs)
        copies.finish()


def down_grad(info, weights, g, saved, before):
    hid = saved[6]
    parts, rows, dim = hid.shape
    fresh = before is None
    ins = [info, weights, g, hid] + ([] if fresh else list(before))

    def kernel(*refs):
        down_kernel(*refs, fresh=fresh)

    scratch = [vmem_like(g), vmem_like(hid), pltpu.VMEM((parts, dim, dim), BF)]
    aliases = {} if fresh else {4 + i: i for i in range(4)}
    return call(kernel, buffer_shapes(dim), ins, scratch, 16, aliases, "down_grad")


def up_kernel(*refs, fresh):
    info, weights, g_h, mid_h, gp_h, gain_h, shift_h, downw_h, upw_h = refs[:9]
    refs = refs[9 if fresh else 13 :]
    bufs = refs[:4]
    gmid_h, small_h = refs[4:6]
    g_s, mid_s, gp_s, gain, shift, downw, upw = refs[6:13]
    gu_s, block_s, gmid_s, small_s, sems = refs[13:]
    parts, rows, dim = gp_s.shape

    @pl.when(info[0] != 0)
    def _():
        copies = Copies(sems)
        loads = [
            copies.start(h, s)
            for h, s in (
                (g_h, g_s),
                (mid_h, mid_s),
                (gain_h, gain),
                (shift_h, shift),
                (downw_h, downw),
                (gp_h, gp_s),
                (upw_h, upw),
            )
        ]
        for copy in loads[:4]:
            copy.wait()
        grad = g_s[...].astype(F32) * row_weights(weights, rows)
        low = grad.astype(BF)
        small_s[...] = jnp.zeros_like(small_s)
        small_s[ROW_DOWN : ROW_DOWN + 1, :] = jnp.sum(low.astype(F32), axis=0, keepdims=True)
        unit, inverse = unit_rows_of(mid_s[...])
        normed_t = (unit * gain[1:2, :] + shift[1:2, :]).astype(BF).T
        for copy in loads[4:6]:
            copy.wait()
        for c in range(parts):
            grad_up = mm(low, downw[c * dim : (c + 1) * dim, :], NT) * gp_s[c].astype(F32)
            grad_up = grad_up.astype(BF)
            gu_s[c] = grad_up
            small_s[ROW_UP + c : ROW_UP + c + 1, :] = jnp.sum(
                grad_up.astype(F32), axis=0, keepdims=True
            )
        loads[6].wait()
        back = mm(gu_s[0], upw[:, :dim], NT)
        for c in range(1, parts):
            back = back + mm(gu_s[c], upw[:, c * dim : (c + 1) * dim], NT)
        gmid_s[...] = grad + norm_back(back, unit, inverse, gain[1:2, :])
        copies.save(gmid_s, gmid_h)
        small_s[ROW_GAIN + 1 : ROW_GAIN + 2, :] = jnp.sum(back * unit, axis=0, keepdims=True)
        small_s[ROW_SHIFT + 1 : ROW_SHIFT + 2, :] = jnp.sum(back, axis=0, keepdims=True)
        copies.save(small_s, small_h)
        count = dim // parts
        for c in range(parts):
            block_s[c] = mm(normed_t, gu_s[c]).astype(BF)
            place(
                copies,
                info,
                block_s.at[c],
                [(s * count, count, s, c // 2, (c % 2) * count) for s in range(parts)],
                bufs,
            )
        copies.finish()


def up_grad(info, weights, g, saved, params, before):
    mid, gp = saved[4], saved[5]
    upw, downw, gain, shift = params[4], params[6], params[8], params[9]
    parts, rows, dim = gp.shape
    fresh = before is None
    ins = [g, mid, gp, gain, shift, downw, upw]
    scratch = [vmem_like(a) for a in ins] + [
        pltpu.VMEM((parts, rows, dim), BF),
        pltpu.VMEM((parts, dim, dim), BF),
        pltpu.VMEM((rows, dim), F32),
        pltpu.VMEM((PAD, dim), F32),
    ]
    ins = [info, weights] + ins + ([] if fresh else list(before))

    def kernel(*refs):
        up_kernel(*refs, fresh=fresh)

    aliases = {} if fresh else {9 + i: i for i in range(4)}
    outs = buffer_shapes(dim) + [shape((rows, dim), F32), shape((PAD, dim), F32)]
    out = call(kernel, outs, ins, scratch, 40, aliases, "up_grad")
    return out[:4], out[4], out[5]


def attention_kernel(*refs, fresh):
    (info, gmid_h, small_h, x_h, qkv_h, prob_h, mixt_h, gain_h, shift_h, tab_h, outw_h, qkvw_h) = (
        refs[:12]
    )
    refs = refs[12 if fresh else 13 :]
    dx_h = refs[0]
    bufs = refs[1:5]
    gmid_s, small_s, x_s, qkv_s, prob_s, mixt_s, gain, shift, tab, outw, qkvw = refs[5:16]
    dx_s, low_s, gm_s, gmt_s, delta_s, da_s, ds_s, gqkv_s, dqt_s, block_s, tail_s, sems = refs[16:]
    rows, dim = x_s.shape
    blocks = dim // 128
    per = 128 // HEAD_DIM

    @pl.when(info[0] != 0)
    def _():
        copies = Copies(sems)
        loads = [
            copies.start(h, s)
            for h, s in (
                (gmid_h, gmid_s),
                (outw_h, outw),
                (qkv_h, qkv_s),
                (mixt_h, mixt_s),
                (prob_h, prob_s),
                (small_h, small_s),
                (x_h, x_s),
                (gain_h, gain),
                (shift_h, shift),
                (tab_h, tab),
                (qkvw_h, qkvw),
            )
        ]
        loads[0].wait()
        low = gmid_s[...].astype(BF)
        low_s[...] = low
        loads[1].wait()
        gm_s[...] = mm(low, outw[...], NT).astype(BF)
        gmt_s[...] = mm(outw[...], low, NT).astype(BF)
        for copy in loads[2:5]:
            copy.wait()
        for c in range(rows // LEN):
            crop = slice(c * LEN, (c + 1) * LEN)
            product = gmt_s[:, crop].astype(F32) * mixt_s[:, crop].astype(F32)
            delta_s[...] = jnp.sum(product.reshape(HEADS, HEAD_DIM, LEN), axis=1)[:, None, :]
            for j in range(blocks):
                v = qkv_s[crop, 2 * dim + 128 * j : 2 * dim + 128 * j + 128]
                da_s[per * LEN * j : per * LEN * (j + 1), :] = mm(
                    head_stack(v, per), gmt_s[128 * j : 128 * j + 128, crop]
                )

            def scores(h, _):
                da = da_s[pl.ds(pl.multiple_of(h * LEN, LEN), LEN), :]
                ds_s[h] = (prob_s[c * HEADS + h].astype(F32) * (da - delta_s[h])).astype(BF)
                return 0

            lax.fori_loop(0, HEADS, scores, 0, unroll=2)
            kt = qkv_s[crop, dim : 2 * dim].T
            for h in range(HEADS):
                at = slice(HEAD_DIM * h, HEAD_DIM * (h + 1))
                dqt_s[at, :] = mm(kt[at, :], ds_s[h])
            if c == 0:
                for copy in loads[5:]:
                    copy.wait()
            for j in range(blocks):
                heads = range(per * j, per * (j + 1))
                ps = jnp.concatenate([prob_s[c * HEADS + h] for h in heads], axis=1)
                dss = jnp.concatenate([ds_s[h] for h in heads], axis=1)
                cols = slice(128 * j, 128 * j + 128)
                gqkv_s[crop, 2 * dim + 128 * j : 2 * dim + 128 * j + 128] = mm(
                    ps, head_stack(gm_s[crop, cols], per)
                ).astype(BF)
                dk = mm(dss, head_stack(qkv_s[crop, cols], per))
                dk = dk * tab[0] - swap_halves(dk) * tab[1]
                gqkv_s[crop, dim + 128 * j : dim + 128 * j + 128] = dk.astype(BF)
                dq = dqt_s[cols, :].T * HEAD_DIM**-0.5
                dq = dq * tab[0] - swap_halves(dq) * tab[1]
                gqkv_s[crop, cols] = dq.astype(BF)
        back = mm(gqkv_s[...], qkvw[...], NT)
        unit, inverse = unit_rows_of(x_s[...].astype(F32))
        dx_s[...] = (gmid_s[...] + norm_back(back, unit, inverse, gain[0:1, :])).astype(BF)
        copies.save(dx_s, dx_h)
        small_s[ROW_GAIN : ROW_GAIN + 1, :] = jnp.sum(back * unit, axis=0, keepdims=True)
        small_s[ROW_SHIFT : ROW_SHIFT + 1, :] = jnp.sum(back, axis=0, keepdims=True)
        small_s[ROW_OUT : ROW_OUT + 1, :] = jnp.sum(
            low_s[...].astype(F32), axis=0, keepdims=True
        )
        normed_t = (unit * gain[0:1, :] + shift[0:1, :]).astype(BF).T
        parts = 4
        count = dim // parts
        for c in range(parts):
            if c < 3:
                third = gqkv_s[:, c * dim : (c + 1) * dim]
                small_s[ROW_QKV + c : ROW_QKV + c + 1, :] = jnp.sum(
                    third.astype(F32), axis=0, keepdims=True
                )
                block_s[c] = mm(normed_t, third).astype(BF)
            else:
                block_s[c] = mm(mixt_s[...], low_s[...]).astype(BF)
            place(
                copies,
                info,
                block_s.at[c],
                [(s * count, count, s, c // 2, (c % 2) * count) for s in range(parts)],
                bufs,
            )
        tail_s[...] = small_s[...].astype(BF)
        copies.save(tail_s, bufs[0].at[pl.ds(dim, PAD)])
        copies.save(tail_s, bufs[1].at[pl.ds(dim, PAD)])
        copies.finish()


def attention_grad(info, gmid, small, x, saved, params, tab, before):
    _, qkv, prob, mixt = saved[:4]
    qkvw, outw, gain, shift = params[0], params[2], params[8], params[9]
    rows, dim = x.shape
    fresh = before is None
    ins = [gmid, small, x, qkv, prob, mixt, gain, shift, tab, outw, qkvw]
    scratch = [vmem_like(a) for a in ins] + [
        pltpu.VMEM((rows, dim), BF),
        pltpu.VMEM((rows, dim), BF),
        pltpu.VMEM((rows, dim), BF),
        pltpu.VMEM((dim, rows), BF),
        pltpu.VMEM((HEADS, 1, LEN), F32),
        pltpu.VMEM((HEADS * LEN, LEN), F32),
        pltpu.VMEM((HEADS, LEN, LEN), BF),
        pltpu.VMEM((rows, 3 * dim), BF),
        pltpu.VMEM((dim, LEN), F32),
        pltpu.VMEM((4, dim, dim), BF),
        pltpu.VMEM((PAD, dim), BF),
    ]
    ins = [info] + ins + ([] if fresh else [before])

    def kernel(*refs):
        attention_kernel(*refs, fresh=fresh)

    aliases = {} if fresh else {12: 0}
    outs = [shape((rows, dim), BF)] + buffer_shapes(dim)
    out = call(kernel, outs, ins, scratch, 40, aliases, "attention_grad")
    return out[0], out[1:]


def first_sum_kernel(info, ka_h, ra_h, kb_h, rb_h, sa_h, na_h, sb_h, nb_h, *rest):
    ka, ra, kb, rb, sa, na, sb, nb, sems = rest
    half = kb.shape[0] // 2

    @pl.when(info[0] != 0)
    def _():
        copies = Copies(sems)
        loads = [
            copies.start(h, s) for h, s in ((ka_h, ka), (ra_h, ra), (kb_h, kb), (rb_h, rb))
        ]

        def add(one, two, rows):
            return (one[rows, :].astype(F32) + two[rows, :].astype(F32)).astype(BF)

        for own, one, two, new, out in ((info[2], ka, ra, na, sa), (info[1], kb, rb, nb, sb)):
            for copy in loads[:2]:
                copy.wait()
            loads = loads[2:]
            mine = pl.ds(pl.multiple_of(own * half, half), half)
            other = pl.ds(pl.multiple_of((1 - own) * half, half), half)
            new[:half, :] = add(one, two, mine)
            out[:half, :] = add(one, two, other)
            if one.shape[0] > 2 * half:
                tail = add(one, two, pl.ds(2 * half, PAD))
                new[half:, :] = tail
                out[half:, :] = tail
            copies.save(out, sa_h if out is sa else sb_h)
            copies.save(new, na_h if out is sa else nb_h)
        copies.finish()


def first_sum(info, keep_a, recv_a, keep_b, recv_b):
    dim = keep_b.shape[1]
    half = dim // 2
    outs = [shape((half + PAD, dim), BF)] * 2 + [shape((half, dim), BF)] * 2
    ins = [keep_a, recv_a, keep_b, recv_b]
    scratch = [vmem_like(a) for a in ins + outs]
    return call(first_sum_kernel, outs, [info] + ins, scratch, 8, {}, "first_sum")


def second_sum_kernel(info, ka_h, ra_h, kb_h, rb_h, out_h, ka, ra, kb, rb, out, sems):
    @pl.when(info[0] != 0)
    def _():
        copies = Copies(sems)
        loads = [
            copies.start(h, s) for h, s in ((ka_h, ka), (ra_h, ra), (kb_h, kb), (rb_h, rb))
        ]
        for copy in loads:
            copy.wait()
        top = ka.shape[0]
        out[:top, :] = (ka[...].astype(F32) + ra[...].astype(F32)).astype(BF)
        out[top:, :] = (kb[...].astype(F32) + rb[...].astype(F32)).astype(BF)
        copies.save(out, out_h)
        copies.finish()


def second_sum(info, keep_a, recv_a, keep_b, recv_b):
    dim = keep_b.shape[1]
    outs = [shape((dim + PAD, dim), BF)]
    ins = [keep_a, recv_a, keep_b, recv_b]
    scratch = [vmem_like(a) for a in ins + outs]
    return call(second_sum_kernel, outs, [info] + ins, scratch, 8, {}, "second_sum")[0]


def pair_sum_kernel(info, one_h, two_h, out_h, one, two, out, sems):
    @pl.when(info[0] != 0)
    def _():
        copies = Copies(sems)
        loads = [copies.start(h, s) for h, s in ((one_h, one), (two_h, two))]
        for copy in loads:
            copy.wait()
        out[...] = (one[...].astype(F32) + two[...].astype(F32)).astype(BF)
        copies.save(out, out_h)
        copies.finish()


def pair_sum(info, one, two):
    outs = [shape(one.shape, BF)]
    scratch = [vmem_like(a) for a in (one, two, one)]
    return call(pair_sum_kernel, outs, [info, one, two], scratch, 4, {}, "pair_sum")[0]


def flow(shard, axis, pairs, sections):
    if sections == (0, 1):
        return lax.ppermute(shard, axis, pairs)
    peers = lax.axis_size(axis)
    pairs = [(s * peers + i, s * peers + j) for s in sections for i, j in pairs]
    return lax.ppermute(shard, ("section", axis), pairs)


class Reduction:
    def __init__(self, info, middle, sections, bufs):
        self.info, self.middle, self.sections, self.bufs = info, middle, sections, bufs

    def group_one(self):
        send_a, _, send_b, _ = self.bufs
        groups = range(lax.axis_size("group"))
        self.across = [(g, g ^ 1) for g in groups]
        self.along = [(g, g ^ 2) for g in groups]
        self.got = (
            flow(send_a, "group", self.across, self.sections),
            flow(send_b, "group", self.along, self.sections),
        )

    def group_two(self):
        _, keep_a, _, keep_b = self.bufs
        send_a, keep_a, send_b, keep_b = first_sum(
            self.info, keep_a, self.got[0], keep_b, self.got[1]
        )
        self.kept = (keep_a, keep_b)
        self.got = (
            flow(send_a, "group", self.along, self.sections),
            flow(send_b, "group", self.across, self.sections),
        )

    def replica_one(self):
        self.part = second_sum(
            self.info, self.kept[0], self.got[0], self.kept[1], self.got[1]
        )
        if lax.axis_size("replica") != 4:
            self.total = lax.psum(self.part, "replica")
            return
        self.got = flow(self.part, "replica", [(0, 1), (3, 2)], self.sections)

    def replica_two(self):
        if lax.axis_size("replica") != 4:
            return
        self.part = pair_sum(self.middle, self.part, self.got)
        self.got = flow(self.part, "replica", [(1, 2), (2, 1)], self.sections)

    def replica_three(self):
        if lax.axis_size("replica") != 4:
            return
        self.part = pair_sum(self.middle, self.part, self.got)
        self.got = flow(self.part, "replica", [(1, 0), (2, 3)], self.sections)

    def result(self):
        if lax.axis_size("replica") != 4:
            return self.total
        replica = lax.axis_index("replica")
        return jnp.where((replica == 1) | (replica == 2), self.part, self.got)


def shards(
    block_input,
    cotangent,
    crop_count,
    mask_count,
    qkv_weight,
    qkv_bias,
    out_weight,
    out_bias,
    up_weight,
    up_bias,
    down_weight,
    down_bias,
    norm_gain,
    norm_shift,
):
    params = (
        qkv_weight[0],
        qkv_bias,
        out_weight[0],
        out_bias,
        up_weight[0],
        up_bias,
        down_weight[0],
        down_bias,
        norm_gain[0],
        norm_shift[0],
    )
    rows, dim = block_input.shape
    tab = jnp.asarray(rotary_tables())
    section = lax.axis_index("section")
    group = lax.axis_index("group")
    replica = lax.axis_index("replica")
    groups = lax.axis_size("group")
    first = section == 0
    middle = (replica == 1) | (replica == 2)

    def info_of(flag):
        return jnp.stack([flag.astype(jnp.int32), group % 2, group // 2]).astype(jnp.int32)

    is_first, is_second, is_any = info_of(first), info_of(~first), info_of(group >= 0)
    live = (jnp.arange(CROP_DEV) < crop_count[0]).astype(F32)
    loss_weight = live * mask_count.astype(F32) / MASK_MEAN
    ones = jnp.ones((CROP_DEV,), F32)

    def to_other(shard, pairs):
        return lax.ppermute(shard, "section", pairs)

    saved = forward(is_first, block_input, params, tab, None)
    arrived = to_other(saved[0], [(0, 1)])
    saved = forward(is_second, arrived, params, tab, saved)

    def reduction(sections, bufs):
        if sections == (0, 1):
            return Reduction(is_any, info_of(middle), sections, bufs)
        flag = section == sections[0]
        return Reduction(info_of(flag), info_of(flag & middle), sections, bufs)

    bufs_one = down_grad(is_second, loss_weight, cotangent, saved, None)
    set_one = reduction((1,), bufs_one)
    set_one.group_one()
    bufs_two, gmid, small = up_grad(is_second, loss_weight, cotangent, saved, params, None)
    set_one.group_two()
    dx, bufs_three = attention_grad(is_second, gmid, small, arrived, saved, params, tab, None)
    grad_back = to_other(dx, [(1, 0)])
    set_one.replica_one()
    bufs_two = down_grad(is_first, ones, grad_back, saved, bufs_two)
    set_two = reduction((0, 1), bufs_two)
    set_two.group_one()
    bufs_three, gmid, small = up_grad(is_first, ones, grad_back, saved, params, bufs_three)
    set_one.replica_two()
    set_two.group_two()
    set_three = reduction((0, 1), bufs_three)
    set_three.group_one()
    dx, bufs_four = attention_grad(is_first, gmid, small, block_input, saved, params, tab, dx)
    set_one.replica_three()
    set_two.replica_one()
    set_three.group_two()
    set_four = reduction((0,), bufs_four)
    set_four.group_one()
    set_two.replica_two()
    set_three.replica_one()
    set_four.group_two()
    set_two.replica_three()
    set_three.replica_two()
    set_four.replica_one()
    set_three.replica_three()
    set_four.replica_two()
    set_four.replica_three()

    half = dim // 2
    results = [s.result() for s in (set_one, set_two, set_three, set_four)]

    def chosen(index):
        return jnp.where(first, results[index + 1], results[index]).astype(F32)

    def wide(block, count):
        rows_a, rows_b = block[:half], block[half + PAD :]
        quarter = half // 2
        pieces = [rows_a[:quarter], rows_a[quarter:], rows_b[:quarter], rows_b[quarter:]]
        return jnp.concatenate(pieces[:count], axis=1)[None], pieces[3][None]

    down = chosen(0)
    grad_down = jnp.concatenate([down[:half], down[half + PAD :]], axis=0)[None]
    grad_up, _ = wide(chosen(1), 4)
    last = chosen(2)
    grad_qkv, grad_out = wide(last, 3)
    small = last[half : half + PAD]

    def own(row, count):
        flat = small[row : row + count].reshape(groups, -1)
        return lax.dynamic_index_in_dim(flat, group, 0, keepdims=True)

    def own_pair(row):
        pair = small[row : row + 2].reshape(2, groups, -1)
        return lax.dynamic_index_in_dim(pair, group, 1, keepdims=False)[None]

    live_rows = jnp.repeat(live, LEN)[:, None].astype(BF)
    activations = jnp.where(live_rows > 0, saved[0], jnp.zeros_like(saved[0]))[None]
    return (
        activations,
        dx[None],
        grad_qkv,
        own(ROW_QKV, 3),
        grad_out,
        own(ROW_OUT, 1),
        grad_up,
        own(ROW_UP, 4),
        grad_down,
        own(ROW_DOWN, 1),
        own_pair(ROW_GAIN),
        own_pair(ROW_SHIFT),
    )


def solution(mesh):
    rows = P(("group", "replica"))
    stack = P("section")
    return jax.shard_map(
        shards,
        mesh=mesh,
        in_specs=(rows,) * 4 + (stack,) * 10,
        out_specs=(
            P("section", ("group", "replica"), None),
            P("section", ("group", "replica"), None),
            P("section", "group", None),
            P("section", "group"),
            P("section", "group", None),
            P("section", "group"),
            P("section", "group", None),
            P("section", "group"),
            P("section", "group", None),
            P("section", "group"),
            P("section", None, "group"),
            P("section", None, "group"),
        ),
        check_vma=False,
    )
```

```python
import jax
import jax.numpy as jnp
import numpy as np
from jax import lax
from jax.experimental import pallas as pl
from jax.experimental.pallas import tpu as pltpu
from jax.sharding import PartitionSpec as P

HEADS = 20
HEAD_DIM = 32
LEN = 256
MASK_MEAN = 38
CROP_DEV = 2
EPSILON = 1e-05
ROTARY_BASE = 10000.0

BF = jnp.bfloat16
F32 = jnp.float32
NN = (((1,), (0,)), ((), ()))
NT = (((1,), (1,)), ((), ()))
TN = (((0,), (0,)), ((), ()))

PAD = 16
ROW_QKV, ROW_OUT, ROW_UP, ROW_DOWN, ROW_GAIN, ROW_SHIFT = 0, 3, 4, 8, 9, 11

ANY = pl.BlockSpec(memory_space=pl.ANY)
HBM = pl.BlockSpec(memory_space=pltpu.HBM)
VMEM = pl.BlockSpec(memory_space=pltpu.VMEM)
SMEM = pl.BlockSpec(memory_space=pltpu.SMEM)


def shape(dims, dtype):
    return jax.ShapeDtypeStruct(dims, dtype)


def mm(left, right, dims=NN):
    return lax.dot_general(left, right, dims, preferred_element_type=F32)


def unit_rows_of(values):
    centred = values - jnp.mean(values, axis=-1, keepdims=True)
    inverse = lax.rsqrt(jnp.mean(centred * centred, axis=-1, keepdims=True) + EPSILON)
    return centred * inverse, inverse


def norm_back(grad, unit, inverse, gain):
    scaled = grad * gain
    return inverse * (
        scaled
        - jnp.mean(scaled, axis=-1, keepdims=True)
        - unit * jnp.mean(scaled * unit, axis=-1, keepdims=True)
    )


def rotary_tables():
    lane = np.arange(128) % HEAD_DIM
    half = HEAD_DIM // 2
    freq = ROTARY_BASE ** (-(lane % half).astype(np.float64) * (2.0 / HEAD_DIM))
    angles = np.arange(LEN)[:, None] * freq[None, :]
    sign = np.where(lane < half, -1.0, 1.0)[None, :]
    return np.stack([np.cos(angles), np.sin(angles) * sign]).astype(np.float32)


def swap_halves(values):
    lane = lax.broadcasted_iota(jnp.int32, values.shape, 1) % HEAD_DIM
    half = HEAD_DIM // 2
    return jnp.where(
        lane < half,
        pltpu.roll(values, 128 - half, axis=1),
        pltpu.roll(values, half, axis=1),
    )


def head_stack(block, per):
    head = lax.broadcasted_iota(jnp.int32, block.shape, 1) // HEAD_DIM
    return jnp.concatenate(
        [jnp.where(head == h, block, jnp.zeros_like(block)) for h in range(per)], axis=0
    )


class Copies:
    def __init__(self, sems):
        self.sems = sems
        self.used = 0
        self.open = []

    def start(self, src, dst):
        copy = pltpu.make_async_copy(src, dst, self.sems.at[self.used])
        self.used += 1
        copy.start()
        return copy

    def save(self, src, dst):
        self.open.append(self.start(src, dst))

    def finish(self):
        for copy in self.open:
            copy.wait()


def call(kernel, outs, ins, scratch, sems, aliases, name, after=None, limit=60, specs=None, out_specs=None, loose=()):
    count = len(ins)
    in_specs = specs or [
        SMEM if a.ndim == 1 else ANY if any(a is b for b in loose) else HBM for a in ins
    ]
    body = kernel
    if after is not None:
        ins = list(ins) + [after]
        in_specs = in_specs + [ANY]

        def body(*refs):
            kernel(*refs[:count], *refs[count + 1 :])

    return pl.pallas_call(
        body,
        out_shape=outs,
        in_specs=in_specs,
        out_specs=out_specs or [HBM] * len(outs),
        scratch_shapes=scratch + ([pltpu.SemaphoreType.DMA((sems,))] if sems else []),
        input_output_aliases=aliases,
        compiler_params=pltpu.CompilerParams(vmem_limit_bytes=limit << 20),
        name=name,
    )(*ins)


TOKEN = jax.ShapeDtypeStruct((8, 128), F32)


def vmem_like(arr):
    return pltpu.VMEM(arr.shape, arr.dtype)


def forward_kernel(*refs, fresh, section):
    info, live_h, x_h, qkvb_h, outb_h, upb_h, downb_h, gain_h, shift_h, tab_h = refs[:10]
    qkvw_h, outw_h, upw_h, downw_h = refs[10:14]
    refs = refs[14 if fresh else 22 :]
    act_h, y_h, qkv_h, prob_h, mixt_h, mid_h, gp_h, hid_h = refs[:8]
    x_s, qkvb, outb, upb, downb, gain, shift, tab, qkvw, outw, upw, downw = refs[8:20]
    act_s, y_s, qkv_s, prob_s, mixt_s, mid_s, gp_s, hid_s, vt_s, score_s, up_s, sems = refs[20:]
    rows, dim = x_s.shape
    blocks = dim // 128
    parts = upw.shape[1] // dim
    per = 128 // HEAD_DIM

    @pl.when(info[0] == section)
    def _():
        copies = Copies(sems)
        small = [
            copies.start(h, s)
            for h, s in (
                (x_h, x_s),
                (gain_h, gain),
                (shift_h, shift),
                (qkvb_h, qkvb),
                (tab_h, tab),
                (outb_h, outb),
                (upb_h, upb),
                (downb_h, downb),
            )
        ]
        loads = [
            copies.start(h, s)
            for h, s in ((qkvw_h, qkvw), (outw_h, outw), (upw_h, upw), (downw_h, downw))
        ]
        for copy in small:
            copy.wait()
        x = x_s[...].astype(F32)
        unit, _ = unit_rows_of(x)
        normed = (unit * gain[0:1, :] + shift[0:1, :]).astype(BF)
        loads[0].wait()
        for part in range(3):
            cols = slice(part * dim, (part + 1) * dim)
            third = mm(normed, qkvw[:, cols]) + qkvb[:, cols]
            for c in range(rows // LEN):
                crop = slice(c * LEN, (c + 1) * LEN)
                if part == 2:
                    low = third[crop].astype(BF)
                    qkv_s[crop, cols] = low
                    vt_s[c] = low.T
                    continue
                for j in range(blocks):
                    b = third[crop, 128 * j : 128 * j + 128]
                    b = b * tab[0] + swap_halves(b) * tab[1]
                    if part == 0:
                        b = b * HEAD_DIM**-0.5
                    at = part * dim + 128 * j
                    qkv_s[crop, at : at + 128] = b.astype(BF)
        copies.save(qkv_s, qkv_h)
        for c in range(rows // LEN):
            crop = slice(c * LEN, (c + 1) * LEN)
            for j in range(blocks):
                q = qkv_s[crop, 128 * j : 128 * j + 128]
                k = qkv_s[crop, dim + 128 * j : dim + 128 * j + 128]
                score_s[per * LEN * j : per * LEN * (j + 1), :] = mm(head_stack(k, per), q, NT)

            def soft(h, _):
                s = score_s[pl.ds(pl.multiple_of(h * LEN, LEN), LEN), :]
                e = jnp.exp(s - jnp.max(s, axis=0, keepdims=True))
                prob_s[c * HEADS + h] = (e * (1.0 / jnp.sum(e, axis=0, keepdims=True))).astype(BF)
                return 0

            lax.fori_loop(0, HEADS, soft, 0, unroll=2)
            copies.save(
                prob_s.at[pl.ds(c * HEADS, HEADS)], prob_h.at[pl.ds(c * HEADS, HEADS)]
            )
            for h in range(HEADS):
                at = slice(HEAD_DIM * h, HEAD_DIM * (h + 1))
                mixt_s[at, crop] = mm(vt_s[c, at, :], prob_s[c * HEADS + h]).astype(BF)
        copies.save(mixt_s, mixt_h)
        loads[1].wait()
        mid = x + mm(mixt_s[...], outw[...], TN) + outb[...]
        mid_s[...] = mid
        copies.save(mid_s, mid_h)
        unit, _ = unit_rows_of(mid)
        normed = (unit * gain[1:2, :] + shift[1:2, :]).astype(BF)
        loads[2].wait()
        for c in range(parts):
            cols = slice(c * dim, (c + 1) * dim)
            up_s[c] = mm(normed, upw[:, cols]) + upb[:, cols]
        for c in range(parts):
            u = up_s[c]
            cdf = 0.5 + 0.5 * lax.erf(u * 0.5**0.5)
            hid_s[c] = (u * cdf).astype(BF)
            gp_s[c] = (cdf + u * (jnp.exp(u * u * -0.5) * (2 * np.pi) ** -0.5)).astype(BF)
            copies.save(hid_s.at[c], hid_h.at[c])
            copies.save(gp_s.at[c], gp_h.at[c])
        loads[3].wait()
        out = mid + downb[...]
        for c in range(parts):
            out = out + mm(hid_s[c], downw[c * dim : (c + 1) * dim, :])
        low = out.astype(BF)
        y_s[...] = low
        copies.save(y_s, y_h)
        crop = lax.broadcasted_iota(jnp.int32, (rows, 1), 0) // LEN
        act_s[...] = jnp.where(crop < live_h[0], low, jnp.zeros_like(low))
        copies.save(act_s, act_h)
        copies.finish()


def forward(section, info, live, x, params, tab, before):
    qkvw, qkvb, outw, outb, upw, upb, downw, downb, gain, shift = params
    rows, dim = x.shape
    crops = rows // LEN
    parts = upw.shape[1] // dim
    outs = [
        shape((rows, dim), BF),
        shape((rows, dim), BF),
        shape((rows, 3 * dim), BF),
        shape((crops * HEADS, LEN, LEN), BF),
        shape((dim, rows), BF),
        shape((rows, dim), F32),
        shape((parts, rows, dim), BF),
        shape((parts, rows, dim), BF),
    ]
    ins = [x, qkvb, outb, upb, downb, gain, shift, tab, qkvw, outw, upw, downw]
    scratch = [vmem_like(a) for a in ins + outs]
    scratch += [
        pltpu.VMEM((crops, dim, LEN), BF),
        pltpu.VMEM((HEADS * LEN, LEN), F32),
        pltpu.VMEM((parts, rows, dim), F32),
    ]
    fresh = before is None
    ins = [info, live] + ins + ([] if fresh else list(before))

    def kernel(*refs):
        forward_kernel(*refs, fresh=fresh, section=section)

    aliases = {} if fresh else {14 + i: i for i in range(8)}
    return call(kernel, outs, ins, scratch, 48, aliases, "layer_forward", limit=57, loose=[x])


def gradient_rows(g, live, masks, section):
    grad = g.astype(F32)
    if section == 0:
        return grad
    crop = lax.broadcasted_iota(jnp.int32, (g.shape[0], 1), 0) // LEN
    weight = jnp.zeros_like(crop)
    for c in range(CROP_DEV):
        weight = jnp.where(crop == c, masks[c], weight)
    weight = jnp.where(crop < live[0], weight, 0)
    return grad * (weight.astype(F32) / MASK_MEAN)


def place(copies, info, block, pieces, bufs):
    send_a, keep_a, send_b, keep_b = bufs
    half_rows = send_b.shape[0] // 2
    waits = []
    for src_row, count, shard, half, at in pieces:
        x, y = shard % 2, shard // 2
        own, index, keep, send = (
            (info[1] == x, y, keep_a, send_a) if half == 0 else (info[2] == y, x, keep_b, send_b)
        )
        src = block.at[pl.ds(src_row, count)]
        dst = pl.ds(index * half_rows + at, count)
        sem = copies.sems.at[copies.used]
        copies.used += 1

        @pl.when(own)
        def _():
            pltpu.make_async_copy(src, keep.at[dst], sem).start()

        @pl.when(jnp.logical_not(own))
        def _():
            pltpu.make_async_copy(src, send.at[dst], sem).start()

        waits.append(pltpu.make_async_copy(src, keep.at[dst], sem))
    copies.open += waits


def buffer_shapes(dim):
    return [
        shape((dim + PAD, dim), BF),
        shape((dim + PAD, dim), BF),
        shape((dim, dim), BF),
        shape((dim, dim), BF),
    ]


def down_kernel(*refs, fresh, section):
    info, live, masks, g_h, hid_h = refs[:5]
    refs = refs[5 if fresh else 9 :]
    bufs = refs[:4]
    g_s, hid_s, block_s, sems = refs[5:]
    parts, rows, dim = hid_s.shape

    @pl.when(info[0] == section)
    def _():
        copies = Copies(sems)
        load = copies.start(g_h, g_s)
        loads = [copies.start(hid_h.at[c], hid_s.at[c]) for c in range(parts)]
        load.wait()
        low = gradient_rows(g_s[...], live, masks, section).astype(BF)
        for c in range(parts):
            loads[c].wait()
            block_s[c] = mm(hid_s[c], low, TN).astype(BF)
            half = dim // 2
            place(copies, info, block_s.at[c], [(0, half, c, 0, 0), (half, half, c, 1, 0)], bufs)
        copies.finish()


def down_grad(section, info, live, masks, g, saved, before, after):
    hid = saved[7]
    parts, rows, dim = hid.shape
    fresh = before is None
    ins = [info, live, masks, g, hid] + ([] if fresh else list(before))

    def kernel(*refs):
        down_kernel(*refs, fresh=fresh, section=section)

    scratch = [vmem_like(g), vmem_like(hid), pltpu.VMEM((parts, dim, dim), BF)]
    aliases = {} if fresh else {5 + i: i for i in range(4)}
    out = call(kernel, buffer_shapes(dim) + [TOKEN], ins, scratch, 16, aliases, "down_grad", after, 57, loose=[g])
    return out[:4], out[4]


def up_kernel(*refs, fresh, section):
    info, live, masks, g_h, mid_h, gp_h, gain_h, shift_h, downw_h, upw_h = refs[:10]
    refs = refs[10 if fresh else 14 :]
    bufs = refs[:4]
    gmid_h, small_h = refs[4:6]
    g_s, mid_s, gp_s, gain, shift, downw, upw = refs[7:14]
    gu_s, block_s, gmid_s, small_s, sems = refs[14:]
    parts, rows, dim = gp_s.shape

    @pl.when(info[0] == section)
    def _():
        copies = Copies(sems)
        loads = [
            copies.start(h, s)
            for h, s in (
                (g_h, g_s),
                (mid_h, mid_s),
                (gain_h, gain),
                (shift_h, shift),
                (downw_h, downw),
                (gp_h, gp_s),
                (upw_h, upw),
            )
        ]
        for copy in loads[:4]:
            copy.wait()
        grad = gradient_rows(g_s[...], live, masks, section)
        low = grad.astype(BF)
        small_s[...] = jnp.zeros_like(small_s)
        small_s[ROW_DOWN : ROW_DOWN + 1, :] = jnp.sum(low.astype(F32), axis=0, keepdims=True)
        unit, inverse = unit_rows_of(mid_s[...])
        normed_t = (unit * gain[1:2, :] + shift[1:2, :]).astype(BF).T
        for copy in loads[4:6]:
            copy.wait()
        for c in range(parts):
            grad_up = mm(low, downw[c * dim : (c + 1) * dim, :], NT) * gp_s[c].astype(F32)
            grad_up = grad_up.astype(BF)
            gu_s[c] = grad_up
            small_s[ROW_UP + c : ROW_UP + c + 1, :] = jnp.sum(
                grad_up.astype(F32), axis=0, keepdims=True
            )
        loads[6].wait()
        back = mm(gu_s[0], upw[:, :dim], NT)
        for c in range(1, parts):
            back = back + mm(gu_s[c], upw[:, c * dim : (c + 1) * dim], NT)
        gmid_s[...] = grad + norm_back(back, unit, inverse, gain[1:2, :])
        copies.save(gmid_s, gmid_h)
        small_s[ROW_GAIN + 1 : ROW_GAIN + 2, :] = jnp.sum(back * unit, axis=0, keepdims=True)
        small_s[ROW_SHIFT + 1 : ROW_SHIFT + 2, :] = jnp.sum(back, axis=0, keepdims=True)
        copies.save(small_s, small_h)
        count = dim // parts
        for c in range(parts):
            block_s[c] = mm(normed_t, gu_s[c]).astype(BF)
            place(
                copies,
                info,
                block_s.at[c],
                [(s * count, count, s, c // 2, (c % 2) * count) for s in range(parts)],
                bufs,
            )
        copies.finish()


def up_grad(section, info, live, masks, g, saved, params, before, after):
    mid, gp = saved[5], saved[6]
    upw, downw, gain, shift = params[4], params[6], params[8], params[9]
    parts, rows, dim = gp.shape
    fresh = before is None
    ins = [g, mid, gp, gain, shift, downw, upw]
    scratch = [vmem_like(a) for a in ins] + [
        pltpu.VMEM((parts, rows, dim), BF),
        pltpu.VMEM((parts, dim, dim), BF),
        pltpu.VMEM((rows, dim), F32),
        pltpu.VMEM((PAD, dim), F32),
    ]
    ins = [info, live, masks] + ins + ([] if fresh else list(before))

    def kernel(*refs):
        up_kernel(*refs, fresh=fresh, section=section)

    aliases = {} if fresh else {10 + i: i for i in range(4)}
    outs = buffer_shapes(dim) + [shape((rows, dim), F32), shape((PAD, dim), F32), TOKEN]
    out = call(kernel, outs, ins, scratch, 40, aliases, "up_grad", after, 57, loose=[g])
    return out[:4], out[4], out[5], out[6]


def attention_kernel(*refs, fresh, section):
    (info, gmid_h, small_h, x_h, qkv_h, prob_h, mixt_h, gain_h, shift_h, tab_h, outw_h, qkvw_h) = (
        refs[:12]
    )
    refs = refs[12 if fresh else 13 :]
    dx_h = refs[0]
    bufs = refs[1:5]
    gmid_s, small_s, x_s, qkv_s, prob_s, mixt_s, gain, shift, tab, outw, qkvw = refs[6:17]
    dx_s, low_s, gm_s, gmt_s, delta_s, da_s, ds_s, gqkv_s, dqt_s, block_s, tail_s, sems = refs[17:]
    rows, dim = x_s.shape
    blocks = dim // 128
    per = 128 // HEAD_DIM

    @pl.when(info[0] == section)
    def _():
        copies = Copies(sems)
        loads = [
            copies.start(h, s)
            for h, s in (
                (gmid_h, gmid_s),
                (outw_h, outw),
                (qkv_h, qkv_s),
                (mixt_h, mixt_s),
                (prob_h, prob_s),
                (small_h, small_s),
                (x_h, x_s),
                (gain_h, gain),
                (shift_h, shift),
                (tab_h, tab),
                (qkvw_h, qkvw),
            )
        ]
        loads[0].wait()
        low = gmid_s[...].astype(BF)
        low_s[...] = low
        loads[1].wait()
        gm_s[...] = mm(low, outw[...], NT).astype(BF)
        gmt_s[...] = mm(outw[...], low, NT).astype(BF)
        for copy in loads[2:5]:
            copy.wait()
        for c in range(rows // LEN):
            crop = slice(c * LEN, (c + 1) * LEN)
            product = gmt_s[:, crop].astype(F32) * mixt_s[:, crop].astype(F32)
            delta_s[...] = jnp.sum(product.reshape(HEADS, HEAD_DIM, LEN), axis=1)[:, None, :]
            for j in range(blocks):
                v = qkv_s[crop, 2 * dim + 128 * j : 2 * dim + 128 * j + 128]
                da_s[per * LEN * j : per * LEN * (j + 1), :] = mm(
                    head_stack(v, per), gmt_s[128 * j : 128 * j + 128, crop]
                )

            def scores(h, _):
                da = da_s[pl.ds(pl.multiple_of(h * LEN, LEN), LEN), :]
                ds_s[h] = (prob_s[c * HEADS + h].astype(F32) * (da - delta_s[h])).astype(BF)
                return 0

            lax.fori_loop(0, HEADS, scores, 0, unroll=2)
            kt = qkv_s[crop, dim : 2 * dim].T
            for h in range(HEADS):
                at = slice(HEAD_DIM * h, HEAD_DIM * (h + 1))
                dqt_s[at, :] = mm(kt[at, :], ds_s[h])
            if c == 0:
                for copy in loads[5:]:
                    copy.wait()
            for j in range(blocks):
                heads = range(per * j, per * (j + 1))
                ps = jnp.concatenate([prob_s[c * HEADS + h] for h in heads], axis=1)
                dss = jnp.concatenate([ds_s[h] for h in heads], axis=1)
                cols = slice(128 * j, 128 * j + 128)
                gqkv_s[crop, 2 * dim + 128 * j : 2 * dim + 128 * j + 128] = mm(
                    ps, head_stack(gm_s[crop, cols], per)
                ).astype(BF)
                dk = mm(dss, head_stack(qkv_s[crop, cols], per))
                dk = dk * tab[0] - swap_halves(dk) * tab[1]
                gqkv_s[crop, dim + 128 * j : dim + 128 * j + 128] = dk.astype(BF)
                dq = dqt_s[cols, :].T * HEAD_DIM**-0.5
                dq = dq * tab[0] - swap_halves(dq) * tab[1]
                gqkv_s[crop, cols] = dq.astype(BF)
        back = mm(gqkv_s[...], qkvw[...], NT)
        unit, inverse = unit_rows_of(x_s[...].astype(F32))
        dx_s[...] = (gmid_s[...] + norm_back(back, unit, inverse, gain[0:1, :])).astype(BF)
        copies.save(dx_s, dx_h)
        small_s[ROW_GAIN : ROW_GAIN + 1, :] = jnp.sum(back * unit, axis=0, keepdims=True)
        small_s[ROW_SHIFT : ROW_SHIFT + 1, :] = jnp.sum(back, axis=0, keepdims=True)
        small_s[ROW_OUT : ROW_OUT + 1, :] = jnp.sum(
            low_s[...].astype(F32), axis=0, keepdims=True
        )
        normed_t = (unit * gain[0:1, :] + shift[0:1, :]).astype(BF).T
        parts = 4
        count = dim // parts
        for c in range(parts):
            if c < 3:
                third = gqkv_s[:, c * dim : (c + 1) * dim]
                small_s[ROW_QKV + c : ROW_QKV + c + 1, :] = jnp.sum(
                    third.astype(F32), axis=0, keepdims=True
                )
                block_s[c] = mm(normed_t, third).astype(BF)
            else:
                block_s[c] = mm(mixt_s[...], low_s[...]).astype(BF)
            place(
                copies,
                info,
                block_s.at[c],
                [(s * count, count, s, c // 2, (c % 2) * count) for s in range(parts)],
                bufs,
            )
        tail_s[...] = small_s[...].astype(BF)
        copies.save(tail_s, bufs[0].at[pl.ds(dim, PAD)])
        copies.save(tail_s, bufs[1].at[pl.ds(dim, PAD)])
        copies.finish()


def attention_grad(section, info, gmid, small, x, saved, params, tab, before, after):
    _, _, qkv, prob, mixt = saved[:5]
    qkvw, outw, gain, shift = params[0], params[2], params[8], params[9]
    rows, dim = x.shape
    fresh = before is None
    ins = [gmid, small, x, qkv, prob, mixt, gain, shift, tab, outw, qkvw]
    scratch = [vmem_like(a) for a in ins] + [
        pltpu.VMEM((rows, dim), BF),
        pltpu.VMEM((rows, dim), BF),
        pltpu.VMEM((rows, dim), BF),
        pltpu.VMEM((dim, rows), BF),
        pltpu.VMEM((HEADS, 1, LEN), F32),
        pltpu.VMEM((HEADS * LEN, LEN), F32),
        pltpu.VMEM((HEADS, LEN, LEN), BF),
        pltpu.VMEM((rows, 3 * dim), BF),
        pltpu.VMEM((dim, LEN), F32),
        pltpu.VMEM((4, dim, dim), BF),
        pltpu.VMEM((PAD, dim), BF),
    ]
    ins = [info] + ins + ([] if fresh else [before])

    def kernel(*refs):
        attention_kernel(*refs, fresh=fresh, section=section)

    aliases = {} if fresh else {12: 0}
    outs = [shape((rows, dim), BF)] + buffer_shapes(dim) + [TOKEN]
    out = call(kernel, outs, ins, scratch, 40, aliases, "attention_grad", after, 57, loose=[x])
    return out[0], out[1:5], out[5]


def plus(one, two):
    return (one.astype(F32) + two.astype(F32)).astype(BF)


def taking_part(info, sections, middle):
    check = None
    if len(sections) == 1:
        check = info[0] == sections[0]
    if middle:
        inner = jnp.logical_or(info[3] == 1, info[3] == 2)
        check = inner if check is None else jnp.logical_and(check, inner)
    return info[3] >= 0 if check is None else check


def vmem_call(kernel, outs, info, ins, name, after):
    return call(
        kernel,
        outs,
        [info] + ins,
        [],
        0,
        {},
        name,
        after,
        8,
        [SMEM] + [VMEM] * len(ins),
        [VMEM] * len(outs),
    )


def first_sum(info, sections, keep_a, recv_a, keep_b, recv_b, after):
    dim = keep_b.shape[1]
    half = dim // 2

    def kernel(info, ka, ra, kb, rb, sa, na, sb, nb):
        @pl.when(taking_part(info, sections, False))
        def _():
            for own, one, two, new, out in ((info[2], ka, ra, na, sa), (info[1], kb, rb, nb, sb)):
                mine = pl.ds(pl.multiple_of(own * half, half), half)
                other = pl.ds(pl.multiple_of((1 - own) * half, half), half)
                out[:half, :] = plus(one[other, :], two[other, :])
                new[:half, :] = plus(one[mine, :], two[mine, :])
                if one.shape[0] > 2 * half:
                    tail = plus(one[2 * half :, :], two[2 * half :, :])
                    new[half:, :] = tail
                    out[half:, :] = tail

    outs = [shape((half + PAD, dim), BF)] * 2 + [shape((half, dim), BF)] * 2
    return vmem_call(kernel, outs, info, [keep_a, recv_a, keep_b, recv_b], "first_sum", after)


def second_sum(info, sections, keep_a, recv_a, keep_b, recv_b, after):
    dim = keep_b.shape[1]

    def kernel(info, ka, ra, kb, rb, out):
        @pl.when(taking_part(info, sections, False))
        def _():
            top = ka.shape[0]
            out[:top, :] = plus(ka[...], ra[...])
            out[top:, :] = plus(kb[...], rb[...])

    outs = [shape((dim + PAD, dim), BF)]
    return vmem_call(kernel, outs, info, [keep_a, recv_a, keep_b, recv_b], "second_sum", after)[0]


def pair_sum(info, sections, one, two, after):
    def kernel(info, one, two, out):
        @pl.when(taking_part(info, sections, True))
        def _():
            out[...] = plus(one[...], two[...])

    return vmem_call(kernel, [shape(one.shape, BF)], info, [one, two], "pair_sum", after)[0]


def finish(info, sources, wide, after):
    (part0, got0), (part1, got1) = sources
    rows, dim = part0.shape
    half = dim // 2
    quarter = half // 2
    if wide == 0:
        outs = [shape((dim, dim), F32)]
    elif wide == 4:
        outs = [shape((quarter, 4 * dim), F32)]
    else:
        outs = [shape((quarter, 3 * dim), F32), shape((quarter, dim), F32), shape((PAD, dim), F32)]

    def kernel(info, p0, g0, p1, g1, *refs):
        out_h = refs[: len(outs)]
        src = refs[len(outs)]
        stage = refs[len(outs) + 1 : -1]
        sems = refs[-1]
        inner = jnp.logical_or(info[3] == 1, info[3] == 2)
        for section, part, got in ((0, p0, g0), (1, p1, g1)):
            mine = info[0] == section

            @pl.when(jnp.logical_and(mine, inner))
            def _():
                pltpu.make_async_copy(part, src, sems.at[0]).start()

            @pl.when(jnp.logical_and(mine, jnp.logical_not(inner)))
            def _():
                pltpu.make_async_copy(got, src, sems.at[0]).start()

        pltpu.make_async_copy(p0, src, sems.at[0]).wait()
        block_a = src[:half, :].astype(F32)
        block_b = src[half + PAD :, :].astype(F32)
        if wide == 0:
            stage[0][:half, :] = block_a
            stage[0][half:, :] = block_b
        else:
            pieces = (block_a[:quarter], block_a[quarter:], block_b[:quarter], block_b[quarter:])
            for i in range(wide):
                stage[0][:, i * dim : (i + 1) * dim] = pieces[i]
            if wide == 3:
                stage[1][...] = pieces[3]
                stage[2][...] = src[half : half + PAD, :].astype(F32)
        copies = [
            pltpu.make_async_copy(s, o, sems.at[1 + i]) for i, (s, o) in enumerate(zip(stage, out_h))
        ]
        for copy in copies:
            copy.start()
        for copy in copies:
            copy.wait()

    scratch = [vmem_like(part0)] + [vmem_like(o) for o in outs]
    return call(
        kernel, outs, [info, part0, got0, part1, got1], scratch, 4, {}, "finish", after, 12, loose=[part0, got0, part1, got1]
    )


def flow(shard, axis, pairs, sections):
    if sections == (0, 1):
        return lax.ppermute(shard, axis, pairs)
    peers = lax.axis_size(axis)
    pairs = [(s * peers + i, s * peers + j) for s in sections for i, j in pairs]
    return lax.ppermute(shard, ("section", axis), pairs)


class Reduction:
    def __init__(self, info, sections, bufs):
        self.info, self.sections, self.bufs = info, sections, bufs
        groups = range(lax.axis_size("group"))
        self.across = [(g, g ^ 1) for g in groups]
        self.along = [(g, g ^ 2) for g in groups]
        self.line = lax.axis_size("replica") == 4
        self.got = (
            flow(bufs[0], "group", self.across, sections),
            flow(bufs[2], "group", self.along, sections),
        )

    def group_two(self, after):
        send_a, keep_a, send_b, keep_b = first_sum(
            self.info, self.sections, self.bufs[1], self.got[0], self.bufs[3], self.got[1], after
        )
        self.kept = (keep_a, keep_b)
        self.got = (
            flow(send_a, "group", self.along, self.sections),
            flow(send_b, "group", self.across, self.sections),
        )
        return keep_a

    def replica_one(self, after):
        self.part = second_sum(
            self.info, self.sections, self.kept[0], self.got[0], self.kept[1], self.got[1], after
        )
        if self.line:
            self.got = flow(self.part, "replica", [(0, 1), (3, 2)], self.sections)
        else:
            self.part = self.got = lax.psum(self.part, "replica")
        return self.part

    def replica_next(self, pairs, after):
        if self.line:
            self.part = pair_sum(self.info, self.sections, self.part, self.got, after)
            self.got = flow(self.part, "replica", pairs, self.sections)
        return self.part

    def replica_two(self, after):
        return self.replica_next([(1, 2), (2, 1)], after)

    def replica_three(self, after):
        return self.replica_next([(1, 0), (2, 3)], after)


def shards(
    block_input,
    cotangent,
    crop_count,
    mask_count,
    qkv_weight,
    qkv_bias,
    out_weight,
    out_bias,
    up_weight,
    up_bias,
    down_weight,
    down_bias,
    norm_gain,
    norm_shift,
):
    params = (
        qkv_weight[0],
        qkv_bias,
        out_weight[0],
        out_bias,
        up_weight[0],
        up_bias,
        down_weight[0],
        down_bias,
        norm_gain[0],
        norm_shift[0],
    )
    rows, dim = block_input.shape
    tab = jnp.asarray(rotary_tables())
    group = lax.axis_index("group")
    groups = lax.axis_size("group")
    info = jnp.stack([lax.axis_index("section"), group % 2, group // 2, lax.axis_index("replica")])

    def to_other(shard, pairs):
        return lax.ppermute(shard, "section", pairs)

    saved = forward(0, info, crop_count, block_input, params, tab, None)
    arrived = to_other(saved[1], [(0, 1)])
    saved = forward(1, info, crop_count, arrived, params, tab, saved)

    common = (info, crop_count, mask_count)
    bufs, last = down_grad(1, *common, cotangent, saved, None, None)
    one = Reduction(info, (1,), bufs)
    bufs_two, gmid, small, last = up_grad(1, *common, cotangent, saved, params, None, last)
    last = one.group_two(last)
    dx, bufs_three, last = attention_grad(
        1, info, gmid, small, arrived, saved, params, tab, None, last
    )
    grad_back = to_other(dx, [(1, 0)])
    last = one.replica_one(last)
    bufs, last = down_grad(0, *common, grad_back, saved, bufs_two, last)
    two = Reduction(info, (0, 1), bufs)
    bufs, gmid, small, last = up_grad(0, *common, grad_back, saved, params, bufs_three, last)
    three = Reduction(info, (0, 1), bufs)
    last = one.replica_two(last)
    last = two.group_two(last)
    last = one.replica_three(last)
    dx, bufs, last = attention_grad(
        0, info, gmid, small, block_input, saved, params, tab, dx, last
    )
    four = Reduction(info, (0,), bufs)
    last = three.group_two(last)
    last = two.replica_one(last)
    last = four.group_two(last)
    last = three.replica_one(last)
    last = two.replica_two(last)
    last = four.replica_one(last)
    last = three.replica_two(last)
    last = two.replica_three(last)
    last = four.replica_two(last)
    last = three.replica_three(last)
    last = four.replica_three(last)

    def both(zero, one):
        return ((zero.part, zero.got), (one.part, one.got))

    (grad_down,) = finish(info, both(two, one), 0, last)
    (grad_up,) = finish(info, both(three, two), 4, grad_down)
    grad_qkv, grad_out, small = finish(info, both(four, three), 3, grad_up)

    def own(row, count):
        flat = small[row : row + count].reshape(groups, -1)
        return lax.dynamic_index_in_dim(flat, group, 0, keepdims=True)

    def own_pair(row):
        pair = small[row : row + 2].reshape(2, groups, -1)
        return lax.dynamic_index_in_dim(pair, group, 1, keepdims=False)[None]

    return (
        saved[0][None],
        dx[None],
        grad_qkv[None],
        own(ROW_QKV, 3),
        grad_out[None],
        own(ROW_OUT, 1),
        grad_up[None],
        own(ROW_UP, 4),
        grad_down[None],
        own(ROW_DOWN, 1),
        own_pair(ROW_GAIN),
        own_pair(ROW_SHIFT),
    )


def solution(mesh):
    rows = P(("group", "replica"))
    stack = P("section")
    return jax.shard_map(
        shards,
        mesh=mesh,
        in_specs=(rows,) * 4 + (stack,) * 10,
        out_specs=(
            P("section", ("group", "replica"), None),
            P("section", ("group", "replica"), None),
            P("section", "group", None),
            P("section", "group"),
            P("section", "group", None),
            P("section", "group"),
            P("section", "group", None),
            P("section", "group"),
            P("section", "group", None),
            P("section", "group"),
            P("section", None, "group"),
            P("section", None, "group"),
        ),
        check_vma=False,
    )
```

```python
import jax
import jax.numpy as jnp
import numpy as np
from jax import lax
from jax.experimental import pallas as pl
from jax.experimental.pallas import tpu as pltpu
from jax.sharding import PartitionSpec as P

HEADS = 20
HEAD_DIM = 32
LEN = 256
MASK_MEAN = 38
CROP_DEV = 2
EPSILON = 1e-05
ROTARY_BASE = 10000.0

BF = jnp.bfloat16
F32 = jnp.float32
NN = (((1,), (0,)), ((), ()))
NT = (((1,), (1,)), ((), ()))
TN = (((0,), (0,)), ((), ()))

LIMIT_FIRST = 60
COST = 1024
LIMIT = 57
PAD = 16
ROW_QKV, ROW_OUT, ROW_UP, ROW_DOWN, ROW_GAIN, ROW_SHIFT = 0, 3, 4, 8, 9, 11

ANY = pl.BlockSpec(memory_space=pl.ANY)
HBM = pl.BlockSpec(memory_space=pltpu.HBM)
VMEM = pl.BlockSpec(memory_space=pltpu.VMEM)
SMEM = pl.BlockSpec(memory_space=pltpu.SMEM)


def shape(dims, dtype):
    return jax.ShapeDtypeStruct(dims, dtype)


def mm(left, right, dims=NN):
    return lax.dot_general(left, right, dims, preferred_element_type=F32)


def unit_rows_of(values):
    centred = values - jnp.mean(values, axis=-1, keepdims=True)
    inverse = lax.rsqrt(jnp.mean(centred * centred, axis=-1, keepdims=True) + EPSILON)
    return centred * inverse, inverse


def norm_back(grad, unit, inverse, gain):
    scaled = grad * gain
    return inverse * (
        scaled
        - jnp.mean(scaled, axis=-1, keepdims=True)
        - unit * jnp.mean(scaled * unit, axis=-1, keepdims=True)
    )


def rotary_tables():
    lane = np.arange(128) % HEAD_DIM
    half = HEAD_DIM // 2
    freq = ROTARY_BASE ** (-(lane % half).astype(np.float64) * (2.0 / HEAD_DIM))
    angles = np.arange(LEN)[:, None] * freq[None, :]
    sign = np.where(lane < half, -1.0, 1.0)[None, :]
    return np.stack([np.cos(angles), np.sin(angles) * sign]).astype(np.float32)


def rotary_columns():
    half = HEAD_DIM // 2
    freq = ROTARY_BASE ** (-np.arange(half, dtype=np.float64) * (2.0 / HEAD_DIM))
    angles = freq[:, None] * np.arange(LEN)[None, :]
    return np.stack([np.cos(angles), np.sin(angles)]).astype(np.float32)


def swap_halves(values):
    lane = lax.broadcasted_iota(jnp.int32, values.shape, 1) % HEAD_DIM
    half = HEAD_DIM // 2
    return jnp.where(
        lane < half,
        pltpu.roll(values, 128 - half, axis=1),
        pltpu.roll(values, half, axis=1),
    )


def head_stack(block, per):
    head = lax.broadcasted_iota(jnp.int32, block.shape, 1) // HEAD_DIM
    return jnp.concatenate(
        [jnp.where(head == h, block, jnp.zeros_like(block)) for h in range(per)], axis=0
    )


class Copies:
    def __init__(self, sems):
        self.sems = sems
        self.used = 0
        self.open = []

    def start(self, src, dst):
        copy = pltpu.make_async_copy(src, dst, self.sems.at[self.used])
        self.used += 1
        copy.start()
        return copy

    def save(self, src, dst):
        self.open.append(self.start(src, dst))

    def finish(self):
        for copy in self.open:
            copy.wait()


def call(kernel, outs, ins, scratch, sems, aliases, name, after=None, limit=60, specs=None, out_specs=None, loose=()):
    count = len(ins)
    in_specs = specs or [
        SMEM if a.ndim == 1 else ANY if any(a is b for b in loose) else HBM for a in ins
    ]
    body = kernel
    if after is not None:
        ins = list(ins) + [after]
        in_specs = in_specs + [ANY]

        def body(*refs):
            kernel(*refs[:count], *refs[count + 1 :])

    return pl.pallas_call(
        body,
        out_shape=outs,
        in_specs=in_specs,
        out_specs=out_specs or [HBM] * len(outs),
        scratch_shapes=scratch + ([pltpu.SemaphoreType.DMA((sems,))] if sems else []),
        input_output_aliases=aliases,
        compiler_params=pltpu.CompilerParams(vmem_limit_bytes=limit << 20),
        cost_estimate=pl.CostEstimate(flops=0, bytes_accessed=COST, transcendentals=0),
        name=name,
    )(*ins)


TOKEN = jax.ShapeDtypeStruct((8, 128), F32)


def vmem_like(arr):
    return pltpu.VMEM(arr.shape, arr.dtype)


def forward(slot, info, live, own, arrived, params, tab, act, after=None):
    qkvw, qkvb, outw, outb, upw, upb, downw, downb, gain, shift = params
    dim = own.shape[1]
    blocks = dim // 128
    wide = upw.shape[1]
    parts = wide // dim
    per = 128 // HEAD_DIM
    saved = [
        shape((LEN, dim), BF),
        shape((LEN, 3 * dim), BF),
        shape((HEADS, LEN, LEN), BF),
        shape((dim, LEN), BF),
        shape((LEN, dim), F32),
        shape((LEN, wide), BF),
        shape((LEN, wide), BF),
    ]
    weights = [qkvb, outb, upb, downb, gain, shift, tab, qkvw, outw, upw, downw]
    sources = [own] if slot == 0 else [arrived] if slot == 2 else [own, arrived]
    before = [] if act is None else [act]
    ins = [info, live] + sources + weights + before
    count = len(sources)

    def kernel(info, live, *refs):
        x_hs = refs[:count]
        small_h = refs[count : count + 7]
        large_h = refs[count + 7 : count + 11]
        act_h, *outs = refs[count + 11 + len(before) : count + 19 + len(before)]
        scratch = refs[count + 19 + len(before) :]
        x_s = scratch[0]
        small = scratch[1:8]
        large = scratch[8:12]
        qkvb, outb, upb, downb, gain, shift, tab = small
        qkvw, outw, upw, downw = large
        y_s, qkv_s, prob_s, mixt_s, mid_s, gp_s, hid_s = scratch[12:19]
        act_s, vt_s, score_s, up_s, sems = scratch[19:]
        y_h, qkv_h, prob_h, mixt_h, mid_h, gp_h, hid_h = outs
        crop = slot - info[0]

        @pl.when(jnp.logical_and(crop >= 0, crop < CROP_DEV))
        def _():
            copies = Copies(sems)
            sem = copies.sems.at[copies.used]
            copies.used += 1
            mine = x_hs[0].at[pl.ds(slot * LEN, LEN)] if slot < 2 else x_hs[0]
            if slot == 1:

                @pl.when(info[0] == 0)
                def _():
                    pltpu.make_async_copy(mine, x_s, sem).start()

                @pl.when(info[0] != 0)
                def _():
                    pltpu.make_async_copy(x_hs[1], x_s, sem).start()

            else:
                pltpu.make_async_copy(mine, x_s, sem).start()
            loads = [copies.start(h, s) for h, s in zip(small_h, small)]
            heavy = [copies.start(h, s) for h, s in zip(large_h, large)]
            pltpu.make_async_copy(mine, x_s, sem).wait()
            for copy in loads:
                copy.wait()
            x = x_s[...].astype(F32)
            unit, _ = unit_rows_of(x)
            normed = (unit * gain[0:1, :] + shift[0:1, :]).astype(BF)
            heavy[0].wait()
            third = mm(normed, qkvw[:, 2 * dim :]) + qkvb[:, 2 * dim :]
            low = third.astype(BF)
            qkv_s[:, 2 * dim :] = low
            vt_s[...] = low.T
            for part in range(2):
                third = mm(normed, qkvw[:, part * dim : (part + 1) * dim])
                third = third + qkvb[:, part * dim : (part + 1) * dim]
                for j in range(blocks):
                    b = third[:, 128 * j : 128 * j + 128]
                    b = b * tab[0] + swap_halves(b) * tab[1]
                    if part == 0:
                        b = b * HEAD_DIM**-0.5
                    at = part * dim + 128 * j
                    qkv_s[:, at : at + 128] = b.astype(BF)
            copies.save(qkv_s, qkv_h)
            for j in range(blocks):
                q = qkv_s[:, 128 * j : 128 * j + 128]
                k = qkv_s[:, dim + 128 * j : dim + 128 * j + 128]
                score_s[per * LEN * j : per * LEN * (j + 1), :] = mm(head_stack(k, per), q, NT)

            def soft(h, _):
                s = score_s[pl.ds(pl.multiple_of(h * LEN, LEN), LEN), :]
                e = jnp.exp(s - jnp.max(s, axis=0, keepdims=True))
                prob_s[h] = (e * (1.0 / jnp.sum(e, axis=0, keepdims=True))).astype(BF)
                return 0

            lax.fori_loop(0, HEADS, soft, 0, unroll=2)
            copies.save(prob_s, prob_h)
            for h in range(HEADS):
                at = slice(HEAD_DIM * h, HEAD_DIM * (h + 1))
                mixt_s[at, :] = mm(vt_s[at, :], prob_s[h]).astype(BF)
            copies.save(mixt_s, mixt_h)
            heavy[1].wait()
            mid = x + mm(mixt_s[...], outw[...], TN) + outb[...]
            mid_s[...] = mid
            copies.save(mid_s, mid_h)
            unit, _ = unit_rows_of(mid)
            normed = (unit * gain[1:2, :] + shift[1:2, :]).astype(BF)
            heavy[2].wait()
            up_s[...] = mm(normed, upw[...])
            for c in range(parts):
                cols = slice(c * dim, (c + 1) * dim)
                u = up_s[:, cols] + upb[:, cols]
                cdf = 0.5 + 0.5 * lax.erf(u * 0.5**0.5)
                hid_s[:, cols] = (u * cdf).astype(BF)
                gp_s[:, cols] = (
                    cdf + u * (jnp.exp(u * u * -0.5) * (2 * np.pi) ** -0.5)
                ).astype(BF)
            copies.save(gp_s, gp_h)
            copies.save(hid_s, hid_h)
            heavy[3].wait()
            low = (mid_s[...] + downb[...] + mm(hid_s[...], downw[...])).astype(BF)
            y_s[...] = low
            copies.save(y_s, y_h)
            act_s[...] = jnp.where(crop < live[0], low, jnp.zeros_like(low))
            at = pl.multiple_of(crop * LEN, LEN)
            copies.save(act_s, act_h.at[pl.ds(at, LEN)])
            copies.finish()

    outs = [shape(own.shape, BF)] + saved
    scratch = [pltpu.VMEM((LEN, dim), BF)]
    scratch += [vmem_like(a) for a in weights + saved]
    scratch += [
        pltpu.VMEM((LEN, dim), BF),
        pltpu.VMEM((dim, LEN), BF),
        pltpu.VMEM((HEADS * LEN, LEN), F32),
        pltpu.VMEM((LEN, wide), F32),
    ]
    aliases = {} if act is None else {len(ins) - 1: 0}
    out = call(
        kernel,
        outs,
        ins,
        scratch,
        32,
        aliases,
        "layer_forward",
        after,
        LIMIT_FIRST if slot == 0 else LIMIT,
        loose=[a for a in sources if a is not own],
    )
    return out[0], out[1:]


def gradient_rows(g, live, masks, section):
    grad = g.astype(F32)
    if section == 0:
        return grad
    crop = lax.broadcasted_iota(jnp.int32, (g.shape[0], 1), 0) // LEN
    weight = jnp.zeros_like(crop)
    for c in range(CROP_DEV):
        weight = jnp.where(crop == c, masks[c], weight)
    weight = jnp.where(crop < live[0], weight, 0)
    return grad * (weight.astype(F32) / MASK_MEAN)


class Stage:
    def __init__(self, info, stage_a, stage_b, half):
        self.x, self.y = info[1], info[2]
        self.stage_a, self.stage_b, self.half = stage_a, stage_b, half

    def put(self, value, shard, is_b, at):
        x, y = shard % 2, shard // 2
        if is_b:
            stage, keep, index = self.stage_b, self.y == y, x
        else:
            stage, keep, index = self.stage_a, self.x == x, y
        start = index * self.half + at
        stage[keep.astype(jnp.int32), start : start + value.shape[0], :] = value.astype(BF)

    def save(self, copies, bufs, is_b):
        stage, first = (self.stage_b, 2) if is_b else (self.stage_a, 0)
        for kept in range(2):
            copies.save(stage.at[kept], bufs[first + kept])

    @staticmethod
    def scratch(dim):
        return [pltpu.VMEM((2, dim + PAD, dim), BF), pltpu.VMEM((2, dim, dim), BF)]


def buffer_shapes(dim):
    return [shape((dim + PAD, dim), BF)] * 2 + [shape((dim, dim), BF)] * 2


def stacked(arrs, axis):
    dims = list(arrs[0].shape)
    dims[axis] *= len(arrs)
    return pltpu.VMEM(tuple(dims), arrs[0].dtype)


def load_stacked(copies, arrs, scratch, axis):
    waits = []
    for i, arr in enumerate(arrs):
        size = arr.shape[axis]
        at = tuple(
            pl.ds(i * size, size) if d == axis else slice(None) for d in range(len(arr.shape))
        )
        waits.append(copies.start(arr, scratch.at[at]))
    return waits


def wait_all(copies):
    for copy in copies:
        copy.wait()


def down_grad(section, info, live, masks, g, saved, before, after):
    hids = [s[6] for s in saved]
    rows, dim = g.shape
    parts = hids[0].shape[1] // dim
    given = [] if before is None else list(before)
    ins = [info, live, masks, g] + hids + given

    def kernel(info, live, masks, g_h, *refs):
        hid_hs = refs[: len(hids)]
        bufs = refs[len(hids) + len(given) : len(hids) + len(given) + 4]
        g_s, hid_s, stage_a, stage_b, sems = refs[len(hids) + len(given) + 5 :]

        @pl.when(info[0] == section)
        def _():
            copies = Copies(sems)
            load = copies.start(g_h, g_s)
            loads = load_stacked(copies, hid_hs, hid_s, 0)
            load.wait()
            low = gradient_rows(g_s[...], live, masks, section).astype(BF)
            stage = Stage(info, stage_a, stage_b, dim // 2)
            wait_all(loads)
            for c in range(parts):
                block = mm(hid_s[:, c * dim : (c + 1) * dim], low, TN)
                stage.put(block[: dim // 2], c, False, 0)
                stage.put(block[dim // 2 :], c, True, 0)
            stage.save(copies, bufs, False)
            stage.save(copies, bufs, True)
            copies.finish()

    scratch = [vmem_like(g), stacked(hids, 0)] + Stage.scratch(dim)
    aliases = {len(ins) - 4 + i: i for i in range(4)} if given else {}
    outs = buffer_shapes(dim) + [TOKEN]
    out = call(kernel, outs, ins, scratch, 16, aliases, "down_grad", after, LIMIT, loose=[g])
    return out[:4], out[4]


def up_grad(section, info, live, masks, g, saved, params, before, after):
    mids, gps = [s[4] for s in saved], [s[5] for s in saved]
    upw, downw, gain, shift = params[4], params[6], params[8], params[9]
    rows, dim = g.shape
    wide = upw.shape[1]
    parts = wide // dim
    crops = len(saved)
    given = [] if before is None else list(before)
    singles = [g, gain, shift, downw, upw]
    ins = [info, live, masks] + singles + mids + gps + given

    def kernel(info, live, masks, g_h, gain_h, shift_h, downw_h, upw_h, *refs):
        mid_hs, gp_hs = refs[:crops], refs[crops : 2 * crops]
        refs = refs[2 * crops + len(given) :]
        bufs, gmid_h, small_h = refs[:4], refs[4], refs[5]
        g_s, gain, shift, downw, upw, mid_s, gp_s = refs[7:14]
        gu_s, gmid_s, small_s, stage_a, stage_b, sems = refs[14:]

        @pl.when(info[0] == section)
        def _():
            copies = Copies(sems)
            loads = [copies.start(h, s) for h, s in ((g_h, g_s), (gain_h, gain), (shift_h, shift))]
            loads += load_stacked(copies, mid_hs, mid_s, 0)
            first = [copies.start(downw_h, downw)] + load_stacked(copies, gp_hs, gp_s, 0)
            later = copies.start(upw_h, upw)
            wait_all(loads)
            grad = gradient_rows(g_s[...], live, masks, section)
            low = grad.astype(BF)
            small_s[...] = jnp.zeros_like(small_s)
            small_s[ROW_DOWN : ROW_DOWN + 1, :] = jnp.sum(low.astype(F32), axis=0, keepdims=True)
            unit, inverse = unit_rows_of(mid_s[...])
            normed_t = (unit * gain[1:2, :] + shift[1:2, :]).astype(BF).T
            wait_all(first)
            for c in range(parts):
                cols = slice(c * dim, (c + 1) * dim)
                grad_up = mm(low, downw[cols, :], NT) * gp_s[:, cols].astype(F32)
                grad_up = grad_up.astype(BF)
                gu_s[:, cols] = grad_up
                small_s[ROW_UP + c : ROW_UP + c + 1, :] = jnp.sum(
                    grad_up.astype(F32), axis=0, keepdims=True
                )
            later.wait()
            back = mm(gu_s[...], upw[...], NT)
            gmid_s[...] = grad + norm_back(back, unit, inverse, gain[1:2, :])
            copies.save(gmid_s, gmid_h)
            small_s[ROW_GAIN + 1 : ROW_GAIN + 2, :] = jnp.sum(back * unit, axis=0, keepdims=True)
            small_s[ROW_SHIFT + 1 : ROW_SHIFT + 2, :] = jnp.sum(back, axis=0, keepdims=True)
            copies.save(small_s, small_h)
            count = dim // parts
            stage = Stage(info, stage_a, stage_b, dim // 2)
            for c in range(parts):
                block = mm(normed_t, gu_s[:, c * dim : (c + 1) * dim])
                for s in range(parts):
                    stage.put(block[s * count : (s + 1) * count], s, c >= 2, (c % 2) * count)
                if c % 2 == 1:
                    stage.save(copies, bufs, c >= 2)
            copies.finish()

    scratch = [vmem_like(a) for a in singles] + [stacked(mids, 0), stacked(gps, 0)]
    scratch += [
        pltpu.VMEM((rows, wide), BF),
        pltpu.VMEM((rows, dim), F32),
        pltpu.VMEM((PAD, dim), F32),
    ] + Stage.scratch(dim)
    aliases = {len(ins) - 4 + i: i for i in range(4)} if given else {}
    outs = buffer_shapes(dim) + [shape((rows, dim), F32), shape((PAD, dim), F32), TOKEN]
    out = call(kernel, outs, ins, scratch, 32, aliases, "up_grad", after, LIMIT, loose=[g])
    return out[:4], out[4], out[5], out[6]


def rotate_back(block, tab_t):
    half = HEAD_DIM // 2
    cos, sin = tab_t[0], tab_t[1]
    out = []
    for at in range(0, block.shape[0], HEAD_DIM):
        a, b = block[at : at + half], block[at + half : at + HEAD_DIM]
        out += [a * cos + b * sin, b * cos - a * sin]
    return jnp.concatenate(out, axis=0)


def attention_grad(section, info, gmid, small, xs, saved, params, tab_t, before, after):
    qkvs, probs, mixts = [s[1] for s in saved], [s[2] for s in saved], [s[3] for s in saved]
    qkvw, outw, gain, shift = params[0], params[2], params[8], params[9]
    rows, dim = gmid.shape
    blocks = dim // 128
    per = 128 // HEAD_DIM
    crops = len(saved)
    singles = [gmid, outw, small, gain, shift, tab_t, qkvw]
    given = [] if before is None else [before]
    ins = [info] + singles + qkvs + probs + mixts + list(xs) + given
    split = len(xs) > 1

    def kernel(info, gmid_h, outw_h, small_h, gain_h, shift_h, tab_h, qkvw_h, *refs):
        qkv_hs, prob_hs, mixt_hs = (refs[i * crops : (i + 1) * crops] for i in range(3))
        x_hs = refs[3 * crops : 3 * crops + len(xs)]
        refs = refs[3 * crops + len(xs) + len(given) :]
        dx_h, gqkv_h, normt_h, low_h, small_out = refs[:5]
        gmid_s, outw, small_s, gain, shift, tab_t, qkvw, qkv_s, prob_s, mixt_s, x_s = refs[6:17]
        dx_s, low_s, gmt_s, delta_s, da_s, ds_s, gqkv_s, dt_s, normt_s, kt_s, sems = refs[17:]

        @pl.when(info[0] == section)
        def _():
            copies = Copies(sems)
            loads = [copies.start(gmid_h, gmid_s), copies.start(outw_h, outw)]
            early = load_stacked(copies, mixt_hs, mixt_s, 1)
            early += load_stacked(copies, qkv_hs, qkv_s, 0)
            early += load_stacked(copies, prob_hs, prob_s, 0)
            late = [
                copies.start(h, s)
                for h, s in (
                    (small_h, small_s),
                    (gain_h, gain),
                    (shift_h, shift),
                    (tab_h, tab_t),
                    (qkvw_h, qkvw),
                )
            ]
            late += load_stacked(copies, x_hs, x_s, 0)
            wait_all(loads)
            low = gmid_s[...].astype(BF)
            low_s[...] = low
            copies.save(low_s, low_h)
            gmt_s[...] = mm(outw[...], low, NT).astype(BF)
            wait_all(early)
            wait_all(late)
            for c in range(crops):
                crop = slice(c * LEN, (c + 1) * LEN)
                product = gmt_s[:, crop].astype(F32) * mixt_s[:, crop].astype(F32)
                delta_s[...] = jnp.sum(product.reshape(HEADS, HEAD_DIM, LEN), axis=1)[:, None, :]
                kt_s[0] = qkv_s[crop, dim : 2 * dim].T
                kt_s[1] = qkv_s[crop, :dim].T
                for j in range(blocks):
                    v = qkv_s[crop, 2 * dim + 128 * j : 2 * dim + 128 * j + 128]
                    da_s[per * LEN * j : per * LEN * (j + 1), :] = mm(
                        head_stack(v, per), gmt_s[128 * j : 128 * j + 128, crop]
                    )

                def scores(h, _):
                    da = da_s[pl.ds(pl.multiple_of(h * LEN, LEN), LEN), :]
                    ds_s[h] = (prob_s[c * HEADS + h].astype(F32) * (da - delta_s[h])).astype(BF)
                    return 0

                lax.fori_loop(0, HEADS, scores, 0, unroll=2)
                for h in range(HEADS):
                    at = slice(HEAD_DIM * h, HEAD_DIM * (h + 1))
                    dt_s[0, at, :] = mm(kt_s[0, at, :], ds_s[h])
                    dt_s[1, at, :] = mm(kt_s[1, at, :], ds_s[h], NT)
                    dt_s[2, at, :] = mm(gmt_s[at, crop], prob_s[c * HEADS + h], NT)
                dq = rotate_back(dt_s[0] * HEAD_DIM**-0.5, tab_t)
                gqkv_s[crop, :dim] = dq.astype(BF).T
                gqkv_s[crop, dim : 2 * dim] = rotate_back(dt_s[1], tab_t).astype(BF).T
                gqkv_s[crop, 2 * dim :] = dt_s[2].astype(BF).T
            copies.save(gqkv_s, gqkv_h)
            unit, inverse = unit_rows_of(x_s[...].astype(F32))
            normt_s[...] = (unit * gain[0:1, :] + shift[0:1, :]).astype(BF).T
            copies.save(normt_s, normt_h)
            back = mm(gqkv_s[...], qkvw[...], NT)
            dx_s[...] = (gmid_s[...] + norm_back(back, unit, inverse, gain[0:1, :])).astype(BF)
            copies.save(dx_s, dx_h)
            small_s[ROW_GAIN : ROW_GAIN + 1, :] = jnp.sum(back * unit, axis=0, keepdims=True)
            small_s[ROW_SHIFT : ROW_SHIFT + 1, :] = jnp.sum(back, axis=0, keepdims=True)
            copies.save(small_s, small_out)
            copies.finish()

    outs = [
        shape((rows, dim), BF),
        shape((rows, 3 * dim), BF),
        shape((dim, rows), BF),
        shape((rows, dim), BF),
        shape(small.shape, F32),
        TOKEN,
    ]
    scratch = [vmem_like(a) for a in singles]
    scratch += [stacked(qkvs, 0), stacked(probs, 0), stacked(mixts, 1), stacked(xs, 0)]
    scratch += [
        pltpu.VMEM((rows, dim), BF),
        pltpu.VMEM((rows, dim), BF),
        pltpu.VMEM((dim, rows), BF),
        pltpu.VMEM((HEADS, 1, LEN), F32),
        pltpu.VMEM((HEADS * LEN, LEN), F32),
        pltpu.VMEM((HEADS, LEN, LEN), BF),
        pltpu.VMEM((rows, 3 * dim), BF),
        pltpu.VMEM((3, dim, LEN), F32),
        pltpu.VMEM((dim, rows), BF),
        pltpu.VMEM((2, dim, LEN), BF),
    ]
    aliases = {len(ins) - 1: 0} if given else {}
    loose = list(xs) if split else []
    out = call(
        kernel, outs, ins, scratch, 32, aliases, "attention_grad", after, LIMIT, loose=loose
    )
    return out[0], out[1:5], out[5]


def qkv_grad(section, info, kept, saved, after):
    gqkv, normt, low, small = kept
    mixts = [s[3] for s in saved]
    rows, dim = low.shape
    parts = 4
    singles = [gqkv, normt, low, small]
    ins = [info] + singles + mixts

    def kernel(info, gqkv_h, normt_h, low_h, small_h, *refs):
        mixt_hs = refs[: len(mixts)]
        bufs = refs[len(mixts) : len(mixts) + 4]
        gqkv_s, normt_s, low_s, small_s, mixt_s, stage_a, stage_b, sems = refs[len(mixts) + 5 :]

        @pl.when(info[0] == section)
        def _():
            copies = Copies(sems)
            loads = [
                copies.start(h, s)
                for h, s in (
                    (normt_h, normt_s),
                    (gqkv_h, gqkv_s),
                    (low_h, low_s),
                    (small_h, small_s),
                )
            ]
            loads += load_stacked(copies, mixt_hs, mixt_s, 1)
            wait_all(loads)
            stage = Stage(info, stage_a, stage_b, dim // 2)
            count = dim // parts
            for c in range(3):
                small_s[ROW_QKV + c : ROW_QKV + c + 1, :] = jnp.sum(
                    gqkv_s[:, c * dim : (c + 1) * dim].astype(F32), axis=0, keepdims=True
                )
            small_s[ROW_OUT : ROW_OUT + 1, :] = jnp.sum(
                low_s[...].astype(F32), axis=0, keepdims=True
            )
            tail = small_s[...].astype(BF)
            stage_a[0, dim:, :] = tail
            stage_a[1, dim:, :] = tail
            for c in range(parts):
                if c < 3:
                    block = mm(normt_s[...], gqkv_s[:, c * dim : (c + 1) * dim])
                else:
                    block = mm(mixt_s[...], low_s[...])
                for s in range(parts):
                    stage.put(block[s * count : (s + 1) * count], s, c >= 2, (c % 2) * count)
                if c % 2 == 1:
                    stage.save(copies, bufs, c >= 2)
            copies.finish()

    scratch = [vmem_like(a) for a in singles] + [stacked(mixts, 1)] + Stage.scratch(dim)
    outs = buffer_shapes(dim) + [TOKEN]
    out = call(kernel, outs, ins, scratch, 16, {}, "qkv_grad", after, LIMIT)
    return out[:4], out[4]


def plus(one, two):
    return (one.astype(F32) + two.astype(F32)).astype(BF)


def taking_part(info, sections, middle):
    check = None
    if len(sections) == 1:
        check = info[0] == sections[0]
    if middle:
        inner = jnp.logical_or(info[3] == 1, info[3] == 2)
        check = inner if check is None else jnp.logical_and(check, inner)
    return info[3] >= 0 if check is None else check


def vmem_call(kernel, outs, info, ins, name, after):
    return call(
        kernel,
        outs,
        [info] + ins,
        [],
        0,
        {},
        name,
        after,
        8,
        [SMEM] + [VMEM] * len(ins),
        [VMEM] * len(outs),
    )


def first_sum(info, sections, keep_a, recv_a, keep_b, recv_b, after):
    dim = keep_b.shape[1]
    half = dim // 2

    def kernel(info, ka, ra, kb, rb, sa, na, sb, nb):
        @pl.when(taking_part(info, sections, False))
        def _():
            for own, one, two, new, out in ((info[2], ka, ra, na, sa), (info[1], kb, rb, nb, sb)):
                mine = pl.ds(pl.multiple_of(own * half, half), half)
                other = pl.ds(pl.multiple_of((1 - own) * half, half), half)
                out[:half, :] = plus(one[other, :], two[other, :])
                new[:half, :] = plus(one[mine, :], two[mine, :])
                if one.shape[0] > 2 * half:
                    tail = plus(one[2 * half :, :], two[2 * half :, :])
                    new[half:, :] = tail
                    out[half:, :] = tail

    outs = [shape((half + PAD, dim), BF)] * 2 + [shape((half, dim), BF)] * 2
    return vmem_call(kernel, outs, info, [keep_a, recv_a, keep_b, recv_b], "first_sum", after)


def second_sum(info, sections, keep_a, recv_a, keep_b, recv_b, after):
    dim = keep_b.shape[1]

    def kernel(info, ka, ra, kb, rb, out):
        @pl.when(taking_part(info, sections, False))
        def _():
            top = ka.shape[0]
            out[:top, :] = plus(ka[...], ra[...])
            out[top:, :] = plus(kb[...], rb[...])

    outs = [shape((dim + PAD, dim), BF)]
    return vmem_call(kernel, outs, info, [keep_a, recv_a, keep_b, recv_b], "second_sum", after)[0]


def pair_sum(info, sections, one, two, after):
    def kernel(info, one, two, out):
        @pl.when(taking_part(info, sections, True))
        def _():
            out[...] = plus(one[...], two[...])

    return vmem_call(kernel, [shape(one.shape, BF)], info, [one, two], "pair_sum", after)[0]


def finish(info, sources, wide, after):
    (part0, got0), (part1, got1) = sources
    rows, dim = part0.shape
    half = dim // 2
    quarter = half // 2
    if wide == 0:
        outs = [shape((dim, dim), F32)]
    elif wide == 4:
        outs = [shape((quarter, 4 * dim), F32)]
    else:
        outs = [shape((quarter, 3 * dim), F32), shape((quarter, dim), F32), shape((PAD, dim), F32)]

    def kernel(info, p0, g0, p1, g1, *refs):
        out_h = refs[: len(outs)]
        src = refs[len(outs)]
        stage = refs[len(outs) + 1 : -1]
        sems = refs[-1]
        inner = jnp.logical_or(info[3] == 1, info[3] == 2)
        for section, part, got in ((0, p0, g0), (1, p1, g1)):
            mine = info[0] == section

            @pl.when(jnp.logical_and(mine, inner))
            def _():
                pltpu.make_async_copy(part, src, sems.at[0]).start()

            @pl.when(jnp.logical_and(mine, jnp.logical_not(inner)))
            def _():
                pltpu.make_async_copy(got, src, sems.at[0]).start()

        pltpu.make_async_copy(p0, src, sems.at[0]).wait()
        block_a = src[:half, :].astype(F32)
        block_b = src[half + PAD :, :].astype(F32)
        if wide == 0:
            stage[0][:half, :] = block_a
            stage[0][half:, :] = block_b
        else:
            pieces = (block_a[:quarter], block_a[quarter:], block_b[:quarter], block_b[quarter:])
            for i in range(wide):
                stage[0][:, i * dim : (i + 1) * dim] = pieces[i]
            if wide == 3:
                stage[1][...] = pieces[3]
                stage[2][...] = src[half : half + PAD, :].astype(F32)
        copies = [
            pltpu.make_async_copy(s, o, sems.at[1 + i]) for i, (s, o) in enumerate(zip(stage, out_h))
        ]
        for copy in copies:
            copy.start()
        for copy in copies:
            copy.wait()

    scratch = [vmem_like(part0)] + [vmem_like(o) for o in outs]
    return call(
        kernel, outs, [info, part0, got0, part1, got1], scratch, 4, {}, "finish", after, LIMIT, loose=[part0, got0, part1, got1]
    )


def flow(shard, axis, pairs, sections):
    if sections == (0, 1):
        return lax.ppermute(shard, axis, pairs)
    peers = lax.axis_size(axis)
    pairs = [(s * peers + i, s * peers + j) for s in sections for i, j in pairs]
    return lax.ppermute(shard, ("section", axis), pairs)


class Reduction:
    def __init__(self, info, sections, bufs):
        self.info, self.sections, self.bufs = info, sections, bufs
        groups = range(lax.axis_size("group"))
        self.across = [(g, g ^ 1) for g in groups]
        self.along = [(g, g ^ 2) for g in groups]
        self.line = lax.axis_size("replica") == 4
        self.got = (
            flow(bufs[0], "group", self.across, sections),
            flow(bufs[2], "group", self.along, sections),
        )

    def group_two(self, after):
        send_a, keep_a, send_b, keep_b = first_sum(
            self.info, self.sections, self.bufs[1], self.got[0], self.bufs[3], self.got[1], after
        )
        self.kept = (keep_a, keep_b)
        self.got = (
            flow(send_a, "group", self.along, self.sections),
            flow(send_b, "group", self.across, self.sections),
        )
        return keep_a

    def replica_one(self, after):
        self.part = second_sum(
            self.info, self.sections, self.kept[0], self.got[0], self.kept[1], self.got[1], after
        )
        if self.line:
            self.got = flow(self.part, "replica", [(0, 1), (3, 2)], self.sections)
        else:
            self.part = self.got = lax.psum(self.part, "replica")
        return self.part

    def replica_next(self, pairs, after):
        if self.line:
            self.part = pair_sum(self.info, self.sections, self.part, self.got, after)
            self.got = flow(self.part, "replica", pairs, self.sections)
        return self.part

    def replica_two(self, after):
        return self.replica_next([(1, 2), (2, 1)], after)

    def replica_three(self, after):
        return self.replica_next([(1, 0), (2, 3)], after)


def shards(
    block_input,
    cotangent,
    crop_count,
    mask_count,
    qkv_weight,
    qkv_bias,
    out_weight,
    out_bias,
    up_weight,
    up_bias,
    down_weight,
    down_bias,
    norm_gain,
    norm_shift,
):
    params = (
        qkv_weight[0],
        qkv_bias,
        out_weight[0],
        out_bias,
        up_weight[0],
        up_bias,
        down_weight[0],
        down_bias,
        norm_gain[0],
        norm_shift[0],
    )
    rows, dim = block_input.shape
    tab = jnp.asarray(rotary_tables())
    tab_t = jnp.asarray(rotary_columns())
    group = lax.axis_index("group")
    groups = lax.axis_size("group")
    info = jnp.stack([lax.axis_index("section"), group % 2, group // 2, lax.axis_index("replica")])

    def to_other(shard, pairs):
        return lax.ppermute(shard, "section", pairs)

    act, first = forward(0, info, crop_count, block_input, None, params, tab, None)
    arrived = [to_other(first[0], [(0, 1)])]
    act, second = forward(1, info, crop_count, block_input, arrived[0], params, tab, act)
    arrived.append(to_other(second[0], [(0, 1)]))
    act, third = forward(2, info, crop_count, block_input, arrived[1], params, tab, act)
    kept_one, kept_zero = (second, third), (first, second)

    common = (info, crop_count, mask_count)
    bufs, last = down_grad(1, *common, cotangent, kept_one, None, None)
    one = Reduction(info, (1,), bufs)
    bufs_two, gmid, small, last = up_grad(1, *common, cotangent, kept_one, params, None, last)
    last = one.group_two(last)
    dx, kept, last = attention_grad(
        1, info, gmid, small, arrived, kept_one, params, tab_t, None, last
    )
    grad_back = to_other(dx, [(1, 0)])
    bufs_three, last = qkv_grad(1, info, kept, kept_one, last)
    last = one.replica_one(last)
    bufs, last = down_grad(0, *common, grad_back, kept_zero, bufs_two, last)
    two = Reduction(info, (0, 1), bufs)
    bufs, gmid, small, last = up_grad(0, *common, grad_back, kept_zero, params, bufs_three, last)
    three = Reduction(info, (0, 1), bufs)
    dx, kept, last = attention_grad(
        0, info, gmid, small, [block_input], kept_zero, params, tab_t, dx, last
    )
    last = two.group_two(last)
    bufs, last = qkv_grad(0, info, kept, kept_zero, last)
    four = Reduction(info, (0,), bufs)
    last = one.replica_two(last)
    last = three.group_two(last)
    last = two.replica_one(last)
    last = one.replica_three(last)
    last = four.group_two(last)
    last = three.replica_one(last)
    last = two.replica_two(last)
    last = four.replica_one(last)
    last = three.replica_two(last)
    last = two.replica_three(last)
    last = four.replica_two(last)
    last = three.replica_three(last)

    def both(zero, one):
        return ((zero.part, zero.got), (one.part, one.got))

    (grad_down,) = finish(info, both(two, one), 0, last)
    last = four.replica_three(grad_down)
    (grad_up,) = finish(info, both(three, two), 4, last)
    grad_qkv, grad_out, small = finish(info, both(four, three), 3, grad_up)

    def own(row, count):
        flat = small[row : row + count].reshape(groups, -1)
        return lax.dynamic_index_in_dim(flat, group, 0, keepdims=True)

    def own_pair(row):
        pair = small[row : row + 2].reshape(2, groups, -1)
        return lax.dynamic_index_in_dim(pair, group, 1, keepdims=False)[None]

    return (
        act[None],
        dx[None],
        grad_qkv[None],
        own(ROW_QKV, 3),
        grad_out[None],
        own(ROW_OUT, 1),
        grad_up[None],
        own(ROW_UP, 4),
        grad_down[None],
        own(ROW_DOWN, 1),
        own_pair(ROW_GAIN),
        own_pair(ROW_SHIFT),
    )


def solution(mesh):
    rows = P(("group", "replica"))
    stack = P("section")
    return jax.shard_map(
        shards,
        mesh=mesh,
        in_specs=(rows,) * 4 + (stack,) * 10,
        out_specs=(
            P("section", ("group", "replica"), None),
            P("section", ("group", "replica"), None),
            P("section", "group", None),
            P("section", "group"),
            P("section", "group", None),
            P("section", "group"),
            P("section", "group", None),
            P("section", "group"),
            P("section", "group", None),
            P("section", "group"),
            P("section", None, "group"),
            P("section", None, "group"),
        ),
        check_vma=False,
    )
```

```python
import jax
import jax.numpy as jnp
import numpy as np
from jax import lax
from jax.experimental import pallas as pl
from jax.experimental.pallas import tpu as pltpu
from jax.sharding import PartitionSpec as P

HEADS = 20
HEAD_DIM = 32
LEN = 256
MASK_MEAN = 38
CROP_DEV = 2
EPSILON = 1e-05
ROTARY_BASE = 10000.0

BF = jnp.bfloat16
F32 = jnp.float32
NN = (((1,), (0,)), ((), ()))
NT = (((1,), (1,)), ((), ()))
TN = (((0,), (0,)), ((), ()))

FIRST_LIMIT, FORWARD_LIMIT, DOWN_LIMIT, UP_LIMIT, ATTENTION_LIMIT = 40, 24, 12, 20, 24
PAD = 16
ROW_QKV, ROW_OUT, ROW_UP, ROW_DOWN, ROW_GAIN, ROW_SHIFT = 0, 3, 4, 8, 9, 11

ANY = pl.BlockSpec(memory_space=pl.ANY)
HBM = pl.BlockSpec(memory_space=pltpu.HBM)
VMEM = pl.BlockSpec(memory_space=pltpu.VMEM)
SMEM = pl.BlockSpec(memory_space=pltpu.SMEM)


def shape(dims, dtype):
    return jax.ShapeDtypeStruct(dims, dtype)


def mm(left, right, dims=NN):
    return lax.dot_general(left, right, dims, preferred_element_type=F32)


def unit_rows_of(values):
    centred = values - jnp.mean(values, axis=-1, keepdims=True)
    inverse = lax.rsqrt(jnp.mean(centred * centred, axis=-1, keepdims=True) + EPSILON)
    return centred * inverse, inverse


def norm_back(grad, unit, inverse, gain):
    scaled = grad * gain
    return inverse * (
        scaled
        - jnp.mean(scaled, axis=-1, keepdims=True)
        - unit * jnp.mean(scaled * unit, axis=-1, keepdims=True)
    )


def rotary_tables():
    lane = np.arange(128) % HEAD_DIM
    half = HEAD_DIM // 2
    freq = ROTARY_BASE ** (-(lane % half).astype(np.float64) * (2.0 / HEAD_DIM))
    angles = np.arange(LEN)[:, None] * freq[None, :]
    sign = np.where(lane < half, -1.0, 1.0)[None, :]
    return np.stack([np.cos(angles), np.sin(angles) * sign]).astype(np.float32)


def rotary_columns():
    half = HEAD_DIM // 2
    freq = ROTARY_BASE ** (-np.arange(half, dtype=np.float64) * (2.0 / HEAD_DIM))
    angles = freq[:, None] * np.arange(LEN)[None, :]
    return np.stack([np.cos(angles), np.sin(angles)]).astype(np.float32)


def swap_halves(values):
    lane = lax.broadcasted_iota(jnp.int32, values.shape, 1) % HEAD_DIM
    half = HEAD_DIM // 2
    return jnp.where(
        lane < half,
        pltpu.roll(values, 128 - half, axis=1),
        pltpu.roll(values, half, axis=1),
    )


def head_stack(block, per):
    head = lax.broadcasted_iota(jnp.int32, block.shape, 1) // HEAD_DIM
    return jnp.concatenate(
        [jnp.where(head == h, block, jnp.zeros_like(block)) for h in range(per)], axis=0
    )


class Copies:
    def __init__(self, sems):
        self.sems = sems
        self.used = 0
        self.open = []

    def start(self, src, dst):
        copy = pltpu.make_async_copy(src, dst, self.sems.at[self.used])
        self.used += 1
        copy.start()
        return copy

    def save(self, src, dst):
        self.open.append(self.start(src, dst))

    def finish(self):
        for copy in self.open:
            copy.wait()


def call(kernel, outs, ins, scratch, sems, aliases, name, after=None, limit=16, spaces=None, out_spaces=None):
    count = len(ins)
    places = {"v": VMEM, "h": HBM, "a": ANY, "s": SMEM}
    spaces = spaces or "v" * count
    out_spaces = out_spaces or "v" * len(outs)
    in_specs = [SMEM if a.ndim == 1 else places[p] for a, p in zip(ins, spaces)]
    ins = [pltpu.with_memory_space_constraint(a, pltpu.HBM) if p == "h" else a for a, p in zip(ins, spaces)]
    body = kernel
    if after is not None:
        ins = list(ins) + [after]
        in_specs = in_specs + [ANY]

        def body(*refs):
            kernel(*refs[:count], *refs[count + 1 :])

    return pl.pallas_call(
        body,
        out_shape=outs,
        in_specs=in_specs,
        out_specs=[places[p] for p in out_spaces],
        scratch_shapes=scratch + ([pltpu.SemaphoreType.DMA((sems,))] if sems else []),
        input_output_aliases=aliases,
        compiler_params=pltpu.CompilerParams(vmem_limit_bytes=limit << 20),
        name=name,
    )(*ins)


TOKEN = jax.ShapeDtypeStruct((8, 128), F32)


def vmem_like(arr):
    return pltpu.VMEM(arr.shape, arr.dtype)


def forward(slot, info, live, own, arrived, params, tab, act, after=None):
    qkvw, qkvb, outw, outb, upw, upb, downw, downb, gain, shift = params
    dim = own.shape[1]
    blocks = dim // 128
    wide = upw.shape[1]
    parts = wide // dim
    per = 128 // HEAD_DIM
    manual = slot == 0
    saved = [
        shape((LEN, dim), BF),
        shape((LEN, 3 * dim), BF),
        shape((HEADS, LEN, LEN), BF),
        shape((dim, LEN), BF),
        shape((LEN, dim), F32),
        shape((LEN, wide), BF),
        shape((LEN, wide), BF),
    ]
    weights = [qkvb, outb, upb, downb, gain, shift, tab, qkvw, outw, upw, downw]
    sources = [own] if slot == 0 else [arrived] if slot == 2 else [own, arrived]
    before = [] if act is None else [act]
    ins = [info, live] + sources + weights + before
    count = len(sources)

    def kernel(info, live, *refs):
        xs = refs[:count]
        given = refs[count : count + 11]
        act_h, *outs = refs[count + 11 + len(before) : count + 19 + len(before)]
        scratch = refs[count + 19 + len(before) :]
        act_s, vt_s, score_s, up_s = scratch[:4]
        sems = scratch[-1]
        y_s, qkv_s, prob_s, mixt_s, mid_s, gp_s, hid_s = outs
        used = scratch[4:-1] if manual else xs[-1:] + given
        qkvb, outb, upb, downb, gain, shift, tab, qkvw, outw, upw, downw = used[1:]
        crop = slot - info[0]

        @pl.when(jnp.logical_and(crop >= 0, crop < CROP_DEV))
        def _():
            copies = Copies(sems)
            heavy = []
            if manual:
                rows = xs[0].at[pl.ds(0, LEN)]
                loads = [copies.start(h, s) for h, s in zip((rows,) + given, used)]
                heavy = loads[8:]
                wait_all(loads[:8])
                x = used[0][...].astype(F32)
            elif slot == 1:
                x = jnp.where(info[0] == 0, xs[0][LEN:, :], xs[1][...]).astype(F32)
            else:
                x = xs[0][...].astype(F32)

            def ready(index):
                if manual:
                    heavy[index].wait()

            unit, _ = unit_rows_of(x)
            normed = (unit * gain[0:1, :] + shift[0:1, :]).astype(BF)
            ready(0)
            third = mm(normed, qkvw[:, 2 * dim :]) + qkvb[:, 2 * dim :]
            low = third.astype(BF)
            qkv_s[:, 2 * dim :] = low
            vt_s[...] = low.T
            for part in range(2):
                third = mm(normed, qkvw[:, part * dim : (part + 1) * dim])
                third = third + qkvb[:, part * dim : (part + 1) * dim]
                for j in range(blocks):
                    b = third[:, 128 * j : 128 * j + 128]
                    b = b * tab[0] + swap_halves(b) * tab[1]
                    if part == 0:
                        b = b * HEAD_DIM**-0.5
                    at = part * dim + 128 * j
                    qkv_s[:, at : at + 128] = b.astype(BF)
            for j in range(blocks):
                q = qkv_s[:, 128 * j : 128 * j + 128]
                k = qkv_s[:, dim + 128 * j : dim + 128 * j + 128]
                score_s[per * LEN * j : per * LEN * (j + 1), :] = mm(head_stack(k, per), q, NT)

            def soft(h, _):
                s = score_s[pl.ds(pl.multiple_of(h * LEN, LEN), LEN), :]
                e = jnp.exp(s - jnp.max(s, axis=0, keepdims=True))
                prob_s[h] = (e * (1.0 / jnp.sum(e, axis=0, keepdims=True))).astype(BF)
                return 0

            lax.fori_loop(0, HEADS, soft, 0, unroll=2)
            for h in range(HEADS):
                at = slice(HEAD_DIM * h, HEAD_DIM * (h + 1))
                mixt_s[at, :] = mm(vt_s[at, :], prob_s[h]).astype(BF)
            ready(1)
            mid = x + mm(mixt_s[...], outw[...], TN) + outb[...]
            mid_s[...] = mid
            unit, _ = unit_rows_of(mid)
            normed = (unit * gain[1:2, :] + shift[1:2, :]).astype(BF)
            ready(2)
            up_s[...] = mm(normed, upw[...])
            for c in range(parts):
                cols = slice(c * dim, (c + 1) * dim)
                u = up_s[:, cols] + upb[:, cols]
                cdf = 0.5 + 0.5 * lax.erf(u * 0.5**0.5)
                hid_s[:, cols] = (u * cdf).astype(BF)
                gp_s[:, cols] = (
                    cdf + u * (jnp.exp(u * u * -0.5) * (2 * np.pi) ** -0.5)
                ).astype(BF)
            ready(3)
            low = (mid_s[...] + downb[...] + mm(hid_s[...], downw[...])).astype(BF)
            y_s[...] = low
            act_s[...] = jnp.where(crop < live[0], low, jnp.zeros_like(low))
            at = pl.multiple_of(crop * LEN, LEN)
            copies.save(act_s, act_h.at[pl.ds(at, LEN)])
            copies.finish()

    outs = [shape(own.shape, BF)] + saved
    scratch = [
        pltpu.VMEM((LEN, dim), BF),
        pltpu.VMEM((dim, LEN), BF),
        pltpu.VMEM((HEADS * LEN, LEN), F32),
        pltpu.VMEM((LEN, wide), F32),
    ]
    if manual:
        scratch += [pltpu.VMEM((LEN, dim), BF)] + [vmem_like(a) for a in weights]
    aliases = {} if act is None else {len(ins) - 1: 0}
    spaces = "ss" + ("h" if manual else "v") * (count + 11) + "h" * len(before)
    out = call(
        kernel,
        outs,
        ins,
        scratch,
        16,
        aliases,
        "layer_forward",
        after,
        FIRST_LIMIT if manual else FORWARD_LIMIT,
        spaces,
        "h" + "v" * 7,
    )
    return out[0], out[1:]


def gradient_rows(g, live, masks, section):
    grad = g.astype(F32)
    if section == 0:
        return grad
    crop = lax.broadcasted_iota(jnp.int32, (g.shape[0], 1), 0) // LEN
    weight = jnp.zeros_like(crop)
    for c in range(CROP_DEV):
        weight = jnp.where(crop == c, masks[c], weight)
    weight = jnp.where(crop < live[0], weight, 0)
    return grad * (weight.astype(F32) / MASK_MEAN)


def lay_out(info, bufs, block, pieces):
    send_a, keep_a, send_b, keep_b = bufs
    half_rows = send_b.shape[0] // 2
    for row, count, shard, is_b, at in pieces:
        x, y = shard % 2, shard // 2
        own, index, keep, send = (
            (info[2] == y, x, keep_b, send_b) if is_b else (info[1] == x, y, keep_a, send_a)
        )
        start = index * half_rows + at

        @pl.when(own)
        def _():
            keep[start : start + count, :] = block[row : row + count, :]

        @pl.when(jnp.logical_not(own))
        def _():
            send[start : start + count, :] = block[row : row + count, :]


def keep_given(active, given, bufs):
    @pl.when(jnp.logical_not(active))
    def _():
        for old, new in zip(given, bufs):
            new[...] = old[...]


def quarters(block, dim, parts):
    count = dim // parts
    return [(s * count, count, s, block >= 2, (block % 2) * count) for s in range(parts)]


def buffer_shapes(dim):
    return [shape((dim + PAD, dim), BF)] * 2 + [shape((dim, dim), BF)] * 2


def joined(refs, cols):
    return jnp.concatenate([r[:, cols] for r in refs], axis=0)


def wait_all(copies):
    for copy in copies:
        copy.wait()


def down_grad(section, info, live, masks, g, saved, before, after):
    hids = [s[6] for s in saved]
    rows, dim = g.shape
    parts = hids[0].shape[1] // dim
    given = [] if before is None else list(before)
    ins = [info, live, masks, g] + hids + given

    def kernel(info, live, masks, g_s, *refs):
        hid_s = refs[: len(hids)]
        old = refs[len(hids) : len(hids) + len(given)]
        bufs = refs[len(hids) + len(given) : len(hids) + len(given) + 4]
        (block_s,) = refs[len(hids) + len(given) + 5 :]
        keep_given(info[0] == section, old, bufs)

        @pl.when(info[0] == section)
        def _():
            low = gradient_rows(g_s[...], live, masks, section).astype(BF)
            for c in range(parts):
                cols = slice(c * dim, (c + 1) * dim)
                block_s[c] = mm(joined(hid_s, cols), low, TN).astype(BF)
            half = dim // 2
            for c in range(parts):
                pieces = [(0, half, c, False, 0), (half, half, c, True, 0)]
                lay_out(info, bufs, block_s.at[c], pieces)

    scratch = [pltpu.VMEM((parts, dim, dim), BF)]
    aliases = {len(ins) - 4 + i: i for i in range(4)} if given else {}
    outs = buffer_shapes(dim) + [TOKEN]
    out = call(kernel, outs, ins, scratch, 0, aliases, "down_grad", after, DOWN_LIMIT)
    return out[:4], out[4]


def up_grad(section, info, live, masks, g, saved, params, before, after):
    mids, gps = [s[4] for s in saved], [s[5] for s in saved]
    upw, downw, gain, shift = params[4], params[6], params[8], params[9]
    rows, dim = g.shape
    wide = upw.shape[1]
    parts = wide // dim
    crops = len(saved)
    given = [] if before is None else list(before)
    ins = [info, live, masks, g, gain, shift, downw, upw] + mids + gps + given

    def kernel(info, live, masks, g_s, gain, shift, downw, upw, *refs):
        mid_s, gp_s = refs[:crops], refs[crops : 2 * crops]
        old = refs[2 * crops : 2 * crops + len(given)]
        refs = refs[2 * crops + len(given) :]
        bufs, gmid_s, small_s = refs[:4], refs[4], refs[5]
        gu_s, block_s = refs[7:]
        keep_given(info[0] == section, old, bufs)

        @pl.when(info[0] == section)
        def _():
            grad = gradient_rows(g_s[...], live, masks, section)
            low = grad.astype(BF)
            small_s[...] = jnp.zeros_like(small_s)
            small_s[ROW_DOWN : ROW_DOWN + 1, :] = jnp.sum(low.astype(F32), axis=0, keepdims=True)
            unit, inverse = unit_rows_of(joined(mid_s, slice(None)))
            normed_t = (unit * gain[1:2, :] + shift[1:2, :]).astype(BF).T
            for c in range(parts):
                cols = slice(c * dim, (c + 1) * dim)
                grad_up = mm(low, downw[cols, :], NT) * joined(gp_s, cols).astype(F32)
                grad_up = grad_up.astype(BF)
                gu_s[:, cols] = grad_up
                small_s[ROW_UP + c : ROW_UP + c + 1, :] = jnp.sum(
                    grad_up.astype(F32), axis=0, keepdims=True
                )
            back = mm(gu_s[...], upw[...], NT)
            gmid_s[...] = grad + norm_back(back, unit, inverse, gain[1:2, :])
            small_s[ROW_GAIN + 1 : ROW_GAIN + 2, :] = jnp.sum(back * unit, axis=0, keepdims=True)
            small_s[ROW_SHIFT + 1 : ROW_SHIFT + 2, :] = jnp.sum(back, axis=0, keepdims=True)
            for c in range(parts):
                block_s[c] = mm(normed_t, gu_s[:, c * dim : (c + 1) * dim]).astype(BF)
            for c in range(parts):
                lay_out(info, bufs, block_s.at[c], quarters(c, dim, parts))

    scratch = [pltpu.VMEM((rows, wide), BF), pltpu.VMEM((parts, dim, dim), BF)]
    aliases = {len(ins) - 4 + i: i for i in range(4)} if given else {}
    outs = buffer_shapes(dim) + [shape((rows, dim), F32), shape((PAD, dim), F32), TOKEN]
    out = call(kernel, outs, ins, scratch, 0, aliases, "up_grad", after, UP_LIMIT)
    return out[:4], out[4], out[5], out[6]


def rotate_back(block, tab_t):
    half = HEAD_DIM // 2
    cos, sin = tab_t[0], tab_t[1]
    out = []
    for at in range(0, block.shape[0], HEAD_DIM):
        a, b = block[at : at + half], block[at + half : at + HEAD_DIM]
        out += [a * cos + b * sin, b * cos - a * sin]
    return jnp.concatenate(out, axis=0)


def attention_grad(section, info, gmid, small, xs, saved, params, tab_t, before, after):
    qkvs, probs, mixts = [s[1] for s in saved], [s[2] for s in saved], [s[3] for s in saved]
    qkvw, outw, gain, shift = params[0], params[2], params[8], params[9]
    rows, dim = gmid.shape
    blocks = dim // 128
    per = 128 // HEAD_DIM
    crops = len(saved)
    given = [] if before is None else [before]
    ins = [info, gmid, outw, small, gain, shift, tab_t, qkvw]
    ins += qkvs + probs + mixts + list(xs) + given

    def kernel(info, gmid_s, outw, small_s, gain, shift, tab_t, qkvw, *refs):
        qkv_s, prob_s, mixt_s = (refs[i * crops : (i + 1) * crops] for i in range(3))
        x_s = refs[3 * crops : 3 * crops + len(xs)]
        old = refs[3 * crops + len(xs) : 3 * crops + len(xs) + len(given)]
        refs = refs[3 * crops + len(xs) + len(given) :]
        keep_given(info[0] == section, old, refs[:1])
        dx_s, gqkv_s, normt_s, low_s, small_out = refs[:5]
        gmt_s, delta_s, da_s, ds_s, dt_s, kt_s = refs[6:]

        @pl.when(info[0] == section)
        def _():
            low = gmid_s[...].astype(BF)
            low_s[...] = low
            gmt_s[...] = mm(outw[...], low, NT).astype(BF)
            for c in range(crops):
                crop = slice(c * LEN, (c + 1) * LEN)
                qkv, prob = qkv_s[c], prob_s[c]
                product = gmt_s[:, crop].astype(F32) * mixt_s[c][...].astype(F32)
                delta_s[...] = jnp.sum(product.reshape(HEADS, HEAD_DIM, LEN), axis=1)[:, None, :]
                kt_s[0] = qkv[:, dim : 2 * dim].T
                kt_s[1] = qkv[:, :dim].T
                for j in range(blocks):
                    v = qkv[:, 2 * dim + 128 * j : 2 * dim + 128 * j + 128]
                    da_s[per * LEN * j : per * LEN * (j + 1), :] = mm(
                        head_stack(v, per), gmt_s[128 * j : 128 * j + 128, crop]
                    )

                def scores(h, _):
                    da = da_s[pl.ds(pl.multiple_of(h * LEN, LEN), LEN), :]
                    ds_s[h] = (prob[h].astype(F32) * (da - delta_s[h])).astype(BF)
                    return 0

                lax.fori_loop(0, HEADS, scores, 0, unroll=2)
                for h in range(HEADS):
                    at = slice(HEAD_DIM * h, HEAD_DIM * (h + 1))
                    dt_s[0, at, :] = mm(kt_s[0, at, :], ds_s[h])
                    dt_s[1, at, :] = mm(kt_s[1, at, :], ds_s[h], NT)
                    dt_s[2, at, :] = mm(gmt_s[at, crop], prob[h], NT)
                dq = rotate_back(dt_s[0] * HEAD_DIM**-0.5, tab_t)
                gqkv_s[crop, :dim] = dq.astype(BF).T
                gqkv_s[crop, dim : 2 * dim] = rotate_back(dt_s[1], tab_t).astype(BF).T
                gqkv_s[crop, 2 * dim :] = dt_s[2].astype(BF).T
            unit, inverse = unit_rows_of(joined(x_s, slice(None)).astype(F32))
            normt_s[...] = (unit * gain[0:1, :] + shift[0:1, :]).astype(BF).T
            back = mm(gqkv_s[...], qkvw[...], NT)
            dx_s[...] = (gmid_s[...] + norm_back(back, unit, inverse, gain[0:1, :])).astype(BF)
            small_out[...] = small_s[...]
            small_out[ROW_GAIN : ROW_GAIN + 1, :] = jnp.sum(back * unit, axis=0, keepdims=True)
            small_out[ROW_SHIFT : ROW_SHIFT + 1, :] = jnp.sum(back, axis=0, keepdims=True)

    outs = [
        shape((rows, dim), BF),
        shape((rows, 3 * dim), BF),
        shape((dim, rows), BF),
        shape((rows, dim), BF),
        shape(small.shape, F32),
        TOKEN,
    ]
    scratch = [
        pltpu.VMEM((dim, rows), BF),
        pltpu.VMEM((HEADS, 1, LEN), F32),
        pltpu.VMEM((HEADS * LEN, LEN), F32),
        pltpu.VMEM((HEADS, LEN, LEN), BF),
        pltpu.VMEM((3, dim, LEN), F32),
        pltpu.VMEM((2, dim, LEN), BF),
    ]
    aliases = {len(ins) - 1: 0} if given else {}
    out = call(kernel, outs, ins, scratch, 0, aliases, "attention_grad", after, ATTENTION_LIMIT)
    return out[0], out[1:5], out[5]


def qkv_grad(section, info, kept, saved, after):
    gqkv, normt, low, small = kept
    mixts = [s[3] for s in saved]
    rows, dim = low.shape
    parts = 4
    ins = [info, gqkv, normt, low, small] + mixts

    def kernel(info, gqkv_s, normt_s, low_s, small_s, *refs):
        mixt_s = refs[: len(mixts)]
        bufs = refs[len(mixts) : len(mixts) + 4]
        (block_s,) = refs[len(mixts) + 5 :]

        @pl.when(info[0] == section)
        def _():
            sums = [
                jnp.sum(gqkv_s[:, c * dim : (c + 1) * dim].astype(F32), axis=0, keepdims=True)
                for c in range(3)
            ]
            sums.append(jnp.sum(low_s[...].astype(F32), axis=0, keepdims=True))
            tail = jnp.concatenate(sums + [small_s[ROW_UP:, :]], axis=0).astype(BF)
            bufs[0][dim:, :] = tail
            bufs[1][dim:, :] = tail
            for c in range(3):
                block_s[c] = mm(normt_s[...], gqkv_s[:, c * dim : (c + 1) * dim]).astype(BF)
            mixt = jnp.concatenate([m[...] for m in mixt_s], axis=1)
            block_s[3] = mm(mixt, low_s[...]).astype(BF)
            for c in range(parts):
                lay_out(info, bufs, block_s.at[c], quarters(c, dim, parts))

    scratch = [pltpu.VMEM((parts, dim, dim), BF)]
    outs = buffer_shapes(dim) + [TOKEN]
    out = call(kernel, outs, ins, scratch, 0, {}, "qkv_grad", after, DOWN_LIMIT)
    return out[:4], out[4]


def plus(one, two):
    return (one.astype(F32) + two.astype(F32)).astype(BF)


def taking_part(info, sections, middle):
    check = None
    if len(sections) == 1:
        check = info[0] == sections[0]
    if middle:
        inner = jnp.logical_or(info[3] == 1, info[3] == 2)
        check = inner if check is None else jnp.logical_and(check, inner)
    return info[3] >= 0 if check is None else check


def vmem_call(kernel, outs, info, ins, name, after):
    return call(kernel, outs, [info] + ins, [], 0, {}, name, after, 8)


def first_sum(info, sections, keep_a, recv_a, keep_b, recv_b, after):
    dim = keep_b.shape[1]
    half = dim // 2

    def kernel(info, ka, ra, kb, rb, sa, na, sb, nb):
        @pl.when(taking_part(info, sections, False))
        def _():
            for own, one, two, new, out in ((info[2], ka, ra, na, sa), (info[1], kb, rb, nb, sb)):
                mine = pl.ds(pl.multiple_of(own * half, half), half)
                other = pl.ds(pl.multiple_of((1 - own) * half, half), half)
                out[:half, :] = plus(one[other, :], two[other, :])
                new[:half, :] = plus(one[mine, :], two[mine, :])
                if one.shape[0] > 2 * half:
                    tail = plus(one[2 * half :, :], two[2 * half :, :])
                    new[half:, :] = tail
                    out[half:, :] = tail

    outs = [shape((half + PAD, dim), BF)] * 2 + [shape((half, dim), BF)] * 2
    return vmem_call(kernel, outs, info, [keep_a, recv_a, keep_b, recv_b], "first_sum", after)


def second_sum(info, sections, keep_a, recv_a, keep_b, recv_b, after):
    dim = keep_b.shape[1]

    def kernel(info, ka, ra, kb, rb, out):
        @pl.when(taking_part(info, sections, False))
        def _():
            top = ka.shape[0]
            out[:top, :] = plus(ka[...], ra[...])
            out[top:, :] = plus(kb[...], rb[...])

    outs = [shape((dim + PAD, dim), BF)]
    return vmem_call(kernel, outs, info, [keep_a, recv_a, keep_b, recv_b], "second_sum", after)[0]


def pair_sum(info, sections, one, two, after):
    def kernel(info, one, two, out):
        @pl.when(taking_part(info, sections, True))
        def _():
            out[...] = plus(one[...], two[...])

    return vmem_call(kernel, [shape(one.shape, BF)], info, [one, two], "pair_sum", after)[0]


def finish(info, sources, wide, after):
    (part0, got0), (part1, got1) = sources
    rows, dim = part0.shape
    half = dim // 2
    quarter = half // 2
    if wide == 0:
        outs = [shape((dim, dim), F32)]
    elif wide == 4:
        outs = [shape((quarter, 4 * dim), F32)]
    else:
        outs = [shape((quarter, 3 * dim), F32), shape((quarter, dim), F32), shape((PAD, dim), F32)]

    def kernel(info, p0, g0, p1, g1, *refs):
        out_h = refs[: len(outs)]
        src = refs[len(outs)]
        stage = refs[len(outs) + 1 : -1]
        sems = refs[-1]
        inner = jnp.logical_or(info[3] == 1, info[3] == 2)
        for section, part, got in ((0, p0, g0), (1, p1, g1)):
            mine = info[0] == section

            @pl.when(jnp.logical_and(mine, inner))
            def _():
                pltpu.make_async_copy(part, src, sems.at[0]).start()

            @pl.when(jnp.logical_and(mine, jnp.logical_not(inner)))
            def _():
                pltpu.make_async_copy(got, src, sems.at[0]).start()

        pltpu.make_async_copy(p0, src, sems.at[0]).wait()
        block_a = src[:half, :].astype(F32)
        block_b = src[half + PAD :, :].astype(F32)
        if wide == 0:
            stage[0][:half, :] = block_a
            stage[0][half:, :] = block_b
        else:
            pieces = (block_a[:quarter], block_a[quarter:], block_b[:quarter], block_b[quarter:])
            for i in range(wide):
                stage[0][:, i * dim : (i + 1) * dim] = pieces[i]
            if wide == 3:
                stage[1][...] = pieces[3]
                stage[2][...] = src[half : half + PAD, :].astype(F32)
        copies = [
            pltpu.make_async_copy(s, o, sems.at[1 + i]) for i, (s, o) in enumerate(zip(stage, out_h))
        ]
        for copy in copies:
            copy.start()
        for copy in copies:
            copy.wait()

    scratch = [vmem_like(part0)] + [vmem_like(o) for o in outs]
    ins = [info, part0, got0, part1, got1]
    return call(kernel, outs, ins, scratch, 4, {}, "finish", after, 12, "saaaa", "h" * len(outs))


def flow(shard, axis, pairs, sections):
    if sections == (0, 1):
        return lax.ppermute(shard, axis, pairs)
    peers = lax.axis_size(axis)
    pairs = [(s * peers + i, s * peers + j) for s in sections for i, j in pairs]
    return lax.ppermute(shard, ("section", axis), pairs)


class Reduction:
    def __init__(self, info, sections, bufs):
        self.info, self.sections, self.bufs = info, sections, bufs
        groups = range(lax.axis_size("group"))
        self.across = [(g, g ^ 1) for g in groups]
        self.along = [(g, g ^ 2) for g in groups]
        self.line = lax.axis_size("replica") == 4
        self.got = (
            flow(bufs[0], "group", self.across, sections),
            flow(bufs[2], "group", self.along, sections),
        )

    def group_two(self, after):
        send_a, keep_a, send_b, keep_b = first_sum(
            self.info, self.sections, self.bufs[1], self.got[0], self.bufs[3], self.got[1], after
        )
        self.kept = (keep_a, keep_b)
        self.got = (
            flow(send_a, "group", self.along, self.sections),
            flow(send_b, "group", self.across, self.sections),
        )
        return keep_a

    def replica_one(self, after):
        self.part = second_sum(
            self.info, self.sections, self.kept[0], self.got[0], self.kept[1], self.got[1], after
        )
        if self.line:
            self.got = flow(self.part, "replica", [(0, 1), (3, 2)], self.sections)
        else:
            self.part = self.got = lax.psum(self.part, "replica")
        return self.part

    def replica_next(self, pairs, after):
        if self.line:
            self.part = pair_sum(self.info, self.sections, self.part, self.got, after)
            self.got = flow(self.part, "replica", pairs, self.sections)
        return self.part

    def replica_two(self, after):
        return self.replica_next([(1, 2), (2, 1)], after)

    def replica_three(self, after):
        return self.replica_next([(1, 0), (2, 3)], after)


def shards(
    block_input,
    cotangent,
    crop_count,
    mask_count,
    qkv_weight,
    qkv_bias,
    out_weight,
    out_bias,
    up_weight,
    up_bias,
    down_weight,
    down_bias,
    norm_gain,
    norm_shift,
):
    params = (
        qkv_weight[0],
        qkv_bias,
        out_weight[0],
        out_bias,
        up_weight[0],
        up_bias,
        down_weight[0],
        down_bias,
        norm_gain[0],
        norm_shift[0],
    )
    rows, dim = block_input.shape
    tab = jnp.asarray(rotary_tables())
    tab_t = jnp.asarray(rotary_columns())
    group = lax.axis_index("group")
    groups = lax.axis_size("group")
    info = jnp.stack([lax.axis_index("section"), group % 2, group // 2, lax.axis_index("replica")])

    def to_other(shard, pairs):
        return lax.ppermute(shard, "section", pairs)

    act, first = forward(0, info, crop_count, block_input, None, params, tab, None)
    arrived = [to_other(first[0], [(0, 1)])]
    act, second = forward(1, info, crop_count, block_input, arrived[0], params, tab, act)
    arrived.append(to_other(second[0], [(0, 1)]))
    act, third = forward(2, info, crop_count, block_input, arrived[1], params, tab, act)
    kept_one, kept_zero = (second, third), (first, second)

    common = (info, crop_count, mask_count)
    bufs, last = down_grad(1, *common, cotangent, kept_one, None, None)
    one = Reduction(info, (1,), bufs)
    bufs_two, gmid, small, last = up_grad(1, *common, cotangent, kept_one, params, None, last)
    last = one.group_two(last)
    dx, kept, last = attention_grad(
        1, info, gmid, small, arrived, kept_one, params, tab_t, None, last
    )
    grad_back = to_other(dx, [(1, 0)])
    bufs_three, last = qkv_grad(1, info, kept, kept_one, last)
    last = one.replica_one(last)
    bufs, last = down_grad(0, *common, grad_back, kept_zero, bufs_two, last)
    two = Reduction(info, (0, 1), bufs)
    bufs, gmid, small, last = up_grad(0, *common, grad_back, kept_zero, params, bufs_three, last)
    three = Reduction(info, (0, 1), bufs)
    dx, kept, last = attention_grad(
        0, info, gmid, small, [block_input], kept_zero, params, tab_t, dx, last
    )
    last = two.group_two(last)
    bufs, last = qkv_grad(0, info, kept, kept_zero, last)
    four = Reduction(info, (0,), bufs)
    last = one.replica_two(last)
    last = three.group_two(last)
    last = two.replica_one(last)
    last = one.replica_three(last)
    last = four.group_two(last)
    last = three.replica_one(last)
    last = two.replica_two(last)
    last = four.replica_one(last)
    last = three.replica_two(last)
    last = two.replica_three(last)
    last = four.replica_two(last)
    last = three.replica_three(last)

    def both(zero, one):
        return ((zero.part, zero.got), (one.part, one.got))

    (grad_down,) = finish(info, both(two, one), 0, last)
    last = four.replica_three(grad_down)
    (grad_up,) = finish(info, both(three, two), 4, last)
    grad_qkv, grad_out, small = finish(info, both(four, three), 3, grad_up)

    def own(row, count):
        flat = small[row : row + count].reshape(groups, -1)
        return lax.dynamic_index_in_dim(flat, group, 0, keepdims=True)

    def own_pair(row):
        pair = small[row : row + 2].reshape(2, groups, -1)
        return lax.dynamic_index_in_dim(pair, group, 1, keepdims=False)[None]

    return (
        act[None],
        dx[None],
        grad_qkv[None],
        own(ROW_QKV, 3),
        grad_out[None],
        own(ROW_OUT, 1),
        grad_up[None],
        own(ROW_UP, 4),
        grad_down[None],
        own(ROW_DOWN, 1),
        own_pair(ROW_GAIN),
        own_pair(ROW_SHIFT),
    )


def solution(mesh):
    rows = P(("group", "replica"))
    stack = P("section")
    return jax.shard_map(
        shards,
        mesh=mesh,
        in_specs=(rows,) * 4 + (stack,) * 10,
        out_specs=(
            P("section", ("group", "replica"), None),
            P("section", ("group", "replica"), None),
            P("section", "group", None),
            P("section", "group"),
            P("section", "group", None),
            P("section", "group"),
            P("section", "group", None),
            P("section", "group"),
            P("section", "group", None),
            P("section", "group"),
            P("section", None, "group"),
            P("section", None, "group"),
        ),
        check_vma=False,
    )
```

```python
import jax
import jax.numpy as jnp
import numpy as np
from jax import lax
from jax.experimental import pallas as pl
from jax.experimental.pallas import tpu as pltpu
from jax.sharding import PartitionSpec as P

HEADS = 20
HEAD_DIM = 32
LEN = 256
MASK_MEAN = 38
CROP_DEV = 2
EPSILON = 1e-05
ROTARY_BASE = 10000.0

BF = jnp.bfloat16
F32 = jnp.float32
NN = (((1,), (0,)), ((), ()))
NT = (((1,), (1,)), ((), ()))
TN = (((0,), (0,)), ((), ()))

FIRST_LIMIT, FORWARD_LIMIT, DOWN_LIMIT, UP_LIMIT, ATTENTION_LIMIT = 40, 24, 12, 20, 24
GROUPS = 4
PAD = 16
ROW_QKV, ROW_OUT, ROW_UP, ROW_DOWN, ROW_GAIN, ROW_SHIFT = 0, 3, 4, 8, 9, 11

ANY = pl.BlockSpec(memory_space=pl.ANY)
HBM = pl.BlockSpec(memory_space=pltpu.HBM)
VMEM = pl.BlockSpec(memory_space=pltpu.VMEM)
SMEM = pl.BlockSpec(memory_space=pltpu.SMEM)


def shape(dims, dtype):
    return jax.ShapeDtypeStruct(dims, dtype)


def mm(left, right, dims=NN):
    return lax.dot_general(left, right, dims, preferred_element_type=F32)


def unit_rows_of(values):
    centred = values - jnp.mean(values, axis=-1, keepdims=True)
    inverse = lax.rsqrt(jnp.mean(centred * centred, axis=-1, keepdims=True) + EPSILON)
    return centred * inverse, inverse


def norm_back(grad, unit, inverse, gain):
    scaled = grad * gain
    return inverse * (
        scaled
        - jnp.mean(scaled, axis=-1, keepdims=True)
        - unit * jnp.mean(scaled * unit, axis=-1, keepdims=True)
    )


def rotary_tables():
    lane = np.arange(128) % HEAD_DIM
    half = HEAD_DIM // 2
    freq = ROTARY_BASE ** (-(lane % half).astype(np.float64) * (2.0 / HEAD_DIM))
    angles = np.arange(LEN)[:, None] * freq[None, :]
    sign = np.where(lane < half, -1.0, 1.0)[None, :]
    return np.stack([np.cos(angles), np.sin(angles) * sign]).astype(np.float32)


def rotary_columns():
    half = HEAD_DIM // 2
    freq = ROTARY_BASE ** (-np.arange(half, dtype=np.float64) * (2.0 / HEAD_DIM))
    angles = freq[:, None] * np.arange(LEN)[None, :]
    return np.stack([np.cos(angles), np.sin(angles)]).astype(np.float32)


def swap_halves(values):
    lane = lax.broadcasted_iota(jnp.int32, values.shape, 1) % HEAD_DIM
    half = HEAD_DIM // 2
    return jnp.where(
        lane < half,
        pltpu.roll(values, 128 - half, axis=1),
        pltpu.roll(values, half, axis=1),
    )


def head_stack(block, per):
    head = lax.broadcasted_iota(jnp.int32, block.shape, 1) // HEAD_DIM
    return jnp.concatenate(
        [jnp.where(head == h, block, jnp.zeros_like(block)) for h in range(per)], axis=0
    )


class Copies:
    def __init__(self, sems):
        self.sems = sems
        self.used = 0
        self.open = []

    def start(self, src, dst):
        copy = pltpu.make_async_copy(src, dst, self.sems.at[self.used])
        self.used += 1
        copy.start()
        return copy

    def save(self, src, dst):
        self.open.append(self.start(src, dst))

    def finish(self):
        for copy in self.open:
            copy.wait()


def call(kernel, outs, ins, scratch, sems, aliases, name, after=None, limit=16, spaces=None, out_spaces=None):
    count = len(ins)
    places = {"v": VMEM, "h": HBM, "a": ANY, "s": SMEM}
    spaces = spaces or "v" * count
    out_spaces = out_spaces or "v" * len(outs)
    in_specs = [SMEM if a.ndim == 1 else places[p] for a, p in zip(ins, spaces)]
    ins = [pltpu.with_memory_space_constraint(a, pltpu.HBM) if p == "h" else a for a, p in zip(ins, spaces)]
    body = kernel
    if after is not None:
        ins = list(ins) + [after]
        in_specs = in_specs + [ANY]

        def body(*refs):
            kernel(*refs[:count], *refs[count + 1 :])

    outs = [pltpu.HBM(o.shape, o.dtype) if p == "h" else o for o, p in zip(outs, out_spaces)]
    return pl.pallas_call(
        body,
        out_shape=outs,
        in_specs=in_specs,
        out_specs=[places[p] for p in out_spaces],
        scratch_shapes=scratch + ([pltpu.SemaphoreType.DMA((sems,))] if sems else []),
        input_output_aliases=aliases,
        compiler_params=pltpu.CompilerParams(vmem_limit_bytes=limit << 20),
        name=name,
    )(*ins)


TOKEN = jax.ShapeDtypeStruct((8, 128), F32)


def vmem_like(arr):
    return pltpu.VMEM(arr.shape, arr.dtype)


def forward(slot, info, live, own, arrived, params, tab, act, after=None):
    qkvw, qkvb, outw, outb, upw, upb, downw, downb, gain, shift = params
    dim = own.shape[1]
    blocks = dim // 128
    wide = upw.shape[1]
    parts = wide // dim
    per = 128 // HEAD_DIM
    manual = slot == 0
    saved = [
        shape((LEN, dim), BF),
        shape((LEN, 3 * dim), BF),
        shape((HEADS, LEN, LEN), BF),
        shape((dim, LEN), BF),
        shape((LEN, dim), F32),
        shape((LEN, wide), BF),
        shape((LEN, wide), BF),
    ]
    weights = [qkvb, outb, upb, downb, gain, shift, tab, qkvw, outw, upw, downw]
    sources = [own] if slot == 0 else [arrived] if slot == 2 else [own, arrived]
    before = [] if act is None else [act]
    ins = [info, live] + sources + weights + before
    count = len(sources)

    def kernel(info, live, *refs):
        xs = refs[:count]
        given = refs[count : count + 11]
        act_h, *outs = refs[count + 11 + len(before) : count + 19 + len(before)]
        scratch = refs[count + 19 + len(before) :]
        act_s, vt_s, score_s, up_s = scratch[:4]
        sems = scratch[-1]
        y_s, qkv_s, prob_s, mixt_s, mid_s, gp_s, hid_s = outs
        used = scratch[4:-1] if manual else xs[-1:] + given
        qkvb, outb, upb, downb, gain, shift, tab, qkvw, outw, upw, downw = used[1:]
        crop = slot - info[0]

        @pl.when(jnp.logical_and(crop >= 0, crop < CROP_DEV))
        def _():
            copies = Copies(sems)
            heavy = []
            if manual:
                rows = xs[0].at[pl.ds(0, LEN)]
                loads = [copies.start(h, s) for h, s in zip((rows,) + given, used)]
                heavy = loads[8:]
                wait_all(loads[:8])
                x = used[0][...].astype(F32)
            elif slot == 1:
                x = jnp.where(info[0] == 0, xs[0][LEN:, :], xs[1][...]).astype(F32)
            else:
                x = xs[0][...].astype(F32)

            def ready(index):
                if manual:
                    heavy[index].wait()

            unit, _ = unit_rows_of(x)
            normed = (unit * gain[0:1, :] + shift[0:1, :]).astype(BF)
            ready(0)
            third = mm(normed, qkvw[:, 2 * dim :]) + qkvb[:, 2 * dim :]
            low = third.astype(BF)
            qkv_s[:, 2 * dim :] = low
            vt_s[...] = low.T
            for part in range(2):
                third = mm(normed, qkvw[:, part * dim : (part + 1) * dim])
                third = third + qkvb[:, part * dim : (part + 1) * dim]
                for j in range(blocks):
                    b = third[:, 128 * j : 128 * j + 128]
                    b = b * tab[0] + swap_halves(b) * tab[1]
                    if part == 0:
                        b = b * HEAD_DIM**-0.5
                    at = part * dim + 128 * j
                    qkv_s[:, at : at + 128] = b.astype(BF)
            for j in range(blocks):
                q = qkv_s[:, 128 * j : 128 * j + 128]
                k = qkv_s[:, dim + 128 * j : dim + 128 * j + 128]
                score_s[per * LEN * j : per * LEN * (j + 1), :] = mm(head_stack(k, per), q, NT)

            def soft(h, _):
                s = score_s[pl.ds(pl.multiple_of(h * LEN, LEN), LEN), :]
                e = jnp.exp(s - jnp.max(s, axis=0, keepdims=True))
                prob_s[h] = (e * (1.0 / jnp.sum(e, axis=0, keepdims=True))).astype(BF)
                return 0

            lax.fori_loop(0, HEADS, soft, 0, unroll=2)
            for h in range(HEADS):
                at = slice(HEAD_DIM * h, HEAD_DIM * (h + 1))
                mixt_s[at, :] = mm(vt_s[at, :], prob_s[h]).astype(BF)
            ready(1)
            mid = x + mm(mixt_s[...], outw[...], TN) + outb[...]
            mid_s[...] = mid
            unit, _ = unit_rows_of(mid)
            normed = (unit * gain[1:2, :] + shift[1:2, :]).astype(BF)
            ready(2)
            up_s[...] = mm(normed, upw[...])
            for c in range(parts):
                cols = slice(c * dim, (c + 1) * dim)
                u = up_s[:, cols] + upb[:, cols]
                cdf = 0.5 + 0.5 * lax.erf(u * 0.5**0.5)
                hid_s[:, cols] = (u * cdf).astype(BF)
                gp_s[:, cols] = (
                    cdf + u * (jnp.exp(u * u * -0.5) * (2 * np.pi) ** -0.5)
                ).astype(BF)
            ready(3)
            low = (mid_s[...] + downb[...] + mm(hid_s[...], downw[...])).astype(BF)
            y_s[...] = low
            act_s[...] = jnp.where(crop < live[0], low, jnp.zeros_like(low))
            at = pl.multiple_of(crop * LEN, LEN)
            copies.save(act_s, act_h.at[pl.ds(at, LEN)])
            copies.finish()

    outs = [shape(own.shape, BF)] + saved
    scratch = [
        pltpu.VMEM((LEN, dim), BF),
        pltpu.VMEM((dim, LEN), BF),
        pltpu.VMEM((HEADS * LEN, LEN), F32),
        pltpu.VMEM((LEN, wide), F32),
    ]
    if manual:
        scratch += [pltpu.VMEM((LEN, dim), BF)] + [vmem_like(a) for a in weights]
    aliases = {} if act is None else {len(ins) - 1: 0}
    spaces = "ss" + ("h" if manual else "v") * (count + 11) + "h" * len(before)
    out = call(
        kernel,
        outs,
        ins,
        scratch,
        16,
        aliases,
        "layer_forward",
        after,
        FIRST_LIMIT if manual else FORWARD_LIMIT,
        spaces,
        "h" + "v" * 7,
    )
    return out[0], out[1:]


def gradient_rows(g, live, masks, section):
    grad = g.astype(F32)
    if section == 0:
        return grad
    crop = lax.broadcasted_iota(jnp.int32, (g.shape[0], 1), 0) // LEN
    weight = jnp.zeros_like(crop)
    for c in range(CROP_DEV):
        weight = jnp.where(crop == c, masks[c], weight)
    weight = jnp.where(crop < live[0], weight, 0)
    return grad * (weight.astype(F32) / MASK_MEAN)


def lay_out(info, bufs, block, pieces):
    send_a, keep_a, send_b, keep_b = bufs
    half_rows = send_b.shape[0] // 2
    for row, count, shard, is_b, at in pieces:
        x, y = shard % 2, shard // 2
        own, index, keep, send = (
            (info[2] == y, x, keep_b, send_b) if is_b else (info[1] == x, y, keep_a, send_a)
        )
        start = index * half_rows + at

        @pl.when(own)
        def _():
            keep[start : start + count, :] = block[row : row + count, :]

        @pl.when(jnp.logical_not(own))
        def _():
            send[start : start + count, :] = block[row : row + count, :]


def keep_given(active, given, bufs):
    @pl.when(jnp.logical_not(active))
    def _():
        for old, new in zip(given, bufs):
            new[...] = old[...]


def quarters(block, dim, parts):
    count = dim // parts
    return [(s * count, count, s, block >= 2, (block % 2) * count) for s in range(parts)]


def buffer_shapes(dim):
    return [shape((dim + PAD, dim), BF)] * 2 + [shape((dim, dim), BF)] * 2


def joined(refs, cols):
    return jnp.concatenate([r[:, cols] for r in refs], axis=0)


def wait_all(copies):
    for copy in copies:
        copy.wait()


def down_grad(section, info, live, masks, g, saved, before, after):
    hids = [s[6] for s in saved]
    rows, dim = g.shape
    parts = hids[0].shape[1] // dim
    given = [] if before is None else list(before)
    ins = [info, live, masks, g] + hids + given

    def kernel(info, live, masks, g_s, *refs):
        hid_s = refs[: len(hids)]
        old = refs[len(hids) : len(hids) + len(given)]
        bufs = refs[len(hids) + len(given) : len(hids) + len(given) + 4]
        (block_s,) = refs[len(hids) + len(given) + 5 :]
        keep_given(info[0] == section, old, bufs)

        @pl.when(info[0] == section)
        def _():
            low = gradient_rows(g_s[...], live, masks, section).astype(BF)
            for c in range(parts):
                cols = slice(c * dim, (c + 1) * dim)
                block_s[c] = mm(joined(hid_s, cols), low, TN).astype(BF)
            half = dim // 2
            for c in range(parts):
                pieces = [(0, half, c, False, 0), (half, half, c, True, 0)]
                lay_out(info, bufs, block_s.at[c], pieces)

    scratch = [pltpu.VMEM((parts, dim, dim), BF)]
    aliases = {len(ins) - 4 + i: i for i in range(4)} if given else {}
    outs = buffer_shapes(dim) + [TOKEN]
    out = call(kernel, outs, ins, scratch, 0, aliases, "down_grad", after, DOWN_LIMIT)
    return out[:4], out[4]


def up_grad(section, info, live, masks, g, saved, params, before, after):
    mids, gps = [s[4] for s in saved], [s[5] for s in saved]
    upw, downw, gain, shift = params[4], params[6], params[8], params[9]
    rows, dim = g.shape
    wide = upw.shape[1]
    parts = wide // dim
    crops = len(saved)
    given = [] if before is None else list(before)
    ins = [info, live, masks, g, gain, shift, downw, upw] + mids + gps + given

    def kernel(info, live, masks, g_s, gain, shift, downw, upw, *refs):
        mid_s, gp_s = refs[:crops], refs[crops : 2 * crops]
        old = refs[2 * crops : 2 * crops + len(given)]
        refs = refs[2 * crops + len(given) :]
        bufs, gmid_s, small_s = refs[:4], refs[4], refs[5]
        gu_s, block_s = refs[7:]
        keep_given(info[0] == section, old, bufs)

        @pl.when(info[0] == section)
        def _():
            grad = gradient_rows(g_s[...], live, masks, section)
            low = grad.astype(BF)
            small_s[...] = jnp.zeros_like(small_s)
            small_s[ROW_DOWN : ROW_DOWN + 1, :] = jnp.sum(low.astype(F32), axis=0, keepdims=True)
            unit, inverse = unit_rows_of(joined(mid_s, slice(None)))
            normed_t = (unit * gain[1:2, :] + shift[1:2, :]).astype(BF).T
            for c in range(parts):
                cols = slice(c * dim, (c + 1) * dim)
                grad_up = mm(low, downw[cols, :], NT) * joined(gp_s, cols).astype(F32)
                grad_up = grad_up.astype(BF)
                gu_s[:, cols] = grad_up
                small_s[ROW_UP + c : ROW_UP + c + 1, :] = jnp.sum(
                    grad_up.astype(F32), axis=0, keepdims=True
                )
            back = mm(gu_s[...], upw[...], NT)
            gmid_s[...] = grad + norm_back(back, unit, inverse, gain[1:2, :])
            small_s[ROW_GAIN + 1 : ROW_GAIN + 2, :] = jnp.sum(back * unit, axis=0, keepdims=True)
            small_s[ROW_SHIFT + 1 : ROW_SHIFT + 2, :] = jnp.sum(back, axis=0, keepdims=True)
            for c in range(parts):
                block_s[c] = mm(normed_t, gu_s[:, c * dim : (c + 1) * dim]).astype(BF)
            for c in range(parts):
                lay_out(info, bufs, block_s.at[c], quarters(c, dim, parts))

    scratch = [pltpu.VMEM((rows, wide), BF), pltpu.VMEM((parts, dim, dim), BF)]
    aliases = {len(ins) - 4 + i: i for i in range(4)} if given else {}
    outs = buffer_shapes(dim) + [shape((rows, dim), F32), shape((PAD, dim), F32), TOKEN]
    out = call(kernel, outs, ins, scratch, 0, aliases, "up_grad", after, UP_LIMIT)
    return out[:4], out[4], out[5], out[6]


def rotate_back(block, tab_t):
    half = HEAD_DIM // 2
    cos, sin = tab_t[0], tab_t[1]
    out = []
    for at in range(0, block.shape[0], HEAD_DIM):
        a, b = block[at : at + half], block[at + half : at + HEAD_DIM]
        out += [a * cos + b * sin, b * cos - a * sin]
    return jnp.concatenate(out, axis=0)


def attention_grad(section, info, gmid, small, xs, saved, params, tab_t, before, after):
    qkvs, probs, mixts = [s[1] for s in saved], [s[2] for s in saved], [s[3] for s in saved]
    qkvw, outw, gain, shift = params[0], params[2], params[8], params[9]
    rows, dim = gmid.shape
    blocks = dim // 128
    per = 128 // HEAD_DIM
    crops = len(saved)
    given = [] if before is None else [before]
    ins = [info, gmid, outw, small, gain, shift, tab_t, qkvw]
    ins += qkvs + probs + mixts + list(xs) + given

    def kernel(info, gmid_s, outw, small_s, gain, shift, tab_t, qkvw, *refs):
        qkv_s, prob_s, mixt_s = (refs[i * crops : (i + 1) * crops] for i in range(3))
        x_s = refs[3 * crops : 3 * crops + len(xs)]
        old = refs[3 * crops + len(xs) : 3 * crops + len(xs) + len(given)]
        refs = refs[3 * crops + len(xs) + len(given) :]
        keep_given(info[0] == section, old, refs[:1])
        dx_s, gqkv_s, normt_s, low_s, small_out = refs[:5]
        gmt_s, delta_s, da_s, ds_s, dt_s, kt_s = refs[6:]

        @pl.when(info[0] == section)
        def _():
            low = gmid_s[...].astype(BF)
            low_s[...] = low
            gmt_s[...] = mm(outw[...], low, NT).astype(BF)
            for c in range(crops):
                crop = slice(c * LEN, (c + 1) * LEN)
                qkv, prob = qkv_s[c], prob_s[c]
                product = gmt_s[:, crop].astype(F32) * mixt_s[c][...].astype(F32)
                delta_s[...] = jnp.sum(product.reshape(HEADS, HEAD_DIM, LEN), axis=1)[:, None, :]
                kt_s[0] = qkv[:, dim : 2 * dim].T
                kt_s[1] = qkv[:, :dim].T
                for j in range(blocks):
                    v = qkv[:, 2 * dim + 128 * j : 2 * dim + 128 * j + 128]
                    da_s[per * LEN * j : per * LEN * (j + 1), :] = mm(
                        head_stack(v, per), gmt_s[128 * j : 128 * j + 128, crop]
                    )

                def scores(h, _):
                    da = da_s[pl.ds(pl.multiple_of(h * LEN, LEN), LEN), :]
                    ds_s[h] = (prob[h].astype(F32) * (da - delta_s[h])).astype(BF)
                    return 0

                lax.fori_loop(0, HEADS, scores, 0, unroll=2)
                for h in range(HEADS):
                    at = slice(HEAD_DIM * h, HEAD_DIM * (h + 1))
                    dt_s[0, at, :] = mm(kt_s[0, at, :], ds_s[h])
                    dt_s[1, at, :] = mm(kt_s[1, at, :], ds_s[h], NT)
                    dt_s[2, at, :] = mm(gmt_s[at, crop], prob[h], NT)
                dq = rotate_back(dt_s[0] * HEAD_DIM**-0.5, tab_t)
                gqkv_s[crop, :dim] = dq.astype(BF).T
                gqkv_s[crop, dim : 2 * dim] = rotate_back(dt_s[1], tab_t).astype(BF).T
                gqkv_s[crop, 2 * dim :] = dt_s[2].astype(BF).T
            unit, inverse = unit_rows_of(joined(x_s, slice(None)).astype(F32))
            normt_s[...] = (unit * gain[0:1, :] + shift[0:1, :]).astype(BF).T
            back = mm(gqkv_s[...], qkvw[...], NT)
            dx_s[...] = (gmid_s[...] + norm_back(back, unit, inverse, gain[0:1, :])).astype(BF)
            small_out[...] = small_s[...]
            small_out[ROW_GAIN : ROW_GAIN + 1, :] = jnp.sum(back * unit, axis=0, keepdims=True)
            small_out[ROW_SHIFT : ROW_SHIFT + 1, :] = jnp.sum(back, axis=0, keepdims=True)

    outs = [
        shape((rows, dim), BF),
        shape((rows, 3 * dim), BF),
        shape((dim, rows), BF),
        shape((rows, dim), BF),
        shape(small.shape, F32),
        TOKEN,
    ]
    scratch = [
        pltpu.VMEM((dim, rows), BF),
        pltpu.VMEM((HEADS, 1, LEN), F32),
        pltpu.VMEM((HEADS * LEN, LEN), F32),
        pltpu.VMEM((HEADS, LEN, LEN), BF),
        pltpu.VMEM((3, dim, LEN), F32),
        pltpu.VMEM((2, dim, LEN), BF),
    ]
    aliases = {len(ins) - 1: 0} if given else {}
    out = call(kernel, outs, ins, scratch, 0, aliases, "attention_grad", after, ATTENTION_LIMIT)
    return out[0], out[1:5], out[5]


def qkv_grad(section, info, kept, saved, after):
    gqkv, normt, low, small = kept
    mixts = [s[3] for s in saved]
    rows, dim = low.shape
    parts = 4
    ins = [info, gqkv, normt, low, small] + mixts

    def kernel(info, gqkv_s, normt_s, low_s, small_s, *refs):
        mixt_s = refs[: len(mixts)]
        bufs = refs[len(mixts) : len(mixts) + 4]
        (block_s,) = refs[len(mixts) + 5 :]

        @pl.when(info[0] == section)
        def _():
            sums = [
                jnp.sum(gqkv_s[:, c * dim : (c + 1) * dim].astype(F32), axis=0, keepdims=True)
                for c in range(3)
            ]
            sums.append(jnp.sum(low_s[...].astype(F32), axis=0, keepdims=True))
            tail = jnp.concatenate(sums + [small_s[ROW_UP:, :]], axis=0).astype(BF)
            bufs[0][dim:, :] = tail
            bufs[1][dim:, :] = tail
            for c in range(3):
                block_s[c] = mm(normt_s[...], gqkv_s[:, c * dim : (c + 1) * dim]).astype(BF)
            mixt = jnp.concatenate([m[...] for m in mixt_s], axis=1)
            block_s[3] = mm(mixt, low_s[...]).astype(BF)
            for c in range(parts):
                lay_out(info, bufs, block_s.at[c], quarters(c, dim, parts))

    scratch = [pltpu.VMEM((parts, dim, dim), BF)]
    outs = buffer_shapes(dim) + [TOKEN]
    out = call(kernel, outs, ins, scratch, 0, {}, "qkv_grad", after, DOWN_LIMIT)
    return out[:4], out[4]


def plus(one, two):
    return (one.astype(F32) + two.astype(F32)).astype(BF)


def taking_part(info, sections, middle):
    check = None
    if len(sections) == 1:
        check = info[0] == sections[0]
    if middle:
        inner = jnp.logical_or(info[3] == 1, info[3] == 2)
        check = inner if check is None else jnp.logical_and(check, inner)
    return info[3] >= 0 if check is None else check


def vmem_call(kernel, outs, info, ins, name, after):
    return call(kernel, outs, [info] + ins, [], 0, {}, name, after, 8)


def first_sum(info, sections, keep_a, recv_a, keep_b, recv_b, after):
    dim = keep_b.shape[1]
    half = dim // 2

    def kernel(info, ka, ra, kb, rb, sa, na, sb, nb):
        @pl.when(taking_part(info, sections, False))
        def _():
            for own, one, two, new, out in ((info[2], ka, ra, na, sa), (info[1], kb, rb, nb, sb)):
                mine = pl.ds(pl.multiple_of(own * half, half), half)
                other = pl.ds(pl.multiple_of((1 - own) * half, half), half)
                out[:half, :] = plus(one[other, :], two[other, :])
                new[:half, :] = plus(one[mine, :], two[mine, :])
                if one.shape[0] > 2 * half:
                    tail = plus(one[2 * half :, :], two[2 * half :, :])
                    new[half:, :] = tail
                    out[half:, :] = tail

    outs = [shape((half + PAD, dim), BF)] * 2 + [shape((half, dim), BF)] * 2
    return vmem_call(kernel, outs, info, [keep_a, recv_a, keep_b, recv_b], "first_sum", after)


def second_sum(info, sections, keep_a, recv_a, keep_b, recv_b, after):
    dim = keep_b.shape[1]

    def kernel(info, ka, ra, kb, rb, out):
        @pl.when(taking_part(info, sections, False))
        def _():
            top = ka.shape[0]
            out[:top, :] = plus(ka[...], ra[...])
            out[top:, :] = plus(kb[...], rb[...])

    outs = [shape((dim + PAD, dim), BF)]
    return vmem_call(kernel, outs, info, [keep_a, recv_a, keep_b, recv_b], "second_sum", after)[0]


def pair_sum(info, sections, one, two, after):
    def kernel(info, one, two, out):
        @pl.when(taking_part(info, sections, True))
        def _():
            out[...] = plus(one[...], two[...])

    return vmem_call(kernel, [shape(one.shape, BF)], info, [one, two], "pair_sum", after)[0]


def own_pieces(row, count, width, group):
    share = count * width // GROUPS
    at, pieces = group * share, []
    while at < (group + 1) * share:
        size = min((group + 1) * share - at, width - at % width)
        pieces.append((row + at // width, at % width, size, at - group * share))
        at += size
    return pieces


def finish(info, sources, wide, after):
    (part0, got0), (part1, got1) = sources
    rows, dim = part0.shape
    half = dim // 2
    quarter = half // 2
    vectors = ((ROW_QKV, 3), (ROW_OUT, 1), (ROW_UP, 4), (ROW_DOWN, 1))
    if wide == 0:
        outs = [shape((dim, dim), F32)]
    elif wide == 4:
        outs = [shape((quarter, 4 * dim), F32)]
    else:
        outs = [shape((quarter, 3 * dim), F32), shape((quarter, dim), F32)]
    large = len(outs)
    if wide == 3:
        outs += [shape((1, count * dim // GROUPS), F32) for _, count in vectors]
        outs += [shape((2, dim // GROUPS), F32)] * 2

    def kernel(info, p0, g0, p1, g1, *refs):
        out_h = refs[:large]
        small = refs[large : len(outs)]
        src = refs[len(outs)]
        stage = refs[len(outs) + 1 : -1]
        sems = refs[-1]
        inner = jnp.logical_or(info[3] == 1, info[3] == 2)
        for section, part, got in ((0, p0, g0), (1, p1, g1)):
            mine = info[0] == section

            @pl.when(jnp.logical_and(mine, inner))
            def _():
                pltpu.make_async_copy(part, src, sems.at[0]).start()

            @pl.when(jnp.logical_and(mine, jnp.logical_not(inner)))
            def _():
                pltpu.make_async_copy(got, src, sems.at[0]).start()

        pltpu.make_async_copy(p0, src, sems.at[0]).wait()
        block_a = src[:half, :].astype(F32)
        block_b = src[half + PAD :, :].astype(F32)
        if wide == 0:
            stage[0][:half, :] = block_a
            stage[0][half:, :] = block_b
        else:
            pieces = (block_a[:quarter], block_a[quarter:], block_b[:quarter], block_b[quarter:])
            for i in range(wide):
                stage[0][:, i * dim : (i + 1) * dim] = pieces[i]
            if wide == 3:
                stage[1][...] = pieces[3]
        copies = [
            pltpu.make_async_copy(s, o, sems.at[1 + i]) for i, (s, o) in enumerate(zip(stage, out_h))
        ]
        for copy in copies:
            copy.start()
        if wide == 3:
            tail = src[half : half + PAD, :].astype(F32)
            for group in range(GROUPS):

                @pl.when(info[1] + 2 * info[2] == group)
                def _():
                    for out, (row, count) in zip(small, vectors):
                        for r, c, size, at in own_pieces(row, count, dim, group):
                            out[:, at : at + size] = tail[r : r + 1, c : c + size]
                    share = dim // GROUPS
                    for out, row in zip(small[4:], (ROW_GAIN, ROW_SHIFT)):
                        out[...] = tail[row : row + 2, group * share : (group + 1) * share]

        for copy in copies:
            copy.wait()

    scratch = [vmem_like(part0)] + [vmem_like(o) for o in outs[:large]]
    ins = [info, part0, got0, part1, got1]
    places = "h" * large + "v" * (len(outs) - large)
    return call(kernel, outs, ins, scratch, 4, {}, "finish", after, 12, "saaaa", places)


def flow(shard, axis, pairs, sections):
    if sections == (0, 1):
        return lax.ppermute(shard, axis, pairs)
    peers = lax.axis_size(axis)
    pairs = [(s * peers + i, s * peers + j) for s in sections for i, j in pairs]
    return lax.ppermute(shard, ("section", axis), pairs)


class Reduction:
    def __init__(self, info, sections, bufs):
        self.info, self.sections, self.bufs = info, sections, bufs
        groups = range(lax.axis_size("group"))
        self.across = [(g, g ^ 1) for g in groups]
        self.along = [(g, g ^ 2) for g in groups]
        self.line = lax.axis_size("replica") == 4
        self.got = (
            flow(bufs[0], "group", self.across, sections),
            flow(bufs[2], "group", self.along, sections),
        )

    def group_two(self, after):
        send_a, keep_a, send_b, keep_b = first_sum(
            self.info, self.sections, self.bufs[1], self.got[0], self.bufs[3], self.got[1], after
        )
        self.kept = (keep_a, keep_b)
        self.got = (
            flow(send_a, "group", self.along, self.sections),
            flow(send_b, "group", self.across, self.sections),
        )
        return keep_a

    def replica_one(self, after):
        self.part = second_sum(
            self.info, self.sections, self.kept[0], self.got[0], self.kept[1], self.got[1], after
        )
        if self.line:
            self.got = flow(self.part, "replica", [(0, 1), (3, 2)], self.sections)
        else:
            self.part = self.got = lax.psum(self.part, "replica")
        return self.part

    def replica_next(self, pairs, after):
        if self.line:
            self.part = pair_sum(self.info, self.sections, self.part, self.got, after)
            self.got = flow(self.part, "replica", pairs, self.sections)
        return self.part

    def replica_two(self, after):
        return self.replica_next([(1, 2), (2, 1)], after)

    def replica_three(self, after):
        return self.replica_next([(1, 0), (2, 3)], after)


def shards(
    block_input,
    cotangent,
    crop_count,
    mask_count,
    qkv_weight,
    qkv_bias,
    out_weight,
    out_bias,
    up_weight,
    up_bias,
    down_weight,
    down_bias,
    norm_gain,
    norm_shift,
):
    params = (
        qkv_weight[0],
        qkv_bias,
        out_weight[0],
        out_bias,
        up_weight[0],
        up_bias,
        down_weight[0],
        down_bias,
        norm_gain[0],
        norm_shift[0],
    )
    rows, dim = block_input.shape
    tab = jnp.asarray(rotary_tables())
    tab_t = jnp.asarray(rotary_columns())
    group = lax.axis_index("group")
    assert lax.axis_size("group") == GROUPS
    info = jnp.stack([lax.axis_index("section"), group % 2, group // 2, lax.axis_index("replica")])

    def to_other(shard, pairs):
        return lax.ppermute(shard, "section", pairs)

    act, first = forward(0, info, crop_count, block_input, None, params, tab, None)
    arrived = [to_other(first[0], [(0, 1)])]
    act, second = forward(1, info, crop_count, block_input, arrived[0], params, tab, act)
    arrived.append(to_other(second[0], [(0, 1)]))
    act, third = forward(2, info, crop_count, block_input, arrived[1], params, tab, act)
    kept_one, kept_zero = (second, third), (first, second)

    common = (info, crop_count, mask_count)
    bufs, last = down_grad(1, *common, cotangent, kept_one, None, None)
    one = Reduction(info, (1,), bufs)
    bufs, gmid, small, last = up_grad(1, *common, cotangent, kept_one, params, None, last)
    two = Reduction(info, (1,), bufs)
    last = one.group_two(last)
    dx, kept, last = attention_grad(
        1, info, gmid, small, arrived, kept_one, params, tab_t, None, last
    )
    grad_back = to_other(dx, [(1, 0)])
    last = one.replica_one(last)
    last = two.group_two(last)
    bufs_three, last = qkv_grad(1, info, kept, kept_one, last)
    bufs, last = down_grad(0, *common, grad_back, kept_zero, bufs_three, last)
    three = Reduction(info, (0, 1), bufs)
    bufs, gmid, small, last = up_grad(0, *common, grad_back, kept_zero, params, None, last)
    four = Reduction(info, (0,), bufs)
    last = one.replica_two(last)
    last = two.replica_one(last)
    dx, kept, last = attention_grad(
        0, info, gmid, small, [block_input], kept_zero, params, tab_t, dx, last
    )
    last = one.replica_three(last)
    last = two.replica_two(last)
    last = three.group_two(last)
    last = four.group_two(last)
    bufs, last = qkv_grad(0, info, kept, kept_zero, last)
    five = Reduction(info, (0,), bufs)
    last = two.replica_three(last)
    last = three.replica_one(last)
    last = four.replica_one(last)
    last = five.group_two(last)
    last = three.replica_two(last)
    last = four.replica_two(last)
    last = five.replica_one(last)
    last = three.replica_three(last)
    last = four.replica_three(last)
    last = five.replica_two(last)

    def both(zero, one):
        return ((zero.part, zero.got), (one.part, one.got))

    (grad_down,) = finish(info, both(three, one), 0, last)
    (grad_up,) = finish(info, both(four, two), 4, grad_down)
    last = five.replica_three(grad_up)
    grad_qkv, grad_out, *small = finish(info, both(five, three), 3, last)
    qkv_b, out_b, up_b, down_b, gain, shift = small
    return (
        act[None],
        dx[None],
        grad_qkv[None],
        qkv_b,
        grad_out[None],
        out_b,
        grad_up[None],
        up_b,
        grad_down[None],
        down_b,
        gain[None],
        shift[None],
    )


def solution(mesh):
    rows = P(("group", "replica"))
    stack = P("section")
    return jax.shard_map(
        shards,
        mesh=mesh,
        in_specs=(rows,) * 4 + (stack,) * 10,
        out_specs=(
            P("section", ("group", "replica"), None),
            P("section", ("group", "replica"), None),
            P("section", "group", None),
            P("section", "group"),
            P("section", "group", None),
            P("section", "group"),
            P("section", "group", None),
            P("section", "group"),
            P("section", "group", None),
            P("section", "group"),
            P("section", None, "group"),
            P("section", None, "group"),
        ),
        check_vma=False,
    )
```

```python
import jax
import jax.numpy as jnp
import numpy as np
from jax import lax
from jax.experimental import pallas as pl
from jax.experimental.pallas import tpu as pltpu
from jax.sharding import PartitionSpec as P

HEADS = 20
HEAD_DIM = 32
LEN = 256
MASK_MEAN = 38
CROP_DEV = 2
EPSILON = 1e-05
ROTARY_BASE = 10000.0

BF = jnp.bfloat16
F32 = jnp.float32
NN = (((1,), (0,)), ((), ()))
NT = (((1,), (1,)), ((), ()))
TN = (((0,), (0,)), ((), ()))

FIRST_LIMIT, FORWARD_LIMIT, MLP_LIMIT, ATTENTION_LIMIT, QKV_LIMIT = 40, 16, 15, 16, 8
ATTENTION_MICROS = 12
GROUPS = 4
PAD = 16
ROW_QKV, ROW_OUT, ROW_UP, ROW_DOWN, ROW_GAIN, ROW_SHIFT = 0, 3, 4, 8, 9, 11

ANY = pl.BlockSpec(memory_space=pl.ANY)
HBM = pl.BlockSpec(memory_space=pltpu.HBM)
VMEM = pl.BlockSpec(memory_space=pltpu.VMEM)
SMEM = pl.BlockSpec(memory_space=pltpu.SMEM)


def shape(dims, dtype):
    return jax.ShapeDtypeStruct(dims, dtype)


def mm(left, right, dims=NN):
    return lax.dot_general(left, right, dims, preferred_element_type=F32)


def unit_rows_of(values):
    centred = values - jnp.mean(values, axis=-1, keepdims=True)
    inverse = lax.rsqrt(jnp.mean(centred * centred, axis=-1, keepdims=True) + EPSILON)
    return centred * inverse, inverse


def norm_back(grad, unit, inverse, gain):
    scaled = grad * gain
    return inverse * (
        scaled
        - jnp.mean(scaled, axis=-1, keepdims=True)
        - unit * jnp.mean(scaled * unit, axis=-1, keepdims=True)
    )


def rotary_tables():
    lane = np.arange(128) % HEAD_DIM
    half = HEAD_DIM // 2
    freq = ROTARY_BASE ** (-(lane % half).astype(np.float64) * (2.0 / HEAD_DIM))
    angles = np.arange(LEN)[:, None] * freq[None, :]
    sign = np.where(lane < half, -1.0, 1.0)[None, :]
    return np.stack([np.cos(angles), np.sin(angles) * sign]).astype(np.float32)


def rotary_columns():
    half = HEAD_DIM // 2
    freq = ROTARY_BASE ** (-np.arange(half, dtype=np.float64) * (2.0 / HEAD_DIM))
    angles = freq[:, None] * np.arange(LEN)[None, :]
    return np.stack([np.cos(angles), np.sin(angles)]).astype(np.float32)


def swap_halves(values):
    lane = lax.broadcasted_iota(jnp.int32, values.shape, 1) % HEAD_DIM
    half = HEAD_DIM // 2
    return jnp.where(
        lane < half,
        pltpu.roll(values, 128 - half, axis=1),
        pltpu.roll(values, half, axis=1),
    )


def head_stack(block, per):
    head = lax.broadcasted_iota(jnp.int32, block.shape, 1) // HEAD_DIM
    return jnp.concatenate(
        [jnp.where(head == h, block, jnp.zeros_like(block)) for h in range(per)], axis=0
    )


class Copies:
    def __init__(self, sems):
        self.sems = sems
        self.used = 0
        self.open = []

    def start(self, src, dst):
        copy = pltpu.make_async_copy(src, dst, self.sems.at[self.used])
        self.used += 1
        copy.start()
        return copy

    def save(self, src, dst):
        self.open.append(self.start(src, dst))

    def finish(self):
        for copy in self.open:
            copy.wait()


def call(kernel, outs, ins, scratch, sems, aliases, name, after=None, limit=16, spaces=None, out_spaces=None, micros=0.1):
    count = len(ins)
    places = {"v": VMEM, "h": HBM, "a": ANY, "s": SMEM}
    spaces = spaces or "v" * count
    out_spaces = out_spaces or "v" * len(outs)
    in_specs = [SMEM if a.ndim == 1 else places[p] for a, p in zip(ins, spaces)]
    ins = [pltpu.with_memory_space_constraint(a, pltpu.HBM) if p == "h" else a for a, p in zip(ins, spaces)]
    body = kernel
    if after is not None:
        ins = list(ins) + [after]
        in_specs = in_specs + [ANY]

        def body(*refs):
            kernel(*refs[:count], *refs[count + 1 :])

    outs = [pltpu.HBM(o.shape, o.dtype) if p == "h" else o for o, p in zip(outs, out_spaces)]
    return pl.pallas_call(
        body,
        out_shape=outs,
        in_specs=in_specs,
        out_specs=[places[p] for p in out_spaces],
        scratch_shapes=scratch + ([pltpu.SemaphoreType.DMA((sems,))] if sems else []),
        input_output_aliases=aliases,
        compiler_params=pltpu.CompilerParams(vmem_limit_bytes=limit << 20),
        cost_estimate=pl.CostEstimate(
            flops=int(micros * 1.15e9), bytes_accessed=0, transcendentals=0
        ),
        name=name,
    )(*ins)


TOKEN = jax.ShapeDtypeStruct((8, 128), F32)


def vmem_like(arr):
    return pltpu.VMEM(arr.shape, arr.dtype)


def forward(slot, info, live, own, arrived, params, tab, act, after=None):
    qkvw, qkvb, outw, outb, upw, upb, downw, downb, gain, shift = params
    dim = own.shape[1]
    blocks = dim // 128
    wide = upw.shape[1]
    parts = wide // dim
    per = 128 // HEAD_DIM
    manual = slot == 0
    saved = [
        shape((LEN, dim), BF),
        shape((LEN, 3 * dim), BF),
        shape((HEADS, LEN, LEN), BF),
        shape((dim, LEN), BF),
        shape((LEN, dim), F32),
        shape((LEN, wide), BF),
        shape((LEN, wide), BF),
    ]
    weights = [qkvb, outb, upb, downb, gain, shift, tab, qkvw, outw, upw, downw]
    sources = [own] if slot == 0 else [arrived] if slot == 2 else [own, arrived]
    before = [] if act is None else [act]
    ins = [info, live] + sources + weights + before
    count = len(sources)

    def kernel(info, live, *refs):
        xs = refs[:count]
        given = refs[count : count + 11]
        act_h, *outs = refs[count + 11 + len(before) : count + 19 + len(before)]
        scratch = refs[count + 19 + len(before) :]
        act_s, vt_s, score_s, up_s = scratch[:4]
        sems = scratch[-1]
        y_s, qkv_s, prob_s, mixt_s, mid_s, gp_s, hid_s = outs
        used = scratch[4:-1] if manual else xs[-1:] + given
        qkvb, outb, upb, downb, gain, shift, tab, qkvw, outw, upw, downw = used[1:]
        crop = slot - info[0]

        @pl.when(jnp.logical_and(crop >= 0, crop < CROP_DEV))
        def _():
            copies = Copies(sems)
            heavy = []
            if manual:
                rows = xs[0].at[pl.ds(0, LEN)]
                loads = [copies.start(h, s) for h, s in zip((rows,) + given, used)]
                heavy = loads[8:]
                wait_all(loads[:8])
                x = used[0][...].astype(F32)
            elif slot == 1:
                x = jnp.where(info[0] == 0, xs[0][LEN:, :], xs[1][...]).astype(F32)
            else:
                x = xs[0][...].astype(F32)

            def ready(index):
                if manual:
                    heavy[index].wait()

            unit, _ = unit_rows_of(x)
            normed = (unit * gain[0:1, :] + shift[0:1, :]).astype(BF)
            ready(0)
            third = mm(normed, qkvw[:, 2 * dim :]) + qkvb[:, 2 * dim :]
            low = third.astype(BF)
            qkv_s[:, 2 * dim :] = low
            vt_s[...] = low.T
            for part in range(2):
                third = mm(normed, qkvw[:, part * dim : (part + 1) * dim])
                third = third + qkvb[:, part * dim : (part + 1) * dim]
                for j in range(blocks):
                    b = third[:, 128 * j : 128 * j + 128]
                    b = b * tab[0] + swap_halves(b) * tab[1]
                    if part == 0:
                        b = b * HEAD_DIM**-0.5
                    at = part * dim + 128 * j
                    qkv_s[:, at : at + 128] = b.astype(BF)
            for j in range(blocks):
                q = qkv_s[:, 128 * j : 128 * j + 128]
                k = qkv_s[:, dim + 128 * j : dim + 128 * j + 128]
                score_s[per * LEN * j : per * LEN * (j + 1), :] = mm(head_stack(k, per), q, NT)

            def soft(h, _):
                s = score_s[pl.ds(pl.multiple_of(h * LEN, LEN), LEN), :]
                e = jnp.exp(s - jnp.max(s, axis=0, keepdims=True))
                prob_s[h] = (e * (1.0 / jnp.sum(e, axis=0, keepdims=True))).astype(BF)
                return 0

            lax.fori_loop(0, HEADS, soft, 0, unroll=2)
            for h in range(HEADS):
                at = slice(HEAD_DIM * h, HEAD_DIM * (h + 1))
                mixt_s[at, :] = mm(vt_s[at, :], prob_s[h]).astype(BF)
            ready(1)
            mid = x + mm(mixt_s[...], outw[...], TN) + outb[...]
            mid_s[...] = mid
            unit, _ = unit_rows_of(mid)
            normed = (unit * gain[1:2, :] + shift[1:2, :]).astype(BF)
            ready(2)
            up_s[...] = mm(normed, upw[...])
            for c in range(parts):
                cols = slice(c * dim, (c + 1) * dim)
                u = up_s[:, cols] + upb[:, cols]
                cdf = 0.5 + 0.5 * lax.erf(u * 0.5**0.5)
                hid_s[:, cols] = (u * cdf).astype(BF)
                gp_s[:, cols] = (
                    cdf + u * (jnp.exp(u * u * -0.5) * (2 * np.pi) ** -0.5)
                ).astype(BF)
            ready(3)
            low = (mid_s[...] + downb[...] + mm(hid_s[...], downw[...])).astype(BF)
            y_s[...] = low
            act_s[...] = jnp.where(crop < live[0], low, jnp.zeros_like(low))
            at = pl.multiple_of(crop * LEN, LEN)
            copies.save(act_s, act_h.at[pl.ds(at, LEN)])
            copies.finish()

    outs = [shape(own.shape, BF)] + saved
    scratch = [
        pltpu.VMEM((LEN, dim), BF),
        pltpu.VMEM((dim, LEN), BF),
        pltpu.VMEM((HEADS * LEN, LEN), F32),
        pltpu.VMEM((LEN, wide), F32),
    ]
    if manual:
        scratch += [pltpu.VMEM((LEN, dim), BF)] + [vmem_like(a) for a in weights]
    aliases = {} if act is None else {len(ins) - 1: 0}
    spaces = "ss" + ("h" if manual else "v") * (count + 11) + "h" * len(before)
    out = call(
        kernel,
        outs,
        ins,
        scratch,
        16,
        aliases,
        "layer_forward",
        after,
        FIRST_LIMIT if manual else FORWARD_LIMIT,
        spaces,
        "h" + "v" * 7,
    )
    return out[0], out[1:]


def gradient_rows(g, live, masks, section):
    grad = g.astype(F32)
    if section == 0:
        return grad
    crop = lax.broadcasted_iota(jnp.int32, (g.shape[0], 1), 0) // LEN
    weight = jnp.zeros_like(crop)
    for c in range(CROP_DEV):
        weight = jnp.where(crop == c, masks[c], weight)
    weight = jnp.where(crop < live[0], weight, 0)
    return grad * (weight.astype(F32) / MASK_MEAN)


def lay_out(own, keep, send, block, pieces):
    for row, count, bit, at in pieces:
        mine = own == bit

        @pl.when(mine)
        def _():
            keep[at : at + count, :] = block[row : row + count, :]

        @pl.when(jnp.logical_not(mine))
        def _():
            send[at : at + count, :] = block[row : row + count, :]


def keep_given(active, given, bufs):
    @pl.when(jnp.logical_not(active))
    def _():
        for old, new in zip(given, bufs):
            new[...] = old[...]


def pair_shapes(rows, dim):
    return [shape((rows, dim), BF)] * 2


def joined(refs, cols):
    return jnp.concatenate([r[:, cols] for r in refs], axis=0)


def wait_all(copies):
    for copy in copies:
        copy.wait()


def mlp_grad(section, info, live, masks, g, saved, params, after):
    mixts = [s[3] for s in saved]
    mids, gps, hids = ([s[k] for s in saved] for k in (4, 5, 6))
    upw, downw, gain, shift = params[4], params[6], params[8], params[9]
    rows, dim = g.shape
    wide = upw.shape[1]
    parts = wide // dim
    crops = len(saved)
    share = dim // GROUPS
    ins = [info, live, masks, g, gain, shift, downw, upw] + mids + gps + hids + mixts

    def kernel(info, live, masks, g_s, gain, shift, downw, upw, *refs):
        mid_s, gp_s, hid_s, mixt_s = (refs[i * crops : (i + 1) * crops] for i in range(4))
        refs = refs[4 * crops :]
        send_a, keep_a, send_b, keep_b, gmid_s, small_s = refs[:6]
        gu_s, block_s = refs[7:]

        @pl.when(info[0] == section)
        def _():
            grad = gradient_rows(g_s[...], live, masks, section)
            low = grad.astype(BF)
            small_s[...] = jnp.zeros_like(small_s)
            small_s[ROW_DOWN : ROW_DOWN + 1, :] = jnp.sum(low.astype(F32), axis=0, keepdims=True)
            unit, inverse = unit_rows_of(joined(mid_s, slice(None)))
            normed_t = (unit * gain[1:2, :] + shift[1:2, :]).astype(BF).T
            for c in range(parts):
                cols = slice(c * dim, (c + 1) * dim)
                block_s[c] = mm(joined(hid_s, cols), low, TN).astype(BF)
            for shard in range(GROUPS):
                piece = [(0, dim, shard % 2, shard // 2 * dim)]
                lay_out(info[1], keep_a, send_a, block_s.at[shard], piece)
            for c in range(parts):
                cols = slice(c * dim, (c + 1) * dim)
                grad_up = mm(low, downw[cols, :], NT) * joined(gp_s, cols).astype(F32)
                grad_up = grad_up.astype(BF)
                gu_s[:, cols] = grad_up
                small_s[ROW_UP + c : ROW_UP + c + 1, :] = jnp.sum(
                    grad_up.astype(F32), axis=0, keepdims=True
                )
            back = mm(gu_s[...], upw[...], NT)
            gmid = grad + norm_back(back, unit, inverse, gain[1:2, :])
            gmid_s[...] = gmid
            small_s[ROW_GAIN + 1 : ROW_GAIN + 2, :] = jnp.sum(back * unit, axis=0, keepdims=True)
            small_s[ROW_SHIFT + 1 : ROW_SHIFT + 2, :] = jnp.sum(back, axis=0, keepdims=True)
            low = gmid.astype(BF)
            small_s[ROW_OUT : ROW_OUT + 1, :] = jnp.sum(low.astype(F32), axis=0, keepdims=True)
            for c in range(parts):
                block_s[c] = mm(normed_t, gu_s[:, c * dim : (c + 1) * dim]).astype(BF)
            mixt = jnp.concatenate([m[...] for m in mixt_s], axis=1)
            block_s[parts] = mm(mixt, low).astype(BF)
            for shard in range(GROUPS):
                x, y = shard % 2, shard // 2
                for c in range(parts + 1):
                    at = (x * (parts + 1) + c) * share
                    lay_out(info[2], keep_b, send_b, block_s.at[c], [(shard * share, share, y, at)])

    scratch = [
        pltpu.VMEM((rows, wide), BF),
        pltpu.VMEM((parts + 1, dim, dim), BF),
    ]
    outs = pair_shapes(2 * dim, dim) + pair_shapes(2 * (parts + 1) * share, dim)
    outs += [shape((rows, dim), F32), shape((PAD, dim), F32), TOKEN]
    out = call(kernel, outs, ins, scratch, 0, {}, "mlp_grad", after, MLP_LIMIT)
    return out[:4], out[4], out[5], out[6]


def rotate_back(block, tab_t):
    half = HEAD_DIM // 2
    cos, sin = tab_t[0], tab_t[1]
    out = []
    for at in range(0, block.shape[0], HEAD_DIM):
        a, b = block[at : at + half], block[at + half : at + HEAD_DIM]
        out += [a * cos + b * sin, b * cos - a * sin]
    return jnp.concatenate(out, axis=0)


def attention_grad(section, info, gmid, small, xs, saved, params, tab_t, before, after):
    qkvs, probs, mixts = [s[1] for s in saved], [s[2] for s in saved], [s[3] for s in saved]
    qkvw, outw, gain, shift = params[0], params[2], params[8], params[9]
    rows, dim = gmid.shape
    blocks = dim // 128
    per = 128 // HEAD_DIM
    crops = len(saved)
    given = [] if before is None else [before]
    ins = [info, gmid, outw, small, gain, shift, tab_t, qkvw]
    ins += qkvs + probs + mixts + list(xs) + given

    def kernel(info, gmid_s, outw, small_s, gain, shift, tab_t, qkvw, *refs):
        qkv_s, prob_s, mixt_s = (refs[i * crops : (i + 1) * crops] for i in range(3))
        x_s = refs[3 * crops : 3 * crops + len(xs)]
        old = refs[3 * crops + len(xs) : 3 * crops + len(xs) + len(given)]
        refs = refs[3 * crops + len(xs) + len(given) :]
        keep_given(info[0] == section, old, refs[:1])
        dx_s, gqkv_s, normt_s, small_out = refs[:4]
        gmt_s, delta_s, da_s, ds_s, dt_s, kt_s = refs[5:]

        @pl.when(info[0] == section)
        def _():
            low = gmid_s[...].astype(BF)
            gmt_s[...] = mm(outw[...], low, NT).astype(BF)
            for c in range(crops):
                crop = slice(c * LEN, (c + 1) * LEN)
                qkv, prob = qkv_s[c], prob_s[c]
                product = gmt_s[:, crop].astype(F32) * mixt_s[c][...].astype(F32)
                delta_s[...] = jnp.sum(product.reshape(HEADS, HEAD_DIM, LEN), axis=1)[:, None, :]
                kt_s[0] = qkv[:, dim : 2 * dim].T
                kt_s[1] = qkv[:, :dim].T
                for j in range(blocks):
                    v = qkv[:, 2 * dim + 128 * j : 2 * dim + 128 * j + 128]
                    da_s[per * LEN * j : per * LEN * (j + 1), :] = mm(
                        head_stack(v, per), gmt_s[128 * j : 128 * j + 128, crop]
                    )

                def scores(h, _):
                    da = da_s[pl.ds(pl.multiple_of(h * LEN, LEN), LEN), :]
                    ds_s[h] = (prob[h].astype(F32) * (da - delta_s[h])).astype(BF)
                    return 0

                lax.fori_loop(0, HEADS, scores, 0, unroll=2)
                for h in range(HEADS):
                    at = slice(HEAD_DIM * h, HEAD_DIM * (h + 1))
                    dt_s[0, at, :] = mm(kt_s[0, at, :], ds_s[h])
                    dt_s[1, at, :] = mm(kt_s[1, at, :], ds_s[h], NT)
                    dt_s[2, at, :] = mm(gmt_s[at, crop], prob[h], NT)
                dq = rotate_back(dt_s[0] * HEAD_DIM**-0.5, tab_t)
                gqkv_s[crop, :dim] = dq.astype(BF).T
                gqkv_s[crop, dim : 2 * dim] = rotate_back(dt_s[1], tab_t).astype(BF).T
                gqkv_s[crop, 2 * dim :] = dt_s[2].astype(BF).T
            unit, inverse = unit_rows_of(joined(x_s, slice(None)).astype(F32))
            normt_s[...] = (unit * gain[0:1, :] + shift[0:1, :]).astype(BF).T
            back = mm(gqkv_s[...], qkvw[...], NT)
            dx_s[...] = (gmid_s[...] + norm_back(back, unit, inverse, gain[0:1, :])).astype(BF)
            small_out[...] = small_s[...]
            small_out[ROW_GAIN : ROW_GAIN + 1, :] = jnp.sum(back * unit, axis=0, keepdims=True)
            small_out[ROW_SHIFT : ROW_SHIFT + 1, :] = jnp.sum(back, axis=0, keepdims=True)

    outs = [
        shape((rows, dim), BF),
        shape((rows, 3 * dim), BF),
        shape((dim, rows), BF),
        shape(small.shape, F32),
        TOKEN,
    ]
    scratch = [
        pltpu.VMEM((dim, rows), BF),
        pltpu.VMEM((HEADS, 1, LEN), F32),
        pltpu.VMEM((HEADS * LEN, LEN), F32),
        pltpu.VMEM((HEADS, LEN, LEN), BF),
        pltpu.VMEM((3, dim, LEN), F32),
        pltpu.VMEM((2, dim, LEN), BF),
    ]
    aliases = {len(ins) - 1: 0} if given else {}
    out = call(kernel, outs, ins, scratch, 0, aliases, "attention_grad", after, ATTENTION_LIMIT, micros=ATTENTION_MICROS)
    return out[0], out[1:4], out[4]


def qkv_grad(section, info, kept, before, after):
    gqkv, normt, small = kept
    dim, rows = normt.shape
    share = dim // GROUPS
    half = 3 * share // 2
    given = [] if before is None else list(before)
    ins = [info, gqkv, normt, small] + given

    def kernel(info, gqkv_s, normt_s, small_s, *refs):
        old = refs[: len(given)]
        bufs = refs[len(given) : len(given) + 4]
        send_a, keep_a, send_b, keep_b = bufs
        (block_s,) = refs[len(given) + 5 :]
        keep_given(info[0] == section, old, bufs)

        @pl.when(info[0] == section)
        def _():
            sums = [
                jnp.sum(gqkv_s[:, c * dim : (c + 1) * dim].astype(F32), axis=0, keepdims=True)
                for c in range(3)
            ]
            tail = jnp.concatenate(sums + [small_s[ROW_OUT:, :]], axis=0).astype(BF)
            send_a[2 * half :, :] = tail
            keep_a[2 * half :, :] = tail
            for c in range(3):
                block_s[c] = mm(normt_s[...], gqkv_s[:, c * dim : (c + 1) * dim]).astype(BF)
            for shard in range(GROUPS):
                x, y = shard % 2, shard // 2
                for c in range(3):
                    row, at, left = shard * share, c * share, share
                    while left:
                        count = min(left, half - at % half)
                        if at < half:
                            piece = [(row, count, x, y * half + at)]
                            lay_out(info[1], keep_a, send_a, block_s.at[c], piece)
                        else:
                            piece = [(row, count, y, x * half + at - half)]
                            lay_out(info[2], keep_b, send_b, block_s.at[c], piece)
                        row, at, left = row + count, at + count, left - count

    scratch = [pltpu.VMEM((3, dim, dim), BF)]
    aliases = {len(ins) - 4 + i: i for i in range(4)} if given else {}
    outs = pair_shapes(2 * half + PAD, dim) + pair_shapes(2 * half, dim) + [TOKEN]
    out = call(kernel, outs, ins, scratch, 0, aliases, "qkv_grad", after, QKV_LIMIT)
    return out[:4], out[4]


def plus(one, two):
    return (one.astype(F32) + two.astype(F32)).astype(BF)


def taking_part(info, sections, middle):
    check = None
    if len(sections) == 1:
        check = info[0] == sections[0]
    if middle:
        inner = jnp.logical_or(info[3] == 1, info[3] == 2)
        check = inner if check is None else jnp.logical_and(check, inner)
    return info[3] >= 0 if check is None else check


def vmem_call(kernel, outs, info, ins, name, after):
    return call(kernel, outs, [info] + ins, [], 0, {}, name, after, 8)


def first_sum(info, sections, keep_a, recv_a, keep_b, recv_b, after):
    dim = keep_b.shape[1]
    sizes = [(k.shape[0] // (2 * PAD) * PAD, k.shape[0] % (2 * PAD)) for k in (keep_a, keep_b)]

    def kernel(info, ka, ra, kb, rb, sa, na, sb, nb):
        @pl.when(taking_part(info, sections, False))
        def _():
            for own, one, two, new, out, (half, extra) in (
                (info[2], ka, ra, na, sa, sizes[0]),
                (info[1], kb, rb, nb, sb, sizes[1]),
            ):
                mine = pl.ds(pl.multiple_of(own * half, PAD), half)
                other = pl.ds(pl.multiple_of((1 - own) * half, PAD), half)
                out[:half, :] = plus(one[other, :], two[other, :])
                new[:half, :] = plus(one[mine, :], two[mine, :])
                if extra:
                    tail = plus(one[2 * half :, :], two[2 * half :, :])
                    new[half:, :] = tail
                    out[half:, :] = tail

    outs = [shape((sum(size), dim), BF) for size in sizes for _ in range(2)]
    return vmem_call(kernel, outs, info, [keep_a, recv_a, keep_b, recv_b], "first_sum", after)


def second_sum(info, sections, keep_a, recv_a, keep_b, recv_b, joint, after):
    dim = keep_b.shape[1]
    top, rest = keep_a.shape[0], keep_b.shape[0]

    def kernel(info, ka, ra, kb, rb, *out):
        @pl.when(taking_part(info, sections, False))
        def _():
            out[0][:top, :] = plus(ka[...], ra[...])
            out[-1][out[-1].shape[0] - rest :, :] = plus(kb[...], rb[...])

    outs = [shape((top + rest, dim), BF)]
    if not joint:
        outs = [shape((top, dim), BF), shape((rest, dim), BF)]
    return vmem_call(kernel, outs, info, [keep_a, recv_a, keep_b, recv_b], "second_sum", after)


def pair_sum(info, sections, one, two, after):
    def kernel(info, one, two, out):
        @pl.when(taking_part(info, sections, True))
        def _():
            out[...] = plus(one[...], two[...])

    return vmem_call(kernel, [shape(one.shape, BF)], info, [one, two], "pair_sum", after)[0]


def own_pieces(row, count, width, group):
    share = count * width // GROUPS
    at, pieces = group * share, []
    while at < (group + 1) * share:
        size = min((group + 1) * share - at, width - at % width)
        pieces.append((row + at // width, at % width, size, at - group * share))
        at += size
    return pieces


def finish(info, sources, kind, after):
    dim = sources[0][0].shape[1]
    share = dim // GROUPS
    half = 3 * share // 2
    vectors = ((ROW_QKV, 3), (ROW_OUT, 1), (ROW_UP, 4), (ROW_DOWN, 1))
    if kind == "down":
        rows, outs = dim, [shape((dim, dim), F32)]
    elif kind == "up":
        rows, outs = 5 * share, [shape((share, 4 * dim), F32), shape((share, dim), F32)]
    else:
        rows, outs = 3 * share + PAD, [shape((share, 3 * dim), F32)]
    large = len(outs)
    if kind == "qkv":
        outs += [shape((1, count * dim // GROUPS), F32) for _, count in vectors]
        outs += [shape((2, share), F32)] * 2

    def kernel(info, p0, g0, p1, g1, *refs):
        out_h = refs[:large]
        small = refs[large : len(outs)]
        src = refs[len(outs)]
        stage = refs[len(outs) + 1 : -1]
        sems = refs[-1]
        inner = jnp.logical_or(info[3] == 1, info[3] == 2)
        for section, part, got in ((0, p0, g0), (1, p1, g1)):
            mine = info[0] == section
            lines = pl.ds(sources[section][2], rows)

            @pl.when(jnp.logical_and(mine, inner))
            def _():
                pltpu.make_async_copy(part.at[lines], src, sems.at[0]).start()

            @pl.when(jnp.logical_and(mine, jnp.logical_not(inner)))
            def _():
                pltpu.make_async_copy(got.at[lines], src, sems.at[0]).start()

        pltpu.make_async_copy(p0.at[pl.ds(sources[0][2], rows)], src, sems.at[0]).wait()
        if kind == "down":
            stage[0][...] = src[...].astype(F32)
        elif kind == "up":
            for i in range(4):
                block = src[i * share : (i + 1) * share, :].astype(F32)
                stage[0][:, i * dim : (i + 1) * dim] = block
            stage[1][...] = src[4 * share :, :].astype(F32)
        else:
            for i in range(3):
                at, left, to = i * share, share, 0
                while left:
                    count = min(left, half - at % half)
                    row = at if at < half else at + PAD
                    block = src[row : row + count, :].astype(F32)
                    stage[0][to : to + count, i * dim : (i + 1) * dim] = block
                    at, left, to = at + count, left - count, to + count
        copies = [
            pltpu.make_async_copy(s, o, sems.at[1 + i]) for i, (s, o) in enumerate(zip(stage, out_h))
        ]
        for copy in copies:
            copy.start()
        if kind == "qkv":
            tail = src[half : half + PAD, :].astype(F32)
            for group in range(GROUPS):

                @pl.when(info[1] + 2 * info[2] == group)
                def _():
                    for out, (row, count) in zip(small, vectors):
                        for r, c, size, at in own_pieces(row, count, dim, group):
                            out[:, at : at + size] = tail[r : r + 1, c : c + size]
                    for out, row in zip(small[4:], (ROW_GAIN, ROW_SHIFT)):
                        out[...] = tail[row : row + 2, group * share : (group + 1) * share]

        for copy in copies:
            copy.wait()

    scratch = [pltpu.VMEM((rows, dim), BF)] + [vmem_like(o) for o in outs[:large]]
    ins = [info] + [a for source in sources for a in source[:2]]
    places = "h" * large + "v" * (len(outs) - large)
    return call(kernel, outs, ins, scratch, 4, {}, "finish", after, 12, "saaaa", places)


def flow(shard, axis, pairs, sections):
    if sections == (0, 1):
        return lax.ppermute(shard, axis, pairs)
    peers = lax.axis_size(axis)
    pairs = [(s * peers + i, s * peers + j) for s in sections for i, j in pairs]
    return lax.ppermute(shard, ("section", axis), pairs)


class Reduction:
    def __init__(self, info, sections, bufs, joint):
        self.info, self.sections, self.joint = info, sections, joint
        groups = range(GROUPS)
        self.across = [(g, g ^ 1) for g in groups]
        self.along = [(g, g ^ 2) for g in groups]
        self.line = lax.axis_size("replica") == 4
        send_a, keep_a, send_b, keep_b = bufs
        self.kept = (keep_a, keep_b)
        self.got = (
            flow(send_a, "group", self.across, sections),
            flow(send_b, "group", self.along, sections),
        )

    def group_two(self, after):
        send_a, keep_a, send_b, keep_b = first_sum(
            self.info, self.sections, self.kept[0], self.got[0], self.kept[1], self.got[1], after
        )
        self.kept = (keep_a, keep_b)
        self.got = (
            flow(send_a, "group", self.along, self.sections),
            flow(send_b, "group", self.across, self.sections),
        )
        return keep_a

    def replica_one(self, after):
        self.parts = list(
            second_sum(
                self.info,
                self.sections,
                self.kept[0],
                self.got[0],
                self.kept[1],
                self.got[1],
                self.joint,
                after,
            )
        )
        if self.line:
            self.got = [
                flow(part, "replica", [(0, 1), (3, 2)], self.sections) for part in self.parts
            ]
        else:
            self.parts = [lax.psum(part, "replica") for part in self.parts]
            self.got = list(self.parts)
        return self.parts[0]

    def replica_next(self, pairs, after):
        for i in range(len(self.parts)):
            if self.line:
                self.parts[i] = after = pair_sum(
                    self.info, self.sections, self.parts[i], self.got[i], after
                )
                self.got[i] = flow(self.parts[i], "replica", pairs, self.sections)
        return after

    def replica_two(self, after):
        return self.replica_next([(1, 2), (2, 1)], after)

    def replica_three(self, after):
        return self.replica_next([(1, 0), (2, 3)], after)

    def source(self, half, row):
        index = 0 if self.joint else half
        return self.parts[index], self.got[index], row


def shards(
    block_input,
    cotangent,
    crop_count,
    mask_count,
    qkv_weight,
    qkv_bias,
    out_weight,
    out_bias,
    up_weight,
    up_bias,
    down_weight,
    down_bias,
    norm_gain,
    norm_shift,
):
    params = (
        qkv_weight[0],
        qkv_bias,
        out_weight[0],
        out_bias,
        up_weight[0],
        up_bias,
        down_weight[0],
        down_bias,
        norm_gain[0],
        norm_shift[0],
    )
    rows, dim = block_input.shape
    tab = jnp.asarray(rotary_tables())
    tab_t = jnp.asarray(rotary_columns())
    group = lax.axis_index("group")
    assert lax.axis_size("group") == GROUPS
    info = jnp.stack([lax.axis_index("section"), group % 2, group // 2, lax.axis_index("replica")])

    def to_other(shard, pairs):
        return lax.ppermute(shard, "section", pairs)

    act, first = forward(0, info, crop_count, block_input, None, params, tab, None)
    arrived = [to_other(first[0], [(0, 1)])]
    act, second = forward(1, info, crop_count, block_input, arrived[0], params, tab, act)
    arrived.append(to_other(second[0], [(0, 1)]))
    act, third = forward(2, info, crop_count, block_input, arrived[1], params, tab, act)
    kept_one, kept_zero = (second, third), (first, second)

    common = (info, crop_count, mask_count)
    bufs, gmid, small, last = mlp_grad(1, *common, cotangent, kept_one, params, None)
    one = Reduction(info, (1,), bufs, True)
    dx, kept, last = attention_grad(
        1, info, gmid, small, arrived, kept_one, params, tab_t, None, last
    )
    grad_back = to_other(dx, [(1, 0)])
    bufs_three, last = qkv_grad(1, info, kept, None, last)
    bufs, gmid, small, last = mlp_grad(0, *common, grad_back, kept_zero, params, last)
    two = Reduction(info, (0,), bufs, False)
    last = one.group_two(last)
    dx, kept, last = attention_grad(
        0, info, gmid, small, [block_input], kept_zero, params, tab_t, dx, last
    )
    bufs, last = qkv_grad(0, info, kept, bufs_three, last)
    three = Reduction(info, (0, 1), bufs, True)
    last = two.group_two(last)
    last = one.replica_one(last)
    last = three.group_two(last)
    last = two.replica_one(last)
    last = one.replica_two(last)
    last = three.replica_one(last)
    last = two.replica_two(last)
    last = one.replica_three(last)
    last = three.replica_two(last)
    last = two.replica_three(last)
    last = three.replica_three(last)

    (grad_down,) = finish(info, (two.source(0, 0), one.source(0, 0)), "down", last)
    grad_up, grad_out = finish(info, (two.source(1, 0), one.source(1, dim)), "up", grad_down)
    grad_qkv, *small = finish(info, (three.source(0, 0), three.source(0, 0)), "qkv", grad_out)
    qkv_b, out_b, up_b, down_b, gain, shift = small
    return (
        act[None],
        dx[None],
        grad_qkv[None],
        qkv_b,
        grad_out[None],
        out_b,
        grad_up[None],
        up_b,
        grad_down[None],
        down_b,
        gain[None],
        shift[None],
    )


def solution(mesh):
    rows = P(("group", "replica"))
    stack = P("section")
    return jax.shard_map(
        shards,
        mesh=mesh,
        in_specs=(rows,) * 4 + (stack,) * 10,
        out_specs=(
            P("section", ("group", "replica"), None),
            P("section", ("group", "replica"), None),
            P("section", "group", None),
            P("section", "group"),
            P("section", "group", None),
            P("section", "group"),
            P("section", "group", None),
            P("section", "group"),
            P("section", "group", None),
            P("section", "group"),
            P("section", None, "group"),
            P("section", None, "group"),
        ),
        check_vma=False,
    )
```

```python
import jax
import jax.numpy as jnp
import numpy as np
from jax import lax
from jax.experimental import pallas as pl
from jax.experimental.pallas import tpu as pltpu
from jax.sharding import PartitionSpec as P

HEADS = 20
HEAD_DIM = 32
LEN = 256
MASK_MEAN = 38
CROP_DEV = 2
EPSILON = 1e-05
ROTARY_BASE = 10000.0

BF = jnp.bfloat16
F32 = jnp.float32
NN = (((1,), (0,)), ((), ()))
NT = (((1,), (1,)), ((), ()))
TN = (((0,), (0,)), ((), ()))

FIRST_LIMIT, FORWARD_LIMIT, MLP_LIMIT, ATTENTION_LIMIT, QKV_LIMIT = 40, 16, 15, 16, 8
ATTENTION_MICROS = 12
GROUPS = 4
PAD = 16
ROW_QKV, ROW_OUT, ROW_UP, ROW_DOWN, ROW_GAIN, ROW_SHIFT = 0, 3, 4, 8, 9, 11

ANY = pl.BlockSpec(memory_space=pl.ANY)
HBM = pl.BlockSpec(memory_space=pltpu.HBM)
VMEM = pl.BlockSpec(memory_space=pltpu.VMEM)
SMEM = pl.BlockSpec(memory_space=pltpu.SMEM)


def shape(dims, dtype):
    return jax.ShapeDtypeStruct(dims, dtype)


def mm(left, right, dims=NN):
    return lax.dot_general(left, right, dims, preferred_element_type=F32)


def unit_rows_of(values):
    centred = values - jnp.mean(values, axis=-1, keepdims=True)
    inverse = lax.rsqrt(jnp.mean(centred * centred, axis=-1, keepdims=True) + EPSILON)
    return centred * inverse, inverse


def norm_back(grad, unit, inverse, gain):
    scaled = grad * gain
    return inverse * (
        scaled
        - jnp.mean(scaled, axis=-1, keepdims=True)
        - unit * jnp.mean(scaled * unit, axis=-1, keepdims=True)
    )


def rotary_tables():
    lane = np.arange(128) % HEAD_DIM
    half = HEAD_DIM // 2
    freq = ROTARY_BASE ** (-(lane % half).astype(np.float64) * (2.0 / HEAD_DIM))
    angles = np.arange(LEN)[:, None] * freq[None, :]
    sign = np.where(lane < half, -1.0, 1.0)[None, :]
    return np.stack([np.cos(angles), np.sin(angles) * sign]).astype(np.float32)


def rotary_columns():
    half = HEAD_DIM // 2
    freq = ROTARY_BASE ** (-np.arange(half, dtype=np.float64) * (2.0 / HEAD_DIM))
    angles = freq[:, None] * np.arange(LEN)[None, :]
    return np.stack([np.cos(angles), np.sin(angles)]).astype(np.float32)


def swap_halves(values):
    lane = lax.broadcasted_iota(jnp.int32, values.shape, 1) % HEAD_DIM
    half = HEAD_DIM // 2
    return jnp.where(
        lane < half,
        pltpu.roll(values, 128 - half, axis=1),
        pltpu.roll(values, half, axis=1),
    )


def head_stack(block, per):
    head = lax.broadcasted_iota(jnp.int32, block.shape, 1) // HEAD_DIM
    return jnp.concatenate(
        [jnp.where(head == h, block, jnp.zeros_like(block)) for h in range(per)], axis=0
    )


class Copies:
    def __init__(self, sems):
        self.sems = sems
        self.used = 0
        self.open = []

    def start(self, src, dst):
        copy = pltpu.make_async_copy(src, dst, self.sems.at[self.used])
        self.used += 1
        copy.start()
        return copy

    def save(self, src, dst):
        self.open.append(self.start(src, dst))

    def finish(self):
        for copy in self.open:
            copy.wait()


def call(kernel, outs, ins, scratch, sems, aliases, name, after=None, limit=16, spaces=None, out_spaces=None, micros=0.1):
    count = len(ins)
    places = {"v": VMEM, "h": HBM, "a": ANY, "s": SMEM}
    spaces = spaces or "v" * count
    out_spaces = out_spaces or "v" * len(outs)
    in_specs = [SMEM if a.ndim == 1 else places[p] for a, p in zip(ins, spaces)]
    ins = [pltpu.with_memory_space_constraint(a, pltpu.HBM) if p == "h" else a for a, p in zip(ins, spaces)]
    body = kernel
    if after is not None:
        ins = list(ins) + [after]
        in_specs = in_specs + [ANY]

        def body(*refs):
            kernel(*refs[:count], *refs[count + 1 :])

    outs = [pltpu.HBM(o.shape, o.dtype) if p == "h" else o for o, p in zip(outs, out_spaces)]
    return pl.pallas_call(
        body,
        out_shape=outs,
        in_specs=in_specs,
        out_specs=[places[p] for p in out_spaces],
        scratch_shapes=scratch + ([pltpu.SemaphoreType.DMA((sems,))] if sems else []),
        input_output_aliases=aliases,
        compiler_params=pltpu.CompilerParams(vmem_limit_bytes=limit << 20),
        cost_estimate=pl.CostEstimate(
            flops=int(micros * 1.15e9), bytes_accessed=0, transcendentals=0
        ),
        name=name,
    )(*ins)


TOKEN = jax.ShapeDtypeStruct((8, 128), F32)


def vmem_like(arr):
    return pltpu.VMEM(arr.shape, arr.dtype)


def forward(slot, info, live, own, arrived, params, tab, act, after=None):
    qkvw, qkvb, outw, outb, upw, upb, downw, downb, gain, shift = params
    dim = own.shape[1]
    blocks = dim // 128
    wide = upw.shape[1]
    parts = wide // dim
    per = 128 // HEAD_DIM
    manual = slot == 0
    saved = [
        shape((LEN, dim), BF),
        shape((LEN, 3 * dim), BF),
        shape((HEADS, LEN, LEN), BF),
        shape((dim, LEN), BF),
        shape((LEN, dim), F32),
        shape((LEN, wide), BF),
        shape((LEN, wide), BF),
    ]
    weights = [qkvb, outb, upb, downb, gain, shift, tab, qkvw, outw, upw, downw]
    sources = [own] if slot == 0 else [arrived] if slot == 2 else [own, arrived]
    before = [] if act is None else [act]
    ins = [info, live] + sources + weights + before
    count = len(sources)

    def kernel(info, live, *refs):
        xs = refs[:count]
        given = refs[count : count + 11]
        act_h, *outs = refs[count + 11 + len(before) : count + 19 + len(before)]
        scratch = refs[count + 19 + len(before) :]
        act_s, vt_s, score_s, up_s, normed_s, x_keep = scratch[:6]
        sems = scratch[-1]
        y_s, qkv_s, prob_s, mixt_s, mid_s, gp_s, hid_s = outs
        used = scratch[6:-1] if manual else xs[-1:] + given
        qkvb, outb, upb, downb, gain, shift, tab, qkvw, outw, upw, downw = used[1:]
        crop = slot - info[0]

        @pl.when(jnp.logical_and(crop >= 0, crop < CROP_DEV))
        def _():
            copies = Copies(sems)
            heavy = []
            if manual:
                rows = xs[0].at[pl.ds(0, LEN)]
                loads = [copies.start(h, s) for h, s in zip((rows,) + given, used)]
                heavy = loads[8:]
                wait_all(loads[:8])
                x = used[0][...].astype(F32)
            elif slot == 1:
                x = jnp.where(info[0] == 0, xs[0][LEN:, :], xs[1][...]).astype(F32)
            else:
                x = xs[0][...].astype(F32)

            def ready(index):
                if manual:
                    heavy[index].wait()

            unit, _ = unit_rows_of(x)
            normed_s[...] = (unit * gain[0:1, :] + shift[0:1, :]).astype(BF)
            x_keep[...] = x
            ready(0)

            def third(part):
                cols = pl.ds(pl.multiple_of(part * dim, dim), dim)
                return mm(normed_s[...], qkvw[:, cols]) + qkvb[:, cols]

            low = third(2).astype(BF)
            qkv_s[:, 2 * dim :] = low
            vt_s[...] = low.T

            @pl.loop(0, 2)
            def _(part):
                up_s[:, :dim] = third(part)
                scale = jnp.where(part == 0, HEAD_DIM**-0.5, 1.0).astype(F32)

                @pl.loop(0, blocks)
                def _(j):
                    b = up_s[:, pl.ds(pl.multiple_of(j * 128, 128), 128)]
                    b = (b * tab[0] + swap_halves(b) * tab[1]) * scale
                    at = pl.multiple_of(part * dim + j * 128, 128)
                    qkv_s[:, pl.ds(at, 128)] = b.astype(BF)

            @pl.loop(0, blocks)
            def _(j):
                at = pl.multiple_of(j * 128, 128)
                k = qkv_s[:, pl.ds(pl.multiple_of(dim + at, 128), 128)]
                rows = pl.ds(pl.multiple_of(j * (per * LEN), per * LEN), per * LEN)
                score_s[rows, :] = mm(head_stack(k, per), qkv_s[:, pl.ds(at, 128)], NT)

            def soft(h, _):
                s = score_s[pl.ds(pl.multiple_of(h * LEN, LEN), LEN), :]
                e = jnp.exp(s - jnp.max(s, axis=0, keepdims=True))
                prob_s[h] = (e * (1.0 / jnp.sum(e, axis=0, keepdims=True))).astype(BF)
                return 0

            lax.fori_loop(0, HEADS, soft, 0, unroll=2)

            @pl.loop(0, blocks)
            def _(j):
                for h in range(per):
                    at = pl.ds(pl.multiple_of(j * 128 + h * HEAD_DIM, HEAD_DIM), HEAD_DIM)
                    mixt_s[at, :] = mm(vt_s[at, :], prob_s[per * j + h]).astype(BF)

            ready(1)
            mid = x_keep[...] + mm(mixt_s[...], outw[...], TN) + outb[...]
            mid_s[...] = mid
            unit, _ = unit_rows_of(mid)
            normed_s[...] = (unit * gain[1:2, :] + shift[1:2, :]).astype(BF)
            ready(2)

            @pl.loop(0, parts)
            def _(c):
                cols = pl.ds(pl.multiple_of(c * dim, dim), dim)
                up_s[:, cols] = mm(normed_s[...], upw[:, cols]) + upb[:, cols]

            @pl.loop(0, wide // 256)
            def _(c):
                cols = pl.ds(pl.multiple_of(c * 256, 256), 256)
                u = up_s[:, cols]
                cdf = 0.5 + 0.5 * lax.erf(u * 0.5**0.5)
                hid_s[:, cols] = (u * cdf).astype(BF)
                gp_s[:, cols] = (
                    cdf + u * (jnp.exp(u * u * -0.5) * (2 * np.pi) ** -0.5)
                ).astype(BF)

            ready(3)
            low = (mid_s[...] + downb[...] + mm(hid_s[...], downw[...])).astype(BF)
            y_s[...] = low
            act_s[...] = jnp.where(crop < live[0], low, jnp.zeros_like(low))
            at = pl.multiple_of(crop * LEN, LEN)
            copies.save(act_s, act_h.at[pl.ds(at, LEN)])
            copies.finish()

    outs = [shape(own.shape, BF)] + saved
    scratch = [
        pltpu.VMEM((LEN, dim), BF),
        pltpu.VMEM((dim, LEN), BF),
        pltpu.VMEM((HEADS * LEN, LEN), F32),
        pltpu.VMEM((LEN, wide), F32),
        pltpu.VMEM((LEN, dim), BF),
        pltpu.VMEM((LEN, dim), F32),
    ]
    if manual:
        scratch += [pltpu.VMEM((LEN, dim), BF)] + [vmem_like(a) for a in weights]
    aliases = {} if act is None else {len(ins) - 1: 0}
    spaces = "ss" + ("h" if manual else "v") * (count + 11) + "h" * len(before)
    out = call(
        kernel,
        outs,
        ins,
        scratch,
        16,
        aliases,
        "layer_forward",
        after,
        FIRST_LIMIT if manual else FORWARD_LIMIT,
        spaces,
        "h" + "v" * 7,
    )
    return out[0], out[1:]


def crop_weight(live, masks, crop, section):
    if section == 0:
        return 1.0
    count = jnp.where(live[0] > crop, masks[crop], 0)
    return jnp.full((1, 1), count, jnp.int32).astype(F32) / MASK_MEAN


def add_row(ref, row, values):
    ref[row : row + 1, :] = ref[row : row + 1, :] + jnp.sum(values, axis=0, keepdims=True)


def lay_out(sem, own, bit, keep, send, src, at):
    dst = pl.ds(pl.multiple_of(at, PAD), src.shape[0])
    mine = own == bit

    @pl.when(mine)
    def _():
        pltpu.make_async_copy(src, keep.at[dst], sem).start()

    @pl.when(jnp.logical_not(mine))
    def _():
        pltpu.make_async_copy(src, send.at[dst], sem).start()

    return pltpu.make_async_copy(src, keep.at[dst], sem)


def keep_given(active, given, bufs):
    @pl.when(jnp.logical_not(active))
    def _():
        for old, new in zip(given, bufs):
            new[...] = old[...]


def pair_shapes(rows, dim):
    return [shape((rows, dim), BF)] * 2


def joined(refs, cols):
    return jnp.concatenate([r[:, cols] for r in refs], axis=0)


def wait_all(copies):
    for copy in copies:
        copy.wait()


def mlp_grad(section, info, live, masks, g, saved, params, after):
    mixts = [s[3] for s in saved]
    mids, gps, hids = ([s[k] for s in saved] for k in (4, 5, 6))
    upw, downw, gain, shift = params[4], params[6], params[8], params[9]
    rows, dim = g.shape
    wide = upw.shape[1]
    parts = wide // dim
    crops = len(saved)
    share = dim // GROUPS
    ins = [info, live, masks, g, gain, shift, downw, upw] + mids + gps + hids + mixts

    def kernel(info, live, masks, g_s, gain, shift, downw, upw, *refs):
        mid_s, gp_s, hid_s, mixt_s = (refs[i * crops : (i + 1) * crops] for i in range(4))
        refs = refs[4 * crops :]
        send_a, keep_a, send_b, keep_b, gmid_s, small_s = refs[:6]
        gu_s, block_s, low_s, normt_s, back_s, sems = refs[7:]

        @pl.when(info[0] == section)
        def _():
            small_s[...] = jnp.zeros_like(small_s)
            for c in range(crops):
                crop = slice(c * LEN, (c + 1) * LEN)
                grad = g_s[crop, :].astype(F32) * crop_weight(live, masks, c, section)
                low = grad.astype(BF)
                low_s[crop, :] = low
                add_row(small_s, ROW_DOWN, low.astype(F32))
                unit, _ = unit_rows_of(mid_s[c][...])
                normt_s[:, crop] = (unit * gain[1:2, :] + shift[1:2, :]).astype(BF).T

            @pl.loop(0, parts)
            def _(c):
                cols = pl.ds(pl.multiple_of(c * dim, dim), dim)
                block_s[c] = mm(joined(hid_s, cols), low_s[...], TN).astype(BF)
                at = (c // 2) * dim
                lay_out(sems.at[c], info[1], c % 2, keep_a, send_a, block_s.at[c], at)

            @pl.loop(0, parts)
            def _(c):
                cols = pl.ds(pl.multiple_of(c * dim, dim), dim)
                grad_up = mm(low_s[...], downw[cols, :], NT) * joined(gp_s, cols).astype(F32)
                grad_up = grad_up.astype(BF)
                gu_s[:, cols] = grad_up
                small_s[pl.ds(ROW_UP + c, 1), :] = jnp.sum(
                    grad_up.astype(F32), axis=0, keepdims=True
                )

            back_s[...] = mm(gu_s[...], upw[...], NT)
            for c in range(crops):
                crop = slice(c * LEN, (c + 1) * LEN)
                grad = g_s[crop, :].astype(F32) * crop_weight(live, masks, c, section)
                unit, inverse = unit_rows_of(mid_s[c][...])
                back = back_s[crop, :]
                gmid = grad + norm_back(back, unit, inverse, gain[1:2, :])
                gmid_s[crop, :] = gmid
                low = gmid.astype(BF)
                low_s[crop, :] = low
                add_row(small_s, ROW_GAIN + 1, back * unit)
                add_row(small_s, ROW_SHIFT + 1, back)
                add_row(small_s, ROW_OUT, low.astype(F32))

            @pl.loop(0, parts)
            def _(c):
                pltpu.make_async_copy(block_s.at[c], keep_a.at[pl.ds(0, dim)], sems.at[c]).wait()

            @pl.loop(0, parts)
            def _(c):
                cols = pl.ds(pl.multiple_of(c * dim, dim), dim)
                block_s[c] = mm(normt_s[...], gu_s[:, cols]).astype(BF)

            mixt = jnp.concatenate([m[...] for m in mixt_s], axis=1)
            block_s[parts] = mm(mixt, low_s[...]).astype(BF)

            @pl.loop(0, GROUPS * (parts + 1))
            def _(i):
                shard, c = i // (parts + 1), i % (parts + 1)
                src = block_s.at[c, pl.ds(pl.multiple_of(shard * share, PAD), share)]
                at = ((shard % 2) * (parts + 1) + c) * share
                lay_out(sems.at[i], info[2], shard // 2, keep_b, send_b, src, at)

            @pl.loop(0, GROUPS * (parts + 1))
            def _(i):
                src = block_s.at[0, pl.ds(0, share)]
                pltpu.make_async_copy(src, keep_b.at[pl.ds(0, share)], sems.at[i]).wait()

    scratch = [
        pltpu.VMEM((rows, wide), BF),
        pltpu.VMEM((parts + 1, dim, dim), BF),
        pltpu.VMEM((rows, dim), BF),
        pltpu.VMEM((dim, rows), BF),
        pltpu.VMEM((rows, dim), F32),
    ]
    outs = pair_shapes(2 * dim, dim) + pair_shapes(2 * (parts + 1) * share, dim)
    outs += [shape((rows, dim), F32), shape((PAD, dim), F32), TOKEN]
    out = call(kernel, outs, ins, scratch, 20, {}, "mlp_grad", after, MLP_LIMIT)
    return out[:4], out[4], out[5], out[6]


def rotate_back(block, tab_t):
    half = HEAD_DIM // 2
    cos, sin = tab_t[0], tab_t[1]
    out = []
    for at in range(0, block.shape[0], HEAD_DIM):
        a, b = block[at : at + half], block[at + half : at + HEAD_DIM]
        out += [a * cos + b * sin, b * cos - a * sin]
    return jnp.concatenate(out, axis=0)


def attention_grad(section, info, gmid, small, xs, saved, params, tab_t, before, after):
    qkvs, probs, mixts = [s[1] for s in saved], [s[2] for s in saved], [s[3] for s in saved]
    qkvw, outw, gain, shift = params[0], params[2], params[8], params[9]
    rows, dim = gmid.shape
    blocks = dim // 128
    per = 128 // HEAD_DIM
    crops = len(saved)
    given = [] if before is None else [before]
    ins = [info, gmid, outw, small, gain, shift, tab_t, qkvw]
    ins += qkvs + probs + mixts + list(xs) + given

    def kernel(info, gmid_s, outw, small_s, gain, shift, tab_t, qkvw, *refs):
        qkv_s, prob_s, mixt_s = (refs[i * crops : (i + 1) * crops] for i in range(3))
        x_s = refs[3 * crops : 3 * crops + len(xs)]
        old = refs[3 * crops + len(xs) : 3 * crops + len(xs) + len(given)]
        refs = refs[3 * crops + len(xs) + len(given) :]
        keep_given(info[0] == section, old, refs[:1])
        dx_s, gqkv_s, normt_s, small_out = refs[:4]
        gmt_s, delta_s, da_s, ds_s, dt_s, kt_s, back_s = refs[5:]

        @pl.when(info[0] == section)
        def _():
            gmt_s[...] = mm(outw[...], gmid_s[...].astype(BF), NT).astype(BF)
            for c in range(crops):
                crop = slice(c * LEN, (c + 1) * LEN)
                qkv, prob, mixt = qkv_s[c], prob_s[c], mixt_s[c]

                @pl.loop(0, blocks)
                def _(j):
                    at = pl.multiple_of(j * 128, 128)
                    lanes = pl.ds(at, 128)
                    gmt = gmt_s[lanes, crop]
                    product = gmt.astype(F32) * mixt[lanes, :].astype(F32)
                    delta = jnp.sum(product.reshape(per, HEAD_DIM, LEN), axis=1)
                    delta_s[pl.ds(per * j, per)] = delta[:, None, :]
                    kt_s[0, lanes, :] = qkv[:, pl.ds(pl.multiple_of(dim + at, 128), 128)].T
                    kt_s[1, lanes, :] = qkv[:, lanes].T
                    v = qkv[:, pl.ds(pl.multiple_of(2 * dim + at, 128), 128)]
                    lines = pl.ds(pl.multiple_of(j * (per * LEN), per * LEN), per * LEN)
                    da_s[lines, :] = mm(head_stack(v, per), gmt)

                def scores(h, _):
                    da = da_s[pl.ds(pl.multiple_of(h * LEN, LEN), LEN), :]
                    ds_s[h] = (prob[h].astype(F32) * (da - delta_s[h])).astype(BF)
                    return 0

                lax.fori_loop(0, HEADS, scores, 0, unroll=2)

                @pl.loop(0, blocks)
                def _(j):
                    for h in range(per):
                        at = pl.ds(pl.multiple_of(j * 128 + h * HEAD_DIM, HEAD_DIM), HEAD_DIM)
                        head = per * j + h
                        dt_s[0, at, :] = mm(kt_s[0, at, :], ds_s[head])
                        dt_s[1, at, :] = mm(kt_s[1, at, :], ds_s[head], NT)
                        dt_s[2, at, :] = mm(gmt_s[at, crop], prob[head], NT)

                @pl.loop(0, blocks)
                def _(j):
                    at = pl.multiple_of(j * 128, 128)
                    lines = pl.ds(at, 128)
                    dq = rotate_back(dt_s[0, lines, :] * HEAD_DIM**-0.5, tab_t)
                    gqkv_s[crop, pl.ds(at, 128)] = dq.astype(BF).T
                    dk = rotate_back(dt_s[1, lines, :], tab_t)
                    gqkv_s[crop, pl.ds(pl.multiple_of(dim + at, 128), 128)] = dk.astype(BF).T
                    dv = dt_s[2, lines, :]
                    gqkv_s[crop, pl.ds(pl.multiple_of(2 * dim + at, 128), 128)] = dv.astype(BF).T

            back_s[...] = mm(gqkv_s[...], qkvw[...], NT)
            small_out[...] = small_s[...]
            for c in range(crops):
                crop = slice(c * LEN, (c + 1) * LEN)
                x = x_s[c][...] if len(xs) > 1 else x_s[0][crop, :]
                unit, inverse = unit_rows_of(x.astype(F32))
                normt_s[:, crop] = (unit * gain[0:1, :] + shift[0:1, :]).astype(BF).T
                back = back_s[crop, :]
                dx = gmid_s[crop, :] + norm_back(back, unit, inverse, gain[0:1, :])
                dx_s[crop, :] = dx.astype(BF)
                add_row(small_out, ROW_GAIN, back * unit)
                add_row(small_out, ROW_SHIFT, back)

    outs = [
        shape((rows, dim), BF),
        shape((rows, 3 * dim), BF),
        shape((dim, rows), BF),
        shape(small.shape, F32),
        TOKEN,
    ]
    scratch = [
        pltpu.VMEM((dim, rows), BF),
        pltpu.VMEM((HEADS, 1, LEN), F32),
        pltpu.VMEM((HEADS * LEN, LEN), F32),
        pltpu.VMEM((HEADS, LEN, LEN), BF),
        pltpu.VMEM((3, dim, LEN), F32),
        pltpu.VMEM((2, dim, LEN), BF),
        pltpu.VMEM((rows, dim), F32),
    ]
    aliases = {len(ins) - 1: 0} if given else {}
    out = call(kernel, outs, ins, scratch, 0, aliases, "attention_grad", after, ATTENTION_LIMIT, micros=ATTENTION_MICROS)
    return out[0], out[1:4], out[4]


def qkv_grad(section, info, kept, before, after):
    gqkv, normt, small = kept
    dim, rows = normt.shape
    share = dim // GROUPS
    half = 3 * share // 2
    given = [] if before is None else list(before)
    ins = [info, gqkv, normt, small] + given

    def kernel(info, gqkv_s, normt_s, small_s, *refs):
        old = refs[: len(given)]
        bufs = refs[len(given) : len(given) + 4]
        send_a, keep_a, send_b, keep_b = bufs
        block_s, sems = refs[len(given) + 5 :]
        keep_given(info[0] == section, old, bufs)

        @pl.when(info[0] == section)
        def _():
            sums = [
                jnp.sum(gqkv_s[:, c * dim : (c + 1) * dim].astype(F32), axis=0, keepdims=True)
                for c in range(3)
            ]
            tail = jnp.concatenate(sums + [small_s[ROW_OUT:, :]], axis=0).astype(BF)
            send_a[2 * half :, :] = tail
            keep_a[2 * half :, :] = tail

            @pl.loop(0, 3)
            def _(c):
                cols = pl.ds(pl.multiple_of(c * dim, dim), dim)
                block_s[c] = mm(normt_s[...], gqkv_s[:, cols]).astype(BF)

            waits = []
            for shard in range(GROUPS):
                x, y = shard % 2, shard // 2
                for c in range(3):
                    row, at, left = shard * share, c * share, share
                    while left:
                        count = min(left, half - at % half)
                        src, sem = block_s.at[c, pl.ds(row, count)], sems.at[len(waits)]
                        waits.append(
                            lay_out(sem, info[1], x, keep_a, send_a, src, y * half + at)
                            if at < half
                            else lay_out(sem, info[2], y, keep_b, send_b, src, x * half + at - half)
                        )
                        row, at, left = row + count, at + count, left - count
            wait_all(waits)

    scratch = [pltpu.VMEM((3, dim, dim), BF)]
    aliases = {len(ins) - 4 + i: i for i in range(4)} if given else {}
    outs = pair_shapes(2 * half + PAD, dim) + pair_shapes(2 * half, dim) + [TOKEN]
    out = call(kernel, outs, ins, scratch, 16, aliases, "qkv_grad", after, QKV_LIMIT)
    return out[:4], out[4]


STEP = 80


def plus(one, two):
    return (one.astype(F32) + two.astype(F32)).astype(BF)


def add_rows(out, at, one, two, start, count):
    whole = count // STEP * STEP

    @pl.loop(0, whole // STEP)
    def _(i):
        src = pl.ds(pl.multiple_of(start + i * STEP, PAD), STEP)
        dst = pl.ds(pl.multiple_of(at + i * STEP, PAD), STEP)
        out[dst, :] = plus(one[src, :], two[src, :])

    if count > whole:
        src = pl.ds(pl.multiple_of(start + whole, PAD), count - whole)
        out[pl.ds(at + whole, count - whole), :] = plus(one[src, :], two[src, :])


def taking_part(info, sections, middle):
    check = None
    if len(sections) == 1:
        check = info[0] == sections[0]
    if middle:
        inner = jnp.logical_or(info[3] == 1, info[3] == 2)
        check = inner if check is None else jnp.logical_and(check, inner)
    return info[3] >= 0 if check is None else check


def vmem_call(kernel, outs, info, ins, name, after):
    return call(kernel, outs, [info] + ins, [], 0, {}, name, after, 8)


def first_sum(info, sections, keep_a, recv_a, keep_b, recv_b, after):
    dim = keep_b.shape[1]
    sizes = [(k.shape[0] // (2 * PAD) * PAD, k.shape[0] % (2 * PAD)) for k in (keep_a, keep_b)]

    def kernel(info, ka, ra, kb, rb, sa, na, sb, nb):
        @pl.when(taking_part(info, sections, False))
        def _():
            for own, one, two, new, out, (half, extra) in (
                (info[2], ka, ra, na, sa, sizes[0]),
                (info[1], kb, rb, nb, sb, sizes[1]),
            ):
                add_rows(out, 0, one, two, (1 - own) * half, half)
                add_rows(new, 0, one, two, own * half, half)
                if extra:
                    tail = plus(one[2 * half :, :], two[2 * half :, :])
                    new[half:, :] = tail
                    out[half:, :] = tail

    outs = [shape((sum(size), dim), BF) for size in sizes for _ in range(2)]
    return vmem_call(kernel, outs, info, [keep_a, recv_a, keep_b, recv_b], "first_sum", after)


def second_sum(info, sections, keep_a, recv_a, keep_b, recv_b, joint, after):
    dim = keep_b.shape[1]
    top, rest = keep_a.shape[0], keep_b.shape[0]

    def kernel(info, ka, ra, kb, rb, *out):
        @pl.when(taking_part(info, sections, False))
        def _():
            add_rows(out[0], 0, ka, ra, 0, top)
            add_rows(out[-1], out[-1].shape[0] - rest, kb, rb, 0, rest)

    outs = [shape((top + rest, dim), BF)]
    if not joint:
        outs = [shape((top, dim), BF), shape((rest, dim), BF)]
    return vmem_call(kernel, outs, info, [keep_a, recv_a, keep_b, recv_b], "second_sum", after)


def pair_sum(info, sections, one, two, after):
    def kernel(info, one, two, out):
        @pl.when(taking_part(info, sections, True))
        def _():
            add_rows(out, 0, one, two, 0, one.shape[0])

    return vmem_call(kernel, [shape(one.shape, BF)], info, [one, two], "pair_sum", after)[0]


def own_pieces(row, count, width, group):
    share = count * width // GROUPS
    at, pieces = group * share, []
    while at < (group + 1) * share:
        size = min((group + 1) * share - at, width - at % width)
        pieces.append((row + at // width, at % width, size, at - group * share))
        at += size
    return pieces


def finish(info, sources, kind, after):
    dim = sources[0][0].shape[1]
    share = dim // GROUPS
    half = 3 * share // 2
    vectors = ((ROW_QKV, 3), (ROW_OUT, 1), (ROW_UP, 4), (ROW_DOWN, 1))
    if kind == "down":
        rows, outs = dim, [shape((dim, dim), F32)]
    elif kind == "up":
        rows, outs = 5 * share, [shape((share, 4 * dim), F32), shape((share, dim), F32)]
    else:
        rows, outs = 3 * share + PAD, [shape((share, 3 * dim), F32)]
    large = len(outs)
    if kind == "qkv":
        outs += [shape((1, count * dim // GROUPS), F32) for _, count in vectors]
        outs += [shape((2, share), F32)] * 2

    def kernel(info, p0, g0, p1, g1, *refs):
        out_h = refs[:large]
        small = refs[large : len(outs)]
        src = refs[len(outs)]
        stage = refs[len(outs) + 1 : -1]
        sems = refs[-1]
        inner = jnp.logical_or(info[3] == 1, info[3] == 2)
        for section, part, got in ((0, p0, g0), (1, p1, g1)):
            mine = info[0] == section
            lines = pl.ds(sources[section][2], rows)

            @pl.when(jnp.logical_and(mine, inner))
            def _():
                pltpu.make_async_copy(part.at[lines], src, sems.at[0]).start()

            @pl.when(jnp.logical_and(mine, jnp.logical_not(inner)))
            def _():
                pltpu.make_async_copy(got.at[lines], src, sems.at[0]).start()

        pltpu.make_async_copy(p0.at[pl.ds(sources[0][2], rows)], src, sems.at[0]).wait()
        if kind == "down":
            stage[0][...] = src[...].astype(F32)
        elif kind == "up":
            for i in range(4):
                block = src[i * share : (i + 1) * share, :].astype(F32)
                stage[0][:, i * dim : (i + 1) * dim] = block
            stage[1][...] = src[4 * share :, :].astype(F32)
        else:
            for i in range(3):
                at, left, to = i * share, share, 0
                while left:
                    count = min(left, half - at % half)
                    row = at if at < half else at + PAD
                    block = src[row : row + count, :].astype(F32)
                    stage[0][to : to + count, i * dim : (i + 1) * dim] = block
                    at, left, to = at + count, left - count, to + count
        copies = [
            pltpu.make_async_copy(s, o, sems.at[1 + i]) for i, (s, o) in enumerate(zip(stage, out_h))
        ]
        for copy in copies:
            copy.start()
        if kind == "qkv":
            tail = src[half : half + PAD, :].astype(F32)
            for group in range(GROUPS):

                @pl.when(info[1] + 2 * info[2] == group)
                def _():
                    for out, (row, count) in zip(small, vectors):
                        for r, c, size, at in own_pieces(row, count, dim, group):
                            out[:, at : at + size] = tail[r : r + 1, c : c + size]
                    for out, row in zip(small[4:], (ROW_GAIN, ROW_SHIFT)):
                        out[...] = tail[row : row + 2, group * share : (group + 1) * share]

        for copy in copies:
            copy.wait()

    scratch = [pltpu.VMEM((rows, dim), BF)] + [vmem_like(o) for o in outs[:large]]
    ins = [info] + [a for source in sources for a in source[:2]]
    places = "h" * large + "v" * (len(outs) - large)
    return call(kernel, outs, ins, scratch, 4, {}, "finish", after, 12, "saaaa", places)


def flow(shard, axis, pairs, sections):
    if sections == (0, 1):
        return lax.ppermute(shard, axis, pairs)
    peers = lax.axis_size(axis)
    pairs = [(s * peers + i, s * peers + j) for s in sections for i, j in pairs]
    return lax.ppermute(shard, ("section", axis), pairs)


class Reduction:
    def __init__(self, info, sections, bufs, joint):
        self.info, self.sections, self.joint = info, sections, joint
        groups = range(GROUPS)
        self.across = [(g, g ^ 1) for g in groups]
        self.along = [(g, g ^ 2) for g in groups]
        self.line = lax.axis_size("replica") == 4
        send_a, keep_a, send_b, keep_b = bufs
        self.kept = (keep_a, keep_b)
        self.got = (
            flow(send_a, "group", self.across, sections),
            flow(send_b, "group", self.along, sections),
        )

    def group_two(self, after):
        send_a, keep_a, send_b, keep_b = first_sum(
            self.info, self.sections, self.kept[0], self.got[0], self.kept[1], self.got[1], after
        )
        self.kept = (keep_a, keep_b)
        self.got = (
            flow(send_a, "group", self.along, self.sections),
            flow(send_b, "group", self.across, self.sections),
        )
        return keep_a

    def replica_one(self, after):
        self.parts = list(
            second_sum(
                self.info,
                self.sections,
                self.kept[0],
                self.got[0],
                self.kept[1],
                self.got[1],
                self.joint,
                after,
            )
        )
        if self.line:
            self.got = [
                flow(part, "replica", [(0, 1), (3, 2)], self.sections) for part in self.parts
            ]
        else:
            self.parts = [lax.psum(part, "replica") for part in self.parts]
            self.got = list(self.parts)
        return self.parts[0]

    def replica_next(self, pairs, after):
        for i in range(len(self.parts)):
            if self.line:
                self.parts[i] = after = pair_sum(
                    self.info, self.sections, self.parts[i], self.got[i], after
                )
                self.got[i] = flow(self.parts[i], "replica", pairs, self.sections)
        return after

    def replica_two(self, after):
        return self.replica_next([(1, 2), (2, 1)], after)

    def replica_three(self, after):
        return self.replica_next([(1, 0), (2, 3)], after)

    def source(self, half, row):
        index = 0 if self.joint else half
        return self.parts[index], self.got[index], row


def shards(
    block_input,
    cotangent,
    crop_count,
    mask_count,
    qkv_weight,
    qkv_bias,
    out_weight,
    out_bias,
    up_weight,
    up_bias,
    down_weight,
    down_bias,
    norm_gain,
    norm_shift,
):
    params = (
        qkv_weight[0],
        qkv_bias,
        out_weight[0],
        out_bias,
        up_weight[0],
        up_bias,
        down_weight[0],
        down_bias,
        norm_gain[0],
        norm_shift[0],
    )
    rows, dim = block_input.shape
    tab = jnp.asarray(rotary_tables())
    tab_t = jnp.asarray(rotary_columns())
    group = lax.axis_index("group")
    assert lax.axis_size("group") == GROUPS
    info = jnp.stack([lax.axis_index("section"), group % 2, group // 2, lax.axis_index("replica")])

    def to_other(shard, pairs):
        return lax.ppermute(shard, "section", pairs)

    act, first = forward(0, info, crop_count, block_input, None, params, tab, None)
    arrived = [to_other(first[0], [(0, 1)])]
    act, second = forward(1, info, crop_count, block_input, arrived[0], params, tab, act)
    arrived.append(to_other(second[0], [(0, 1)]))
    act, third = forward(2, info, crop_count, block_input, arrived[1], params, tab, act)
    kept_one, kept_zero = (second, third), (first, second)

    common = (info, crop_count, mask_count)
    bufs, gmid, small, last = mlp_grad(1, *common, cotangent, kept_one, params, None)
    one = Reduction(info, (1,), bufs, True)
    dx, kept, last = attention_grad(
        1, info, gmid, small, arrived, kept_one, params, tab_t, None, last
    )
    grad_back = to_other(dx, [(1, 0)])
    bufs_three, last = qkv_grad(1, info, kept, None, last)
    bufs, gmid, small, last = mlp_grad(0, *common, grad_back, kept_zero, params, last)
    two = Reduction(info, (0,), bufs, False)
    last = one.group_two(last)
    dx, kept, last = attention_grad(
        0, info, gmid, small, [block_input], kept_zero, params, tab_t, dx, last
    )
    bufs, last = qkv_grad(0, info, kept, bufs_three, last)
    three = Reduction(info, (0, 1), bufs, True)
    last = two.group_two(last)
    last = one.replica_one(last)
    last = two.replica_one(last)
    last = three.group_two(last)
    last = one.replica_two(last)
    last = two.replica_two(last)
    last = three.replica_one(last)
    last = one.replica_three(last)
    last = two.replica_three(last)
    last = three.replica_two(last)
    (grad_down,) = finish(info, (two.source(0, 0), one.source(0, 0)), "down", last)
    last = three.replica_three(grad_down)
    grad_up, grad_out = finish(info, (two.source(1, 0), one.source(1, dim)), "up", last)
    grad_qkv, *small = finish(info, (three.source(0, 0), three.source(0, 0)), "qkv", grad_out)
    qkv_b, out_b, up_b, down_b, gain, shift = small
    return (
        act[None],
        dx[None],
        grad_qkv[None],
        qkv_b,
        grad_out[None],
        out_b,
        grad_up[None],
        up_b,
        grad_down[None],
        down_b,
        gain[None],
        shift[None],
    )


def solution(mesh):
    rows = P(("group", "replica"))
    stack = P("section")
    return jax.shard_map(
        shards,
        mesh=mesh,
        in_specs=(rows,) * 4 + (stack,) * 10,
        out_specs=(
            P("section", ("group", "replica"), None),
            P("section", ("group", "replica"), None),
            P("section", "group", None),
            P("section", "group"),
            P("section", "group", None),
            P("section", "group"),
            P("section", "group", None),
            P("section", "group"),
            P("section", "group", None),
            P("section", "group"),
            P("section", None, "group"),
            P("section", None, "group"),
        ),
        check_vma=False,
    )
```

```python
import jax
import jax.numpy as jnp
import numpy as np
from jax import lax
from jax.experimental import pallas as pl
from jax.experimental.pallas import tpu as pltpu
from jax.sharding import PartitionSpec as P

HEADS = 20
HEAD_DIM = 32
LEN = 256
MASK_MEAN = 38
CROP_DEV = 2
EPSILON = 1e-05
ROTARY_BASE = 10000.0

BF = jnp.bfloat16
F32 = jnp.float32
NN = (((1,), (0,)), ((), ()))
NT = (((1,), (1,)), ((), ()))
TN = (((0,), (0,)), ((), ()))

FIRST_LIMIT, FORWARD_LIMIT, MLP_LIMIT, ATTENTION_LIMIT, QKV_LIMIT = 40, 14, 13, 16, 7
ATTENTION_MICROS = 12
GROUPS = 4
PAD = 16
ROW_QKV, ROW_OUT, ROW_UP, ROW_DOWN, ROW_GAIN, ROW_SHIFT = 0, 3, 4, 8, 9, 11

ANY = pl.BlockSpec(memory_space=pl.ANY)
HBM = pl.BlockSpec(memory_space=pltpu.HBM)
VMEM = pl.BlockSpec(memory_space=pltpu.VMEM)
SMEM = pl.BlockSpec(memory_space=pltpu.SMEM)


def shape(dims, dtype):
    return jax.ShapeDtypeStruct(dims, dtype)


def mm(left, right, dims=NN):
    return lax.dot_general(left, right, dims, preferred_element_type=F32)


def unit_rows_of(values):
    centred = values - jnp.mean(values, axis=-1, keepdims=True)
    inverse = lax.rsqrt(jnp.mean(centred * centred, axis=-1, keepdims=True) + EPSILON)
    return centred * inverse, inverse


def norm_back(grad, unit, inverse, gain):
    scaled = grad * gain
    return inverse * (
        scaled
        - jnp.mean(scaled, axis=-1, keepdims=True)
        - unit * jnp.mean(scaled * unit, axis=-1, keepdims=True)
    )


def rotary_tables():
    lane = np.arange(128) % HEAD_DIM
    half = HEAD_DIM // 2
    freq = ROTARY_BASE ** (-(lane % half).astype(np.float64) * (2.0 / HEAD_DIM))
    angles = np.arange(LEN)[:, None] * freq[None, :]
    sign = np.where(lane < half, -1.0, 1.0)[None, :]
    return np.stack([np.cos(angles), np.sin(angles) * sign]).astype(np.float32)


def rotary_columns():
    half = HEAD_DIM // 2
    freq = ROTARY_BASE ** (-np.arange(half, dtype=np.float64) * (2.0 / HEAD_DIM))
    angles = freq[:, None] * np.arange(LEN)[None, :]
    return np.stack([np.cos(angles), np.sin(angles)]).astype(np.float32)


def swap_halves(values):
    lane = lax.broadcasted_iota(jnp.int32, values.shape, 1) % HEAD_DIM
    half = HEAD_DIM // 2
    return jnp.where(
        lane < half,
        pltpu.roll(values, 128 - half, axis=1),
        pltpu.roll(values, half, axis=1),
    )


def head_stack(block, per):
    head = lax.broadcasted_iota(jnp.int32, block.shape, 1) // HEAD_DIM
    return jnp.concatenate(
        [jnp.where(head == h, block, jnp.zeros_like(block)) for h in range(per)], axis=0
    )


class Copies:
    def __init__(self, sems):
        self.sems = sems
        self.used = 0
        self.open = []

    def start(self, src, dst):
        copy = pltpu.make_async_copy(src, dst, self.sems.at[self.used])
        self.used += 1
        copy.start()
        return copy

    def save(self, src, dst):
        self.open.append(self.start(src, dst))

    def finish(self):
        for copy in self.open:
            copy.wait()


def call(kernel, outs, ins, scratch, sems, aliases, name, after=None, limit=16, spaces=None, out_spaces=None, micros=0.1):
    count = len(ins)
    places = {"v": VMEM, "h": HBM, "a": ANY, "s": SMEM}
    spaces = spaces or "v" * count
    out_spaces = out_spaces or "v" * len(outs)
    in_specs = [SMEM if a.ndim == 1 else places[p] for a, p in zip(ins, spaces)]
    ins = [pltpu.with_memory_space_constraint(a, pltpu.HBM) if p == "h" else a for a, p in zip(ins, spaces)]
    body = kernel
    if after is not None:
        ins = list(ins) + [after]
        in_specs = in_specs + [ANY]

        def body(*refs):
            kernel(*refs[:count], *refs[count + 1 :])

    outs = [pltpu.HBM(o.shape, o.dtype) if p == "h" else o for o, p in zip(outs, out_spaces)]
    return pl.pallas_call(
        body,
        out_shape=outs,
        in_specs=in_specs,
        out_specs=[places[p] for p in out_spaces],
        scratch_shapes=scratch + ([pltpu.SemaphoreType.DMA((sems,))] if sems else []),
        input_output_aliases=aliases,
        compiler_params=pltpu.CompilerParams(vmem_limit_bytes=limit << 20),
        cost_estimate=pl.CostEstimate(
            flops=int(micros * 1.15e9), bytes_accessed=0, transcendentals=0
        ),
        name=name,
    )(*ins)


TOKEN = jax.ShapeDtypeStruct((8, 128), F32)


def vmem_like(arr):
    return pltpu.VMEM(arr.shape, arr.dtype)


def forward(slot, info, live, own, arrived, params, tab, act, after=None):
    qkvw, qkvb, outw, outb, upw, upb, downw, downb, gain, shift = params
    dim = own.shape[1]
    blocks = dim // 128
    wide = upw.shape[1]
    parts = wide // dim
    per = 128 // HEAD_DIM
    manual = slot == 0
    saved = [
        shape((LEN, dim), BF),
        shape((LEN, 3 * dim), BF),
        shape((HEADS, LEN, LEN), BF),
        shape((dim, LEN), BF),
        shape((LEN, dim), F32),
        shape((LEN, wide), BF),
        shape((LEN, wide), BF),
    ]
    weights = [qkvb, outb, upb, downb, gain, shift, tab, qkvw, outw, upw, downw]
    sources = [own] if slot == 0 else [arrived] if slot == 2 else [own, arrived]
    before = [] if act is None else [act]
    ins = [info, live] + sources + weights + before
    count = len(sources)

    def kernel(info, live, *refs):
        xs = refs[:count]
        given = refs[count : count + 11]
        act_h, *outs = refs[count + 11 + len(before) : count + 19 + len(before)]
        scratch = refs[count + 19 + len(before) :]
        act_s, vt_s, score_s, up_s = scratch[:4]
        sems = scratch[-1]
        y_s, qkv_s, prob_s, mixt_s, mid_s, gp_s, hid_s = outs
        used = scratch[4:-1] if manual else xs[-1:] + given
        qkvb, outb, upb, downb, gain, shift, tab, qkvw, outw, upw, downw = used[1:]
        crop = slot - info[0]

        @pl.when(jnp.logical_and(crop >= 0, crop < CROP_DEV))
        def _():
            copies = Copies(sems)
            heavy = []
            if manual:
                rows = xs[0].at[pl.ds(0, LEN)]
                loads = [copies.start(h, s) for h, s in zip((rows,) + given, used)]
                heavy = loads[8:]
                wait_all(loads[:8])
                x = used[0][...].astype(F32)
            elif slot == 1:
                x = jnp.where(info[0] == 0, xs[0][LEN:, :], xs[1][...]).astype(F32)
            else:
                x = xs[0][...].astype(F32)

            def ready(index):
                if manual:
                    heavy[index].wait()

            unit, _ = unit_rows_of(x)
            normed = (unit * gain[0:1, :] + shift[0:1, :]).astype(BF)
            ready(0)
            third = mm(normed, qkvw[:, 2 * dim :]) + qkvb[:, 2 * dim :]
            low = third.astype(BF)
            qkv_s[:, 2 * dim :] = low
            vt_s[...] = low.T
            for part in range(2):
                third = mm(normed, qkvw[:, part * dim : (part + 1) * dim])
                third = third + qkvb[:, part * dim : (part + 1) * dim]
                for j in range(blocks):
                    b = third[:, 128 * j : 128 * j + 128]
                    b = b * tab[0] + swap_halves(b) * tab[1]
                    if part == 0:
                        b = b * HEAD_DIM**-0.5
                    at = part * dim + 128 * j
                    qkv_s[:, at : at + 128] = b.astype(BF)
            for j in range(blocks):
                q = qkv_s[:, 128 * j : 128 * j + 128]
                k = qkv_s[:, dim + 128 * j : dim + 128 * j + 128]
                score_s[per * LEN * j : per * LEN * (j + 1), :] = mm(head_stack(k, per), q, NT)

            def soft(h, _):
                s = score_s[pl.ds(pl.multiple_of(h * LEN, LEN), LEN), :]
                e = jnp.exp(s - jnp.max(s, axis=0, keepdims=True))
                prob_s[h] = (e * (1.0 / jnp.sum(e, axis=0, keepdims=True))).astype(BF)
                return 0

            lax.fori_loop(0, HEADS, soft, 0, unroll=2)
            for h in range(HEADS):
                at = slice(HEAD_DIM * h, HEAD_DIM * (h + 1))
                mixt_s[at, :] = mm(vt_s[at, :], prob_s[h]).astype(BF)
            ready(1)
            mid = x + mm(mixt_s[...], outw[...], TN) + outb[...]
            mid_s[...] = mid
            unit, _ = unit_rows_of(mid)
            normed = (unit * gain[1:2, :] + shift[1:2, :]).astype(BF)
            ready(2)
            up_s[...] = mm(normed, upw[...])
            for c in range(parts):
                cols = slice(c * dim, (c + 1) * dim)
                u = up_s[:, cols] + upb[:, cols]
                cdf = 0.5 + 0.5 * lax.erf(u * 0.5**0.5)
                hid_s[:, cols] = (u * cdf).astype(BF)
                gp_s[:, cols] = (
                    cdf + u * (jnp.exp(u * u * -0.5) * (2 * np.pi) ** -0.5)
                ).astype(BF)
            ready(3)
            low = (mid_s[...] + downb[...] + mm(hid_s[...], downw[...])).astype(BF)
            y_s[...] = low
            act_s[...] = jnp.where(crop < live[0], low, jnp.zeros_like(low))
            at = pl.multiple_of(crop * LEN, LEN)
            copies.save(act_s, act_h.at[pl.ds(at, LEN)])
            copies.finish()

    outs = [shape(own.shape, BF)] + saved
    scratch = [
        pltpu.VMEM((LEN, dim), BF),
        pltpu.VMEM((dim, LEN), BF),
        pltpu.VMEM((HEADS * LEN, LEN), F32),
        pltpu.VMEM((LEN, wide), F32),
    ]
    if manual:
        scratch += [pltpu.VMEM((LEN, dim), BF)] + [vmem_like(a) for a in weights]
    aliases = {} if act is None else {len(ins) - 1: 0}
    spaces = "ss" + ("h" if manual else "v") * (count + 11) + "h" * len(before)
    out = call(
        kernel,
        outs,
        ins,
        scratch,
        16,
        aliases,
        "layer_forward",
        after,
        FIRST_LIMIT if manual else FORWARD_LIMIT,
        spaces,
        "h" + "v" * 7,
    )
    return out[0], out[1:]


def crop_weight(live, masks, crop, section):
    if section == 0:
        return 1.0
    count = jnp.where(live[0] > crop, masks[crop], 0)
    return jnp.full((1, 1), count, jnp.int32).astype(F32) / MASK_MEAN


def add_row(ref, row, values):
    ref[row : row + 1, :] = ref[row : row + 1, :] + jnp.sum(values, axis=0, keepdims=True)


def lay_out(own, bit, keep, send, block, index, row, count, at):
    src = pl.ds(row if isinstance(row, int) else pl.multiple_of(row, PAD), count)
    dst = pl.ds(at if isinstance(at, int) else pl.multiple_of(at, PAD), count)
    mine = own == bit

    @pl.when(mine)
    def _():
        keep[dst, :] = block[index, src, :]

    @pl.when(jnp.logical_not(mine))
    def _():
        send[dst, :] = block[index, src, :]


def keep_given(active, given, bufs):
    @pl.when(jnp.logical_not(active))
    def _():
        for old, new in zip(given, bufs):
            new[...] = old[...]


def pair_shapes(rows, dim):
    return [shape((rows, dim), BF)] * 2


def joined(refs, cols):
    return jnp.concatenate([r[:, cols] for r in refs], axis=0)


def wait_all(copies):
    for copy in copies:
        copy.wait()


def mlp_grad(section, info, live, masks, g, saved, params, after):
    mixts = [s[3] for s in saved]
    mids, gps, hids = ([s[k] for s in saved] for k in (4, 5, 6))
    upw, downw, gain, shift = params[4], params[6], params[8], params[9]
    rows, dim = g.shape
    wide = upw.shape[1]
    parts = wide // dim
    crops = len(saved)
    share = dim // GROUPS
    ins = [info, live, masks, g, gain, shift, downw, upw] + mids + gps + hids + mixts

    def kernel(info, live, masks, g_s, gain, shift, downw, upw, *refs):
        mid_s, gp_s, hid_s, mixt_s = (refs[i * crops : (i + 1) * crops] for i in range(4))
        refs = refs[4 * crops :]
        send_a, keep_a, send_b, keep_b, gmid_s, small_s = refs[:6]
        gu_s, block_s, low_s, normt_s, back_s = refs[7:]

        @pl.when(info[0] == section)
        def _():
            small_s[...] = jnp.zeros_like(small_s)
            for c in range(crops):
                crop = slice(c * LEN, (c + 1) * LEN)
                grad = g_s[crop, :].astype(F32) * crop_weight(live, masks, c, section)
                low = grad.astype(BF)
                low_s[crop, :] = low
                add_row(small_s, ROW_DOWN, low.astype(F32))
                unit, _ = unit_rows_of(mid_s[c][...])
                normt_s[:, crop] = (unit * gain[1:2, :] + shift[1:2, :]).astype(BF).T
            for c in range(parts):
                cols = slice(c * dim, (c + 1) * dim)
                block_s[c] = mm(joined(hid_s, cols), low_s[...], TN).astype(BF)

            @pl.loop(0, GROUPS * parts)
            def _(i):
                shard, row = i // parts, (i % parts) * share
                at = (shard // 2) * dim + row
                lay_out(info[1], shard % 2, keep_a, send_a, block_s, shard, row, share, at)

            for c in range(parts):
                cols = slice(c * dim, (c + 1) * dim)
                grad_up = mm(low_s[...], downw[cols, :], NT) * joined(gp_s, cols).astype(F32)
                grad_up = grad_up.astype(BF)
                gu_s[:, cols] = grad_up
                small_s[ROW_UP + c : ROW_UP + c + 1, :] = jnp.sum(
                    grad_up.astype(F32), axis=0, keepdims=True
                )
            back_s[...] = mm(gu_s[...], upw[...], NT)
            for c in range(crops):
                crop = slice(c * LEN, (c + 1) * LEN)
                grad = g_s[crop, :].astype(F32) * crop_weight(live, masks, c, section)
                unit, inverse = unit_rows_of(mid_s[c][...])
                back = back_s[crop, :]
                gmid = grad + norm_back(back, unit, inverse, gain[1:2, :])
                gmid_s[crop, :] = gmid
                low = gmid.astype(BF)
                low_s[crop, :] = low
                add_row(small_s, ROW_GAIN + 1, back * unit)
                add_row(small_s, ROW_SHIFT + 1, back)
                add_row(small_s, ROW_OUT, low.astype(F32))
            for c in range(parts):
                block_s[c] = mm(normt_s[...], gu_s[:, c * dim : (c + 1) * dim]).astype(BF)
            mixt = jnp.concatenate([m[...] for m in mixt_s], axis=1)
            block_s[parts] = mm(mixt, low_s[...]).astype(BF)

            @pl.loop(0, GROUPS * (parts + 1))
            def _(i):
                shard, c = i // (parts + 1), i % (parts + 1)
                at = ((shard % 2) * (parts + 1) + c) * share
                lay_out(info[2], shard // 2, keep_b, send_b, block_s, c, shard * share, share, at)

    scratch = [
        pltpu.VMEM((rows, wide), BF),
        pltpu.VMEM((parts + 1, dim, dim), BF),
        pltpu.VMEM((rows, dim), BF),
        pltpu.VMEM((dim, rows), BF),
        pltpu.VMEM((rows, dim), F32),
    ]
    outs = pair_shapes(2 * dim, dim) + pair_shapes(2 * (parts + 1) * share, dim)
    outs += [shape((rows, dim), F32), shape((PAD, dim), F32), TOKEN]
    out = call(kernel, outs, ins, scratch, 0, {}, "mlp_grad", after, MLP_LIMIT, micros=10)
    return out[:4], out[4], out[5], out[6]


def rotate_back(block, tab_t):
    half = HEAD_DIM // 2
    cos, sin = tab_t[0], tab_t[1]
    out = []
    for at in range(0, block.shape[0], HEAD_DIM):
        a, b = block[at : at + half], block[at + half : at + HEAD_DIM]
        out += [a * cos + b * sin, b * cos - a * sin]
    return jnp.concatenate(out, axis=0)


def attention_grad(section, info, gmid, small, xs, saved, params, tab_t, before, after):
    qkvs, probs, mixts = [s[1] for s in saved], [s[2] for s in saved], [s[3] for s in saved]
    qkvw, outw, gain, shift = params[0], params[2], params[8], params[9]
    rows, dim = gmid.shape
    blocks = dim // 128
    per = 128 // HEAD_DIM
    crops = len(saved)
    given = [] if before is None else [before]
    ins = [info, gmid, outw, small, gain, shift, tab_t, qkvw]
    ins += qkvs + probs + mixts + list(xs) + given

    def kernel(info, gmid_s, outw, small_s, gain, shift, tab_t, qkvw, *refs):
        qkv_s, prob_s, mixt_s = (refs[i * crops : (i + 1) * crops] for i in range(3))
        x_s = refs[3 * crops : 3 * crops + len(xs)]
        old = refs[3 * crops + len(xs) : 3 * crops + len(xs) + len(given)]
        refs = refs[3 * crops + len(xs) + len(given) :]
        keep_given(info[0] == section, old, refs[:1])
        dx_s, gqkv_s, normt_s, small_out = refs[:4]
        gmt_s, delta_s, da_s, ds_s, dt_s, kt_s = refs[5:]

        @pl.when(info[0] == section)
        def _():
            low = gmid_s[...].astype(BF)
            gmt_s[...] = mm(outw[...], low, NT).astype(BF)
            for c in range(crops):
                crop = slice(c * LEN, (c + 1) * LEN)
                qkv, prob = qkv_s[c], prob_s[c]
                product = gmt_s[:, crop].astype(F32) * mixt_s[c][...].astype(F32)
                delta_s[...] = jnp.sum(product.reshape(HEADS, HEAD_DIM, LEN), axis=1)[:, None, :]
                kt_s[0] = qkv[:, dim : 2 * dim].T
                kt_s[1] = qkv[:, :dim].T
                for j in range(blocks):
                    v = qkv[:, 2 * dim + 128 * j : 2 * dim + 128 * j + 128]
                    da_s[per * LEN * j : per * LEN * (j + 1), :] = mm(
                        head_stack(v, per), gmt_s[128 * j : 128 * j + 128, crop]
                    )

                def scores(h, _):
                    da = da_s[pl.ds(pl.multiple_of(h * LEN, LEN), LEN), :]
                    ds_s[h] = (prob[h].astype(F32) * (da - delta_s[h])).astype(BF)
                    return 0

                lax.fori_loop(0, HEADS, scores, 0, unroll=2)
                for h in range(HEADS):
                    at = slice(HEAD_DIM * h, HEAD_DIM * (h + 1))
                    dt_s[0, at, :] = mm(kt_s[0, at, :], ds_s[h])
                    dt_s[1, at, :] = mm(kt_s[1, at, :], ds_s[h], NT)
                    dt_s[2, at, :] = mm(gmt_s[at, crop], prob[h], NT)
                dq = rotate_back(dt_s[0] * HEAD_DIM**-0.5, tab_t)
                gqkv_s[crop, :dim] = dq.astype(BF).T
                gqkv_s[crop, dim : 2 * dim] = rotate_back(dt_s[1], tab_t).astype(BF).T
                gqkv_s[crop, 2 * dim :] = dt_s[2].astype(BF).T
            unit, inverse = unit_rows_of(joined(x_s, slice(None)).astype(F32))
            normt_s[...] = (unit * gain[0:1, :] + shift[0:1, :]).astype(BF).T
            back = mm(gqkv_s[...], qkvw[...], NT)
            dx_s[...] = (gmid_s[...] + norm_back(back, unit, inverse, gain[0:1, :])).astype(BF)
            small_out[...] = small_s[...]
            small_out[ROW_GAIN : ROW_GAIN + 1, :] = jnp.sum(back * unit, axis=0, keepdims=True)
            small_out[ROW_SHIFT : ROW_SHIFT + 1, :] = jnp.sum(back, axis=0, keepdims=True)

    outs = [
        shape((rows, dim), BF),
        shape((rows, 3 * dim), BF),
        shape((dim, rows), BF),
        shape(small.shape, F32),
        TOKEN,
    ]
    scratch = [
        pltpu.VMEM((dim, rows), BF),
        pltpu.VMEM((HEADS, 1, LEN), F32),
        pltpu.VMEM((HEADS * LEN, LEN), F32),
        pltpu.VMEM((HEADS, LEN, LEN), BF),
        pltpu.VMEM((3, dim, LEN), F32),
        pltpu.VMEM((2, dim, LEN), BF),
    ]
    aliases = {len(ins) - 1: 0} if given else {}
    out = call(kernel, outs, ins, scratch, 0, aliases, "attention_grad", after, ATTENTION_LIMIT, micros=ATTENTION_MICROS)
    return out[0], out[1:4], out[4]


def qkv_grad(section, info, kept, before, after):
    gqkv, normt, small = kept
    dim, rows = normt.shape
    share = dim // GROUPS
    half = 3 * share // 2
    given = [] if before is None else list(before)
    ins = [info, gqkv, normt, small] + given

    def kernel(info, gqkv_s, normt_s, small_s, *refs):
        old = refs[: len(given)]
        bufs = refs[len(given) : len(given) + 4]
        send_a, keep_a, send_b, keep_b = bufs
        (block_s,) = refs[len(given) + 5 :]
        keep_given(info[0] == section, old, bufs)

        @pl.when(info[0] == section)
        def _():
            sums = [
                jnp.sum(gqkv_s[:, c * dim : (c + 1) * dim].astype(F32), axis=0, keepdims=True)
                for c in range(3)
            ]
            tail = jnp.concatenate(sums + [small_s[ROW_OUT:, :]], axis=0).astype(BF)
            send_a[2 * half :, :] = tail
            keep_a[2 * half :, :] = tail
            for c in range(3):
                block_s[c] = mm(normt_s[...], gqkv_s[:, c * dim : (c + 1) * dim]).astype(BF)

            @pl.loop(0, GROUPS)
            def _(shard):
                x, y, base = shard % 2, shard // 2, shard * share
                for c in range(3):
                    row, at, left = 0, c * share, share
                    while left:
                        count = min(left, half - at % half)
                        if at < half:
                            own, bit, keep, send, to = info[1], x, keep_a, send_a, y * half + at
                        else:
                            own, bit, keep, send, to = info[2], y, keep_b, send_b, x * half + at - half
                        lay_out(own, bit, keep, send, block_s, c, base + row, count, to)
                        row, at, left = row + count, at + count, left - count

    scratch = [pltpu.VMEM((3, dim, dim), BF)]
    aliases = {len(ins) - 4 + i: i for i in range(4)} if given else {}
    outs = pair_shapes(2 * half + PAD, dim) + pair_shapes(2 * half, dim) + [TOKEN]
    out = call(kernel, outs, ins, scratch, 0, aliases, "qkv_grad", after, QKV_LIMIT)
    return out[:4], out[4]


STEP = 80


def plus(one, two):
    return (one.astype(F32) + two.astype(F32)).astype(BF)


def add_rows(out, at, one, two, start, count):
    whole = count // STEP * STEP

    @pl.loop(0, whole // STEP)
    def _(i):
        src = pl.ds(pl.multiple_of(start + i * STEP, PAD), STEP)
        dst = pl.ds(pl.multiple_of(at + i * STEP, PAD), STEP)
        out[dst, :] = plus(one[src, :], two[src, :])

    if count > whole:
        src = pl.ds(pl.multiple_of(start + whole, PAD), count - whole)
        out[pl.ds(at + whole, count - whole), :] = plus(one[src, :], two[src, :])


def taking_part(info, sections, middle):
    check = None
    if len(sections) == 1:
        check = info[0] == sections[0]
    if middle:
        inner = jnp.logical_or(info[3] == 1, info[3] == 2)
        check = inner if check is None else jnp.logical_and(check, inner)
    return info[3] >= 0 if check is None else check


def vmem_call(kernel, outs, info, ins, name, after):
    return call(kernel, outs, [info] + ins, [], 0, {}, name, after, 8)


def first_sum(info, sections, keep_a, recv_a, keep_b, recv_b, after):
    dim = keep_b.shape[1]
    sizes = [(k.shape[0] // (2 * PAD) * PAD, k.shape[0] % (2 * PAD)) for k in (keep_a, keep_b)]

    def kernel(info, ka, ra, kb, rb, sa, na, sb, nb):
        @pl.when(taking_part(info, sections, False))
        def _():
            for own, one, two, new, out, (half, extra) in (
                (info[2], ka, ra, na, sa, sizes[0]),
                (info[1], kb, rb, nb, sb, sizes[1]),
            ):
                add_rows(out, 0, one, two, (1 - own) * half, half)
                add_rows(new, 0, one, two, own * half, half)
                if extra:
                    tail = plus(one[2 * half :, :], two[2 * half :, :])
                    new[half:, :] = tail
                    out[half:, :] = tail

    outs = [shape((sum(size), dim), BF) for size in sizes for _ in range(2)]
    return vmem_call(kernel, outs, info, [keep_a, recv_a, keep_b, recv_b], "first_sum", after)


def second_sum(info, sections, keep_a, recv_a, keep_b, recv_b, joint, after):
    dim = keep_b.shape[1]
    top, rest = keep_a.shape[0], keep_b.shape[0]

    def kernel(info, ka, ra, kb, rb, *out):
        @pl.when(taking_part(info, sections, False))
        def _():
            add_rows(out[0], 0, ka, ra, 0, top)
            add_rows(out[-1], out[-1].shape[0] - rest, kb, rb, 0, rest)

    outs = [shape((top + rest, dim), BF)]
    if not joint:
        outs = [shape((top, dim), BF), shape((rest, dim), BF)]
    return vmem_call(kernel, outs, info, [keep_a, recv_a, keep_b, recv_b], "second_sum", after)


def pair_sum(info, sections, one, two, after):
    def kernel(info, one, two, out):
        @pl.when(taking_part(info, sections, True))
        def _():
            add_rows(out, 0, one, two, 0, one.shape[0])

    return vmem_call(kernel, [shape(one.shape, BF)], info, [one, two], "pair_sum", after)[0]


def own_pieces(row, count, width, group):
    share = count * width // GROUPS
    at, pieces = group * share, []
    while at < (group + 1) * share:
        size = min((group + 1) * share - at, width - at % width)
        pieces.append((row + at // width, at % width, size, at - group * share))
        at += size
    return pieces


def finish(info, sources, kind, after):
    dim = sources[0][0].shape[1]
    share = dim // GROUPS
    half = 3 * share // 2
    vectors = ((ROW_QKV, 3), (ROW_OUT, 1), (ROW_UP, 4), (ROW_DOWN, 1))
    if kind == "down":
        rows, outs = dim, [shape((dim, dim), F32)]
    elif kind == "up":
        rows, outs = 5 * share, [shape((share, 4 * dim), F32), shape((share, dim), F32)]
    else:
        rows, outs = 3 * share + PAD, [shape((share, 3 * dim), F32)]
    large = len(outs)
    if kind == "qkv":
        outs += [shape((1, count * dim // GROUPS), F32) for _, count in vectors]
        outs += [shape((2, share), F32)] * 2

    def kernel(info, p0, g0, p1, g1, *refs):
        out_h = refs[:large]
        small = refs[large : len(outs)]
        src = refs[len(outs)]
        stage = refs[len(outs) + 1 : -1]
        sems = refs[-1]
        inner = jnp.logical_or(info[3] == 1, info[3] == 2)
        for section, part, got in ((0, p0, g0), (1, p1, g1)):
            mine = info[0] == section
            lines = pl.ds(sources[section][2], rows)

            @pl.when(jnp.logical_and(mine, inner))
            def _():
                pltpu.make_async_copy(part.at[lines], src, sems.at[0]).start()

            @pl.when(jnp.logical_and(mine, jnp.logical_not(inner)))
            def _():
                pltpu.make_async_copy(got.at[lines], src, sems.at[0]).start()

        pltpu.make_async_copy(p0.at[pl.ds(sources[0][2], rows)], src, sems.at[0]).wait()
        if kind == "down":
            stage[0][...] = src[...].astype(F32)
        elif kind == "up":
            for i in range(4):
                block = src[i * share : (i + 1) * share, :].astype(F32)
                stage[0][:, i * dim : (i + 1) * dim] = block
            stage[1][...] = src[4 * share :, :].astype(F32)
        else:
            for i in range(3):
                at, left, to = i * share, share, 0
                while left:
                    count = min(left, half - at % half)
                    row = at if at < half else at + PAD
                    block = src[row : row + count, :].astype(F32)
                    stage[0][to : to + count, i * dim : (i + 1) * dim] = block
                    at, left, to = at + count, left - count, to + count
        copies = [
            pltpu.make_async_copy(s, o, sems.at[1 + i]) for i, (s, o) in enumerate(zip(stage, out_h))
        ]
        for copy in copies:
            copy.start()
        if kind == "qkv":
            tail = src[half : half + PAD, :].astype(F32)
            for group in range(GROUPS):

                @pl.when(info[1] + 2 * info[2] == group)
                def _():
                    for out, (row, count) in zip(small, vectors):
                        for r, c, size, at in own_pieces(row, count, dim, group):
                            out[:, at : at + size] = tail[r : r + 1, c : c + size]
                    for out, row in zip(small[4:], (ROW_GAIN, ROW_SHIFT)):
                        out[...] = tail[row : row + 2, group * share : (group + 1) * share]

        for copy in copies:
            copy.wait()

    scratch = [pltpu.VMEM((rows, dim), BF)] + [vmem_like(o) for o in outs[:large]]
    ins = [info] + [a for source in sources for a in source[:2]]
    places = "h" * large + "v" * (len(outs) - large)
    return call(kernel, outs, ins, scratch, 4, {}, "finish", after, 12, "saaaa", places)


def flow(shard, axis, pairs, sections):
    if sections == (0, 1):
        return lax.ppermute(shard, axis, pairs)
    peers = lax.axis_size(axis)
    pairs = [(s * peers + i, s * peers + j) for s in sections for i, j in pairs]
    return lax.ppermute(shard, ("section", axis), pairs)


class Reduction:
    def __init__(self, info, sections, bufs, joint):
        self.info, self.sections, self.joint = info, sections, joint
        groups = range(GROUPS)
        self.across = [(g, g ^ 1) for g in groups]
        self.along = [(g, g ^ 2) for g in groups]
        self.line = lax.axis_size("replica") == 4
        send_a, keep_a, send_b, keep_b = bufs
        self.kept = (keep_a, keep_b)
        self.got = (
            flow(send_a, "group", self.across, sections),
            flow(send_b, "group", self.along, sections),
        )

    def group_two(self, after):
        send_a, keep_a, send_b, keep_b = first_sum(
            self.info, self.sections, self.kept[0], self.got[0], self.kept[1], self.got[1], after
        )
        self.kept = (keep_a, keep_b)
        self.got = (
            flow(send_a, "group", self.along, self.sections),
            flow(send_b, "group", self.across, self.sections),
        )
        return keep_a

    def replica_one(self, after):
        self.parts = list(
            second_sum(
                self.info,
                self.sections,
                self.kept[0],
                self.got[0],
                self.kept[1],
                self.got[1],
                self.joint,
                after,
            )
        )
        if self.line:
            self.got = [
                flow(part, "replica", [(0, 1), (3, 2)], self.sections) for part in self.parts
            ]
        else:
            self.parts = [lax.psum(part, "replica") for part in self.parts]
            self.got = list(self.parts)
        return self.parts[0]

    def replica_next(self, pairs, after):
        for i in range(len(self.parts)):
            if self.line:
                self.parts[i] = after = pair_sum(
                    self.info, self.sections, self.parts[i], self.got[i], after
                )
                self.got[i] = flow(self.parts[i], "replica", pairs, self.sections)
        return after

    def replica_two(self, after):
        return self.replica_next([(1, 2), (2, 1)], after)

    def replica_three(self, after):
        return self.replica_next([(1, 0), (2, 3)], after)

    def source(self, half, row):
        index = 0 if self.joint else half
        return self.parts[index], self.got[index], row


def shards(
    block_input,
    cotangent,
    crop_count,
    mask_count,
    qkv_weight,
    qkv_bias,
    out_weight,
    out_bias,
    up_weight,
    up_bias,
    down_weight,
    down_bias,
    norm_gain,
    norm_shift,
):
    params = (
        qkv_weight[0],
        qkv_bias,
        out_weight[0],
        out_bias,
        up_weight[0],
        up_bias,
        down_weight[0],
        down_bias,
        norm_gain[0],
        norm_shift[0],
    )
    rows, dim = block_input.shape
    tab = jnp.asarray(rotary_tables())
    tab_t = jnp.asarray(rotary_columns())
    group = lax.axis_index("group")
    assert lax.axis_size("group") == GROUPS
    info = jnp.stack([lax.axis_index("section"), group % 2, group // 2, lax.axis_index("replica")])

    def to_other(shard, pairs):
        return lax.ppermute(shard, "section", pairs)

    act, first = forward(0, info, crop_count, block_input, None, params, tab, None)
    arrived = [to_other(first[0], [(0, 1)])]
    act, second = forward(1, info, crop_count, block_input, arrived[0], params, tab, act)
    arrived.append(to_other(second[0], [(0, 1)]))
    act, third = forward(2, info, crop_count, block_input, arrived[1], params, tab, act)
    kept_one, kept_zero = (second, third), (first, second)

    common = (info, crop_count, mask_count)
    bufs, gmid, small, last = mlp_grad(1, *common, cotangent, kept_one, params, None)
    one = Reduction(info, (1,), bufs, True)
    dx, kept, last = attention_grad(
        1, info, gmid, small, arrived, kept_one, params, tab_t, None, last
    )
    grad_back = to_other(dx, [(1, 0)])
    bufs_three, last = qkv_grad(1, info, kept, None, last)
    last = one.group_two(last)
    bufs, gmid, small, last = mlp_grad(0, *common, grad_back, kept_zero, params, last)
    two = Reduction(info, (0,), bufs, False)
    last = one.replica_one(last)
    dx, kept, last = attention_grad(
        0, info, gmid, small, [block_input], kept_zero, params, tab_t, dx, last
    )
    bufs, last = qkv_grad(0, info, kept, bufs_three, last)
    three = Reduction(info, (0, 1), bufs, True)
    last = two.group_two(last)
    last = one.replica_two(last)
    last = two.replica_one(last)
    last = three.group_two(last)
    last = two.replica_two(last)
    last = three.replica_one(last)
    last = one.replica_three(last)
    last = two.replica_three(last)
    last = three.replica_two(last)
    (grad_down,) = finish(info, (two.source(0, 0), one.source(0, 0)), "down", last)
    last = three.replica_three(grad_down)
    grad_up, grad_out = finish(info, (two.source(1, 0), one.source(1, dim)), "up", last)
    grad_qkv, *small = finish(info, (three.source(0, 0), three.source(0, 0)), "qkv", grad_out)
    qkv_b, out_b, up_b, down_b, gain, shift = small
    return (
        act[None],
        dx[None],
        grad_qkv[None],
        qkv_b,
        grad_out[None],
        out_b,
        grad_up[None],
        up_b,
        grad_down[None],
        down_b,
        gain[None],
        shift[None],
    )


def solution(mesh):
    rows = P(("group", "replica"))
    stack = P("section")
    return jax.shard_map(
        shards,
        mesh=mesh,
        in_specs=(rows,) * 4 + (stack,) * 10,
        out_specs=(
            P("section", ("group", "replica"), None),
            P("section", ("group", "replica"), None),
            P("section", "group", None),
            P("section", "group"),
            P("section", "group", None),
            P("section", "group"),
            P("section", "group", None),
            P("section", "group"),
            P("section", "group", None),
            P("section", "group"),
            P("section", None, "group"),
            P("section", None, "group"),
        ),
        check_vma=False,
    )
```

```python
import jax
import jax.numpy as jnp
import numpy as np
from jax import lax
from jax.experimental import pallas as pl
from jax.experimental.pallas import tpu as pltpu
from jax.sharding import PartitionSpec as P

HEADS = 20
HEAD_DIM = 32
LEN = 256
MASK_MEAN = 38
CROP_DEV = 2
EPSILON = 1e-05
ROTARY_BASE = 10000.0

BF = jnp.bfloat16
F32 = jnp.float32
NN = (((1,), (0,)), ((), ()))
NT = (((1,), (1,)), ((), ()))
TN = (((0,), (0,)), ((), ()))

FIRST_LIMIT, FORWARD_LIMIT, MLP_LIMIT, ATTENTION_LIMIT, QKV_LIMIT = 40, 14, 16, 17, 8
ATTENTION_MICROS = 12
REPLICAS = 4
GROUPS = 4
PAD = 16
ROW_QKV, ROW_OUT, ROW_UP, ROW_DOWN, ROW_GAIN, ROW_SHIFT = 0, 3, 4, 8, 9, 11

ANY = pl.BlockSpec(memory_space=pl.ANY)
HBM = pl.BlockSpec(memory_space=pltpu.HBM)
VMEM = pl.BlockSpec(memory_space=pltpu.VMEM)
SMEM = pl.BlockSpec(memory_space=pltpu.SMEM)


def shape(dims, dtype):
    return jax.ShapeDtypeStruct(dims, dtype)


def mm(left, right, dims=NN):
    return lax.dot_general(left, right, dims, preferred_element_type=F32)


def unit_rows_of(values):
    centred = values - jnp.mean(values, axis=-1, keepdims=True)
    inverse = lax.rsqrt(jnp.mean(centred * centred, axis=-1, keepdims=True) + EPSILON)
    return centred * inverse, inverse


def norm_back(grad, unit, inverse, gain):
    scaled = grad * gain
    return inverse * (
        scaled
        - jnp.mean(scaled, axis=-1, keepdims=True)
        - unit * jnp.mean(scaled * unit, axis=-1, keepdims=True)
    )


def rotary_tables():
    lane = np.arange(128) % HEAD_DIM
    half = HEAD_DIM // 2
    freq = ROTARY_BASE ** (-(lane % half).astype(np.float64) * (2.0 / HEAD_DIM))
    angles = np.arange(LEN)[:, None] * freq[None, :]
    sign = np.where(lane < half, -1.0, 1.0)[None, :]
    return np.stack([np.cos(angles), np.sin(angles) * sign]).astype(np.float32)


def rotary_columns():
    half = HEAD_DIM // 2
    freq = ROTARY_BASE ** (-np.arange(half, dtype=np.float64) * (2.0 / HEAD_DIM))
    angles = freq[:, None] * np.arange(LEN)[None, :]
    return np.stack([np.cos(angles), np.sin(angles)]).astype(np.float32)


def swap_halves(values):
    lane = lax.broadcasted_iota(jnp.int32, values.shape, 1) % HEAD_DIM
    half = HEAD_DIM // 2
    return jnp.where(
        lane < half,
        pltpu.roll(values, 128 - half, axis=1),
        pltpu.roll(values, half, axis=1),
    )


def head_stack(block, per):
    head = lax.broadcasted_iota(jnp.int32, block.shape, 1) // HEAD_DIM
    return jnp.concatenate(
        [jnp.where(head == h, block, jnp.zeros_like(block)) for h in range(per)], axis=0
    )


class Copies:
    def __init__(self, sems):
        self.sems = sems
        self.used = 0
        self.open = []

    def start(self, src, dst):
        copy = pltpu.make_async_copy(src, dst, self.sems.at[self.used])
        self.used += 1
        copy.start()
        return copy

    def save(self, src, dst):
        self.open.append(self.start(src, dst))

    def finish(self):
        for copy in self.open:
            copy.wait()


def call(kernel, outs, ins, scratch, sems, aliases, name, after=None, limit=16, spaces=None, out_spaces=None, micros=0.1):
    count = len(ins)
    places = {"v": VMEM, "h": HBM, "a": ANY, "s": SMEM}
    spaces = spaces or "v" * count
    out_spaces = out_spaces or "v" * len(outs)
    in_specs = [SMEM if a.ndim == 1 else places[p] for a, p in zip(ins, spaces)]
    ins = [pltpu.with_memory_space_constraint(a, pltpu.HBM) if p == "h" else a for a, p in zip(ins, spaces)]
    body = kernel
    if after is not None:
        ins = list(ins) + [after]
        in_specs = in_specs + [ANY]

        def body(*refs):
            kernel(*refs[:count], *refs[count + 1 :])

    outs = [pltpu.HBM(o.shape, o.dtype) if p == "h" else o for o, p in zip(outs, out_spaces)]
    return pl.pallas_call(
        body,
        out_shape=outs,
        in_specs=in_specs,
        out_specs=[places[p] for p in out_spaces],
        scratch_shapes=scratch + ([pltpu.SemaphoreType.DMA((sems,))] if sems else []),
        input_output_aliases=aliases,
        compiler_params=pltpu.CompilerParams(vmem_limit_bytes=limit << 20),
        cost_estimate=pl.CostEstimate(
            flops=int(micros * 1.15e9), bytes_accessed=0, transcendentals=0
        ),
        name=name,
    )(*ins)


TOKEN = jax.ShapeDtypeStruct((8, 128), F32)


def vmem_like(arr):
    return pltpu.VMEM(arr.shape, arr.dtype)


def forward(slot, info, live, own, arrived, params, tab, act, after=None):
    qkvw, qkvb, outw, outb, upw, upb, downw, downb, gain, shift = params
    dim = own.shape[1]
    blocks = dim // 128
    wide = upw.shape[1]
    parts = wide // dim
    per = 128 // HEAD_DIM
    manual = slot == 0
    saved = [
        shape((LEN, dim), BF),
        shape((LEN, 3 * dim), BF),
        shape((HEADS, LEN, LEN), BF),
        shape((dim, LEN), BF),
        shape((LEN, dim), F32),
        shape((LEN, wide), BF),
        shape((LEN, wide), BF),
    ]
    weights = [qkvb, outb, upb, downb, gain, shift, tab, qkvw, outw, upw, downw]
    sources = [own] if slot == 0 else [arrived] if slot == 2 else [own, arrived]
    before = [] if act is None else [act]
    ins = [info, live] + sources + weights + before
    count = len(sources)

    def kernel(info, live, *refs):
        xs = refs[:count]
        given = refs[count : count + 11]
        act_h, *outs = refs[count + 11 + len(before) : count + 19 + len(before)]
        scratch = refs[count + 19 + len(before) :]
        act_s, vt_s, score_s, up_s = scratch[:4]
        sems = scratch[-1]
        y_s, qkv_s, prob_s, mixt_s, mid_s, gp_s, hid_s = outs
        used = scratch[4:-1] if manual else xs[-1:] + given
        qkvb, outb, upb, downb, gain, shift, tab, qkvw, outw, upw, downw = used[1:]
        crop = slot - info[0]

        @pl.when(jnp.logical_and(crop >= 0, crop < CROP_DEV))
        def _():
            copies = Copies(sems)
            heavy = []
            if manual:
                rows = xs[0].at[pl.ds(0, LEN)]
                loads = [copies.start(h, s) for h, s in zip((rows,) + given, used)]
                heavy = loads[8:]
                wait_all(loads[:8])
                x = used[0][...].astype(F32)
            elif slot == 1:
                x = jnp.where(info[0] == 0, xs[0][LEN:, :], xs[1][...]).astype(F32)
            else:
                x = xs[0][...].astype(F32)

            def ready(index):
                if manual:
                    heavy[index].wait()

            unit, _ = unit_rows_of(x)
            normed = (unit * gain[0:1, :] + shift[0:1, :]).astype(BF)
            ready(0)
            third = mm(normed, qkvw[:, 2 * dim :]) + qkvb[:, 2 * dim :]
            low = third.astype(BF)
            qkv_s[:, 2 * dim :] = low
            vt_s[...] = low.T
            for part in range(2):
                third = mm(normed, qkvw[:, part * dim : (part + 1) * dim])
                third = third + qkvb[:, part * dim : (part + 1) * dim]
                for j in range(blocks):
                    b = third[:, 128 * j : 128 * j + 128]
                    b = b * tab[0] + swap_halves(b) * tab[1]
                    if part == 0:
                        b = b * HEAD_DIM**-0.5
                    at = part * dim + 128 * j
                    qkv_s[:, at : at + 128] = b.astype(BF)
            for j in range(blocks):
                q = qkv_s[:, 128 * j : 128 * j + 128]
                k = qkv_s[:, dim + 128 * j : dim + 128 * j + 128]
                score_s[per * LEN * j : per * LEN * (j + 1), :] = mm(head_stack(k, per), q, NT)

            def soft(h, _):
                s = score_s[pl.ds(pl.multiple_of(h * LEN, LEN), LEN), :]
                e = jnp.exp(s - jnp.max(s, axis=0, keepdims=True))
                prob_s[h] = (e * (1.0 / jnp.sum(e, axis=0, keepdims=True))).astype(BF)
                return 0

            lax.fori_loop(0, HEADS, soft, 0, unroll=2)
            for h in range(HEADS):
                at = slice(HEAD_DIM * h, HEAD_DIM * (h + 1))
                mixt_s[at, :] = mm(vt_s[at, :], prob_s[h]).astype(BF)
            ready(1)
            mid = x + mm(mixt_s[...], outw[...], TN) + outb[...]
            mid_s[...] = mid
            unit, _ = unit_rows_of(mid)
            normed = (unit * gain[1:2, :] + shift[1:2, :]).astype(BF)
            ready(2)
            up_s[...] = mm(normed, upw[...])
            for c in range(parts):
                cols = slice(c * dim, (c + 1) * dim)
                u = up_s[:, cols] + upb[:, cols]
                cdf = 0.5 + 0.5 * lax.erf(u * 0.5**0.5)
                hid_s[:, cols] = (u * cdf).astype(BF)
                gp_s[:, cols] = (
                    cdf + u * (jnp.exp(u * u * -0.5) * (2 * np.pi) ** -0.5)
                ).astype(BF)
            ready(3)
            low = (mid_s[...] + downb[...] + mm(hid_s[...], downw[...])).astype(BF)
            y_s[...] = low
            act_s[...] = jnp.where(crop < live[0], low, jnp.zeros_like(low))
            at = pl.multiple_of(crop * LEN, LEN)
            copies.save(act_s, act_h.at[pl.ds(at, LEN)])
            copies.finish()

    outs = [shape(own.shape, BF)] + saved
    scratch = [
        pltpu.VMEM((LEN, dim), BF),
        pltpu.VMEM((dim, LEN), BF),
        pltpu.VMEM((HEADS * LEN, LEN), F32),
        pltpu.VMEM((LEN, wide), F32),
    ]
    if manual:
        scratch += [pltpu.VMEM((LEN, dim), BF)] + [vmem_like(a) for a in weights]
    aliases = {} if act is None else {len(ins) - 1: 0}
    spaces = "ss" + ("h" if manual else "v") * (count + 11) + "h" * len(before)
    out = call(
        kernel,
        outs,
        ins,
        scratch,
        16,
        aliases,
        "layer_forward",
        after,
        FIRST_LIMIT if manual else FORWARD_LIMIT,
        spaces,
        "h" + "v" * 7,
    )
    return out[0], out[1:]


def crop_weight(live, masks, crop, section):
    if section == 0:
        return 1.0
    count = jnp.where(live[0] > crop, masks[crop], 0)
    return jnp.full((1, 1), count, jnp.int32).astype(F32) / MASK_MEAN


def add_row(ref, row, values):
    ref[row : row + 1, :] = ref[row : row + 1, :] + jnp.sum(values, axis=0, keepdims=True)


def lay_out(own, bit, keep, send, block, index, row, count, at):
    src = pl.ds(row if isinstance(row, int) else pl.multiple_of(row, PAD), count)
    dst = pl.ds(at if isinstance(at, int) else pl.multiple_of(at, PAD), count)
    mine = own == bit

    @pl.when(mine)
    def _():
        keep[dst, :] = block[index, src, :]

    @pl.when(jnp.logical_not(mine))
    def _():
        send[dst, :] = block[index, src, :]


def keep_given(active, given, bufs):
    @pl.when(jnp.logical_not(active))
    def _():
        for old, new in zip(given, bufs):
            new[...] = old[...]


def pair_shapes(rows, dim):
    return [shape((rows, dim), BF)] * 2


def joined(refs, cols):
    return jnp.concatenate([r[:, cols] for r in refs], axis=0)


def wait_all(copies):
    for copy in copies:
        copy.wait()


def mlp_grad(section, info, live, masks, g, saved, params, after):
    mixts = [s[3] for s in saved]
    mids, gps, hids = ([s[k] for s in saved] for k in (4, 5, 6))
    upw, downw, gain, shift = params[4], params[6], params[8], params[9]
    rows, dim = g.shape
    wide = upw.shape[1]
    parts = wide // dim
    crops = len(saved)
    share = dim // GROUPS
    ins = [info, live, masks, g, gain, shift, downw, upw] + mids + gps + hids + mixts

    def kernel(info, live, masks, g_s, gain, shift, downw, upw, *refs):
        mid_s, gp_s, hid_s, mixt_s = (refs[i * crops : (i + 1) * crops] for i in range(4))
        refs = refs[4 * crops :]
        send_a, keep_a, send_b, keep_b, gmid_s, small_s = refs[:6]
        gu_s, block_s, low_s, normt_s, back_s = refs[7:]

        @pl.when(info[0] == section)
        def _():
            small_s[...] = jnp.zeros_like(small_s)
            for c in range(crops):
                crop = slice(c * LEN, (c + 1) * LEN)
                grad = g_s[crop, :].astype(F32) * crop_weight(live, masks, c, section)
                low = grad.astype(BF)
                low_s[crop, :] = low
                add_row(small_s, ROW_DOWN, low.astype(F32))
                unit, _ = unit_rows_of(mid_s[c][...])
                normt_s[:, crop] = (unit * gain[1:2, :] + shift[1:2, :]).astype(BF).T
            for c in range(parts):
                cols = slice(c * dim, (c + 1) * dim)
                block_s[c] = mm(joined(hid_s, cols), low_s[...], TN).astype(BF)

            @pl.loop(0, GROUPS * parts)
            def _(i):
                shard, row = i // parts, (i % parts) * share
                at = (shard // 2) * dim + row
                lay_out(info[1], shard % 2, keep_a, send_a, block_s, shard, row, share, at)

            for c in range(parts):
                cols = slice(c * dim, (c + 1) * dim)
                grad_up = mm(low_s[...], downw[cols, :], NT) * joined(gp_s, cols).astype(F32)
                grad_up = grad_up.astype(BF)
                gu_s[:, cols] = grad_up
                small_s[ROW_UP + c : ROW_UP + c + 1, :] = jnp.sum(
                    grad_up.astype(F32), axis=0, keepdims=True
                )
            back_s[...] = mm(gu_s[...], upw[...], NT)
            for c in range(crops):
                crop = slice(c * LEN, (c + 1) * LEN)
                grad = g_s[crop, :].astype(F32) * crop_weight(live, masks, c, section)
                unit, inverse = unit_rows_of(mid_s[c][...])
                back = back_s[crop, :]
                gmid = grad + norm_back(back, unit, inverse, gain[1:2, :])
                gmid_s[crop, :] = gmid
                low = gmid.astype(BF)
                low_s[crop, :] = low
                add_row(small_s, ROW_GAIN + 1, back * unit)
                add_row(small_s, ROW_SHIFT + 1, back)
                add_row(small_s, ROW_OUT, low.astype(F32))
            for c in range(parts):
                block_s[c] = mm(normt_s[...], gu_s[:, c * dim : (c + 1) * dim]).astype(BF)
            mixt = jnp.concatenate([m[...] for m in mixt_s], axis=1)
            block_s[parts] = mm(mixt, low_s[...]).astype(BF)

            @pl.loop(0, GROUPS * (parts + 1))
            def _(i):
                shard, c = i // (parts + 1), i % (parts + 1)
                at = ((shard % 2) * (parts + 1) + c) * share
                lay_out(info[2], shard // 2, keep_b, send_b, block_s, c, shard * share, share, at)

    scratch = [
        pltpu.VMEM((rows, wide), BF),
        pltpu.VMEM((parts + 1, dim, dim), BF),
        pltpu.VMEM((rows, dim), BF),
        pltpu.VMEM((dim, rows), BF),
        pltpu.VMEM((rows, dim), F32),
    ]
    outs = pair_shapes(2 * dim, dim) + pair_shapes(2 * (parts + 1) * share, dim)
    outs += [shape((rows, dim), F32), shape((PAD, dim), F32), TOKEN]
    out = call(kernel, outs, ins, scratch, 0, {}, "mlp_grad", after, MLP_LIMIT, micros=10)
    return out[:4], out[4], out[5], out[6]


def rotate_back(block, tab_t):
    half = HEAD_DIM // 2
    cos, sin = tab_t[0], tab_t[1]
    out = []
    for at in range(0, block.shape[0], HEAD_DIM):
        a, b = block[at : at + half], block[at + half : at + HEAD_DIM]
        out += [a * cos + b * sin, b * cos - a * sin]
    return jnp.concatenate(out, axis=0)


def attention_grad(section, info, gmid, small, xs, saved, params, tab_t, before, after):
    qkvs, probs, mixts = [s[1] for s in saved], [s[2] for s in saved], [s[3] for s in saved]
    qkvw, outw, gain, shift = params[0], params[2], params[8], params[9]
    rows, dim = gmid.shape
    blocks = dim // 128
    per = 128 // HEAD_DIM
    crops = len(saved)
    given = [] if before is None else [before]
    ins = [info, gmid, outw, small, gain, shift, tab_t, qkvw]
    ins += qkvs + probs + mixts + list(xs) + given

    def kernel(info, gmid_s, outw, small_s, gain, shift, tab_t, qkvw, *refs):
        qkv_s, prob_s, mixt_s = (refs[i * crops : (i + 1) * crops] for i in range(3))
        x_s = refs[3 * crops : 3 * crops + len(xs)]
        old = refs[3 * crops + len(xs) : 3 * crops + len(xs) + len(given)]
        refs = refs[3 * crops + len(xs) + len(given) :]
        keep_given(info[0] == section, old, refs[:1])
        dx_s, gqkv_s, normt_s, small_out = refs[:4]
        gmt_s, delta_s, da_s, ds_s, dt_s, kt_s = refs[5:]

        @pl.when(info[0] == section)
        def _():
            low = gmid_s[...].astype(BF)
            gmt_s[...] = mm(outw[...], low, NT).astype(BF)
            for c in range(crops):
                crop = slice(c * LEN, (c + 1) * LEN)
                qkv, prob = qkv_s[c], prob_s[c]
                product = gmt_s[:, crop].astype(F32) * mixt_s[c][...].astype(F32)
                delta_s[...] = jnp.sum(product.reshape(HEADS, HEAD_DIM, LEN), axis=1)[:, None, :]
                kt_s[0] = qkv[:, dim : 2 * dim].T
                kt_s[1] = qkv[:, :dim].T
                for j in range(blocks):
                    v = qkv[:, 2 * dim + 128 * j : 2 * dim + 128 * j + 128]
                    da_s[per * LEN * j : per * LEN * (j + 1), :] = mm(
                        head_stack(v, per), gmt_s[128 * j : 128 * j + 128, crop]
                    )

                def scores(h, _):
                    da = da_s[pl.ds(pl.multiple_of(h * LEN, LEN), LEN), :]
                    ds_s[h] = (prob[h].astype(F32) * (da - delta_s[h])).astype(BF)
                    return 0

                lax.fori_loop(0, HEADS, scores, 0, unroll=2)
                for h in range(HEADS):
                    at = slice(HEAD_DIM * h, HEAD_DIM * (h + 1))
                    dt_s[0, at, :] = mm(kt_s[0, at, :], ds_s[h])
                    dt_s[1, at, :] = mm(kt_s[1, at, :], ds_s[h], NT)
                    dt_s[2, at, :] = mm(gmt_s[at, crop], prob[h], NT)
                dq = rotate_back(dt_s[0] * HEAD_DIM**-0.5, tab_t)
                gqkv_s[crop, :dim] = dq.astype(BF).T
                gqkv_s[crop, dim : 2 * dim] = rotate_back(dt_s[1], tab_t).astype(BF).T
                gqkv_s[crop, 2 * dim :] = dt_s[2].astype(BF).T
            unit, inverse = unit_rows_of(joined(x_s, slice(None)).astype(F32))
            normt_s[...] = (unit * gain[0:1, :] + shift[0:1, :]).astype(BF).T
            back = mm(gqkv_s[...], qkvw[...], NT)
            dx_s[...] = (gmid_s[...] + norm_back(back, unit, inverse, gain[0:1, :])).astype(BF)
            small_out[...] = small_s[...]
            small_out[ROW_GAIN : ROW_GAIN + 1, :] = jnp.sum(back * unit, axis=0, keepdims=True)
            small_out[ROW_SHIFT : ROW_SHIFT + 1, :] = jnp.sum(back, axis=0, keepdims=True)

    outs = [
        shape((rows, dim), BF),
        shape((rows, 3 * dim), BF),
        shape((dim, rows), BF),
        shape(small.shape, F32),
        TOKEN,
    ]
    scratch = [
        pltpu.VMEM((dim, rows), BF),
        pltpu.VMEM((HEADS, 1, LEN), F32),
        pltpu.VMEM((HEADS * LEN, LEN), F32),
        pltpu.VMEM((HEADS, LEN, LEN), BF),
        pltpu.VMEM((3, dim, LEN), F32),
        pltpu.VMEM((2, dim, LEN), BF),
    ]
    aliases = {len(ins) - 1: 0} if given else {}
    out = call(kernel, outs, ins, scratch, 0, aliases, "attention_grad", after, ATTENTION_LIMIT, micros=ATTENTION_MICROS)
    return out[0], out[1:4], out[4]


def qkv_grad(section, info, kept, before, after):
    gqkv, normt, small = kept
    dim, rows = normt.shape
    share = dim // GROUPS
    half = 3 * share // 2
    given = [] if before is None else list(before)
    ins = [info, gqkv, normt, small] + given

    def kernel(info, gqkv_s, normt_s, small_s, *refs):
        old = refs[: len(given)]
        bufs = refs[len(given) : len(given) + 4]
        send_a, keep_a, send_b, keep_b = bufs
        (block_s,) = refs[len(given) + 5 :]
        keep_given(info[0] == section, old, bufs)

        @pl.when(info[0] == section)
        def _():
            sums = [
                jnp.sum(gqkv_s[:, c * dim : (c + 1) * dim].astype(F32), axis=0, keepdims=True)
                for c in range(3)
            ]
            tail = jnp.concatenate(sums + [small_s[ROW_OUT:, :]], axis=0).astype(BF)
            send_a[2 * half :, :] = tail
            keep_a[2 * half :, :] = tail
            for c in range(3):
                block_s[c] = mm(normt_s[...], gqkv_s[:, c * dim : (c + 1) * dim]).astype(BF)

            @pl.loop(0, GROUPS)
            def _(shard):
                x, y, base = shard % 2, shard // 2, shard * share
                for c in range(3):
                    row, at, left = 0, c * share, share
                    while left:
                        count = min(left, half - at % half)
                        if at < half:
                            own, bit, keep, send, to = info[1], x, keep_a, send_a, y * half + at
                        else:
                            own, bit, keep, send, to = info[2], y, keep_b, send_b, x * half + at - half
                        lay_out(own, bit, keep, send, block_s, c, base + row, count, to)
                        row, at, left = row + count, at + count, left - count

    scratch = [pltpu.VMEM((3, dim, dim), BF)]
    aliases = {len(ins) - 4 + i: i for i in range(4)} if given else {}
    outs = pair_shapes(2 * half + PAD, dim) + pair_shapes(2 * half, dim) + [TOKEN]
    out = call(kernel, outs, ins, scratch, 0, aliases, "qkv_grad", after, QKV_LIMIT)
    return out[:4], out[4]


STEP = 80


def plus(one, two):
    return (one.astype(F32) + two.astype(F32)).astype(BF)


def add_rows(out, at, one, two, start, count):
    whole = count // STEP * STEP

    @pl.loop(0, whole // STEP)
    def _(i):
        src = pl.ds(pl.multiple_of(start + i * STEP, PAD), STEP)
        dst = pl.ds(pl.multiple_of(at + i * STEP, PAD), STEP)
        out[dst, :] = plus(one[src, :], two[src, :])

    if count > whole:
        src = pl.ds(pl.multiple_of(start + whole, PAD), count - whole)
        out[pl.ds(at + whole, count - whole), :] = plus(one[src, :], two[src, :])


def vmem_call(kernel, outs, ins, name, after, scratch=()):
    return call(kernel, outs, ins, list(scratch), 0, {}, name, after, 8)


def first_sum(info, sets, after):
    dim = sets[0][0].shape[1]
    sizes = [(k.shape[0] // (2 * PAD) * PAD, k.shape[0] % (2 * PAD)) for k in sets[0][::2]]

    def kernel(info, *refs):
        sa, na, sb, nb = refs[4 * len(sets) :]
        for section in range(len(sets)):
            ka, ra, kb, rb = refs[4 * section : 4 * section + 4]
            active = info[0] == section if len(sets) > 1 else info[0] >= 0

            @pl.when(active)
            def _():
                for own, one, two, new, out, (half, extra) in (
                    (info[2], ka, ra, na, sa, sizes[0]),
                    (info[1], kb, rb, nb, sb, sizes[1]),
                ):
                    add_rows(out, 0, one, two, (1 - own) * half, half)
                    add_rows(new, 0, one, two, own * half, half)
                    if extra:
                        tail = plus(one[2 * half :, :], two[2 * half :, :])
                        new[half:, :] = tail
                        out[half:, :] = tail

    outs = [shape((sum(size), dim), BF) for size in sizes for _ in range(2)]
    return vmem_call(kernel, outs, [info] + [a for s in sets for a in s], "first_sum", after)


def second_sum(info, keep_a, recv_a, keep_b, recv_b, after):
    dim = keep_b.shape[1]
    top, rest = keep_a.shape[0], keep_b.shape[0]
    quarters = lax.axis_size("replica") == REPLICAS
    rows = -(-(top + rest) // (PAD * REPLICAS)) * PAD

    def kernel(info, ka, ra, kb, rb, *refs):
        whole = refs[-1]
        add_rows(whole, 0, ka, ra, 0, top)
        add_rows(whole, top, kb, rb, 0, rest)
        for k in range(REPLICAS if quarters else 0):
            owner = (info[3] + k) % REPLICAS

            @pl.loop(0, rows // PAD)
            def _(i):
                src = pl.ds(pl.multiple_of(owner * rows + i * PAD, PAD), PAD)
                refs[k][pl.ds(pl.multiple_of(i * PAD, PAD), PAD), :] = whole[src, :]

    ins = [info, keep_a, recv_a, keep_b, recv_b]
    if quarters:
        outs = [shape((rows, dim), BF)] * REPLICAS
        scratch = [pltpu.VMEM((REPLICAS * rows, dim), BF)]
    else:
        outs, scratch = [shape((top + rest, dim), BF)], []
    return vmem_call(kernel, outs, ins, "second_sum", after, scratch)


def quarter_sum(parts, after):
    rows, dim = parts[0].shape

    def kernel(*refs):
        out = refs[-1]

        @pl.loop(0, rows // PAD)
        def _(i):
            at = pl.ds(pl.multiple_of(i * PAD, PAD), PAD)
            total = refs[0][at, :].astype(F32)
            for ref in refs[1:-1]:
                total = total + ref[at, :].astype(F32)
            out[at, :] = total.astype(BF)

    return vmem_call(kernel, [shape((rows, dim), BF)], list(parts), "quarter_sum", after)[0]


def own_pieces(row, count, width, group):
    share = count * width // GROUPS
    at, pieces = group * share, []
    while at < (group + 1) * share:
        size = min((group + 1) * share - at, width - at % width)
        pieces.append((row + at // width, at % width, size, at - group * share))
        at += size
    return pieces


def finish(info, quarters, kind, after):
    dim = quarters[0].shape[1]
    share = dim // GROUPS
    half = 3 * share // 2
    vectors = ((ROW_QKV, 3), (ROW_OUT, 1), (ROW_UP, 4), (ROW_DOWN, 1))
    if kind == "mlp":
        outs = [shape((dim, dim), F32), shape((share, 4 * dim), F32), shape((share, dim), F32)]
    else:
        outs = [shape((share, 3 * dim), F32)]
    large = len(outs)
    if kind == "qkv":
        outs += [shape((1, count * dim // GROUPS), F32) for _, count in vectors]
        outs += [shape((2, share), F32)] * 2
    rows = quarters[0].shape[0]

    def kernel(info, *refs):
        given, refs = refs[: len(quarters)], refs[len(quarters) :]
        out_h = refs[:large]
        small = refs[large : len(outs)]
        src = refs[len(outs)]
        stage = refs[len(outs) + 1 : -1]
        sems = refs[-1]
        for owner in range(len(quarters)):
            dst, sem = src.at[pl.ds(owner * rows, rows)], sems.at[owner]
            for k in range(len(quarters)):
                here = (info[3] - owner + REPLICAS) % REPLICAS == k

                @pl.when(here if len(quarters) > 1 else info[3] >= 0)
                def _():
                    pltpu.make_async_copy(given[k], dst, sem).start()

        for owner in range(len(quarters)):
            dst, sem = src.at[pl.ds(owner * rows, rows)], sems.at[owner]
            pltpu.make_async_copy(given[0], dst, sem).wait()
        if kind == "mlp":
            stage[0][...] = src[:dim, :].astype(F32)
            for i in range(4):
                block = src[dim + i * share : dim + (i + 1) * share, :].astype(F32)
                stage[1][:, i * dim : (i + 1) * dim] = block
            stage[2][...] = src[dim + 4 * share : dim + 5 * share, :].astype(F32)
        else:
            for i in range(3):
                at, left, to = i * share, share, 0
                while left:
                    count = min(left, half - at % half)
                    row = at if at < half else at + PAD
                    block = src[row : row + count, :].astype(F32)
                    stage[0][to : to + count, i * dim : (i + 1) * dim] = block
                    at, left, to = at + count, left - count, to + count
        copies = [
            pltpu.make_async_copy(s, o, sems.at[REPLICAS + i])
            for i, (s, o) in enumerate(zip(stage, out_h))
        ]
        for copy in copies:
            copy.start()
        if kind == "qkv":
            tail = src[half : half + PAD, :].astype(F32)
            for group in range(GROUPS):

                @pl.when(info[1] + 2 * info[2] == group)
                def _():
                    for out, (row, count) in zip(small, vectors):
                        for r, c, size, at in own_pieces(row, count, dim, group):
                            out[:, at : at + size] = tail[r : r + 1, c : c + size]
                    for out, row in zip(small[4:], (ROW_GAIN, ROW_SHIFT)):
                        out[...] = tail[row : row + 2, group * share : (group + 1) * share]

        for copy in copies:
            copy.wait()

    scratch = [pltpu.VMEM((len(quarters) * rows, dim), BF)] + [vmem_like(o) for o in outs[:large]]
    places = "h" * large + "v" * (len(outs) - large)
    ins = [info] + list(quarters)
    return call(
        kernel, outs, ins, scratch, 8, {}, "finish", after, 14, "s" + "a" * len(quarters), places
    )


def flow(shard, axis, pairs, sections):
    if sections == (0, 1):
        return lax.ppermute(shard, axis, pairs)
    peers = lax.axis_size(axis)
    pairs = [(s * peers + i, s * peers + j) for s in sections for i, j in pairs]
    return lax.ppermute(shard, ("section", axis), pairs)


ACROSS = [(g, g ^ 1) for g in range(GROUPS)]
ALONG = [(g, g ^ 2) for g in range(GROUPS)]
BOTH = (0, 1)


def exchange(a, b, turned, sections):
    ways = (ALONG, ACROSS) if turned else (ACROSS, ALONG)
    return flow(a, "group", ways[0], sections), flow(b, "group", ways[1], sections)


def replica_send(parts):
    if len(parts) == 1:
        return [lax.psum(parts[0], "replica")]
    return [shift(part, k) if k else part for k, part in enumerate(parts)]


def shift(part, by):
    pairs = [(i, (i + by) % REPLICAS) for i in range(REPLICAS)]
    return lax.ppermute(part, "replica", pairs)


def replica_sum(parts, after):
    if len(parts) == 1:
        return parts
    own = quarter_sum(parts, after)
    return [own] + [shift(own, k) for k in range(1, REPLICAS)]


def shards(
    block_input,
    cotangent,
    crop_count,
    mask_count,
    qkv_weight,
    qkv_bias,
    out_weight,
    out_bias,
    up_weight,
    up_bias,
    down_weight,
    down_bias,
    norm_gain,
    norm_shift,
):
    params = (
        qkv_weight[0],
        qkv_bias,
        out_weight[0],
        out_bias,
        up_weight[0],
        up_bias,
        down_weight[0],
        down_bias,
        norm_gain[0],
        norm_shift[0],
    )
    rows, dim = block_input.shape
    tab = jnp.asarray(rotary_tables())
    tab_t = jnp.asarray(rotary_columns())
    group = lax.axis_index("group")
    assert lax.axis_size("group") == GROUPS
    info = jnp.stack([lax.axis_index("section"), group % 2, group // 2, lax.axis_index("replica")])

    def to_other(shard, pairs):
        return lax.ppermute(shard, "section", pairs)

    act, first = forward(0, info, crop_count, block_input, None, params, tab, None)
    arrived = [to_other(first[0], [(0, 1)])]
    act, second = forward(1, info, crop_count, block_input, arrived[0], params, tab, act)
    arrived.append(to_other(second[0], [(0, 1)]))
    act, third = forward(2, info, crop_count, block_input, arrived[1], params, tab, act)
    kept_one, kept_zero = (second, third), (first, second)

    common = (info, crop_count, mask_count)
    one, gmid, small, last = mlp_grad(1, *common, cotangent, kept_one, params, None)
    came_one = exchange(one[0], one[2], False, (1,))
    dx, kept, last = attention_grad(
        1, info, gmid, small, arrived, kept_one, params, tab_t, None, last
    )
    grad_back = to_other(dx, [(1, 0)])
    third, last = qkv_grad(1, info, kept, None, last)
    zero, gmid, small, last = mlp_grad(0, *common, grad_back, kept_zero, params, last)
    came_zero = exchange(zero[0], zero[2], False, (0,))
    dx, kept, last = attention_grad(
        0, info, gmid, small, [block_input], kept_zero, params, tab_t, dx, last
    )
    third, last = qkv_grad(0, info, kept, third, last)
    came = exchange(third[0], third[2], False, BOTH)

    sets = [(s[1], c[0], s[3], c[1]) for s, c in ((zero, came_zero), (one, came_one))]
    first_mlp = first_sum(info, sets, last)
    came_mlp = exchange(first_mlp[0], first_mlp[2], True, BOTH)
    first_qkv = first_sum(info, [(third[1], came[0], third[3], came[1])], first_mlp[1])
    came_qkv = exchange(first_qkv[0], first_qkv[2], True, BOTH)
    mlp = second_sum(info, first_mlp[1], came_mlp[0], first_mlp[3], came_mlp[1], first_qkv[1])
    last = mlp[0]
    mlp = replica_send(mlp)
    qkv = second_sum(info, first_qkv[1], came_qkv[0], first_qkv[3], came_qkv[1], last)
    last = qkv[0]
    qkv = replica_send(qkv)
    mlp = replica_sum(mlp, last)
    qkv = replica_sum(qkv, mlp[0])
    grad_down, grad_up, grad_out = finish(info, mlp, "mlp", qkv[0])
    grad_qkv, *small = finish(info, qkv, "qkv", grad_out)
    qkv_b, out_b, up_b, down_b, gain, shift = small
    return (
        act[None],
        dx[None],
        grad_qkv[None],
        qkv_b,
        grad_out[None],
        out_b,
        grad_up[None],
        up_b,
        grad_down[None],
        down_b,
        gain[None],
        shift[None],
    )


def solution(mesh):
    rows = P(("group", "replica"))
    stack = P("section")
    return jax.shard_map(
        shards,
        mesh=mesh,
        in_specs=(rows,) * 4 + (stack,) * 10,
        out_specs=(
            P("section", ("group", "replica"), None),
            P("section", ("group", "replica"), None),
            P("section", "group", None),
            P("section", "group"),
            P("section", "group", None),
            P("section", "group"),
            P("section", "group", None),
            P("section", "group"),
            P("section", "group", None),
            P("section", "group"),
            P("section", None, "group"),
            P("section", None, "group"),
        ),
        check_vma=False,
    )
```

```python
import jax
import jax.numpy as jnp
import numpy as np
from jax import lax
from jax.experimental import pallas as pl
from jax.experimental.pallas import tpu as pltpu
from jax.sharding import PartitionSpec as P

HEADS = 20
HEAD_DIM = 32
LEN = 256
MASK_MEAN = 38
CROP_DEV = 2
EPSILON = 1e-05
ROTARY_BASE = 10000.0

BF = jnp.bfloat16
F32 = jnp.float32
NN = (((1,), (0,)), ((), ()))
NT = (((1,), (1,)), ((), ()))
TN = (((0,), (0,)), ((), ()))

FIRST_LIMIT, FORWARD_LIMIT, MLP_LIMIT, ATTENTION_LIMIT, QKV_LIMIT = 40, 14, 16, 17, 8
ATTENTION_MICROS = 12
REPLICAS = 4
GROUPS = 4
PAD = 16
ROW_QKV, ROW_OUT, ROW_UP, ROW_DOWN, ROW_GAIN, ROW_SHIFT = 0, 3, 4, 8, 9, 11

ANY = pl.BlockSpec(memory_space=pl.ANY)
HBM = pl.BlockSpec(memory_space=pltpu.HBM)
VMEM = pl.BlockSpec(memory_space=pltpu.VMEM)
SMEM = pl.BlockSpec(memory_space=pltpu.SMEM)


def shape(dims, dtype):
    return jax.ShapeDtypeStruct(dims, dtype)


def mm(left, right, dims=NN):
    return lax.dot_general(left, right, dims, preferred_element_type=F32)


def unit_rows_of(values):
    centred = values - jnp.mean(values, axis=-1, keepdims=True)
    inverse = lax.rsqrt(jnp.mean(centred * centred, axis=-1, keepdims=True) + EPSILON)
    return centred * inverse, inverse


def norm_back(grad, unit, inverse, gain):
    scaled = grad * gain
    return inverse * (
        scaled
        - jnp.mean(scaled, axis=-1, keepdims=True)
        - unit * jnp.mean(scaled * unit, axis=-1, keepdims=True)
    )


def rotary_tables():
    lane = np.arange(128) % HEAD_DIM
    half = HEAD_DIM // 2
    freq = ROTARY_BASE ** (-(lane % half).astype(np.float64) * (2.0 / HEAD_DIM))
    angles = np.arange(LEN)[:, None] * freq[None, :]
    sign = np.where(lane < half, -1.0, 1.0)[None, :]
    return np.stack([np.cos(angles), np.sin(angles) * sign]).astype(np.float32)


def rotary_columns():
    half = HEAD_DIM // 2
    freq = ROTARY_BASE ** (-np.arange(half, dtype=np.float64) * (2.0 / HEAD_DIM))
    angles = freq[:, None] * np.arange(LEN)[None, :]
    return np.stack([np.cos(angles), np.sin(angles)]).astype(np.float32)


def swap_halves(values):
    lane = lax.broadcasted_iota(jnp.int32, values.shape, 1) % HEAD_DIM
    half = HEAD_DIM // 2
    return jnp.where(
        lane < half,
        pltpu.roll(values, 128 - half, axis=1),
        pltpu.roll(values, half, axis=1),
    )


def head_stack(block, per):
    head = lax.broadcasted_iota(jnp.int32, block.shape, 1) // HEAD_DIM
    return jnp.concatenate(
        [jnp.where(head == h, block, jnp.zeros_like(block)) for h in range(per)], axis=0
    )


class Copies:
    def __init__(self, sems):
        self.sems = sems
        self.used = 0
        self.open = []

    def start(self, src, dst):
        copy = pltpu.make_async_copy(src, dst, self.sems.at[self.used])
        self.used += 1
        copy.start()
        return copy

    def save(self, src, dst):
        self.open.append(self.start(src, dst))

    def finish(self):
        for copy in self.open:
            copy.wait()


def call(kernel, outs, ins, scratch, sems, aliases, name, after=None, limit=16, spaces=None, out_spaces=None, micros=0.1):
    count = len(ins)
    places = {"v": VMEM, "h": HBM, "a": ANY, "s": SMEM}
    spaces = spaces or "v" * count
    out_spaces = out_spaces or "v" * len(outs)
    in_specs = [SMEM if a.ndim == 1 else places[p] for a, p in zip(ins, spaces)]
    ins = [pltpu.with_memory_space_constraint(a, pltpu.HBM) if p == "h" else a for a, p in zip(ins, spaces)]
    body = kernel
    if after is not None:
        ins = list(ins) + [after]
        in_specs = in_specs + [ANY]

        def body(*refs):
            kernel(*refs[:count], *refs[count + 1 :])

    outs = [pltpu.HBM(o.shape, o.dtype) if p == "h" else o for o, p in zip(outs, out_spaces)]
    return pl.pallas_call(
        body,
        out_shape=outs,
        in_specs=in_specs,
        out_specs=[places[p] for p in out_spaces],
        scratch_shapes=scratch + ([pltpu.SemaphoreType.DMA((sems,))] if sems else []),
        input_output_aliases=aliases,
        compiler_params=pltpu.CompilerParams(vmem_limit_bytes=limit << 20),
        cost_estimate=pl.CostEstimate(
            flops=int(micros * 1.15e9), bytes_accessed=0, transcendentals=0
        ),
        name=name,
    )(*ins)


TOKEN = jax.ShapeDtypeStruct((8, 128), F32)


def vmem_like(arr):
    return pltpu.VMEM(arr.shape, arr.dtype)


def forward(slot, info, live, own, arrived, params, tab, act, after=None):
    qkvw, qkvb, outw, outb, upw, upb, downw, downb, gain, shift = params
    dim = own.shape[1]
    blocks = dim // 128
    wide = upw.shape[1]
    parts = wide // dim
    per = 128 // HEAD_DIM
    manual = slot == 0
    saved = [
        shape((LEN, dim), BF),
        shape((LEN, 3 * dim), BF),
        shape((HEADS, LEN, LEN), BF),
        shape((dim, LEN), BF),
        shape((LEN, dim), F32),
        shape((LEN, wide), BF),
        shape((LEN, wide), BF),
    ]
    weights = [qkvb, outb, upb, downb, gain, shift, tab, qkvw, outw, upw, downw]
    sources = [own] if slot == 0 else [arrived] if slot == 2 else [own, arrived]
    before = [] if act is None else [act]
    ins = [info, live] + sources + weights + before
    count = len(sources)

    def kernel(info, live, *refs):
        xs = refs[:count]
        given = refs[count : count + 11]
        act_h, *outs = refs[count + 11 + len(before) : count + 19 + len(before)]
        scratch = refs[count + 19 + len(before) :]
        act_s, vt_s, score_s, up_s = scratch[:4]
        sems = scratch[-1]
        y_s, qkv_s, prob_s, mixt_s, mid_s, gp_s, hid_s = outs
        used = scratch[4:-1] if manual else xs[-1:] + given
        qkvb, outb, upb, downb, gain, shift, tab, qkvw, outw, upw, downw = used[1:]
        crop = slot - info[0]

        @pl.when(jnp.logical_and(crop >= 0, crop < CROP_DEV))
        def _():
            copies = Copies(sems)
            heavy = []
            if manual:
                rows = xs[0].at[pl.ds(0, LEN)]
                loads = [copies.start(h, s) for h, s in zip((rows,) + given, used)]
                heavy = loads[8:]
                wait_all(loads[:8])
                x = used[0][...].astype(F32)
            elif slot == 1:
                x = jnp.where(info[0] == 0, xs[0][LEN:, :], xs[1][...]).astype(F32)
            else:
                x = xs[0][...].astype(F32)

            def ready(index):
                if manual:
                    heavy[index].wait()

            unit, _ = unit_rows_of(x)
            normed = (unit * gain[0:1, :] + shift[0:1, :]).astype(BF)
            ready(0)
            third = mm(normed, qkvw[:, 2 * dim :]) + qkvb[:, 2 * dim :]
            low = third.astype(BF)
            qkv_s[:, 2 * dim :] = low
            vt_s[...] = low.T
            for part in range(2):
                third = mm(normed, qkvw[:, part * dim : (part + 1) * dim])
                third = third + qkvb[:, part * dim : (part + 1) * dim]
                for j in range(blocks):
                    b = third[:, 128 * j : 128 * j + 128]
                    b = b * tab[0] + swap_halves(b) * tab[1]
                    if part == 0:
                        b = b * HEAD_DIM**-0.5
                    at = part * dim + 128 * j
                    qkv_s[:, at : at + 128] = b.astype(BF)
            for j in range(blocks):
                q = qkv_s[:, 128 * j : 128 * j + 128]
                k = qkv_s[:, dim + 128 * j : dim + 128 * j + 128]
                score_s[per * LEN * j : per * LEN * (j + 1), :] = mm(head_stack(k, per), q, NT)

            def soft(h, _):
                s = score_s[pl.ds(pl.multiple_of(h * LEN, LEN), LEN), :]
                e = jnp.exp(s - jnp.max(s, axis=0, keepdims=True))
                prob_s[h] = (e * (1.0 / jnp.sum(e, axis=0, keepdims=True))).astype(BF)
                return 0

            lax.fori_loop(0, HEADS, soft, 0, unroll=2)
            for h in range(HEADS):
                at = slice(HEAD_DIM * h, HEAD_DIM * (h + 1))
                mixt_s[at, :] = mm(vt_s[at, :], prob_s[h]).astype(BF)
            ready(1)
            mid = x + mm(mixt_s[...], outw[...], TN) + outb[...]
            mid_s[...] = mid
            unit, _ = unit_rows_of(mid)
            normed = (unit * gain[1:2, :] + shift[1:2, :]).astype(BF)
            ready(2)
            up_s[...] = mm(normed, upw[...])
            for c in range(parts):
                cols = slice(c * dim, (c + 1) * dim)
                u = up_s[:, cols] + upb[:, cols]
                cdf = 0.5 + 0.5 * lax.erf(u * 0.5**0.5)
                hid_s[:, cols] = (u * cdf).astype(BF)
                gp_s[:, cols] = (
                    cdf + u * (jnp.exp(u * u * -0.5) * (2 * np.pi) ** -0.5)
                ).astype(BF)
            ready(3)
            low = (mid_s[...] + downb[...] + mm(hid_s[...], downw[...])).astype(BF)
            y_s[...] = low
            act_s[...] = jnp.where(crop < live[0], low, jnp.zeros_like(low))
            at = pl.multiple_of(crop * LEN, LEN)
            copies.save(act_s, act_h.at[pl.ds(at, LEN)])
            copies.finish()

    outs = [shape(own.shape, BF)] + saved
    scratch = [
        pltpu.VMEM((LEN, dim), BF),
        pltpu.VMEM((dim, LEN), BF),
        pltpu.VMEM((HEADS * LEN, LEN), F32),
        pltpu.VMEM((LEN, wide), F32),
    ]
    if manual:
        scratch += [pltpu.VMEM((LEN, dim), BF)] + [vmem_like(a) for a in weights]
    aliases = {} if act is None else {len(ins) - 1: 0}
    spaces = "ss" + ("h" if manual else "v") * (count + 11) + "h" * len(before)
    out = call(
        kernel,
        outs,
        ins,
        scratch,
        16,
        aliases,
        "layer_forward",
        after,
        FIRST_LIMIT if manual else FORWARD_LIMIT,
        spaces,
        "h" + "v" * 7,
    )
    return out[0], out[1:]


def crop_weight(live, masks, crop, section):
    if section == 0:
        return 1.0
    count = jnp.where(live[0] > crop, masks[crop], 0)
    return jnp.full((1, 1), count, jnp.int32).astype(F32) / MASK_MEAN


def add_row(ref, row, values):
    ref[row : row + 1, :] = ref[row : row + 1, :] + jnp.sum(values, axis=0, keepdims=True)


def lay_out(own, bit, keep, send, block, index, row, count, at):
    src = pl.ds(row if isinstance(row, int) else pl.multiple_of(row, PAD), count)
    dst = pl.ds(at if isinstance(at, int) else pl.multiple_of(at, PAD), count)
    mine = own == bit

    @pl.when(mine)
    def _():
        keep[dst, :] = block[index, src, :]

    @pl.when(jnp.logical_not(mine))
    def _():
        send[dst, :] = block[index, src, :]


def keep_given(active, given, bufs):
    @pl.when(jnp.logical_not(active))
    def _():
        for old, new in zip(given, bufs):
            new[...] = old[...]


def pair_shapes(rows, dim):
    return [shape((rows, dim), BF)] * 2


def joined(refs, cols):
    return jnp.concatenate([r[:, cols] for r in refs], axis=0)


def wait_all(copies):
    for copy in copies:
        copy.wait()


def mlp_grad(section, info, live, masks, g, saved, params, after):
    mixts = [s[3] for s in saved]
    mids, gps, hids = ([s[k] for s in saved] for k in (4, 5, 6))
    upw, downw, gain, shift = params[4], params[6], params[8], params[9]
    rows, dim = g.shape
    wide = upw.shape[1]
    parts = wide // dim
    crops = len(saved)
    share = dim // GROUPS
    ins = [info, live, masks, g, gain, shift, downw, upw] + mids + gps + hids + mixts

    def kernel(info, live, masks, g_s, gain, shift, downw, upw, *refs):
        mid_s, gp_s, hid_s, mixt_s = (refs[i * crops : (i + 1) * crops] for i in range(4))
        refs = refs[4 * crops :]
        send_a, keep_a, send_b, keep_b, gmid_s, small_s = refs[:6]
        gu_s, block_s, low_s, normt_s, back_s = refs[7:]

        @pl.when(info[0] == section)
        def _():
            small_s[...] = jnp.zeros_like(small_s)
            for c in range(crops):
                crop = slice(c * LEN, (c + 1) * LEN)
                grad = g_s[crop, :].astype(F32) * crop_weight(live, masks, c, section)
                low = grad.astype(BF)
                low_s[crop, :] = low
                add_row(small_s, ROW_DOWN, low.astype(F32))
                unit, _ = unit_rows_of(mid_s[c][...])
                normt_s[:, crop] = (unit * gain[1:2, :] + shift[1:2, :]).astype(BF).T
            for c in range(parts):
                cols = slice(c * dim, (c + 1) * dim)
                block_s[c] = mm(joined(hid_s, cols), low_s[...], TN).astype(BF)

            @pl.loop(0, GROUPS * parts)
            def _(i):
                shard, row = i // parts, (i % parts) * share
                at = (shard // 2) * dim + row
                lay_out(info[1], shard % 2, keep_a, send_a, block_s, shard, row, share, at)

            for c in range(parts):
                cols = slice(c * dim, (c + 1) * dim)
                grad_up = mm(low_s[...], downw[cols, :], NT) * joined(gp_s, cols).astype(F32)
                grad_up = grad_up.astype(BF)
                gu_s[:, cols] = grad_up
                small_s[ROW_UP + c : ROW_UP + c + 1, :] = jnp.sum(
                    grad_up.astype(F32), axis=0, keepdims=True
                )
            back_s[...] = mm(gu_s[...], upw[...], NT)
            for c in range(crops):
                crop = slice(c * LEN, (c + 1) * LEN)
                grad = g_s[crop, :].astype(F32) * crop_weight(live, masks, c, section)
                unit, inverse = unit_rows_of(mid_s[c][...])
                back = back_s[crop, :]
                gmid = grad + norm_back(back, unit, inverse, gain[1:2, :])
                gmid_s[crop, :] = gmid
                low = gmid.astype(BF)
                low_s[crop, :] = low
                add_row(small_s, ROW_GAIN + 1, back * unit)
                add_row(small_s, ROW_SHIFT + 1, back)
                add_row(small_s, ROW_OUT, low.astype(F32))
            for c in range(parts):
                block_s[c] = mm(normt_s[...], gu_s[:, c * dim : (c + 1) * dim]).astype(BF)
            mixt = jnp.concatenate([m[...] for m in mixt_s], axis=1)
            block_s[parts] = mm(mixt, low_s[...]).astype(BF)

            @pl.loop(0, GROUPS * (parts + 1))
            def _(i):
                shard, c = i // (parts + 1), i % (parts + 1)
                at = ((shard % 2) * (parts + 1) + c) * share
                lay_out(info[2], shard // 2, keep_b, send_b, block_s, c, shard * share, share, at)

    scratch = [
        pltpu.VMEM((rows, wide), BF),
        pltpu.VMEM((parts + 1, dim, dim), BF),
        pltpu.VMEM((rows, dim), BF),
        pltpu.VMEM((dim, rows), BF),
        pltpu.VMEM((rows, dim), F32),
    ]
    outs = pair_shapes(2 * dim, dim) + pair_shapes(2 * (parts + 1) * share, dim)
    outs += [shape((rows, dim), F32), shape((PAD, dim), F32), TOKEN]
    out = call(kernel, outs, ins, scratch, 0, {}, "mlp_grad", after, MLP_LIMIT, micros=10)
    return out[:4], out[4], out[5], out[6]


def rotate_back(block, tab_t):
    half = HEAD_DIM // 2
    cos, sin = tab_t[0], tab_t[1]
    out = []
    for at in range(0, block.shape[0], HEAD_DIM):
        a, b = block[at : at + half], block[at + half : at + HEAD_DIM]
        out += [a * cos + b * sin, b * cos - a * sin]
    return jnp.concatenate(out, axis=0)


def attention_grad(section, info, gmid, small, xs, saved, params, tab_t, before, after):
    qkvs, probs, mixts = [s[1] for s in saved], [s[2] for s in saved], [s[3] for s in saved]
    qkvw, outw, gain, shift = params[0], params[2], params[8], params[9]
    rows, dim = gmid.shape
    blocks = dim // 128
    per = 128 // HEAD_DIM
    crops = len(saved)
    given = [] if before is None else [before]
    ins = [info, gmid, outw, small, gain, shift, tab_t, qkvw]
    ins += qkvs + probs + mixts + list(xs) + given

    def kernel(info, gmid_s, outw, small_s, gain, shift, tab_t, qkvw, *refs):
        qkv_s, prob_s, mixt_s = (refs[i * crops : (i + 1) * crops] for i in range(3))
        x_s = refs[3 * crops : 3 * crops + len(xs)]
        old = refs[3 * crops + len(xs) : 3 * crops + len(xs) + len(given)]
        refs = refs[3 * crops + len(xs) + len(given) :]
        keep_given(info[0] == section, old, refs[:1])
        dx_s, gqkv_s, normt_s, small_out = refs[:4]
        gmt_s, delta_s, da_s, ds_s, dt_s, kt_s = refs[5:]

        @pl.when(info[0] == section)
        def _():
            low = gmid_s[...].astype(BF)
            gmt_s[...] = mm(outw[...], low, NT).astype(BF)
            for c in range(crops):
                crop = slice(c * LEN, (c + 1) * LEN)
                qkv, prob = qkv_s[c], prob_s[c]
                product = gmt_s[:, crop].astype(F32) * mixt_s[c][...].astype(F32)
                delta_s[...] = jnp.sum(product.reshape(HEADS, HEAD_DIM, LEN), axis=1)[:, None, :]
                kt_s[0] = qkv[:, dim : 2 * dim].T
                kt_s[1] = qkv[:, :dim].T
                for j in range(blocks):
                    v = qkv[:, 2 * dim + 128 * j : 2 * dim + 128 * j + 128]
                    da_s[per * LEN * j : per * LEN * (j + 1), :] = mm(
                        head_stack(v, per), gmt_s[128 * j : 128 * j + 128, crop]
                    )

                def scores(h, _):
                    da = da_s[pl.ds(pl.multiple_of(h * LEN, LEN), LEN), :]
                    ds_s[h] = (prob[h].astype(F32) * (da - delta_s[h])).astype(BF)
                    return 0

                lax.fori_loop(0, HEADS, scores, 0, unroll=2)
                for h in range(HEADS):
                    at = slice(HEAD_DIM * h, HEAD_DIM * (h + 1))
                    dt_s[0, at, :] = mm(kt_s[0, at, :], ds_s[h])
                    dt_s[1, at, :] = mm(kt_s[1, at, :], ds_s[h], NT)
                    dt_s[2, at, :] = mm(gmt_s[at, crop], prob[h], NT)
                dq = rotate_back(dt_s[0] * HEAD_DIM**-0.5, tab_t)
                gqkv_s[crop, :dim] = dq.astype(BF).T
                gqkv_s[crop, dim : 2 * dim] = rotate_back(dt_s[1], tab_t).astype(BF).T
                gqkv_s[crop, 2 * dim :] = dt_s[2].astype(BF).T
            unit, inverse = unit_rows_of(joined(x_s, slice(None)).astype(F32))
            normt_s[...] = (unit * gain[0:1, :] + shift[0:1, :]).astype(BF).T
            back = mm(gqkv_s[...], qkvw[...], NT)
            dx_s[...] = (gmid_s[...] + norm_back(back, unit, inverse, gain[0:1, :])).astype(BF)
            small_out[...] = small_s[...]
            small_out[ROW_GAIN : ROW_GAIN + 1, :] = jnp.sum(back * unit, axis=0, keepdims=True)
            small_out[ROW_SHIFT : ROW_SHIFT + 1, :] = jnp.sum(back, axis=0, keepdims=True)

    outs = [
        shape((rows, dim), BF),
        shape((rows, 3 * dim), BF),
        shape((dim, rows), BF),
        shape(small.shape, F32),
        TOKEN,
    ]
    scratch = [
        pltpu.VMEM((dim, rows), BF),
        pltpu.VMEM((HEADS, 1, LEN), F32),
        pltpu.VMEM((HEADS * LEN, LEN), F32),
        pltpu.VMEM((HEADS, LEN, LEN), BF),
        pltpu.VMEM((3, dim, LEN), F32),
        pltpu.VMEM((2, dim, LEN), BF),
    ]
    aliases = {len(ins) - 1: 0} if given else {}
    out = call(kernel, outs, ins, scratch, 0, aliases, "attention_grad", after, ATTENTION_LIMIT, micros=ATTENTION_MICROS)
    return out[0], out[1:4], out[4]


def qkv_grad(section, info, kept, before, after):
    gqkv, normt, small = kept
    dim, rows = normt.shape
    share = dim // GROUPS
    half = 3 * share // 2
    given = [] if before is None else list(before)
    ins = [info, gqkv, normt, small] + given

    def kernel(info, gqkv_s, normt_s, small_s, *refs):
        old = refs[: len(given)]
        bufs = refs[len(given) : len(given) + 4]
        send_a, keep_a, send_b, keep_b = bufs
        (block_s,) = refs[len(given) + 5 :]
        keep_given(info[0] == section, old, bufs)

        @pl.when(info[0] == section)
        def _():
            sums = [
                jnp.sum(gqkv_s[:, c * dim : (c + 1) * dim].astype(F32), axis=0, keepdims=True)
                for c in range(3)
            ]
            tail = jnp.concatenate(sums + [small_s[ROW_OUT:, :]], axis=0).astype(BF)
            send_a[2 * half :, :] = tail
            keep_a[2 * half :, :] = tail
            for c in range(3):
                block_s[c] = mm(normt_s[...], gqkv_s[:, c * dim : (c + 1) * dim]).astype(BF)

            @pl.loop(0, GROUPS)
            def _(shard):
                x, y, base = shard % 2, shard // 2, shard * share
                for c in range(3):
                    row, at, left = 0, c * share, share
                    while left:
                        count = min(left, half - at % half)
                        if at < half:
                            own, bit, keep, send, to = info[1], x, keep_a, send_a, y * half + at
                        else:
                            own, bit, keep, send, to = info[2], y, keep_b, send_b, x * half + at - half
                        lay_out(own, bit, keep, send, block_s, c, base + row, count, to)
                        row, at, left = row + count, at + count, left - count

    scratch = [pltpu.VMEM((3, dim, dim), BF)]
    aliases = {len(ins) - 4 + i: i for i in range(4)} if given else {}
    outs = pair_shapes(2 * half + PAD, dim) + pair_shapes(2 * half, dim) + [TOKEN]
    out = call(kernel, outs, ins, scratch, 0, aliases, "qkv_grad", after, QKV_LIMIT)
    return out[:4], out[4]


STEP = 80


def plus(one, two):
    return (one.astype(F32) + two.astype(F32)).astype(BF)


def add_rows(out, at, one, two, start, count):
    whole = count // STEP * STEP

    @pl.loop(0, whole // STEP)
    def _(i):
        src = pl.ds(pl.multiple_of(start + i * STEP, PAD), STEP)
        dst = pl.ds(pl.multiple_of(at + i * STEP, PAD), STEP)
        out[dst, :] = plus(one[src, :], two[src, :])

    if count > whole:
        src = pl.ds(pl.multiple_of(start + whole, PAD), count - whole)
        out[pl.ds(at + whole, count - whole), :] = plus(one[src, :], two[src, :])


def vmem_call(kernel, outs, ins, name, after, scratch=()):
    return call(kernel, outs, ins, list(scratch), 0, {}, name, after, 8)


def copy_rows(out, at, src, start, count):
    whole = count // STEP * STEP

    @pl.loop(0, whole // STEP)
    def _(i):
        lines = pl.ds(pl.multiple_of(start + i * STEP, PAD), STEP)
        out[pl.ds(pl.multiple_of(at + i * STEP, PAD), STEP), :] = src[lines, :]

    if count > whole:
        lines = pl.ds(pl.multiple_of(start + whole, PAD), count - whole)
        out[pl.ds(pl.multiple_of(at + whole, PAD), count - whole), :] = src[lines, :]


def first_sum(info, sets, third, after):
    dim = third[0].shape[1]
    halves = [k.shape[0] // 2 for k in sets[0][::2]]
    riders = (third[2], third[0])

    def kernel(info, *refs):
        given = refs[4 * len(sets) : 4 * len(sets) + 2]
        sa, na, sb, nb = refs[4 * len(sets) + 2 :]
        for out, half, rider in ((sa, halves[0], given[0]), (sb, halves[1], given[1])):
            copy_rows(out, half, rider, 0, rider.shape[0])
        for section in range(len(sets)):
            ka, ra, kb, rb = refs[4 * section : 4 * section + 4]

            @pl.when(info[0] == section)
            def _():
                for own, one, two, new, out, half in (
                    (info[2], ka, ra, na, sa, halves[0]),
                    (info[1], kb, rb, nb, sb, halves[1]),
                ):
                    add_rows(out, 0, one, two, (1 - own) * half, half)
                    add_rows(new, 0, one, two, own * half, half)

    outs = []
    for half, rider in zip(halves, riders):
        outs += [shape((half + rider.shape[0], dim), BF), shape((half, dim), BF)]
    ins = [info] + [a for s in sets for a in s] + list(riders)
    return vmem_call(kernel, outs, ins, "first_sum", after)


def padded(rows):
    return -(-rows // (PAD * REPLICAS)) * PAD * REPLICAS


def split_shapes(rows, dim):
    if lax.axis_size("replica") == REPLICAS:
        return [shape((padded(rows) // 2, dim), BF)] * 2
    return [shape((rows, dim), BF)]


def sum_pieces(info, outs, pieces, rows):
    half = padded(rows) // 2
    if len(outs) == 1:
        for at, one, two, start_one, start_two, count in pieces:
            outs[0][at : at + count, :] = plus(
                one[start_one : start_one + count, :], two[start_two : start_two + count, :]
            )
        return
    for own in range(2):

        @pl.when(info[3] % 2 == own)
        def _():
            for at, one, two, start_one, start_two, count in pieces:
                for out, low in ((outs[1], own * half), (outs[0], (1 - own) * half)):
                    first, last = max(at, low), min(at + count, low + half)
                    if first < last:
                        add_shifted(
                            out, first - low, one, start_one + first - at, two, start_two + first - at, last - first
                        )


def add_shifted(out, at, one, start_one, two, start_two, count):
    whole = count // STEP * STEP

    @pl.loop(0, whole // STEP)
    def _(i):
        a = pl.ds(pl.multiple_of(start_one + i * STEP, PAD), STEP)
        b = pl.ds(pl.multiple_of(start_two + i * STEP, PAD), STEP)
        out[pl.ds(pl.multiple_of(at + i * STEP, PAD), STEP), :] = plus(one[a, :], two[b, :])

    if count > whole:
        size, done = count - whole, whole
        out[at + done : at + count, :] = plus(
            one[start_one + done : start_one + count, :], two[start_two + done : start_two + count, :]
        )


def middle_sum(info, first, along, across, third, after):
    _, na, _, nb = first
    dim = na.shape[1]
    top, rest = na.shape[0], nb.shape[0]
    half_a, half_b = (third[1].shape[0] - PAD) // 2, third[3].shape[0] // 2
    outs = split_shapes(top + rest, dim)
    count = len(outs)

    def kernel(info, na, nb, along, across, ka, kb, *refs):
        sums, (sa, ma, sb, mb) = refs[:count], refs[count:]
        pieces = [(0, na, along, 0, 0, top), (top, nb, across, 0, 0, rest)]
        sum_pieces(info, sums, pieces, top + rest)
        for own, one, two, base, new, out, half in (
            (info[2], ka, across, rest, ma, sa, half_a),
            (info[1], kb, along, top, mb, sb, half_b),
        ):
            for part in range(2):
                mine = own == part

                @pl.when(mine)
                def _():
                    add_shifted(new, 0, one, part * half, two, base + part * half, half)

                @pl.when(jnp.logical_not(mine))
                def _():
                    add_shifted(out, 0, one, part * half, two, base + part * half, half)

            extra = one.shape[0] - 2 * half
            if extra:
                tail = plus(one[2 * half :, :], two[base + 2 * half : base + 2 * half + extra, :])
                new[half:, :] = tail
                out[half:, :] = tail

    outs = outs + [shape((half_a + PAD, dim), BF)] * 2 + [shape((half_b, dim), BF)] * 2
    ins = [info, na, nb, along, across, third[1], third[3]]
    out = vmem_call(kernel, outs, ins, "middle_sum", after)
    return out[:count], out[count:]


def last_sum(info, kept, came, after):
    (ka, kb), (ra, rb) = kept, came
    dim = ka.shape[1]
    top, rest = ka.shape[0], kb.shape[0]

    def kernel(info, ka, kb, ra, rb, *outs):
        pieces = [(0, ka, ra, 0, 0, top), (top, kb, rb, 0, 0, rest)]
        sum_pieces(info, outs, pieces, top + rest)

    outs = split_shapes(top + rest, dim)
    return vmem_call(kernel, outs, [info, ka, kb, ra, rb], "last_sum", after)


class Pairing:
    def __init__(self, info, parts):
        self.info, self.parts = info, parts
        if self.pairs:
            self.came = self.trade(parts[0], 1)
        else:
            self.parts = [lax.psum(parts[0], "replica")]

    @property
    def pairs(self):
        return len(self.parts) == 2

    def trade(self, part, bit):
        return lax.ppermute(part, "replica", [(r, r ^ bit) for r in range(REPLICAS)])

    def halve(self, after):
        if not self.pairs:
            return after
        half, dim = self.parts[1].shape
        quarter = half // 2

        def kernel(info, one, two, send, keep):
            for own in range(2):

                @pl.when(info[3] // 2 == own)
                def _():
                    add_shifted(keep, 0, one, own * quarter, two, own * quarter, quarter)
                    other = (1 - own) * quarter
                    add_shifted(send, 0, one, other, two, other, quarter)

        ins = [self.info, self.parts[1], self.came]
        send, self.kept = vmem_call(kernel, [shape((quarter, dim), BF)] * 2, ins, "halve", after)
        self.came = self.trade(send, 2)
        return self.kept

    def total(self, after):
        if not self.pairs:
            return after

        def kernel(one, two, out):
            add_rows(out, 0, one, two, 0, one.shape[0])

        outs = [shape(self.kept.shape, BF)]
        self.own = vmem_call(kernel, outs, [self.kept, self.came], "total", after)[0]
        self.came = self.trade(self.own, 2)
        return self.own

    def double(self, after):
        if not self.pairs:
            return after
        quarter, dim = self.own.shape

        def kernel(info, one, two, out):
            copy_rows(out, info[3] // 2 * quarter, one, 0, quarter)
            copy_rows(out, (1 - info[3] // 2) * quarter, two, 0, quarter)

        outs = [shape((2 * quarter, dim), BF)]
        half = vmem_call(kernel, outs, [self.info, self.own, self.came], "double", after)[0]
        self.parts = [half, self.trade(half, 1)]
        return half


def own_pieces(row, count, width, group):
    share = count * width // GROUPS
    at, pieces = group * share, []
    while at < (group + 1) * share:
        size = min((group + 1) * share - at, width - at % width)
        pieces.append((row + at // width, at % width, size, at - group * share))
        at += size
    return pieces


def finish(info, halves, kind, after):
    dim = halves[0].shape[1]
    share = dim // GROUPS
    half = 3 * share // 2
    vectors = ((ROW_QKV, 3), (ROW_OUT, 1), (ROW_UP, 4), (ROW_DOWN, 1))
    if kind == "mlp":
        outs = [shape((dim, dim), F32), shape((share, 4 * dim), F32), shape((share, dim), F32)]
    else:
        outs = [shape((share, 3 * dim), F32)]
    large = len(outs)
    if kind == "qkv":
        outs += [shape((1, count * dim // GROUPS), F32) for _, count in vectors]
        outs += [shape((2, share), F32)] * 2
    rows = halves[0].shape[0]

    def kernel(info, *refs):
        given, refs = refs[: len(halves)], refs[len(halves) :]
        out_h = refs[:large]
        small = refs[large : len(outs)]
        src = refs[len(outs)]
        stage = refs[len(outs) + 1 : -1]
        sems = refs[-1]
        for low in range(len(halves)):
            here = info[3] % 2 == low if len(halves) > 1 else info[3] >= 0

            @pl.when(here)
            def _():
                for k, part in enumerate(given):
                    at = (low + k) % len(halves) * rows
                    pltpu.make_async_copy(part, src.at[pl.ds(at, rows)], sems.at[k]).start()

        for k, part in enumerate(given):
            pltpu.make_async_copy(part, src.at[pl.ds(0, rows)], sems.at[k]).wait()
        if kind == "mlp":
            stage[0][...] = src[:dim, :].astype(F32)
            for i in range(4):
                block = src[dim + i * share : dim + (i + 1) * share, :].astype(F32)
                stage[1][:, i * dim : (i + 1) * dim] = block
            stage[2][...] = src[dim + 4 * share : dim + 5 * share, :].astype(F32)
        else:
            for i in range(3):
                at, left, to = i * share, share, 0
                while left:
                    count = min(left, half - at % half)
                    row = at if at < half else at + PAD
                    block = src[row : row + count, :].astype(F32)
                    stage[0][to : to + count, i * dim : (i + 1) * dim] = block
                    at, left, to = at + count, left - count, to + count
        copies = [
            pltpu.make_async_copy(s, o, sems.at[REPLICAS + i])
            for i, (s, o) in enumerate(zip(stage, out_h))
        ]
        for copy in copies:
            copy.start()
        if kind == "qkv":
            tail = src[half : half + PAD, :].astype(F32)
            for group in range(GROUPS):

                @pl.when(info[1] + 2 * info[2] == group)
                def _():
                    for out, (row, count) in zip(small, vectors):
                        for r, c, size, at in own_pieces(row, count, dim, group):
                            out[:, at : at + size] = tail[r : r + 1, c : c + size]
                    for out, row in zip(small[4:], (ROW_GAIN, ROW_SHIFT)):
                        out[...] = tail[row : row + 2, group * share : (group + 1) * share]

        for copy in copies:
            copy.wait()

    scratch = [pltpu.VMEM((len(halves) * rows, dim), BF)] + [vmem_like(o) for o in outs[:large]]
    places = "h" * large + "v" * (len(outs) - large)
    ins = [info] + list(halves)
    return call(
        kernel, outs, ins, scratch, 8, {}, "finish", after, 14, "s" + "a" * len(halves), places
    )


def flow(shard, axis, pairs, sections):
    if sections == (0, 1):
        return lax.ppermute(shard, axis, pairs)
    peers = lax.axis_size(axis)
    pairs = [(s * peers + i, s * peers + j) for s in sections for i, j in pairs]
    return lax.ppermute(shard, ("section", axis), pairs)


ACROSS = [(g, g ^ 1) for g in range(GROUPS)]
ALONG = [(g, g ^ 2) for g in range(GROUPS)]
BOTH = (0, 1)


def exchange(a, b, turned, sections):
    ways = (ALONG, ACROSS) if turned else (ACROSS, ALONG)
    return flow(a, "group", ways[0], sections), flow(b, "group", ways[1], sections)


def shards(
    block_input,
    cotangent,
    crop_count,
    mask_count,
    qkv_weight,
    qkv_bias,
    out_weight,
    out_bias,
    up_weight,
    up_bias,
    down_weight,
    down_bias,
    norm_gain,
    norm_shift,
):
    params = (
        qkv_weight[0],
        qkv_bias,
        out_weight[0],
        out_bias,
        up_weight[0],
        up_bias,
        down_weight[0],
        down_bias,
        norm_gain[0],
        norm_shift[0],
    )
    rows, dim = block_input.shape
    tab = jnp.asarray(rotary_tables())
    tab_t = jnp.asarray(rotary_columns())
    group = lax.axis_index("group")
    assert lax.axis_size("group") == GROUPS
    info = jnp.stack([lax.axis_index("section"), group % 2, group // 2, lax.axis_index("replica")])

    def to_other(shard, pairs):
        return lax.ppermute(shard, "section", pairs)

    act, first = forward(0, info, crop_count, block_input, None, params, tab, None)
    arrived = [to_other(first[0], [(0, 1)])]
    act, second = forward(1, info, crop_count, block_input, arrived[0], params, tab, act)
    arrived.append(to_other(second[0], [(0, 1)]))
    act, third = forward(2, info, crop_count, block_input, arrived[1], params, tab, act)
    kept_one, kept_zero = (second, third), (first, second)

    common = (info, crop_count, mask_count)
    one, gmid, small, last = mlp_grad(1, *common, cotangent, kept_one, params, None)
    came_one = exchange(one[0], one[2], False, (1,))
    dx, kept, last = attention_grad(
        1, info, gmid, small, arrived, kept_one, params, tab_t, None, last
    )
    grad_back = to_other(dx, [(1, 0)])
    third, last = qkv_grad(1, info, kept, None, last)
    zero, gmid, small, last = mlp_grad(0, *common, grad_back, kept_zero, params, last)
    came_zero = exchange(zero[0], zero[2], False, (0,))
    dx, kept, last = attention_grad(
        0, info, gmid, small, [block_input], kept_zero, params, tab_t, dx, last
    )
    third, last = qkv_grad(0, info, kept, third, last)
    sets = [(s[1], c[0], s[3], c[1]) for s, c in ((zero, came_zero), (one, came_one))]
    first = first_sum(info, sets, third, last)
    along, across = exchange(first[0], first[2], True, BOTH)
    sums, (send_a, keep_a, send_b, keep_b) = middle_sum(
        info, first, along, across, third, first[1]
    )
    mlp = Pairing(info, sums)
    came = exchange(send_a, send_b, True, BOTH)
    sums = last_sum(info, (keep_a, keep_b), came, keep_a)
    qkv = Pairing(info, sums)
    last = mlp.halve(sums[-1])
    last = qkv.halve(last)
    last = mlp.total(last)
    last = qkv.total(last)
    last = mlp.double(last)
    last = qkv.double(last)
    grad_down, grad_up, grad_out = finish(info, mlp.parts, "mlp", last)
    grad_qkv, *small = finish(info, qkv.parts, "qkv", grad_out)
    qkv_b, out_b, up_b, down_b, gain, shift = small
    return (
        act[None],
        dx[None],
        grad_qkv[None],
        qkv_b,
        grad_out[None],
        out_b,
        grad_up[None],
        up_b,
        grad_down[None],
        down_b,
        gain[None],
        shift[None],
    )


def solution(mesh):
    rows = P(("group", "replica"))
    stack = P("section")
    return jax.shard_map(
        shards,
        mesh=mesh,
        in_specs=(rows,) * 4 + (stack,) * 10,
        out_specs=(
            P("section", ("group", "replica"), None),
            P("section", ("group", "replica"), None),
            P("section", "group", None),
            P("section", "group"),
            P("section", "group", None),
            P("section", "group"),
            P("section", "group", None),
            P("section", "group"),
            P("section", "group", None),
            P("section", "group"),
            P("section", None, "group"),
            P("section", None, "group"),
        ),
        check_vma=False,
    )
```

```python
import jax
import jax.numpy as jnp
import numpy as np
from jax import lax
from jax.experimental import pallas as pl
from jax.experimental.pallas import tpu as pltpu
from jax.sharding import PartitionSpec as P

HEADS = 20
HEAD_DIM = 32
LEN = 256
MASK_MEAN = 38
CROP_DEV = 2
EPSILON = 1e-05
ROTARY_BASE = 10000.0

BF = jnp.bfloat16
F32 = jnp.float32
NN = (((1,), (0,)), ((), ()))
NT = (((1,), (1,)), ((), ()))
TN = (((0,), (0,)), ((), ()))

FIRST_LIMIT, FORWARD_LIMIT, MLP_LIMIT, ATTENTION_LIMIT, QKV_LIMIT = 40, 14, 16, 17, 8
ATTENTION_MICROS = 12
REPLICAS = 4
GROUPS = 4
PAD = 16
ROW_QKV, ROW_OUT, ROW_UP, ROW_DOWN, ROW_GAIN, ROW_SHIFT = 0, 3, 4, 8, 9, 11

ANY = pl.BlockSpec(memory_space=pl.ANY)
HBM = pl.BlockSpec(memory_space=pltpu.HBM)
VMEM = pl.BlockSpec(memory_space=pltpu.VMEM)
SMEM = pl.BlockSpec(memory_space=pltpu.SMEM)


def shape(dims, dtype):
    return jax.ShapeDtypeStruct(dims, dtype)


def mm(left, right, dims=NN):
    return lax.dot_general(left, right, dims, preferred_element_type=F32)


def unit_rows_of(values):
    centred = values - jnp.mean(values, axis=-1, keepdims=True)
    inverse = lax.rsqrt(jnp.mean(centred * centred, axis=-1, keepdims=True) + EPSILON)
    return centred * inverse, inverse


def norm_back(grad, unit, inverse, gain):
    scaled = grad * gain
    return inverse * (
        scaled
        - jnp.mean(scaled, axis=-1, keepdims=True)
        - unit * jnp.mean(scaled * unit, axis=-1, keepdims=True)
    )


def rotary_tables():
    lane = np.arange(128) % HEAD_DIM
    half = HEAD_DIM // 2
    freq = ROTARY_BASE ** (-(lane % half).astype(np.float64) * (2.0 / HEAD_DIM))
    angles = np.arange(LEN)[:, None] * freq[None, :]
    sign = np.where(lane < half, -1.0, 1.0)[None, :]
    return np.stack([np.cos(angles), np.sin(angles) * sign]).astype(np.float32)


def rotary_columns():
    half = HEAD_DIM // 2
    freq = ROTARY_BASE ** (-np.arange(half, dtype=np.float64) * (2.0 / HEAD_DIM))
    angles = freq[:, None] * np.arange(LEN)[None, :]
    return np.stack([np.cos(angles), np.sin(angles)]).astype(np.float32)


def swap_halves(values):
    lane = lax.broadcasted_iota(jnp.int32, values.shape, 1) % HEAD_DIM
    half = HEAD_DIM // 2
    return jnp.where(
        lane < half,
        pltpu.roll(values, 128 - half, axis=1),
        pltpu.roll(values, half, axis=1),
    )


def head_stack(block, per):
    head = lax.broadcasted_iota(jnp.int32, block.shape, 1) // HEAD_DIM
    return jnp.concatenate(
        [jnp.where(head == h, block, jnp.zeros_like(block)) for h in range(per)], axis=0
    )


class Copies:
    def __init__(self, sems):
        self.sems = sems
        self.used = 0
        self.open = []

    def start(self, src, dst):
        copy = pltpu.make_async_copy(src, dst, self.sems.at[self.used])
        self.used += 1
        copy.start()
        return copy

    def save(self, src, dst):
        self.open.append(self.start(src, dst))

    def finish(self):
        for copy in self.open:
            copy.wait()


def call(kernel, outs, ins, scratch, sems, aliases, name, after=None, limit=16, spaces=None, out_spaces=None, micros=0.1):
    count = len(ins)
    places = {"v": VMEM, "h": HBM, "a": ANY, "s": SMEM}
    spaces = spaces or "v" * count
    out_spaces = out_spaces or "v" * len(outs)
    in_specs = [SMEM if a.ndim == 1 else places[p] for a, p in zip(ins, spaces)]
    ins = [pltpu.with_memory_space_constraint(a, pltpu.HBM) if p == "h" else a for a, p in zip(ins, spaces)]
    body = kernel
    if after is not None:
        ins = list(ins) + [after]
        in_specs = in_specs + [ANY]

        def body(*refs):
            kernel(*refs[:count], *refs[count + 1 :])

    outs = [pltpu.HBM(o.shape, o.dtype) if p == "h" else o for o, p in zip(outs, out_spaces)]
    return pl.pallas_call(
        body,
        out_shape=outs,
        in_specs=in_specs,
        out_specs=[places[p] for p in out_spaces],
        scratch_shapes=scratch + ([pltpu.SemaphoreType.DMA((sems,))] if sems else []),
        input_output_aliases=aliases,
        compiler_params=pltpu.CompilerParams(vmem_limit_bytes=limit << 20),
        cost_estimate=pl.CostEstimate(
            flops=int(micros * 1.15e9), bytes_accessed=0, transcendentals=0
        ),
        name=name,
    )(*ins)


TOKEN = jax.ShapeDtypeStruct((8, 128), F32)


def vmem_like(arr):
    return pltpu.VMEM(arr.shape, arr.dtype)


def forward(slot, info, live, own, arrived, params, tab, act, after=None):
    qkvw, qkvb, outw, outb, upw, upb, downw, downb, gain, shift = params
    dim = own.shape[1]
    blocks = dim // 128
    wide = upw.shape[1]
    parts = wide // dim
    per = 128 // HEAD_DIM
    manual = slot == 0
    saved = [
        shape((LEN, dim), BF),
        shape((LEN, 3 * dim), BF),
        shape((HEADS, LEN, LEN), BF),
        shape((dim, LEN), BF),
        shape((LEN, dim), F32),
        shape((LEN, wide), BF),
        shape((LEN, wide), BF),
    ]
    weights = [qkvb, outb, upb, downb, gain, shift, tab, qkvw, outw, upw, downw]
    sources = [own] if slot == 0 else [arrived] if slot == 2 else [own, arrived]
    before = [] if act is None else [act]
    ins = [info, live] + sources + weights + before
    count = len(sources)

    def kernel(info, live, *refs):
        xs = refs[:count]
        given = refs[count : count + 11]
        act_h, *outs = refs[count + 11 + len(before) : count + 19 + len(before)]
        scratch = refs[count + 19 + len(before) :]
        act_s, vt_s, score_s, up_s = scratch[:4]
        sems = scratch[-1]
        y_s, qkv_s, prob_s, mixt_s, mid_s, gp_s, hid_s = outs
        used = scratch[4:-1] if manual else xs[-1:] + given
        qkvb, outb, upb, downb, gain, shift, tab, qkvw, outw, upw, downw = used[1:]
        crop = slot - info[0]

        @pl.when(jnp.logical_and(crop >= 0, crop < CROP_DEV))
        def _():
            copies = Copies(sems)
            heavy = []
            if manual:
                rows = xs[0].at[pl.ds(0, LEN)]
                loads = [copies.start(h, s) for h, s in zip((rows,) + given, used)]
                heavy = loads[8:]
                wait_all(loads[:8])
                x = used[0][...].astype(F32)
            elif slot == 1:
                x = jnp.where(info[0] == 0, xs[0][LEN:, :], xs[1][...]).astype(F32)
            else:
                x = xs[0][...].astype(F32)

            def ready(index):
                if manual:
                    heavy[index].wait()

            unit, _ = unit_rows_of(x)
            normed = (unit * gain[0:1, :] + shift[0:1, :]).astype(BF)
            ready(0)
            third = mm(normed, qkvw[:, 2 * dim :]) + qkvb[:, 2 * dim :]
            low = third.astype(BF)
            qkv_s[:, 2 * dim :] = low
            vt_s[...] = low.T
            for part in range(2):
                third = mm(normed, qkvw[:, part * dim : (part + 1) * dim])
                third = third + qkvb[:, part * dim : (part + 1) * dim]
                for j in range(blocks):
                    b = third[:, 128 * j : 128 * j + 128]
                    b = b * tab[0] + swap_halves(b) * tab[1]
                    if part == 0:
                        b = b * HEAD_DIM**-0.5
                    at = part * dim + 128 * j
                    qkv_s[:, at : at + 128] = b.astype(BF)
            for j in range(blocks):
                q = qkv_s[:, 128 * j : 128 * j + 128]
                k = qkv_s[:, dim + 128 * j : dim + 128 * j + 128]
                score_s[per * LEN * j : per * LEN * (j + 1), :] = mm(head_stack(k, per), q, NT)

            def soft(h, _):
                s = score_s[pl.ds(pl.multiple_of(h * LEN, LEN), LEN), :]
                e = jnp.exp(s - jnp.max(s, axis=0, keepdims=True))
                prob_s[h] = (e * (1.0 / jnp.sum(e, axis=0, keepdims=True))).astype(BF)
                return 0

            lax.fori_loop(0, HEADS, soft, 0, unroll=2)
            for h in range(HEADS):
                at = slice(HEAD_DIM * h, HEAD_DIM * (h + 1))
                mixt_s[at, :] = mm(vt_s[at, :], prob_s[h]).astype(BF)
            ready(1)
            mid = x + mm(mixt_s[...], outw[...], TN) + outb[...]
            mid_s[...] = mid
            unit, _ = unit_rows_of(mid)
            normed = (unit * gain[1:2, :] + shift[1:2, :]).astype(BF)
            ready(2)
            up_s[...] = mm(normed, upw[...])
            for c in range(parts):
                cols = slice(c * dim, (c + 1) * dim)
                u = up_s[:, cols] + upb[:, cols]
                cdf = 0.5 + 0.5 * lax.erf(u * 0.5**0.5)
                hid_s[:, cols] = (u * cdf).astype(BF)
                gp_s[:, cols] = (
                    cdf + u * (jnp.exp(u * u * -0.5) * (2 * np.pi) ** -0.5)
                ).astype(BF)
            ready(3)
            low = (mid_s[...] + downb[...] + mm(hid_s[...], downw[...])).astype(BF)
            y_s[...] = low
            act_s[...] = jnp.where(crop < live[0], low, jnp.zeros_like(low))
            at = pl.multiple_of(crop * LEN, LEN)
            copies.save(act_s, act_h.at[pl.ds(at, LEN)])
            copies.finish()

    outs = [shape(own.shape, BF)] + saved
    scratch = [
        pltpu.VMEM((LEN, dim), BF),
        pltpu.VMEM((dim, LEN), BF),
        pltpu.VMEM((HEADS * LEN, LEN), F32),
        pltpu.VMEM((LEN, wide), F32),
    ]
    if manual:
        scratch += [pltpu.VMEM((LEN, dim), BF)] + [vmem_like(a) for a in weights]
    aliases = {} if act is None else {len(ins) - 1: 0}
    spaces = "ss" + ("h" if manual else "v") * (count + 11) + "h" * len(before)
    out = call(
        kernel,
        outs,
        ins,
        scratch,
        16,
        aliases,
        "layer_forward",
        after,
        FIRST_LIMIT if manual else FORWARD_LIMIT,
        spaces,
        "h" + "v" * 7,
    )
    return out[0], out[1:]


def crop_weight(live, masks, crop, section):
    if section == 0:
        return 1.0
    count = jnp.where(live[0] > crop, masks[crop], 0)
    return jnp.full((1, 1), count, jnp.int32).astype(F32) / MASK_MEAN


def add_row(ref, row, values):
    ref[row : row + 1, :] = ref[row : row + 1, :] + jnp.sum(values, axis=0, keepdims=True)


def lay_out(own, bit, keep, send, block, index, row, count, at):
    src = pl.ds(row if isinstance(row, int) else pl.multiple_of(row, PAD), count)
    dst = pl.ds(at if isinstance(at, int) else pl.multiple_of(at, PAD), count)
    mine = own == bit

    @pl.when(mine)
    def _():
        keep[dst, :] = block[index, src, :]

    @pl.when(jnp.logical_not(mine))
    def _():
        send[dst, :] = block[index, src, :]


def keep_given(active, given, bufs):
    @pl.when(jnp.logical_not(active))
    def _():
        for old, new in zip(given, bufs):
            new[...] = old[...]


def pair_shapes(rows, dim):
    return [shape((rows, dim), BF)] * 2


def joined(refs, cols):
    return jnp.concatenate([r[:, cols] for r in refs], axis=0)


def wait_all(copies):
    for copy in copies:
        copy.wait()


def mlp_grad(section, info, live, masks, g, saved, params, after):
    mixts = [s[3] for s in saved]
    mids, gps, hids = ([s[k] for s in saved] for k in (4, 5, 6))
    upw, downw, gain, shift = params[4], params[6], params[8], params[9]
    rows, dim = g.shape
    wide = upw.shape[1]
    parts = wide // dim
    crops = len(saved)
    share = dim // GROUPS
    ins = [info, live, masks, g, gain, shift, downw, upw] + mids + gps + hids + mixts

    def kernel(info, live, masks, g_s, gain, shift, downw, upw, *refs):
        mid_s, gp_s, hid_s, mixt_s = (refs[i * crops : (i + 1) * crops] for i in range(4))
        refs = refs[4 * crops :]
        send_a, keep_a, send_b, keep_b, gmid_s, small_s = refs[:6]
        gu_s, block_s, low_s, normt_s, back_s = refs[7:]

        @pl.when(info[0] == section)
        def _():
            small_s[...] = jnp.zeros_like(small_s)
            for c in range(crops):
                crop = slice(c * LEN, (c + 1) * LEN)
                grad = g_s[crop, :].astype(F32) * crop_weight(live, masks, c, section)
                low = grad.astype(BF)
                low_s[crop, :] = low
                add_row(small_s, ROW_DOWN, low.astype(F32))
                unit, _ = unit_rows_of(mid_s[c][...])
                normt_s[:, crop] = (unit * gain[1:2, :] + shift[1:2, :]).astype(BF).T
            for c in range(parts):
                cols = slice(c * dim, (c + 1) * dim)
                block_s[c] = mm(joined(hid_s, cols), low_s[...], TN).astype(BF)

            @pl.loop(0, GROUPS * parts)
            def _(i):
                shard, row = i // parts, (i % parts) * share
                at = (shard // 2) * dim + row
                lay_out(info[1], shard % 2, keep_a, send_a, block_s, shard, row, share, at)

            for c in range(parts):
                cols = slice(c * dim, (c + 1) * dim)
                grad_up = mm(low_s[...], downw[cols, :], NT) * joined(gp_s, cols).astype(F32)
                grad_up = grad_up.astype(BF)
                gu_s[:, cols] = grad_up
                small_s[ROW_UP + c : ROW_UP + c + 1, :] = jnp.sum(
                    grad_up.astype(F32), axis=0, keepdims=True
                )
            back_s[...] = mm(gu_s[...], upw[...], NT)
            for c in range(crops):
                crop = slice(c * LEN, (c + 1) * LEN)
                grad = g_s[crop, :].astype(F32) * crop_weight(live, masks, c, section)
                unit, inverse = unit_rows_of(mid_s[c][...])
                back = back_s[crop, :]
                gmid = grad + norm_back(back, unit, inverse, gain[1:2, :])
                gmid_s[crop, :] = gmid
                low = gmid.astype(BF)
                low_s[crop, :] = low
                add_row(small_s, ROW_GAIN + 1, back * unit)
                add_row(small_s, ROW_SHIFT + 1, back)
                add_row(small_s, ROW_OUT, low.astype(F32))
            for c in range(parts):
                block_s[c] = mm(normt_s[...], gu_s[:, c * dim : (c + 1) * dim]).astype(BF)
            mixt = jnp.concatenate([m[...] for m in mixt_s], axis=1)
            block_s[parts] = mm(mixt, low_s[...]).astype(BF)

            @pl.loop(0, GROUPS * (parts + 1))
            def _(i):
                shard, c = i // (parts + 1), i % (parts + 1)
                at = ((shard % 2) * (parts + 1) + c) * share
                lay_out(info[2], shard // 2, keep_b, send_b, block_s, c, shard * share, share, at)

    scratch = [
        pltpu.VMEM((rows, wide), BF),
        pltpu.VMEM((parts + 1, dim, dim), BF),
        pltpu.VMEM((rows, dim), BF),
        pltpu.VMEM((dim, rows), BF),
        pltpu.VMEM((rows, dim), F32),
    ]
    outs = pair_shapes(2 * dim, dim) + pair_shapes(2 * (parts + 1) * share, dim)
    outs += [shape((rows, dim), F32), shape((PAD, dim), F32), TOKEN]
    out = call(kernel, outs, ins, scratch, 0, {}, "mlp_grad", after, MLP_LIMIT, micros=10)
    return out[:4], out[4], out[5], out[6]


def rotate_back(block, tab_t):
    half = HEAD_DIM // 2
    cos, sin = tab_t[0], tab_t[1]
    out = []
    for at in range(0, block.shape[0], HEAD_DIM):
        a, b = block[at : at + half], block[at + half : at + HEAD_DIM]
        out += [a * cos + b * sin, b * cos - a * sin]
    return jnp.concatenate(out, axis=0)


def attention_grad(section, info, gmid, small, xs, saved, params, tab_t, before, after):
    qkvs, probs, mixts = [s[1] for s in saved], [s[2] for s in saved], [s[3] for s in saved]
    qkvw, outw, gain, shift = params[0], params[2], params[8], params[9]
    rows, dim = gmid.shape
    blocks = dim // 128
    per = 128 // HEAD_DIM
    crops = len(saved)
    given = [] if before is None else [before]
    ins = [info, gmid, outw, small, gain, shift, tab_t, qkvw]
    ins += qkvs + probs + mixts + list(xs) + given

    def kernel(info, gmid_s, outw, small_s, gain, shift, tab_t, qkvw, *refs):
        qkv_s, prob_s, mixt_s = (refs[i * crops : (i + 1) * crops] for i in range(3))
        x_s = refs[3 * crops : 3 * crops + len(xs)]
        old = refs[3 * crops + len(xs) : 3 * crops + len(xs) + len(given)]
        refs = refs[3 * crops + len(xs) + len(given) :]
        keep_given(info[0] == section, old, refs[:1])
        dx_s, gqkv_s, normt_s, small_out = refs[:4]
        gmt_s, delta_s, da_s, ds_s, dt_s, kt_s = refs[5:]

        @pl.when(info[0] == section)
        def _():
            low = gmid_s[...].astype(BF)
            gmt_s[...] = mm(outw[...], low, NT).astype(BF)
            for c in range(crops):
                crop = slice(c * LEN, (c + 1) * LEN)
                qkv, prob = qkv_s[c], prob_s[c]
                product = gmt_s[:, crop].astype(F32) * mixt_s[c][...].astype(F32)
                delta_s[...] = jnp.sum(product.reshape(HEADS, HEAD_DIM, LEN), axis=1)[:, None, :]
                kt_s[0] = qkv[:, dim : 2 * dim].T
                kt_s[1] = qkv[:, :dim].T
                for j in range(blocks):
                    v = qkv[:, 2 * dim + 128 * j : 2 * dim + 128 * j + 128]
                    da_s[per * LEN * j : per * LEN * (j + 1), :] = mm(
                        head_stack(v, per), gmt_s[128 * j : 128 * j + 128, crop]
                    )

                def scores(h, _):
                    da = da_s[pl.ds(pl.multiple_of(h * LEN, LEN), LEN), :]
                    ds_s[h] = (prob[h].astype(F32) * (da - delta_s[h])).astype(BF)
                    return 0

                lax.fori_loop(0, HEADS, scores, 0, unroll=2)
                for h in range(HEADS):
                    at = slice(HEAD_DIM * h, HEAD_DIM * (h + 1))
                    dt_s[0, at, :] = mm(kt_s[0, at, :], ds_s[h])
                    dt_s[1, at, :] = mm(kt_s[1, at, :], ds_s[h], NT)
                    dt_s[2, at, :] = mm(gmt_s[at, crop], prob[h], NT)
                dq = rotate_back(dt_s[0] * HEAD_DIM**-0.5, tab_t)
                gqkv_s[crop, :dim] = dq.astype(BF).T
                gqkv_s[crop, dim : 2 * dim] = rotate_back(dt_s[1], tab_t).astype(BF).T
                gqkv_s[crop, 2 * dim :] = dt_s[2].astype(BF).T
            unit, inverse = unit_rows_of(joined(x_s, slice(None)).astype(F32))
            normt_s[...] = (unit * gain[0:1, :] + shift[0:1, :]).astype(BF).T
            back = mm(gqkv_s[...], qkvw[...], NT)
            dx_s[...] = (gmid_s[...] + norm_back(back, unit, inverse, gain[0:1, :])).astype(BF)
            small_out[...] = small_s[...]
            small_out[ROW_GAIN : ROW_GAIN + 1, :] = jnp.sum(back * unit, axis=0, keepdims=True)
            small_out[ROW_SHIFT : ROW_SHIFT + 1, :] = jnp.sum(back, axis=0, keepdims=True)

    outs = [
        shape((rows, dim), BF),
        shape((rows, 3 * dim), BF),
        shape((dim, rows), BF),
        shape(small.shape, F32),
        TOKEN,
    ]
    scratch = [
        pltpu.VMEM((dim, rows), BF),
        pltpu.VMEM((HEADS, 1, LEN), F32),
        pltpu.VMEM((HEADS * LEN, LEN), F32),
        pltpu.VMEM((HEADS, LEN, LEN), BF),
        pltpu.VMEM((3, dim, LEN), F32),
        pltpu.VMEM((2, dim, LEN), BF),
    ]
    aliases = {len(ins) - 1: 0} if given else {}
    out = call(kernel, outs, ins, scratch, 0, aliases, "attention_grad", after, ATTENTION_LIMIT, micros=ATTENTION_MICROS)
    return out[0], out[1:4], out[4]


def qkv_grad(section, info, kept, before, after):
    gqkv, normt, small = kept
    dim, rows = normt.shape
    share = dim // GROUPS
    half = 3 * share // 2
    given = [] if before is None else list(before)
    ins = [info, gqkv, normt, small] + given

    def kernel(info, gqkv_s, normt_s, small_s, *refs):
        old = refs[: len(given)]
        bufs = refs[len(given) : len(given) + 4]
        send_a, keep_a, send_b, keep_b = bufs
        (block_s,) = refs[len(given) + 5 :]
        keep_given(info[0] == section, old, bufs)

        @pl.when(info[0] == section)
        def _():
            sums = [
                jnp.sum(gqkv_s[:, c * dim : (c + 1) * dim].astype(F32), axis=0, keepdims=True)
                for c in range(3)
            ]
            tail = jnp.concatenate(sums + [small_s[ROW_OUT:, :]], axis=0).astype(BF)
            send_a[2 * half :, :] = tail
            keep_a[2 * half :, :] = tail
            for c in range(3):
                block_s[c] = mm(normt_s[...], gqkv_s[:, c * dim : (c + 1) * dim]).astype(BF)

            @pl.loop(0, GROUPS)
            def _(shard):
                x, y, base = shard % 2, shard // 2, shard * share
                for c in range(3):
                    row, at, left = 0, c * share, share
                    while left:
                        count = min(left, half - at % half)
                        if at < half:
                            own, bit, keep, send, to = info[1], x, keep_a, send_a, y * half + at
                        else:
                            own, bit, keep, send, to = info[2], y, keep_b, send_b, x * half + at - half
                        lay_out(own, bit, keep, send, block_s, c, base + row, count, to)
                        row, at, left = row + count, at + count, left - count

    scratch = [pltpu.VMEM((3, dim, dim), BF)]
    aliases = {len(ins) - 4 + i: i for i in range(4)} if given else {}
    outs = pair_shapes(2 * half + PAD, dim) + pair_shapes(2 * half, dim) + [TOKEN]
    out = call(kernel, outs, ins, scratch, 0, aliases, "qkv_grad", after, QKV_LIMIT)
    return out[:4], out[4]


STEP = 80


def plus(one, two):
    return (one.astype(F32) + two.astype(F32)).astype(BF)


def add_rows(out, at, one, two, start, count):
    whole = count // STEP * STEP

    @pl.loop(0, whole // STEP)
    def _(i):
        src = pl.ds(pl.multiple_of(start + i * STEP, PAD), STEP)
        dst = pl.ds(pl.multiple_of(at + i * STEP, PAD), STEP)
        out[dst, :] = plus(one[src, :], two[src, :])

    if count > whole:
        src = pl.ds(pl.multiple_of(start + whole, PAD), count - whole)
        out[pl.ds(at + whole, count - whole), :] = plus(one[src, :], two[src, :])


def vmem_call(kernel, outs, ins, name, after, scratch=()):
    return call(kernel, outs, ins, list(scratch), 0, {}, name, after, 8)


def copy_rows(out, at, src, start, count):
    whole = count // STEP * STEP

    @pl.loop(0, whole // STEP)
    def _(i):
        lines = pl.ds(pl.multiple_of(start + i * STEP, PAD), STEP)
        out[pl.ds(pl.multiple_of(at + i * STEP, PAD), STEP), :] = src[lines, :]

    if count > whole:
        lines = pl.ds(pl.multiple_of(start + whole, PAD), count - whole)
        out[pl.ds(pl.multiple_of(at + whole, PAD), count - whole), :] = src[lines, :]


def first_sum(section, info, held, came, third, after):
    dim = third[0].shape[1]
    halves = [k.shape[0] // 2 for k in (held[1], held[3])]
    riders = (third[2], third[0])

    def kernel(info, ka, ra, kb, rb, *refs):
        given = refs[:2]
        sa, na, sb, nb = refs[2:]

        @pl.when(info[0] == section)
        def _():
            for own, one, two, new, out, half, rider in (
                (info[2], ka, ra, na, sa, halves[0], given[0]),
                (info[1], kb, rb, nb, sb, halves[1], given[1]),
            ):
                add_rows(out, 0, one, two, (1 - own) * half, half)
                add_rows(new, 0, one, two, own * half, half)
                copy_rows(out, half, rider, 0, rider.shape[0])

    outs = []
    for half, rider in zip(halves, riders):
        outs += [shape((half + rider.shape[0], dim), BF), shape((half, dim), BF)]
    ins = [info, held[1], came[0], held[3], came[1]] + list(riders)
    return vmem_call(kernel, outs, ins, "first_sum", after)


def padded(rows):
    return -(-rows // (PAD * REPLICAS)) * PAD * REPLICAS


def split_shapes(rows, dim):
    if lax.axis_size("replica") == REPLICAS:
        return [shape((padded(rows) // 2, dim), BF)] * 2
    return [shape((rows, dim), BF)]


def sum_pieces(info, outs, pieces, rows):
    half = padded(rows) // 2
    if len(outs) == 1:
        for at, one, two, start_one, start_two, count in pieces:
            outs[0][at : at + count, :] = plus(
                one[start_one : start_one + count, :], two[start_two : start_two + count, :]
            )
        return
    for own in range(2):

        @pl.when(info[3] % 2 == own)
        def _():
            for at, one, two, start_one, start_two, count in pieces:
                for out, low in ((outs[1], own * half), (outs[0], (1 - own) * half)):
                    first, last = max(at, low), min(at + count, low + half)
                    if first < last:
                        add_shifted(
                            out, first - low, one, start_one + first - at, two, start_two + first - at, last - first
                        )


def add_shifted(out, at, one, start_one, two, start_two, count):
    whole = count // STEP * STEP

    @pl.loop(0, whole // STEP)
    def _(i):
        a = pl.ds(pl.multiple_of(start_one + i * STEP, PAD), STEP)
        b = pl.ds(pl.multiple_of(start_two + i * STEP, PAD), STEP)
        out[pl.ds(pl.multiple_of(at + i * STEP, PAD), STEP), :] = plus(one[a, :], two[b, :])

    if count > whole:
        a = pl.ds(pl.multiple_of(start_one + whole, PAD), count - whole)
        b = pl.ds(pl.multiple_of(start_two + whole, PAD), count - whole)
        out[pl.ds(pl.multiple_of(at + whole, PAD), count - whole), :] = plus(one[a, :], two[b, :])


def third_sum(info, flows, third, after):
    dim = third[1].shape[1]
    half_a, half_b = (third[1].shape[0] - PAD) // 2, third[3].shape[0] // 2
    top, rest = flows[0][0].shape[0] - 2 * half_b, flows[0][1].shape[0] - 2 * half_a - PAD

    def kernel(info, ka, kb, *refs):
        sa, ma, sb, mb = refs[4:]
        for section in range(2):
            along, across = refs[2 * section : 2 * section + 2]

            @pl.when(info[0] == section)
            def _():
                for own, one, two, base, new, out, half in (
                    (info[2], ka, across, rest, ma, sa, half_a),
                    (info[1], kb, along, top, mb, sb, half_b),
                ):
                    for target, part in ((new, own), (out, 1 - own)):
                        add_shifted(target, 0, one, part * half, two, base + part * half, half)
                    extra = one.shape[0] - 2 * half
                    if extra:
                        low = base + 2 * half
                        tail = plus(one[2 * half :, :], two[low : low + extra, :])
                        new[half:, :] = tail
                        out[half:, :] = tail

    outs = [shape((half_a + PAD, dim), BF)] * 2 + [shape((half_b, dim), BF)] * 2
    ins = [info, third[1], third[3]] + [a for f in flows for a in f]
    return vmem_call(kernel, outs, ins, "third_sum", after)


def last_sum(info, kept, flows, kept_third, came_third, after):
    dim = kept[0][0].shape[1]
    rows = [a.shape[0] for a in kept[0]] + [a.shape[0] for a in kept_third]
    starts = [sum(rows[:i]) for i in range(4)]

    def kernel(info, *refs):
        ka, kb, ra, rb = refs[8:12]
        outs = refs[12:]
        for section in range(2):
            na, nb, along, across = refs[4 * section : 4 * section + 4]

            @pl.when(info[0] == section)
            def _():
                pairs = ((na, along), (nb, across), (ka, ra), (kb, rb))
                pieces = [(at, a, b, 0, 0, n) for at, (a, b), n in zip(starts, pairs, rows)]
                sum_pieces(info, outs, pieces, sum(rows))

    outs = split_shapes(sum(rows), dim)
    ins = [info]
    for k, f in zip(kept, flows):
        ins += list(k) + list(f)
    return vmem_call(kernel, outs, ins + list(kept_third) + list(came_third), "last_sum", after)


class Pairing:
    def __init__(self, info, parts):
        self.info, self.parts = info, parts
        if self.pairs:
            self.came = self.trade(parts[0], 1)
        else:
            self.parts = [lax.psum(parts[0], "replica")]

    @property
    def pairs(self):
        return len(self.parts) == 2

    def trade(self, part, bit):
        return lax.ppermute(part, "replica", [(r, r ^ bit) for r in range(REPLICAS)])

    def halve(self, after):
        if not self.pairs:
            return after
        half, dim = self.parts[1].shape
        quarter = half // 2

        def kernel(info, one, two, send, keep):
            for own in range(2):

                @pl.when(info[3] // 2 == own)
                def _():
                    add_shifted(keep, 0, one, own * quarter, two, own * quarter, quarter)
                    other = (1 - own) * quarter
                    add_shifted(send, 0, one, other, two, other, quarter)

        ins = [self.info, self.parts[1], self.came]
        send, self.kept = vmem_call(kernel, [shape((quarter, dim), BF)] * 2, ins, "halve", after)
        self.came = self.trade(send, 2)
        return self.kept

    def total(self, after):
        if not self.pairs:
            return after

        def kernel(one, two, out):
            add_rows(out, 0, one, two, 0, one.shape[0])

        outs = [shape(self.kept.shape, BF)]
        self.own = vmem_call(kernel, outs, [self.kept, self.came], "total", after)[0]
        self.came = self.trade(self.own, 2)
        return self.own

    def double(self, after):
        if not self.pairs:
            return after
        quarter, dim = self.own.shape

        def kernel(info, one, two, out):
            copy_rows(out, info[3] // 2 * quarter, one, 0, quarter)
            copy_rows(out, (1 - info[3] // 2) * quarter, two, 0, quarter)

        outs = [shape((2 * quarter, dim), BF)]
        half = vmem_call(kernel, outs, [self.info, self.own, self.came], "double", after)[0]
        self.parts = [half, self.trade(half, 1)]
        return half


def own_pieces(row, count, width, group):
    share = count * width // GROUPS
    at, pieces = group * share, []
    while at < (group + 1) * share:
        size = min((group + 1) * share - at, width - at % width)
        pieces.append((row + at // width, at % width, size, at - group * share))
        at += size
    return pieces


def finish(info, halves, after):
    dim = halves[0].shape[1]
    share = dim // GROUPS
    half = 3 * share // 2
    base = dim + 5 * share
    vectors = ((ROW_QKV, 3), (ROW_OUT, 1), (ROW_UP, 4), (ROW_DOWN, 1))
    outs = [
        shape((dim, dim), F32),
        shape((share, 4 * dim), F32),
        shape((share, dim), F32),
        shape((share, 3 * dim), F32),
    ]
    large = len(outs)
    outs += [shape((1, count * dim // GROUPS), F32) for _, count in vectors]
    outs += [shape((2, share), F32)] * 2
    rows = halves[0].shape[0]

    def kernel(info, *refs):
        given, refs = refs[: len(halves)], refs[len(halves) :]
        out_h = refs[:large]
        small = refs[large : len(outs)]
        src = refs[len(outs)]
        stage = refs[len(outs) + 1 : -1]
        sems = refs[-1]
        for low in range(len(halves)):
            here = info[3] % 2 == low if len(halves) > 1 else info[3] >= 0

            @pl.when(here)
            def _():
                for k, part in enumerate(given):
                    at = (low + k) % len(halves) * rows
                    pltpu.make_async_copy(part, src.at[pl.ds(at, rows)], sems.at[k]).start()

        for k, part in enumerate(given):
            pltpu.make_async_copy(part, src.at[pl.ds(0, rows)], sems.at[k]).wait()
        copies = []

        def save(i):
            copy = pltpu.make_async_copy(stage[i], out_h[i], sems.at[2 + i])
            copy.start()
            copies.append(copy)

        stage[0][...] = src[:dim, :].astype(F32)
        save(0)
        for i in range(4):
            block = src[dim + i * share : dim + (i + 1) * share, :].astype(F32)
            stage[1][:, i * dim : (i + 1) * dim] = block
        save(1)
        for i in range(3):
            at, left, to = i * share, share, 0
            while left:
                count = min(left, half - at % half)
                row = base + (at if at < half else at + PAD)
                block = src[row : row + count, :].astype(F32)
                stage[3][to : to + count, i * dim : (i + 1) * dim] = block
                at, left, to = at + count, left - count, to + count
        save(3)
        stage[2][...] = src[dim + 4 * share : base, :].astype(F32)
        save(2)
        tail = src[base + half : base + half + PAD, :].astype(F32)
        for group in range(GROUPS):

            @pl.when(info[1] + 2 * info[2] == group)
            def _():
                for out, (row, count) in zip(small, vectors):
                    for r, c, size, at in own_pieces(row, count, dim, group):
                        out[:, at : at + size] = tail[r : r + 1, c : c + size]
                for out, row in zip(small[4:], (ROW_GAIN, ROW_SHIFT)):
                    out[...] = tail[row : row + 2, group * share : (group + 1) * share]

        for copy in copies:
            copy.wait()

    scratch = [pltpu.VMEM((len(halves) * rows, dim), BF)] + [vmem_like(o) for o in outs[:large]]
    places = "h" * large + "v" * (len(outs) - large)
    ins = [info] + list(halves)
    return call(
        kernel, outs, ins, scratch, 8, {}, "finish", after, 16, "s" + "a" * len(halves), places
    )


def flow(shard, axis, pairs, sections):
    if sections == (0, 1):
        return lax.ppermute(shard, axis, pairs)
    peers = lax.axis_size(axis)
    pairs = [(s * peers + i, s * peers + j) for s in sections for i, j in pairs]
    return lax.ppermute(shard, ("section", axis), pairs)


ACROSS = [(g, g ^ 1) for g in range(GROUPS)]
ALONG = [(g, g ^ 2) for g in range(GROUPS)]
BOTH = (0, 1)


def exchange(a, b, turned, sections):
    ways = (ALONG, ACROSS) if turned else (ACROSS, ALONG)
    return flow(a, "group", ways[0], sections), flow(b, "group", ways[1], sections)


def shards(
    block_input,
    cotangent,
    crop_count,
    mask_count,
    qkv_weight,
    qkv_bias,
    out_weight,
    out_bias,
    up_weight,
    up_bias,
    down_weight,
    down_bias,
    norm_gain,
    norm_shift,
):
    params = (
        qkv_weight[0],
        qkv_bias,
        out_weight[0],
        out_bias,
        up_weight[0],
        up_bias,
        down_weight[0],
        down_bias,
        norm_gain[0],
        norm_shift[0],
    )
    rows, dim = block_input.shape
    tab = jnp.asarray(rotary_tables())
    tab_t = jnp.asarray(rotary_columns())
    group = lax.axis_index("group")
    assert lax.axis_size("group") == GROUPS
    info = jnp.stack([lax.axis_index("section"), group % 2, group // 2, lax.axis_index("replica")])

    def to_other(shard, pairs):
        return lax.ppermute(shard, "section", pairs)

    act, first = forward(0, info, crop_count, block_input, None, params, tab, None)
    arrived = [to_other(first[0], [(0, 1)])]
    act, second = forward(1, info, crop_count, block_input, arrived[0], params, tab, act)
    arrived.append(to_other(second[0], [(0, 1)]))
    act, third = forward(2, info, crop_count, block_input, arrived[1], params, tab, act)
    kept_one, kept_zero = (second, third), (first, second)

    common = (info, crop_count, mask_count)
    one, gmid, small, last = mlp_grad(1, *common, cotangent, kept_one, params, None)
    came = exchange(one[0], one[2], False, (1,))
    dx, kept, last = attention_grad(
        1, info, gmid, small, arrived, kept_one, params, tab_t, None, last
    )
    grad_back = to_other(dx, [(1, 0)])
    third, last = qkv_grad(1, info, kept, None, last)
    one = first_sum(1, info, one, came, third, last)
    came_one = exchange(one[0], one[2], True, (1,))
    zero, gmid, small, last = mlp_grad(0, *common, grad_back, kept_zero, params, one[1])
    came = exchange(zero[0], zero[2], False, (0,))
    dx, kept, last = attention_grad(
        0, info, gmid, small, [block_input], kept_zero, params, tab_t, dx, last
    )
    third, last = qkv_grad(0, info, kept, third, last)
    zero = first_sum(0, info, zero, came, third, last)
    came_zero = exchange(zero[0], zero[2], True, (0,))
    flows = (came_zero, came_one)
    send_a, keep_a, send_b, keep_b = third_sum(info, flows, third, zero[1])
    came = exchange(send_a, send_b, True, BOTH)
    kept = ((zero[1], zero[3]), (one[1], one[3]))
    total = Pairing(info, last_sum(info, kept, flows, (keep_a, keep_b), came, keep_a))
    last = total.halve(None)
    last = total.total(None)
    last = total.double(None)
    grad_down, grad_up, grad_out, grad_qkv, *small = finish(info, total.parts, None)
    qkv_b, out_b, up_b, down_b, gain, shift = small
    return (
        act[None],
        dx[None],
        grad_qkv[None],
        qkv_b,
        grad_out[None],
        out_b,
        grad_up[None],
        up_b,
        grad_down[None],
        down_b,
        gain[None],
        shift[None],
    )


def solution(mesh):
    rows = P(("group", "replica"))
    stack = P("section")
    return jax.shard_map(
        shards,
        mesh=mesh,
        in_specs=(rows,) * 4 + (stack,) * 10,
        out_specs=(
            P("section", ("group", "replica"), None),
            P("section", ("group", "replica"), None),
            P("section", "group", None),
            P("section", "group"),
            P("section", "group", None),
            P("section", "group"),
            P("section", "group", None),
            P("section", "group"),
            P("section", "group", None),
            P("section", "group"),
            P("section", None, "group"),
            P("section", None, "group"),
        ),
        check_vma=False,
    )
```

```python
import jax
import jax.numpy as jnp
import numpy as np
from jax import lax
from jax.experimental import pallas as pl
from jax.experimental.pallas import tpu as pltpu
from jax.sharding import PartitionSpec as P

HEADS = 20
HEAD_DIM = 32
LEN = 256
MASK_MEAN = 38
CROP_DEV = 2
EPSILON = 1e-05
ROTARY_BASE = 10000.0

BF = jnp.bfloat16
F32 = jnp.float32
NN = (((1,), (0,)), ((), ()))
NT = (((1,), (1,)), ((), ()))
TN = (((0,), (0,)), ((), ()))

FIRST_LIMIT, FORWARD_LIMIT, MLP_LIMIT, ATTENTION_LIMIT, QKV_LIMIT = 40, 14, 16, 17, 8
ATTENTION_MICROS = 12
REPLICAS = 4
GROUPS = 4
PAD = 16
ROW_QKV, ROW_OUT, ROW_UP, ROW_DOWN, ROW_GAIN, ROW_SHIFT = 0, 3, 4, 8, 9, 11

ANY = pl.BlockSpec(memory_space=pl.ANY)
HBM = pl.BlockSpec(memory_space=pltpu.HBM)
VMEM = pl.BlockSpec(memory_space=pltpu.VMEM)
SMEM = pl.BlockSpec(memory_space=pltpu.SMEM)


def shape(dims, dtype):
    return jax.ShapeDtypeStruct(dims, dtype)


def mm(left, right, dims=NN):
    return lax.dot_general(left, right, dims, preferred_element_type=F32)


def unit_rows_of(values):
    centred = values - jnp.mean(values, axis=-1, keepdims=True)
    inverse = lax.rsqrt(jnp.mean(centred * centred, axis=-1, keepdims=True) + EPSILON)
    return centred * inverse, inverse


def norm_back(grad, unit, inverse, gain):
    scaled = grad * gain
    return inverse * (
        scaled
        - jnp.mean(scaled, axis=-1, keepdims=True)
        - unit * jnp.mean(scaled * unit, axis=-1, keepdims=True)
    )


def rotary_tables():
    lane = np.arange(128) % HEAD_DIM
    half = HEAD_DIM // 2
    freq = ROTARY_BASE ** (-(lane % half).astype(np.float64) * (2.0 / HEAD_DIM))
    angles = np.arange(LEN)[:, None] * freq[None, :]
    sign = np.where(lane < half, -1.0, 1.0)[None, :]
    return np.stack([np.cos(angles), np.sin(angles) * sign]).astype(np.float32)


def rotary_columns():
    half = HEAD_DIM // 2
    freq = ROTARY_BASE ** (-np.arange(half, dtype=np.float64) * (2.0 / HEAD_DIM))
    angles = freq[:, None] * np.arange(LEN)[None, :]
    return np.stack([np.cos(angles), np.sin(angles)]).astype(np.float32)


def swap_halves(values):
    lane = lax.broadcasted_iota(jnp.int32, values.shape, 1) % HEAD_DIM
    half = HEAD_DIM // 2
    return jnp.where(
        lane < half,
        pltpu.roll(values, 128 - half, axis=1),
        pltpu.roll(values, half, axis=1),
    )


def head_stack(block, per):
    head = lax.broadcasted_iota(jnp.int32, block.shape, 1) // HEAD_DIM
    return jnp.concatenate(
        [jnp.where(head == h, block, jnp.zeros_like(block)) for h in range(per)], axis=0
    )


class Copies:
    def __init__(self, sems):
        self.sems = sems
        self.used = 0
        self.open = []

    def start(self, src, dst):
        copy = pltpu.make_async_copy(src, dst, self.sems.at[self.used])
        self.used += 1
        copy.start()
        return copy

    def save(self, src, dst):
        self.open.append(self.start(src, dst))

    def finish(self):
        for copy in self.open:
            copy.wait()


def call(kernel, outs, ins, scratch, sems, aliases, name, after=None, limit=16, spaces=None, out_spaces=None, micros=0.1):
    count = len(ins)
    places = {"v": VMEM, "h": HBM, "a": ANY, "s": SMEM}
    spaces = spaces or "v" * count
    out_spaces = out_spaces or "v" * len(outs)
    in_specs = [SMEM if a.ndim == 1 else places[p] for a, p in zip(ins, spaces)]
    ins = [pltpu.with_memory_space_constraint(a, pltpu.HBM) if p == "h" else a for a, p in zip(ins, spaces)]
    body = kernel
    if after is not None:
        ins = list(ins) + [after]
        in_specs = in_specs + [ANY]

        def body(*refs):
            kernel(*refs[:count], *refs[count + 1 :])

    outs = [pltpu.HBM(o.shape, o.dtype) if p == "h" else o for o, p in zip(outs, out_spaces)]
    return pl.pallas_call(
        body,
        out_shape=outs,
        in_specs=in_specs,
        out_specs=[places[p] for p in out_spaces],
        scratch_shapes=scratch + ([pltpu.SemaphoreType.DMA((sems,))] if sems else []),
        input_output_aliases=aliases,
        compiler_params=pltpu.CompilerParams(vmem_limit_bytes=limit << 20),
        cost_estimate=pl.CostEstimate(
            flops=int(micros * 1.15e9), bytes_accessed=0, transcendentals=0
        ),
        name=name,
    )(*ins)


TOKEN = jax.ShapeDtypeStruct((8, 128), F32)


def vmem_like(arr):
    return pltpu.VMEM(arr.shape, arr.dtype)


def forward(slot, info, live, own, arrived, params, tab, act, after=None):
    qkvw, qkvb, outw, outb, upw, upb, downw, downb, gain, shift = params
    dim = own.shape[1]
    blocks = dim // 128
    wide = upw.shape[1]
    parts = wide // dim
    per = 128 // HEAD_DIM
    manual = slot == 0
    saved = [
        shape((LEN, dim), BF),
        shape((LEN, 3 * dim), BF),
        shape((HEADS, LEN, LEN), BF),
        shape((dim, LEN), BF),
        shape((LEN, dim), F32),
        shape((LEN, wide), BF),
        shape((LEN, wide), BF),
    ]
    weights = [qkvb, outb, upb, downb, gain, shift, tab, qkvw, outw, upw, downw]
    sources = [own] if slot == 0 else [arrived] if slot == 2 else [own, arrived]
    before = [] if act is None else [act]
    ins = [info, live] + sources + weights + before
    count = len(sources)

    def kernel(info, live, *refs):
        xs = refs[:count]
        given = refs[count : count + 11]
        act_h, *outs = refs[count + 11 + len(before) : count + 19 + len(before)]
        scratch = refs[count + 19 + len(before) :]
        act_s, vt_s, score_s, up_s = scratch[:4]
        sems = scratch[-1]
        y_s, qkv_s, prob_s, mixt_s, mid_s, gp_s, hid_s = outs
        used = scratch[4:-1] if manual else xs[-1:] + given
        qkvb, outb, upb, downb, gain, shift, tab, qkvw, outw, upw, downw = used[1:]
        crop = slot - info[0]

        @pl.when(jnp.logical_and(crop >= 0, crop < CROP_DEV))
        def _():
            copies = Copies(sems)
            heavy = []
            if manual:
                rows = xs[0].at[pl.ds(0, LEN)]
                loads = [copies.start(h, s) for h, s in zip((rows,) + given, used)]
                heavy = loads[8:]
                wait_all(loads[:8])
                x = used[0][...].astype(F32)
            elif slot == 1:
                x = jnp.where(info[0] == 0, xs[0][LEN:, :], xs[1][...]).astype(F32)
            else:
                x = xs[0][...].astype(F32)

            def ready(index):
                if manual:
                    heavy[index].wait()

            unit, _ = unit_rows_of(x)
            normed = (unit * gain[0:1, :] + shift[0:1, :]).astype(BF)
            ready(0)
            third = mm(normed, qkvw[:, 2 * dim :]) + qkvb[:, 2 * dim :]
            low = third.astype(BF)
            qkv_s[:, 2 * dim :] = low
            vt_s[...] = low.T
            for part in range(2):
                third = mm(normed, qkvw[:, part * dim : (part + 1) * dim])
                third = third + qkvb[:, part * dim : (part + 1) * dim]
                for j in range(blocks):
                    b = third[:, 128 * j : 128 * j + 128]
                    b = b * tab[0] + swap_halves(b) * tab[1]
                    if part == 0:
                        b = b * HEAD_DIM**-0.5
                    at = part * dim + 128 * j
                    qkv_s[:, at : at + 128] = b.astype(BF)
            for j in range(blocks):
                q = qkv_s[:, 128 * j : 128 * j + 128]
                k = qkv_s[:, dim + 128 * j : dim + 128 * j + 128]
                score_s[per * LEN * j : per * LEN * (j + 1), :] = mm(head_stack(k, per), q, NT)

            def soft(h, _):
                s = score_s[pl.ds(pl.multiple_of(h * LEN, LEN), LEN), :]
                e = jnp.exp(s - jnp.max(s, axis=0, keepdims=True))
                prob_s[h] = (e * (1.0 / jnp.sum(e, axis=0, keepdims=True))).astype(BF)
                return 0

            lax.fori_loop(0, HEADS, soft, 0, unroll=2)
            for h in range(HEADS):
                at = slice(HEAD_DIM * h, HEAD_DIM * (h + 1))
                mixt_s[at, :] = mm(vt_s[at, :], prob_s[h]).astype(BF)
            ready(1)
            mid = x + mm(mixt_s[...], outw[...], TN) + outb[...]
            mid_s[...] = mid
            unit, _ = unit_rows_of(mid)
            normed = (unit * gain[1:2, :] + shift[1:2, :]).astype(BF)
            ready(2)
            up_s[...] = mm(normed, upw[...])
            for c in range(parts):
                cols = slice(c * dim, (c + 1) * dim)
                u = up_s[:, cols] + upb[:, cols]
                cdf = 0.5 + 0.5 * lax.erf(u * 0.5**0.5)
                hid_s[:, cols] = (u * cdf).astype(BF)
                gp_s[:, cols] = (
                    cdf + u * (jnp.exp(u * u * -0.5) * (2 * np.pi) ** -0.5)
                ).astype(BF)
            ready(3)
            low = (mid_s[...] + downb[...] + mm(hid_s[...], downw[...])).astype(BF)
            y_s[...] = low
            act_s[...] = jnp.where(crop < live[0], low, jnp.zeros_like(low))
            at = pl.multiple_of(crop * LEN, LEN)
            copies.save(act_s, act_h.at[pl.ds(at, LEN)])
            copies.finish()

    outs = [shape(own.shape, BF)] + saved
    scratch = [
        pltpu.VMEM((LEN, dim), BF),
        pltpu.VMEM((dim, LEN), BF),
        pltpu.VMEM((HEADS * LEN, LEN), F32),
        pltpu.VMEM((LEN, wide), F32),
    ]
    if manual:
        scratch += [pltpu.VMEM((LEN, dim), BF)] + [vmem_like(a) for a in weights]
    aliases = {} if act is None else {len(ins) - 1: 0}
    spaces = "ss" + ("h" if manual else "v") * (count + 11) + "h" * len(before)
    out = call(
        kernel,
        outs,
        ins,
        scratch,
        16,
        aliases,
        "layer_forward",
        after,
        FIRST_LIMIT if manual else FORWARD_LIMIT,
        spaces,
        "h" + "v" * 7,
    )
    return out[0], out[1:]


def crop_weight(live, masks, crop, section):
    if section == 0:
        return 1.0
    count = jnp.where(live[0] > crop, masks[crop], 0)
    return jnp.full((1, 1), count, jnp.int32).astype(F32) / MASK_MEAN


def add_row(ref, row, values):
    ref[row : row + 1, :] = ref[row : row + 1, :] + jnp.sum(values, axis=0, keepdims=True)


def lay_out(own, bit, keep, send, block, index, row, count, at):
    src = pl.ds(row if isinstance(row, int) else pl.multiple_of(row, PAD), count)
    dst = pl.ds(at if isinstance(at, int) else pl.multiple_of(at, PAD), count)
    mine = own == bit

    @pl.when(mine)
    def _():
        keep[dst, :] = block[index, src, :]

    @pl.when(jnp.logical_not(mine))
    def _():
        send[dst, :] = block[index, src, :]


def keep_given(active, given, bufs):
    @pl.when(jnp.logical_not(active))
    def _():
        for old, new in zip(given, bufs):
            new[...] = old[...]


def pair_shapes(rows, dim):
    return [shape((rows, dim), BF)] * 2


def joined(refs, cols):
    return jnp.concatenate([r[:, cols] for r in refs], axis=0)


def wait_all(copies):
    for copy in copies:
        copy.wait()


def mlp_grad(section, info, live, masks, g, saved, params, after):
    mixts = [s[3] for s in saved]
    mids, gps, hids = ([s[k] for s in saved] for k in (4, 5, 6))
    upw, downw, gain, shift = params[4], params[6], params[8], params[9]
    rows, dim = g.shape
    wide = upw.shape[1]
    parts = wide // dim
    crops = len(saved)
    share = dim // GROUPS
    ins = [info, live, masks, g, gain, shift, downw, upw] + mids + gps + hids + mixts

    def kernel(info, live, masks, g_s, gain, shift, downw, upw, *refs):
        mid_s, gp_s, hid_s, mixt_s = (refs[i * crops : (i + 1) * crops] for i in range(4))
        refs = refs[4 * crops :]
        send_a, keep_a, send_b, keep_b, gmid_s, small_s = refs[:6]
        gu_s, block_s, low_s, normt_s, back_s = refs[7:]

        @pl.when(info[0] == section)
        def _():
            small_s[...] = jnp.zeros_like(small_s)
            for c in range(crops):
                crop = slice(c * LEN, (c + 1) * LEN)
                grad = g_s[crop, :].astype(F32) * crop_weight(live, masks, c, section)
                low = grad.astype(BF)
                low_s[crop, :] = low
                add_row(small_s, ROW_DOWN, low.astype(F32))
                unit, _ = unit_rows_of(mid_s[c][...])
                normt_s[:, crop] = (unit * gain[1:2, :] + shift[1:2, :]).astype(BF).T
            for c in range(parts):
                cols = slice(c * dim, (c + 1) * dim)
                block_s[c] = mm(joined(hid_s, cols), low_s[...], TN).astype(BF)

            @pl.loop(0, GROUPS * parts)
            def _(i):
                shard, row = i // parts, (i % parts) * share
                at = (shard // 2) * dim + row
                lay_out(info[1], shard % 2, keep_a, send_a, block_s, shard, row, share, at)

            for c in range(parts):
                cols = slice(c * dim, (c + 1) * dim)
                grad_up = mm(low_s[...], downw[cols, :], NT) * joined(gp_s, cols).astype(F32)
                grad_up = grad_up.astype(BF)
                gu_s[:, cols] = grad_up
                small_s[ROW_UP + c : ROW_UP + c + 1, :] = jnp.sum(
                    grad_up.astype(F32), axis=0, keepdims=True
                )
            back_s[...] = mm(gu_s[...], upw[...], NT)
            for c in range(crops):
                crop = slice(c * LEN, (c + 1) * LEN)
                grad = g_s[crop, :].astype(F32) * crop_weight(live, masks, c, section)
                unit, inverse = unit_rows_of(mid_s[c][...])
                back = back_s[crop, :]
                gmid = grad + norm_back(back, unit, inverse, gain[1:2, :])
                gmid_s[crop, :] = gmid
                low = gmid.astype(BF)
                low_s[crop, :] = low
                add_row(small_s, ROW_GAIN + 1, back * unit)
                add_row(small_s, ROW_SHIFT + 1, back)
                add_row(small_s, ROW_OUT, low.astype(F32))
            for c in range(parts):
                block_s[c] = mm(normt_s[...], gu_s[:, c * dim : (c + 1) * dim]).astype(BF)
            mixt = jnp.concatenate([m[...] for m in mixt_s], axis=1)
            block_s[parts] = mm(mixt, low_s[...]).astype(BF)

            @pl.loop(0, GROUPS * (parts + 1))
            def _(i):
                shard, c = i // (parts + 1), i % (parts + 1)
                at = ((shard % 2) * (parts + 1) + c) * share
                lay_out(info[2], shard // 2, keep_b, send_b, block_s, c, shard * share, share, at)

    scratch = [
        pltpu.VMEM((rows, wide), BF),
        pltpu.VMEM((parts + 1, dim, dim), BF),
        pltpu.VMEM((rows, dim), BF),
        pltpu.VMEM((dim, rows), BF),
        pltpu.VMEM((rows, dim), F32),
    ]
    outs = pair_shapes(2 * dim, dim) + pair_shapes(2 * (parts + 1) * share, dim)
    outs += [shape((rows, dim), F32), shape((PAD, dim), F32), TOKEN]
    out = call(kernel, outs, ins, scratch, 0, {}, "mlp_grad", after, MLP_LIMIT, micros=10)
    return out[:4], out[4], out[5], out[6]


def rotate_back(block, tab_t):
    half = HEAD_DIM // 2
    cos, sin = tab_t[0], tab_t[1]
    out = []
    for at in range(0, block.shape[0], HEAD_DIM):
        a, b = block[at : at + half], block[at + half : at + HEAD_DIM]
        out += [a * cos + b * sin, b * cos - a * sin]
    return jnp.concatenate(out, axis=0)


def attention_grad(section, info, gmid, small, xs, saved, params, tab_t, before, after):
    qkvs, probs, mixts = [s[1] for s in saved], [s[2] for s in saved], [s[3] for s in saved]
    qkvw, outw, gain, shift = params[0], params[2], params[8], params[9]
    rows, dim = gmid.shape
    blocks = dim // 128
    per = 128 // HEAD_DIM
    crops = len(saved)
    given = [] if before is None else [before]
    ins = [info, gmid, outw, small, gain, shift, tab_t, qkvw]
    ins += qkvs + probs + mixts + list(xs) + given

    def kernel(info, gmid_s, outw, small_s, gain, shift, tab_t, qkvw, *refs):
        qkv_s, prob_s, mixt_s = (refs[i * crops : (i + 1) * crops] for i in range(3))
        x_s = refs[3 * crops : 3 * crops + len(xs)]
        old = refs[3 * crops + len(xs) : 3 * crops + len(xs) + len(given)]
        refs = refs[3 * crops + len(xs) + len(given) :]
        keep_given(info[0] == section, old, refs[:1])
        dx_s, gqkv_s, normt_s, small_out = refs[:4]
        gmt_s, delta_s, da_s, ds_s, dt_s, kt_s = refs[5:]

        @pl.when(info[0] == section)
        def _():
            low = gmid_s[...].astype(BF)
            gmt_s[...] = mm(outw[...], low, NT).astype(BF)
            for c in range(crops):
                crop = slice(c * LEN, (c + 1) * LEN)
                qkv, prob = qkv_s[c], prob_s[c]
                product = gmt_s[:, crop].astype(F32) * mixt_s[c][...].astype(F32)
                delta_s[...] = jnp.sum(product.reshape(HEADS, HEAD_DIM, LEN), axis=1)[:, None, :]
                kt_s[0] = qkv[:, dim : 2 * dim].T
                kt_s[1] = qkv[:, :dim].T
                for j in range(blocks):
                    v = qkv[:, 2 * dim + 128 * j : 2 * dim + 128 * j + 128]
                    da_s[per * LEN * j : per * LEN * (j + 1), :] = mm(
                        head_stack(v, per), gmt_s[128 * j : 128 * j + 128, crop]
                    )

                def scores(h, _):
                    da = da_s[pl.ds(pl.multiple_of(h * LEN, LEN), LEN), :]
                    ds_s[h] = (prob[h].astype(F32) * (da - delta_s[h])).astype(BF)
                    return 0

                lax.fori_loop(0, HEADS, scores, 0, unroll=2)
                for h in range(HEADS):
                    at = slice(HEAD_DIM * h, HEAD_DIM * (h + 1))
                    dt_s[0, at, :] = mm(kt_s[0, at, :], ds_s[h])
                    dt_s[1, at, :] = mm(kt_s[1, at, :], ds_s[h], NT)
                    dt_s[2, at, :] = mm(gmt_s[at, crop], prob[h], NT)
                dq = rotate_back(dt_s[0] * HEAD_DIM**-0.5, tab_t)
                gqkv_s[crop, :dim] = dq.astype(BF).T
                gqkv_s[crop, dim : 2 * dim] = rotate_back(dt_s[1], tab_t).astype(BF).T
                gqkv_s[crop, 2 * dim :] = dt_s[2].astype(BF).T
            unit, inverse = unit_rows_of(joined(x_s, slice(None)).astype(F32))
            normt_s[...] = (unit * gain[0:1, :] + shift[0:1, :]).astype(BF).T
            back = mm(gqkv_s[...], qkvw[...], NT)
            dx_s[...] = (gmid_s[...] + norm_back(back, unit, inverse, gain[0:1, :])).astype(BF)
            small_out[...] = small_s[...]
            small_out[ROW_GAIN : ROW_GAIN + 1, :] = jnp.sum(back * unit, axis=0, keepdims=True)
            small_out[ROW_SHIFT : ROW_SHIFT + 1, :] = jnp.sum(back, axis=0, keepdims=True)

    outs = [
        shape((rows, dim), BF),
        shape((rows, 3 * dim), BF),
        shape((dim, rows), BF),
        shape(small.shape, F32),
        TOKEN,
    ]
    scratch = [
        pltpu.VMEM((dim, rows), BF),
        pltpu.VMEM((HEADS, 1, LEN), F32),
        pltpu.VMEM((HEADS * LEN, LEN), F32),
        pltpu.VMEM((HEADS, LEN, LEN), BF),
        pltpu.VMEM((3, dim, LEN), F32),
        pltpu.VMEM((2, dim, LEN), BF),
    ]
    aliases = {len(ins) - 1: 0} if given else {}
    out = call(kernel, outs, ins, scratch, 0, aliases, "attention_grad", after, ATTENTION_LIMIT, micros=ATTENTION_MICROS)
    return out[0], out[1:4], out[4]


def qkv_grad(section, info, kept, before, after):
    gqkv, normt, small = kept
    dim, rows = normt.shape
    share = dim // GROUPS
    half = 3 * share // 2
    given = [] if before is None else list(before)
    ins = [info, gqkv, normt, small] + given

    def kernel(info, gqkv_s, normt_s, small_s, *refs):
        old = refs[: len(given)]
        bufs = refs[len(given) : len(given) + 4]
        send_a, keep_a, send_b, keep_b = bufs
        (block_s,) = refs[len(given) + 5 :]
        keep_given(info[0] == section, old, bufs)

        @pl.when(info[0] == section)
        def _():
            sums = [
                jnp.sum(gqkv_s[:, c * dim : (c + 1) * dim].astype(F32), axis=0, keepdims=True)
                for c in range(3)
            ]
            tail = jnp.concatenate(sums + [small_s[ROW_OUT:, :]], axis=0).astype(BF)
            send_a[2 * half :, :] = tail
            keep_a[2 * half :, :] = tail
            for c in range(3):
                block_s[c] = mm(normt_s[...], gqkv_s[:, c * dim : (c + 1) * dim]).astype(BF)

            @pl.loop(0, GROUPS)
            def _(shard):
                x, y, base = shard % 2, shard // 2, shard * share
                for c in range(3):
                    row, at, left = 0, c * share, share
                    while left:
                        count = min(left, half - at % half)
                        if at < half:
                            own, bit, keep, send, to = info[1], x, keep_a, send_a, y * half + at
                        else:
                            own, bit, keep, send, to = info[2], y, keep_b, send_b, x * half + at - half
                        lay_out(own, bit, keep, send, block_s, c, base + row, count, to)
                        row, at, left = row + count, at + count, left - count

    scratch = [pltpu.VMEM((3, dim, dim), BF)]
    aliases = {len(ins) - 4 + i: i for i in range(4)} if given else {}
    outs = pair_shapes(2 * half + PAD, dim) + pair_shapes(2 * half, dim) + [TOKEN]
    out = call(kernel, outs, ins, scratch, 0, aliases, "qkv_grad", after, QKV_LIMIT)
    return out[:4], out[4]


STEP = 80


def plus(one, two):
    return (one.astype(F32) + two.astype(F32)).astype(BF)


def add_rows(out, at, one, two, start, count):
    whole = count // STEP * STEP

    @pl.loop(0, whole // STEP)
    def _(i):
        src = pl.ds(pl.multiple_of(start + i * STEP, PAD), STEP)
        dst = pl.ds(pl.multiple_of(at + i * STEP, PAD), STEP)
        out[dst, :] = plus(one[src, :], two[src, :])

    if count > whole:
        src = pl.ds(pl.multiple_of(start + whole, PAD), count - whole)
        out[pl.ds(at + whole, count - whole), :] = plus(one[src, :], two[src, :])


def vmem_call(kernel, outs, ins, name, after, scratch=()):
    return call(kernel, outs, ins, list(scratch), 0, {}, name, after, 8)


def copy_rows(out, at, src, start, count):
    whole = count // STEP * STEP

    @pl.loop(0, whole // STEP)
    def _(i):
        lines = pl.ds(pl.multiple_of(start + i * STEP, PAD), STEP)
        out[pl.ds(pl.multiple_of(at + i * STEP, PAD), STEP), :] = src[lines, :]

    if count > whole:
        lines = pl.ds(pl.multiple_of(start + whole, PAD), count - whole)
        out[pl.ds(pl.multiple_of(at + whole, PAD), count - whole), :] = src[lines, :]


def first_sum(section, info, held, came, third, after):
    dim = third[0].shape[1]
    halves = [k.shape[0] // 2 for k in (held[1], held[3])]
    riders = (third[2], third[0])

    def kernel(info, ka, ra, kb, rb, *refs):
        given = refs[:2]
        sa, na, sb, nb = refs[2:]

        @pl.when(info[0] == section)
        def _():
            for own, one, two, new, out, half, rider in (
                (info[2], ka, ra, na, sa, halves[0], given[0]),
                (info[1], kb, rb, nb, sb, halves[1], given[1]),
            ):
                add_rows(out, 0, one, two, (1 - own) * half, half)
                add_rows(new, 0, one, two, own * half, half)
                copy_rows(out, half, rider, 0, rider.shape[0])

    outs = []
    for half, rider in zip(halves, riders):
        outs += [shape((half + rider.shape[0], dim), BF), shape((half, dim), BF)]
    ins = [info, held[1], came[0], held[3], came[1]] + list(riders)
    return vmem_call(kernel, outs, ins, "first_sum", after)


def padded(rows):
    return -(-rows // (PAD * REPLICAS)) * PAD * REPLICAS


def split_shapes(rows, dim):
    if lax.axis_size("replica") == REPLICAS:
        return [shape((padded(rows) // 2, dim), BF)] * 2
    return [shape((rows, dim), BF)]


def sum_pieces(info, outs, pieces, rows):
    half = padded(rows) // 2
    if len(outs) == 1:
        for at, one, two, start_one, start_two, count in pieces:
            outs[0][at : at + count, :] = plus(
                one[start_one : start_one + count, :], two[start_two : start_two + count, :]
            )
        return
    for own in range(2):

        @pl.when(info[3] % 2 == own)
        def _():
            for at, one, two, start_one, start_two, count in pieces:
                for out, low in ((outs[1], own * half), (outs[0], (1 - own) * half)):
                    first, last = max(at, low), min(at + count, low + half)
                    if first < last:
                        add_shifted(
                            out, first - low, one, start_one + first - at, two, start_two + first - at, last - first
                        )


def add_shifted(out, at, one, start_one, two, start_two, count):
    whole = count // STEP * STEP

    @pl.loop(0, whole // STEP)
    def _(i):
        a = pl.ds(pl.multiple_of(start_one + i * STEP, PAD), STEP)
        b = pl.ds(pl.multiple_of(start_two + i * STEP, PAD), STEP)
        out[pl.ds(pl.multiple_of(at + i * STEP, PAD), STEP), :] = plus(one[a, :], two[b, :])

    if count > whole:
        a = pl.ds(pl.multiple_of(start_one + whole, PAD), count - whole)
        b = pl.ds(pl.multiple_of(start_two + whole, PAD), count - whole)
        out[pl.ds(pl.multiple_of(at + whole, PAD), count - whole), :] = plus(one[a, :], two[b, :])


def third_sum(info, flows, third, after):
    dim = third[1].shape[1]
    half_a, half_b = (third[1].shape[0] - PAD) // 2, third[3].shape[0] // 2
    top, rest = flows[0][0].shape[0] - 2 * half_b, flows[0][1].shape[0] - 2 * half_a - PAD

    def kernel(info, ka, kb, *refs):
        sa, ma, sb, mb = refs[4:]
        for section in range(2):
            along, across = refs[2 * section : 2 * section + 2]

            @pl.when(info[0] == section)
            def _():
                for own, one, two, base, new, out, half in (
                    (info[2], ka, across, rest, ma, sa, half_a),
                    (info[1], kb, along, top, mb, sb, half_b),
                ):
                    for target, part in ((new, own), (out, 1 - own)):
                        add_shifted(target, 0, one, part * half, two, base + part * half, half)
                    extra = one.shape[0] - 2 * half
                    if extra:
                        low = base + 2 * half
                        tail = plus(one[2 * half :, :], two[low : low + extra, :])
                        new[half:, :] = tail
                        out[half:, :] = tail

    outs = [shape((half_a + PAD, dim), BF)] * 2 + [shape((half_b, dim), BF)] * 2
    ins = [info, third[1], third[3]] + [a for f in flows for a in f]
    return vmem_call(kernel, outs, ins, "third_sum", after)


def group_sum(section, info, kept, came, given, after):
    rows = [a.shape[0] for a in kept]
    given = list(given or [])

    def kernel(info, ka, kb, ra, rb, *refs):
        outs = refs[len(given) :]
        keep_given(info[0] == section, refs[: len(given)], outs)

        @pl.when(info[0] == section)
        def _():
            pieces = [(0, ka, ra, 0, 0, rows[0]), (rows[0], kb, rb, 0, 0, rows[1])]
            sum_pieces(info, outs, pieces, sum(rows))

    outs = split_shapes(sum(rows), kept[0].shape[1])
    ins = [info] + list(kept) + list(came) + given
    aliases = {5 + i: i for i in range(len(given))}
    return call(kernel, outs, ins, [], 0, aliases, "group_sum", after, 10)


def last_sum(info, kept, came, after):
    rows = [a.shape[0] for a in kept]

    def kernel(info, ka, kb, ra, rb, *outs):
        pieces = [(0, ka, ra, 0, 0, rows[0]), (rows[0], kb, rb, 0, 0, rows[1])]
        sum_pieces(info, outs, pieces, sum(rows))

    outs = split_shapes(sum(rows), kept[0].shape[1])
    return vmem_call(kernel, outs, [info] + list(kept) + list(came), "last_sum", after)


class Pairing:
    def __init__(self, info, parts):
        self.info, self.parts = info, parts
        if self.pairs:
            self.came = self.trade(parts[0], 1)
        else:
            self.parts = [lax.psum(parts[0], "replica")]

    @property
    def pairs(self):
        return len(self.parts) == 2

    def trade(self, part, bit):
        return lax.ppermute(part, "replica", [(r, r ^ bit) for r in range(REPLICAS)])

    def halve(self, after):
        if not self.pairs:
            return after
        half, dim = self.parts[1].shape
        quarter = half // 2

        def kernel(info, one, two, send, keep):
            for own in range(2):

                @pl.when(info[3] // 2 == own)
                def _():
                    add_shifted(keep, 0, one, own * quarter, two, own * quarter, quarter)
                    other = (1 - own) * quarter
                    add_shifted(send, 0, one, other, two, other, quarter)

        ins = [self.info, self.parts[1], self.came]
        send, self.kept = vmem_call(kernel, [shape((quarter, dim), BF)] * 2, ins, "halve", after)
        self.came = self.trade(send, 2)
        return self.kept

    def total(self, after):
        if not self.pairs:
            return after

        def kernel(one, two, out):
            add_rows(out, 0, one, two, 0, one.shape[0])

        outs = [shape(self.kept.shape, BF)]
        self.own = vmem_call(kernel, outs, [self.kept, self.came], "total", after)[0]
        self.came = self.trade(self.own, 2)
        return self.own

    def double(self, after):
        if not self.pairs:
            return after
        quarter, dim = self.own.shape

        def kernel(info, one, two, out):
            copy_rows(out, info[3] // 2 * quarter, one, 0, quarter)
            copy_rows(out, (1 - info[3] // 2) * quarter, two, 0, quarter)

        outs = [shape((2 * quarter, dim), BF)]
        half = vmem_call(kernel, outs, [self.info, self.own, self.came], "double", after)[0]
        self.parts = [half, self.trade(half, 1)]
        return half


def own_pieces(row, count, width, group):
    share = count * width // GROUPS
    at, pieces = group * share, []
    while at < (group + 1) * share:
        size = min((group + 1) * share - at, width - at % width)
        pieces.append((row + at // width, at % width, size, at - group * share))
        at += size
    return pieces


def finish(info, halves, thirds, after):
    dim = halves[0].shape[1]
    share = dim // GROUPS
    half = 3 * share // 2
    top = dim + 5 * share
    base = len(halves) * halves[0].shape[0]
    vectors = ((ROW_QKV, 3), (ROW_OUT, 1), (ROW_UP, 4), (ROW_DOWN, 1))
    outs = [
        shape((dim, dim), F32),
        shape((share, 4 * dim), F32),
        shape((share, dim), F32),
        shape((share, 3 * dim), F32),
    ]
    large = len(outs)
    outs += [shape((1, count * dim // GROUPS), F32) for _, count in vectors]
    outs += [shape((2, share), F32)] * 2
    sides = len(halves)

    def kernel(info, *refs):
        given, refs = refs[: 2 * sides], refs[2 * sides :]
        out_h = refs[:large]
        small = refs[large : len(outs)]
        src = refs[len(outs)]
        stage = refs[len(outs) + 1 : -1]
        sems = refs[-1]
        for low in range(sides):

            @pl.when(info[3] % 2 == low if sides > 1 else info[3] >= 0)
            def _():
                for k, part in enumerate(given):
                    rows = part.shape[0]
                    at = (low + k) % sides * rows + (base if k >= sides else 0)
                    pltpu.make_async_copy(part, src.at[pl.ds(at, rows)], sems.at[k]).start()

        for k, part in enumerate(given):
            pltpu.make_async_copy(part, src.at[pl.ds(0, part.shape[0])], sems.at[k]).wait()
        copies = []

        def save(i):
            copy = pltpu.make_async_copy(stage[i], out_h[i], sems.at[4 + i])
            copy.start()
            copies.append(copy)

        stage[0][...] = src[:dim, :].astype(F32)
        save(0)
        for i in range(4):
            block = src[dim + i * share : dim + (i + 1) * share, :].astype(F32)
            stage[1][:, i * dim : (i + 1) * dim] = block
        save(1)
        for i in range(3):
            at, left, to = i * share, share, 0
            while left:
                count = min(left, half - at % half)
                row = base + (at if at < half else at + PAD)
                block = src[row : row + count, :].astype(F32)
                stage[3][to : to + count, i * dim : (i + 1) * dim] = block
                at, left, to = at + count, left - count, to + count
        save(3)
        stage[2][...] = src[dim + 4 * share : top, :].astype(F32)
        save(2)
        tail = src[base + half : base + half + PAD, :].astype(F32)
        for group in range(GROUPS):

            @pl.when(info[1] + 2 * info[2] == group)
            def _():
                for out, (row, count) in zip(small, vectors):
                    for r, c, size, at in own_pieces(row, count, dim, group):
                        out[:, at : at + size] = tail[r : r + 1, c : c + size]
                for out, row in zip(small[4:], (ROW_GAIN, ROW_SHIFT)):
                    out[...] = tail[row : row + 2, group * share : (group + 1) * share]

        for copy in copies:
            copy.wait()

    scratch = [pltpu.VMEM((base + sides * thirds[0].shape[0], dim), BF)]
    scratch += [vmem_like(o) for o in outs[:large]]
    places = "h" * large + "v" * (len(outs) - large)
    ins = [info] + list(halves) + list(thirds)
    return call(
        kernel, outs, ins, scratch, 8, {}, "finish", after, 16, "s" + "a" * 2 * sides, places
    )


def flow(shard, axis, pairs, sections):
    if sections == (0, 1):
        return lax.ppermute(shard, axis, pairs)
    peers = lax.axis_size(axis)
    pairs = [(s * peers + i, s * peers + j) for s in sections for i, j in pairs]
    return lax.ppermute(shard, ("section", axis), pairs)


ACROSS = [(g, g ^ 1) for g in range(GROUPS)]
ALONG = [(g, g ^ 2) for g in range(GROUPS)]
BOTH = (0, 1)


def exchange(a, b, turned, sections):
    ways = (ALONG, ACROSS) if turned else (ACROSS, ALONG)
    return flow(a, "group", ways[0], sections), flow(b, "group", ways[1], sections)


def shards(
    block_input,
    cotangent,
    crop_count,
    mask_count,
    qkv_weight,
    qkv_bias,
    out_weight,
    out_bias,
    up_weight,
    up_bias,
    down_weight,
    down_bias,
    norm_gain,
    norm_shift,
):
    params = (
        qkv_weight[0],
        qkv_bias,
        out_weight[0],
        out_bias,
        up_weight[0],
        up_bias,
        down_weight[0],
        down_bias,
        norm_gain[0],
        norm_shift[0],
    )
    rows, dim = block_input.shape
    tab = jnp.asarray(rotary_tables())
    tab_t = jnp.asarray(rotary_columns())
    group = lax.axis_index("group")
    assert lax.axis_size("group") == GROUPS
    info = jnp.stack([lax.axis_index("section"), group % 2, group // 2, lax.axis_index("replica")])

    def to_other(shard, pairs):
        return lax.ppermute(shard, "section", pairs)

    act, first = forward(0, info, crop_count, block_input, None, params, tab, None)
    arrived = [to_other(first[0], [(0, 1)])]
    act, second = forward(1, info, crop_count, block_input, arrived[0], params, tab, act)
    arrived.append(to_other(second[0], [(0, 1)]))
    act, third = forward(2, info, crop_count, block_input, arrived[1], params, tab, act)
    kept_one, kept_zero = (second, third), (first, second)

    common = (info, crop_count, mask_count)
    one, gmid, small, last = mlp_grad(1, *common, cotangent, kept_one, params, None)
    came = exchange(one[0], one[2], False, (1,))
    dx, kept, last = attention_grad(
        1, info, gmid, small, arrived, kept_one, params, tab_t, None, last
    )
    grad_back = to_other(dx, [(1, 0)])
    third, last = qkv_grad(1, info, kept, None, last)
    one = first_sum(1, info, one, came, third, last)
    came_one = exchange(one[0], one[2], True, (1,))
    zero, gmid, small, last = mlp_grad(0, *common, grad_back, kept_zero, params, one[1])
    came = exchange(zero[0], zero[2], False, (0,))
    sums = group_sum(1, info, (one[1], one[3]), came_one, None, last)
    dx, kept, last = attention_grad(
        0, info, gmid, small, [block_input], kept_zero, params, tab_t, dx, sums[-1]
    )
    third, last = qkv_grad(0, info, kept, third, last)
    zero = first_sum(0, info, zero, came, third, last)
    came_zero = exchange(zero[0], zero[2], True, (0,))
    sums = group_sum(0, info, (zero[1], zero[3]), came_zero, sums, zero[1])
    mlp = Pairing(info, sums)
    send_a, keep_a, send_b, keep_b = third_sum(info, (came_zero, came_one), third, sums[-1])
    came = exchange(send_a, send_b, True, BOTH)
    qkv = Pairing(info, last_sum(info, (keep_a, keep_b), came, keep_a))
    last = mlp.halve(qkv.parts[-1])
    last = qkv.halve(last)
    last = mlp.total(last)
    last = qkv.total(last)
    last = mlp.double(last)
    last = qkv.double(last)
    grad_down, grad_up, grad_out, grad_qkv, *small = finish(info, mlp.parts, qkv.parts, last)
    qkv_b, out_b, up_b, down_b, gain, shift = small
    return (
        act[None],
        dx[None],
        grad_qkv[None],
        qkv_b,
        grad_out[None],
        out_b,
        grad_up[None],
        up_b,
        grad_down[None],
        down_b,
        gain[None],
        shift[None],
    )


def solution(mesh):
    rows = P(("group", "replica"))
    stack = P("section")
    return jax.shard_map(
        shards,
        mesh=mesh,
        in_specs=(rows,) * 4 + (stack,) * 10,
        out_specs=(
            P("section", ("group", "replica"), None),
            P("section", ("group", "replica"), None),
            P("section", "group", None),
            P("section", "group"),
            P("section", "group", None),
            P("section", "group"),
            P("section", "group", None),
            P("section", "group"),
            P("section", "group", None),
            P("section", "group"),
            P("section", None, "group"),
            P("section", None, "group"),
        ),
        check_vma=False,
    )
```

```python
import jax
import jax.numpy as jnp
import numpy as np
from jax import lax
from jax.experimental import pallas as pl
from jax.experimental.pallas import tpu as pltpu
from jax.sharding import PartitionSpec as P

HEADS = 20
HEAD_DIM = 32
LEN = 256
MASK_MEAN = 38
CROP_DEV = 2
EPSILON = 1e-05
ROTARY_BASE = 10000.0

BF = jnp.bfloat16
F32 = jnp.float32
NN = (((1,), (0,)), ((), ()))
NT = (((1,), (1,)), ((), ()))
TN = (((0,), (0,)), ((), ()))

FIRST_LIMIT, FORWARD_LIMIT, MLP_LIMIT, ATTENTION_LIMIT, QKV_LIMIT = 40, 14, 16, 17, 8
ATTENTION_MICROS = 12
REPLICAS = 4
GROUPS = 4
PAD = 16
ROW_QKV, ROW_OUT, ROW_UP, ROW_DOWN, ROW_GAIN, ROW_SHIFT = 0, 3, 4, 8, 9, 11

ANY = pl.BlockSpec(memory_space=pl.ANY)
HBM = pl.BlockSpec(memory_space=pltpu.HBM)
VMEM = pl.BlockSpec(memory_space=pltpu.VMEM)
SMEM = pl.BlockSpec(memory_space=pltpu.SMEM)


def shape(dims, dtype):
    return jax.ShapeDtypeStruct(dims, dtype)


def mm(left, right, dims=NN):
    return lax.dot_general(left, right, dims, preferred_element_type=F32)


def unit_rows_of(values):
    centred = values - jnp.mean(values, axis=-1, keepdims=True)
    inverse = lax.rsqrt(jnp.mean(centred * centred, axis=-1, keepdims=True) + EPSILON)
    return centred * inverse, inverse


def norm_back(grad, unit, inverse, gain):
    scaled = grad * gain
    return inverse * (
        scaled
        - jnp.mean(scaled, axis=-1, keepdims=True)
        - unit * jnp.mean(scaled * unit, axis=-1, keepdims=True)
    )


def rotary_tables():
    lane = np.arange(128) % HEAD_DIM
    half = HEAD_DIM // 2
    freq = ROTARY_BASE ** (-(lane % half).astype(np.float64) * (2.0 / HEAD_DIM))
    angles = np.arange(LEN)[:, None] * freq[None, :]
    sign = np.where(lane < half, -1.0, 1.0)[None, :]
    return np.stack([np.cos(angles), np.sin(angles) * sign]).astype(np.float32)


def rotary_columns():
    half = HEAD_DIM // 2
    freq = ROTARY_BASE ** (-np.arange(half, dtype=np.float64) * (2.0 / HEAD_DIM))
    angles = freq[:, None] * np.arange(LEN)[None, :]
    return np.stack([np.cos(angles), np.sin(angles)]).astype(np.float32)


def swap_halves(values):
    lane = lax.broadcasted_iota(jnp.int32, values.shape, 1) % HEAD_DIM
    half = HEAD_DIM // 2
    return jnp.where(
        lane < half,
        pltpu.roll(values, 128 - half, axis=1),
        pltpu.roll(values, half, axis=1),
    )


def head_stack(block, per):
    head = lax.broadcasted_iota(jnp.int32, block.shape, 1) // HEAD_DIM
    return jnp.concatenate(
        [jnp.where(head == h, block, jnp.zeros_like(block)) for h in range(per)], axis=0
    )


class Copies:
    def __init__(self, sems):
        self.sems = sems
        self.used = 0
        self.open = []

    def start(self, src, dst):
        copy = pltpu.make_async_copy(src, dst, self.sems.at[self.used])
        self.used += 1
        copy.start()
        return copy

    def save(self, src, dst):
        self.open.append(self.start(src, dst))

    def finish(self):
        for copy in self.open:
            copy.wait()


def call(kernel, outs, ins, scratch, sems, aliases, name, after=None, limit=16, spaces=None, out_spaces=None, micros=0.1):
    count = len(ins)
    places = {"v": VMEM, "h": HBM, "a": ANY, "s": SMEM}
    spaces = spaces or "v" * count
    out_spaces = out_spaces or "v" * len(outs)
    in_specs = [SMEM if a.ndim == 1 else places[p] for a, p in zip(ins, spaces)]
    ins = [pltpu.with_memory_space_constraint(a, pltpu.HBM) if p == "h" else a for a, p in zip(ins, spaces)]
    body = kernel
    if after is not None:
        ins = list(ins) + [after]
        in_specs = in_specs + [ANY]

        def body(*refs):
            kernel(*refs[:count], *refs[count + 1 :])

    outs = [pltpu.HBM(o.shape, o.dtype) if p == "h" else o for o, p in zip(outs, out_spaces)]
    return pl.pallas_call(
        body,
        out_shape=outs,
        in_specs=in_specs,
        out_specs=[places[p] for p in out_spaces],
        scratch_shapes=scratch + ([pltpu.SemaphoreType.DMA((sems,))] if sems else []),
        input_output_aliases=aliases,
        compiler_params=pltpu.CompilerParams(vmem_limit_bytes=limit << 20),
        cost_estimate=pl.CostEstimate(
            flops=int(micros * 1.15e9), bytes_accessed=0, transcendentals=0
        ),
        name=name,
    )(*ins)


TOKEN = jax.ShapeDtypeStruct((8, 128), F32)


def vmem_like(arr):
    return pltpu.VMEM(arr.shape, arr.dtype)


def forward(slot, info, live, own, arrived, params, tab, act, after=None):
    qkvw, qkvb, outw, outb, upw, upb, downw, downb, gain, shift = params
    dim = own.shape[1]
    blocks = dim // 128
    wide = upw.shape[1]
    parts = wide // dim
    per = 128 // HEAD_DIM
    manual = slot == 0
    saved = [
        shape((LEN, dim), BF),
        shape((LEN, 3 * dim), BF),
        shape((HEADS, LEN, LEN), BF),
        shape((dim, LEN), BF),
        shape((LEN, dim), F32),
        shape((LEN, wide), BF),
        shape((LEN, wide), BF),
    ]
    weights = [qkvb, outb, upb, downb, gain, shift, tab, qkvw, outw, upw, downw]
    sources = [own] if slot == 0 else [arrived] if slot == 2 else [own, arrived]
    before = [] if act is None else [act]
    ins = [info, live] + sources + weights + before
    count = len(sources)

    def kernel(info, live, *refs):
        xs = refs[:count]
        given = refs[count : count + 11]
        act_h, *outs = refs[count + 11 + len(before) : count + 19 + len(before)]
        scratch = refs[count + 19 + len(before) :]
        act_s, vt_s, score_s, up_s = scratch[:4]
        sems = scratch[-1]
        y_s, qkv_s, prob_s, mixt_s, mid_s, gp_s, hid_s = outs
        used = scratch[4:-1] if manual else xs[-1:] + given
        qkvb, outb, upb, downb, gain, shift, tab, qkvw, outw, upw, downw = used[1:]
        crop = slot - info[0]

        @pl.when(jnp.logical_and(crop >= 0, crop < CROP_DEV))
        def _():
            copies = Copies(sems)
            heavy = []
            if manual:
                rows = xs[0].at[pl.ds(0, LEN)]
                loads = [copies.start(h, s) for h, s in zip((rows,) + given, used)]
                heavy = loads[8:]
                wait_all(loads[:8])
                x = used[0][...].astype(F32)
            elif slot == 1:
                x = jnp.where(info[0] == 0, xs[0][LEN:, :], xs[1][...]).astype(F32)
            else:
                x = xs[0][...].astype(F32)

            def ready(index):
                if manual:
                    heavy[index].wait()

            unit, _ = unit_rows_of(x)
            normed = (unit * gain[0:1, :] + shift[0:1, :]).astype(BF)
            ready(0)
            third = mm(normed, qkvw[:, 2 * dim :]) + qkvb[:, 2 * dim :]
            low = third.astype(BF)
            qkv_s[:, 2 * dim :] = low
            vt_s[...] = low.T
            for part in range(2):
                third = mm(normed, qkvw[:, part * dim : (part + 1) * dim])
                third = third + qkvb[:, part * dim : (part + 1) * dim]
                for j in range(blocks):
                    b = third[:, 128 * j : 128 * j + 128]
                    b = b * tab[0] + swap_halves(b) * tab[1]
                    if part == 0:
                        b = b * HEAD_DIM**-0.5
                    at = part * dim + 128 * j
                    qkv_s[:, at : at + 128] = b.astype(BF)
            for j in range(blocks):
                q = qkv_s[:, 128 * j : 128 * j + 128]
                k = qkv_s[:, dim + 128 * j : dim + 128 * j + 128]
                score_s[per * LEN * j : per * LEN * (j + 1), :] = mm(head_stack(k, per), q, NT)

            def soft(h, _):
                s = score_s[pl.ds(pl.multiple_of(h * LEN, LEN), LEN), :]
                e = jnp.exp(s - jnp.max(s, axis=0, keepdims=True))
                prob_s[h] = (e * (1.0 / jnp.sum(e, axis=0, keepdims=True))).astype(BF)
                return 0

            lax.fori_loop(0, HEADS, soft, 0, unroll=2)
            for h in range(HEADS):
                at = slice(HEAD_DIM * h, HEAD_DIM * (h + 1))
                mixt_s[at, :] = mm(vt_s[at, :], prob_s[h]).astype(BF)
            ready(1)
            mid = x + mm(mixt_s[...], outw[...], TN) + outb[...]
            mid_s[...] = mid
            unit, _ = unit_rows_of(mid)
            normed = (unit * gain[1:2, :] + shift[1:2, :]).astype(BF)
            ready(2)
            up_s[...] = mm(normed, upw[...])
            for c in range(parts):
                cols = slice(c * dim, (c + 1) * dim)
                u = up_s[:, cols] + upb[:, cols]
                cdf = 0.5 + 0.5 * lax.erf(u * 0.5**0.5)
                hid_s[:, cols] = (u * cdf).astype(BF)
                gp_s[:, cols] = (
                    cdf + u * (jnp.exp(u * u * -0.5) * (2 * np.pi) ** -0.5)
                ).astype(BF)
            ready(3)
            low = (mid_s[...] + downb[...] + mm(hid_s[...], downw[...])).astype(BF)
            y_s[...] = low
            act_s[...] = jnp.where(crop < live[0], low, jnp.zeros_like(low))
            at = pl.multiple_of(crop * LEN, LEN)
            copies.save(act_s, act_h.at[pl.ds(at, LEN)])
            copies.finish()

    outs = [shape(own.shape, BF)] + saved
    scratch = [
        pltpu.VMEM((LEN, dim), BF),
        pltpu.VMEM((dim, LEN), BF),
        pltpu.VMEM((HEADS * LEN, LEN), F32),
        pltpu.VMEM((LEN, wide), F32),
    ]
    if manual:
        scratch += [pltpu.VMEM((LEN, dim), BF)] + [vmem_like(a) for a in weights]
    aliases = {} if act is None else {len(ins) - 1: 0}
    spaces = "ss" + ("h" if manual else "v") * (count + 11) + "h" * len(before)
    out = call(
        kernel,
        outs,
        ins,
        scratch,
        16,
        aliases,
        "layer_forward",
        after,
        FIRST_LIMIT if manual else FORWARD_LIMIT,
        spaces,
        "h" + "v" * 7,
    )
    return out[0], out[1:]


def crop_weight(live, masks, crop, section):
    if section == 0:
        return 1.0
    count = jnp.where(live[0] > crop, masks[crop], 0)
    return jnp.full((1, 1), count, jnp.int32).astype(F32) / MASK_MEAN


def add_row(ref, row, values):
    ref[row : row + 1, :] = ref[row : row + 1, :] + jnp.sum(values, axis=0, keepdims=True)


def lay_out(own, bit, keep, send, block, index, row, count, at):
    src = pl.ds(row if isinstance(row, int) else pl.multiple_of(row, PAD), count)
    dst = pl.ds(at if isinstance(at, int) else pl.multiple_of(at, PAD), count)
    mine = own == bit

    @pl.when(mine)
    def _():
        keep[dst, :] = block[index, src, :]

    @pl.when(jnp.logical_not(mine))
    def _():
        send[dst, :] = block[index, src, :]


def keep_given(active, given, bufs):
    @pl.when(jnp.logical_not(active))
    def _():
        for old, new in zip(given, bufs):
            new[...] = old[...]


def pair_shapes(rows, dim):
    return [shape((rows, dim), BF)] * 2


def joined(refs, cols):
    return jnp.concatenate([r[:, cols] for r in refs], axis=0)


def wait_all(copies):
    for copy in copies:
        copy.wait()


def mlp_grad(section, info, live, masks, g, saved, params, after):
    mixts = [s[3] for s in saved]
    mids, gps, hids = ([s[k] for s in saved] for k in (4, 5, 6))
    upw, downw, gain, shift = params[4], params[6], params[8], params[9]
    rows, dim = g.shape
    wide = upw.shape[1]
    parts = wide // dim
    crops = len(saved)
    share = dim // GROUPS
    ins = [info, live, masks, g, gain, shift, downw, upw] + mids + gps + hids + mixts

    def kernel(info, live, masks, g_s, gain, shift, downw, upw, *refs):
        mid_s, gp_s, hid_s, mixt_s = (refs[i * crops : (i + 1) * crops] for i in range(4))
        refs = refs[4 * crops :]
        send_a, keep_a, send_b, keep_b, gmid_s, small_s = refs[:6]
        gu_s, block_s, low_s, normt_s, back_s = refs[7:]

        @pl.when(info[0] == section)
        def _():
            small_s[...] = jnp.zeros_like(small_s)
            for c in range(crops):
                crop = slice(c * LEN, (c + 1) * LEN)
                grad = g_s[crop, :].astype(F32) * crop_weight(live, masks, c, section)
                low = grad.astype(BF)
                low_s[crop, :] = low
                add_row(small_s, ROW_DOWN, low.astype(F32))
                unit, _ = unit_rows_of(mid_s[c][...])
                normt_s[:, crop] = (unit * gain[1:2, :] + shift[1:2, :]).astype(BF).T
            for c in range(parts):
                cols = slice(c * dim, (c + 1) * dim)
                block_s[c] = mm(joined(hid_s, cols), low_s[...], TN).astype(BF)

            @pl.loop(0, GROUPS * parts)
            def _(i):
                shard, row = i // parts, (i % parts) * share
                at = (shard // 2) * dim + row
                lay_out(info[1], shard % 2, keep_a, send_a, block_s, shard, row, share, at)

            for c in range(parts):
                cols = slice(c * dim, (c + 1) * dim)
                grad_up = mm(low_s[...], downw[cols, :], NT) * joined(gp_s, cols).astype(F32)
                grad_up = grad_up.astype(BF)
                gu_s[:, cols] = grad_up
                small_s[ROW_UP + c : ROW_UP + c + 1, :] = jnp.sum(
                    grad_up.astype(F32), axis=0, keepdims=True
                )
            back_s[...] = mm(gu_s[...], upw[...], NT)
            for c in range(crops):
                crop = slice(c * LEN, (c + 1) * LEN)
                grad = g_s[crop, :].astype(F32) * crop_weight(live, masks, c, section)
                unit, inverse = unit_rows_of(mid_s[c][...])
                back = back_s[crop, :]
                gmid = grad + norm_back(back, unit, inverse, gain[1:2, :])
                gmid_s[crop, :] = gmid
                low = gmid.astype(BF)
                low_s[crop, :] = low
                add_row(small_s, ROW_GAIN + 1, back * unit)
                add_row(small_s, ROW_SHIFT + 1, back)
                add_row(small_s, ROW_OUT, low.astype(F32))
            for c in range(parts):
                block_s[c] = mm(normt_s[...], gu_s[:, c * dim : (c + 1) * dim]).astype(BF)
            mixt = jnp.concatenate([m[...] for m in mixt_s], axis=1)
            block_s[parts] = mm(mixt, low_s[...]).astype(BF)

            @pl.loop(0, GROUPS * (parts + 1))
            def _(i):
                shard, c = i // (parts + 1), i % (parts + 1)
                at = ((shard % 2) * (parts + 1) + c) * share
                lay_out(info[2], shard // 2, keep_b, send_b, block_s, c, shard * share, share, at)

    scratch = [
        pltpu.VMEM((rows, wide), BF),
        pltpu.VMEM((parts + 1, dim, dim), BF),
        pltpu.VMEM((rows, dim), BF),
        pltpu.VMEM((dim, rows), BF),
        pltpu.VMEM((rows, dim), F32),
    ]
    outs = pair_shapes(2 * dim, dim) + pair_shapes(2 * (parts + 1) * share, dim)
    outs += [shape((rows, dim), F32), shape((PAD, dim), F32), TOKEN]
    out = call(kernel, outs, ins, scratch, 0, {}, "mlp_grad", after, MLP_LIMIT, micros=10)
    return out[:4], out[4], out[5], out[6]


def rotate_back(block, tab_t):
    half = HEAD_DIM // 2
    cos, sin = tab_t[0], tab_t[1]
    out = []
    for at in range(0, block.shape[0], HEAD_DIM):
        a, b = block[at : at + half], block[at + half : at + HEAD_DIM]
        out += [a * cos + b * sin, b * cos - a * sin]
    return jnp.concatenate(out, axis=0)


def attention_grad(section, info, gmid, small, xs, saved, params, tab_t, before, after):
    qkvs, probs, mixts = [s[1] for s in saved], [s[2] for s in saved], [s[3] for s in saved]
    qkvw, outw, gain, shift = params[0], params[2], params[8], params[9]
    rows, dim = gmid.shape
    blocks = dim // 128
    per = 128 // HEAD_DIM
    crops = len(saved)
    given = [] if before is None else [before]
    ins = [info, gmid, outw, small, gain, shift, tab_t, qkvw]
    ins += qkvs + probs + mixts + list(xs) + given

    def kernel(info, gmid_s, outw, small_s, gain, shift, tab_t, qkvw, *refs):
        qkv_s, prob_s, mixt_s = (refs[i * crops : (i + 1) * crops] for i in range(3))
        x_s = refs[3 * crops : 3 * crops + len(xs)]
        old = refs[3 * crops + len(xs) : 3 * crops + len(xs) + len(given)]
        refs = refs[3 * crops + len(xs) + len(given) :]
        keep_given(info[0] == section, old, refs[:1])
        dx_s, gqkv_s, normt_s, small_out = refs[:4]
        gmt_s, delta_s, da_s, ds_s, dt_s, kt_s = refs[5:]

        @pl.when(info[0] == section)
        def _():
            low = gmid_s[...].astype(BF)
            gmt_s[...] = mm(outw[...], low, NT).astype(BF)
            for c in range(crops):
                crop = slice(c * LEN, (c + 1) * LEN)
                qkv, prob = qkv_s[c], prob_s[c]
                product = gmt_s[:, crop].astype(F32) * mixt_s[c][...].astype(F32)
                delta_s[...] = jnp.sum(product.reshape(HEADS, HEAD_DIM, LEN), axis=1)[:, None, :]
                kt_s[0] = qkv[:, dim : 2 * dim].T
                kt_s[1] = qkv[:, :dim].T
                for j in range(blocks):
                    v = qkv[:, 2 * dim + 128 * j : 2 * dim + 128 * j + 128]
                    da_s[per * LEN * j : per * LEN * (j + 1), :] = mm(
                        head_stack(v, per), gmt_s[128 * j : 128 * j + 128, crop]
                    )

                def scores(h, _):
                    da = da_s[pl.ds(pl.multiple_of(h * LEN, LEN), LEN), :]
                    ds_s[h] = (prob[h].astype(F32) * (da - delta_s[h])).astype(BF)
                    return 0

                lax.fori_loop(0, HEADS, scores, 0, unroll=2)
                for h in range(HEADS):
                    at = slice(HEAD_DIM * h, HEAD_DIM * (h + 1))
                    dt_s[0, at, :] = mm(kt_s[0, at, :], ds_s[h])
                    dt_s[1, at, :] = mm(kt_s[1, at, :], ds_s[h], NT)
                    dt_s[2, at, :] = mm(gmt_s[at, crop], prob[h], NT)
                dq = rotate_back(dt_s[0] * HEAD_DIM**-0.5, tab_t)
                gqkv_s[crop, :dim] = dq.astype(BF).T
                gqkv_s[crop, dim : 2 * dim] = rotate_back(dt_s[1], tab_t).astype(BF).T
                gqkv_s[crop, 2 * dim :] = dt_s[2].astype(BF).T
            unit, inverse = unit_rows_of(joined(x_s, slice(None)).astype(F32))
            normt_s[...] = (unit * gain[0:1, :] + shift[0:1, :]).astype(BF).T
            back = mm(gqkv_s[...], qkvw[...], NT)
            dx_s[...] = (gmid_s[...] + norm_back(back, unit, inverse, gain[0:1, :])).astype(BF)
            small_out[...] = small_s[...]
            small_out[ROW_GAIN : ROW_GAIN + 1, :] = jnp.sum(back * unit, axis=0, keepdims=True)
            small_out[ROW_SHIFT : ROW_SHIFT + 1, :] = jnp.sum(back, axis=0, keepdims=True)

    outs = [
        shape((rows, dim), BF),
        shape((rows, 3 * dim), BF),
        shape((dim, rows), BF),
        shape(small.shape, F32),
        TOKEN,
    ]
    scratch = [
        pltpu.VMEM((dim, rows), BF),
        pltpu.VMEM((HEADS, 1, LEN), F32),
        pltpu.VMEM((HEADS * LEN, LEN), F32),
        pltpu.VMEM((HEADS, LEN, LEN), BF),
        pltpu.VMEM((3, dim, LEN), F32),
        pltpu.VMEM((2, dim, LEN), BF),
    ]
    aliases = {len(ins) - 1: 0} if given else {}
    out = call(kernel, outs, ins, scratch, 0, aliases, "attention_grad", after, ATTENTION_LIMIT, micros=ATTENTION_MICROS)
    return out[0], out[1:4], out[4]


def qkv_grad(section, info, kept, before, after):
    gqkv, normt, small = kept
    dim, rows = normt.shape
    share = dim // GROUPS
    half = 3 * share // 2
    given = [] if before is None else list(before)
    ins = [info, gqkv, normt, small] + given

    def kernel(info, gqkv_s, normt_s, small_s, *refs):
        old = refs[: len(given)]
        bufs = refs[len(given) : len(given) + 4]
        send_a, keep_a, send_b, keep_b = bufs
        (block_s,) = refs[len(given) + 5 :]
        keep_given(info[0] == section, old, bufs)

        @pl.when(info[0] == section)
        def _():
            sums = [
                jnp.sum(gqkv_s[:, c * dim : (c + 1) * dim].astype(F32), axis=0, keepdims=True)
                for c in range(3)
            ]
            tail = jnp.concatenate(sums + [small_s[ROW_OUT:, :]], axis=0).astype(BF)
            send_a[2 * half :, :] = tail
            keep_a[2 * half :, :] = tail
            for c in range(3):
                block_s[c] = mm(normt_s[...], gqkv_s[:, c * dim : (c + 1) * dim]).astype(BF)

            @pl.loop(0, GROUPS)
            def _(shard):
                x, y, base = shard % 2, shard // 2, shard * share
                for c in range(3):
                    row, at, left = 0, c * share, share
                    while left:
                        count = min(left, half - at % half)
                        if at < half:
                            own, bit, keep, send, to = info[1], x, keep_a, send_a, y * half + at
                        else:
                            own, bit, keep, send, to = info[2], y, keep_b, send_b, x * half + at - half
                        lay_out(own, bit, keep, send, block_s, c, base + row, count, to)
                        row, at, left = row + count, at + count, left - count

    scratch = [pltpu.VMEM((3, dim, dim), BF)]
    aliases = {len(ins) - 4 + i: i for i in range(4)} if given else {}
    outs = pair_shapes(2 * half + PAD, dim) + pair_shapes(2 * half, dim) + [TOKEN]
    out = call(kernel, outs, ins, scratch, 0, aliases, "qkv_grad", after, QKV_LIMIT)
    return out[:4], out[4]


STEP = 80


def plus(one, two):
    return (one.astype(F32) + two.astype(F32)).astype(BF)


def add_rows(out, at, one, two, start, count):
    whole = count // STEP * STEP

    @pl.loop(0, whole // STEP)
    def _(i):
        src = pl.ds(pl.multiple_of(start + i * STEP, PAD), STEP)
        dst = pl.ds(pl.multiple_of(at + i * STEP, PAD), STEP)
        out[dst, :] = plus(one[src, :], two[src, :])

    if count > whole:
        src = pl.ds(pl.multiple_of(start + whole, PAD), count - whole)
        out[pl.ds(at + whole, count - whole), :] = plus(one[src, :], two[src, :])


def vmem_call(kernel, outs, ins, name, after, scratch=()):
    return call(kernel, outs, ins, list(scratch), 0, {}, name, after, 8)


def copy_rows(out, at, src, start, count):
    whole = count // STEP * STEP

    @pl.loop(0, whole // STEP)
    def _(i):
        lines = pl.ds(pl.multiple_of(start + i * STEP, PAD), STEP)
        out[pl.ds(pl.multiple_of(at + i * STEP, PAD), STEP), :] = src[lines, :]

    if count > whole:
        lines = pl.ds(pl.multiple_of(start + whole, PAD), count - whole)
        out[pl.ds(pl.multiple_of(at + whole, PAD), count - whole), :] = src[lines, :]


def first_sum(section, info, held, came, third, after):
    dim = third[0].shape[1]
    halves = [k.shape[0] // 2 for k in (held[1], held[3])]
    riders = (third[2], third[0])

    def kernel(info, ka, ra, kb, rb, *refs):
        given = refs[:2]
        sa, na, sb, nb = refs[2:]

        @pl.when(info[0] == section)
        def _():
            for own, one, two, new, out, half, rider in (
                (info[2], ka, ra, na, sa, halves[0], given[0]),
                (info[1], kb, rb, nb, sb, halves[1], given[1]),
            ):
                add_rows(out, 0, one, two, (1 - own) * half, half)
                add_rows(new, 0, one, two, own * half, half)
                copy_rows(out, half, rider, 0, rider.shape[0])

    outs = []
    for half, rider in zip(halves, riders):
        outs += [shape((half + rider.shape[0], dim), BF), shape((half, dim), BF)]
    ins = [info, held[1], came[0], held[3], came[1]] + list(riders)
    return vmem_call(kernel, outs, ins, "first_sum", after)


def padded(rows):
    return -(-rows // (PAD * REPLICAS)) * PAD * REPLICAS


def split_shapes(rows, dim):
    if lax.axis_size("replica") == REPLICAS:
        return [shape((padded(rows) // 2, dim), BF)] * 2
    return [shape((rows, dim), BF)]


def sum_pieces(info, outs, pieces, rows):
    half = padded(rows) // 2
    if len(outs) == 1:
        for at, one, two, start_one, start_two, count in pieces:
            outs[0][at : at + count, :] = plus(
                one[start_one : start_one + count, :], two[start_two : start_two + count, :]
            )
        return
    for own in range(2):

        @pl.when(info[3] % 2 == own)
        def _():
            for at, one, two, start_one, start_two, count in pieces:
                for out, low in ((outs[1], own * half), (outs[0], (1 - own) * half)):
                    first, last = max(at, low), min(at + count, low + half)
                    if first < last:
                        add_shifted(
                            out, first - low, one, start_one + first - at, two, start_two + first - at, last - first
                        )


def add_shifted(out, at, one, start_one, two, start_two, count):
    whole = count // STEP * STEP

    @pl.loop(0, whole // STEP)
    def _(i):
        a = pl.ds(pl.multiple_of(start_one + i * STEP, PAD), STEP)
        b = pl.ds(pl.multiple_of(start_two + i * STEP, PAD), STEP)
        out[pl.ds(pl.multiple_of(at + i * STEP, PAD), STEP), :] = plus(one[a, :], two[b, :])

    if count > whole:
        a = pl.ds(pl.multiple_of(start_one + whole, PAD), count - whole)
        b = pl.ds(pl.multiple_of(start_two + whole, PAD), count - whole)
        out[pl.ds(pl.multiple_of(at + whole, PAD), count - whole), :] = plus(one[a, :], two[b, :])


def third_sum(info, flows, third, after):
    dim = third[1].shape[1]
    half_a, half_b = (third[1].shape[0] - PAD) // 2, third[3].shape[0] // 2
    top, rest = flows[0][0].shape[0] - 2 * half_b, flows[0][1].shape[0] - 2 * half_a - PAD

    def kernel(info, ka, kb, *refs):
        sa, ma, sb, mb = refs[4:]
        for section in range(2):
            along, across = refs[2 * section : 2 * section + 2]

            @pl.when(info[0] == section)
            def _():
                for own, one, two, base, new, out, half in (
                    (info[2], ka, across, rest, ma, sa, half_a),
                    (info[1], kb, along, top, mb, sb, half_b),
                ):
                    for target, part in ((new, own), (out, 1 - own)):
                        add_shifted(target, 0, one, part * half, two, base + part * half, half)
                    extra = one.shape[0] - 2 * half
                    if extra:
                        low = base + 2 * half
                        tail = plus(one[2 * half :, :], two[low : low + extra, :])
                        new[half:, :] = tail
                        out[half:, :] = tail

    outs = [shape((half_a + PAD, dim), BF)] * 2 + [shape((half_b, dim), BF)] * 2
    ins = [info, third[1], third[3]] + [a for f in flows for a in f]
    return vmem_call(kernel, outs, ins, "third_sum", after)


def group_sum(section, info, kept, came, given, after):
    rows = [a.shape[0] for a in kept]
    given = list(given or [])

    def kernel(info, ka, kb, ra, rb, *refs):
        outs = refs[len(given) :]
        keep_given(info[0] == section, refs[: len(given)], outs)

        @pl.when(info[0] == section)
        def _():
            pieces = [(0, ka, ra, 0, 0, rows[0]), (rows[0], kb, rb, 0, 0, rows[1])]
            sum_pieces(info, outs, pieces, sum(rows))

    outs = split_shapes(sum(rows), kept[0].shape[1])
    ins = [info] + list(kept) + list(came) + given
    aliases = {5 + i: i for i in range(len(given))}
    return call(kernel, outs, ins, [], 0, aliases, "group_sum", after, 10)


def last_sum(info, kept, came, after):
    rows = [a.shape[0] for a in kept]

    def kernel(info, ka, kb, ra, rb, *outs):
        pieces = [(0, ka, ra, 0, 0, rows[0]), (rows[0], kb, rb, 0, 0, rows[1])]
        sum_pieces(info, outs, pieces, sum(rows))

    outs = split_shapes(sum(rows), kept[0].shape[1])
    return vmem_call(kernel, outs, [info] + list(kept) + list(came), "last_sum", after)


def trade(part, bit):
    return lax.ppermute(part, "replica", [(r, r ^ bit) for r in range(REPLICAS)])


def replica_sum(info, sets, came):
    quarters = [s[1].shape[0] // 2 for s in sets]
    starts = [sum(quarters[:i]) for i in range(len(sets))]
    rows, dim = sum(quarters), sets[0][1].shape[1]

    def halve(info, *refs):
        send, keep = refs[2 * len(sets) :]
        high = info[3] // 2
        for i, (size, at) in enumerate(zip(quarters, starts)):
            one, two = refs[2 * i : 2 * i + 2]
            for out, part in ((send, 1 - high), (keep, high)):
                add_shifted(out, at, one, part * size, two, part * size, size)

    def total(one, two, out):
        add_rows(out, 0, one, two, 0, rows)

    def double(info, one, two, out):
        high = info[3] // 2
        for size, at in zip(quarters, starts):
            copy_rows(out, 2 * at + high * size, one, at, size)
            copy_rows(out, 2 * at + (1 - high) * size, two, at, size)

    ins = [info] + [a for s, c in zip(sets, came) for a in (s[1], c)]
    send, keep = vmem_call(halve, [shape((rows, dim), BF)] * 2, ins, "halve", None)
    ins = [keep, trade(send, 2)]
    own = vmem_call(total, [shape((rows, dim), BF)], ins, "total", None)[0]
    ins = [info, own, trade(own, 2)]
    half = vmem_call(double, [shape((2 * rows, dim), BF)], ins, "double", None)[0]
    return half, trade(half, 1)


def own_pieces(row, count, width, group):
    share = count * width // GROUPS
    at, pieces = group * share, []
    while at < (group + 1) * share:
        size = min((group + 1) * share - at, width - at % width)
        pieces.append((row + at // width, at % width, size, at - group * share))
        at += size
    return pieces


def finish(info, given, sizes, after):
    dim = given[0].shape[1]
    share = dim // GROUPS
    half = 3 * share // 2
    top = dim + 5 * share
    sides = 2 if given[0].shape[0] == sum(sizes) else 1
    base = sides * sizes[0]
    vectors = ((ROW_QKV, 3), (ROW_OUT, 1), (ROW_UP, 4), (ROW_DOWN, 1))
    outs = [
        shape((dim, dim), F32),
        shape((share, 4 * dim), F32),
        shape((share, dim), F32),
        shape((share, 3 * dim), F32),
    ]
    large = len(outs)
    outs += [shape((1, count * dim // GROUPS), F32) for _, count in vectors]
    outs += [shape((2, share), F32)] * 2

    def kernel(info, *refs):
        given, refs = refs[:2], refs[2:]
        out_h = refs[:large]
        small = refs[large : len(outs)]
        src = refs[len(outs)]
        stage = refs[len(outs) + 1 : -1]
        sems = refs[-1]
        pieces = [(0, given[0], 0, sizes[0], 0), (1, given[1], 0, sizes[1], base)]
        if sides == 2:
            pieces = [
                (2 * k + i, part, i * sizes[0], sizes[i], i * base)
                for k, part in enumerate(given)
                for i in range(2)
            ]
        for low in range(sides):

            @pl.when(info[3] % 2 == low if sides > 1 else info[3] >= 0)
            def _():
                for n, part, row, size, to in pieces:
                    at = to + (low + n // 2) % sides * size
                    lines = part.at[pl.ds(row, size)]
                    pltpu.make_async_copy(lines, src.at[pl.ds(at, size)], sems.at[n]).start()

        for n, part, row, size, to in pieces:
            lines = part.at[pl.ds(row, size)]
            pltpu.make_async_copy(lines, src.at[pl.ds(to, size)], sems.at[n]).wait()
        copies = []

        def save(i):
            copy = pltpu.make_async_copy(stage[i], out_h[i], sems.at[4 + i])
            copy.start()
            copies.append(copy)

        stage[0][...] = src[:dim, :].astype(F32)
        save(0)
        for i in range(4):
            block = src[dim + i * share : dim + (i + 1) * share, :].astype(F32)
            stage[1][:, i * dim : (i + 1) * dim] = block
        save(1)
        for i in range(3):
            at, left, to = i * share, share, 0
            while left:
                count = min(left, half - at % half)
                row = base + (at if at < half else at + PAD)
                block = src[row : row + count, :].astype(F32)
                stage[3][to : to + count, i * dim : (i + 1) * dim] = block
                at, left, to = at + count, left - count, to + count
        save(3)
        stage[2][...] = src[dim + 4 * share : top, :].astype(F32)
        save(2)
        tail = src[base + half : base + half + PAD, :].astype(F32)
        for group in range(GROUPS):

            @pl.when(info[1] + 2 * info[2] == group)
            def _():
                for out, (row, count) in zip(small, vectors):
                    for r, c, size, at in own_pieces(row, count, dim, group):
                        out[:, at : at + size] = tail[r : r + 1, c : c + size]
                for out, row in zip(small[4:], (ROW_GAIN, ROW_SHIFT)):
                    out[...] = tail[row : row + 2, group * share : (group + 1) * share]

        for copy in copies:
            copy.wait()

    scratch = [pltpu.VMEM((base + sides * sizes[1], dim), BF)]
    scratch += [vmem_like(o) for o in outs[:large]]
    places = "h" * large + "v" * (len(outs) - large)
    ins = [info] + list(given)
    return call(
        kernel, outs, ins, scratch, 8, {}, "finish", after, 16, "saa", places
    )


def flow(shard, axis, pairs, sections):
    if sections == (0, 1):
        return lax.ppermute(shard, axis, pairs)
    peers = lax.axis_size(axis)
    pairs = [(s * peers + i, s * peers + j) for s in sections for i, j in pairs]
    return lax.ppermute(shard, ("section", axis), pairs)


ACROSS = [(g, g ^ 1) for g in range(GROUPS)]
ALONG = [(g, g ^ 2) for g in range(GROUPS)]
BOTH = (0, 1)


def exchange(a, b, turned, sections):
    ways = (ALONG, ACROSS) if turned else (ACROSS, ALONG)
    return flow(a, "group", ways[0], sections), flow(b, "group", ways[1], sections)


def shards(
    block_input,
    cotangent,
    crop_count,
    mask_count,
    qkv_weight,
    qkv_bias,
    out_weight,
    out_bias,
    up_weight,
    up_bias,
    down_weight,
    down_bias,
    norm_gain,
    norm_shift,
):
    params = (
        qkv_weight[0],
        qkv_bias,
        out_weight[0],
        out_bias,
        up_weight[0],
        up_bias,
        down_weight[0],
        down_bias,
        norm_gain[0],
        norm_shift[0],
    )
    rows, dim = block_input.shape
    tab = jnp.asarray(rotary_tables())
    tab_t = jnp.asarray(rotary_columns())
    group = lax.axis_index("group")
    assert lax.axis_size("group") == GROUPS
    info = jnp.stack([lax.axis_index("section"), group % 2, group // 2, lax.axis_index("replica")])

    def to_other(shard, pairs):
        return lax.ppermute(shard, "section", pairs)

    act, first = forward(0, info, crop_count, block_input, None, params, tab, None)
    arrived = [to_other(first[0], [(0, 1)])]
    act, second = forward(1, info, crop_count, block_input, arrived[0], params, tab, act)
    arrived.append(to_other(second[0], [(0, 1)]))
    act, third = forward(2, info, crop_count, block_input, arrived[1], params, tab, act)
    kept_one, kept_zero = (second, third), (first, second)

    common = (info, crop_count, mask_count)
    one, gmid, small, last = mlp_grad(1, *common, cotangent, kept_one, params, None)
    came = exchange(one[0], one[2], False, (1,))
    dx, kept, last = attention_grad(
        1, info, gmid, small, arrived, kept_one, params, tab_t, None, last
    )
    grad_back = to_other(dx, [(1, 0)])
    third, last = qkv_grad(1, info, kept, None, last)
    one = first_sum(1, info, one, came, third, last)
    came_one = exchange(one[0], one[2], True, (1,))
    zero, gmid, small, last = mlp_grad(0, *common, grad_back, kept_zero, params, one[1])
    came = exchange(zero[0], zero[2], False, (0,))
    sums = group_sum(1, info, (one[1], one[3]), came_one, None, last)
    dx, kept, last = attention_grad(
        0, info, gmid, small, [block_input], kept_zero, params, tab_t, dx, sums[-1]
    )
    third, last = qkv_grad(0, info, kept, third, last)
    zero = first_sum(0, info, zero, came, third, last)
    came_zero = exchange(zero[0], zero[2], True, (0,))
    sums = group_sum(0, info, (zero[1], zero[3]), came_zero, sums, zero[1])
    pairs = len(sums) == 2
    came_mlp = trade(sums[0], 1) if pairs else None
    send_a, keep_a, send_b, keep_b = third_sum(info, (came_zero, came_one), third, sums[-1])
    came = exchange(send_a, send_b, True, BOTH)
    thirds = last_sum(info, (keep_a, keep_b), came, keep_a)
    if pairs:
        given = replica_sum(info, (sums, thirds), (came_mlp, trade(thirds[0], 1)))
    else:
        given = [lax.psum(part, "replica") for part in (sums[0], thirds[0])]
    sizes = (sums[-1].shape[0], thirds[-1].shape[0])
    grad_down, grad_up, grad_out, grad_qkv, *small = finish(info, given, sizes, None)
    qkv_b, out_b, up_b, down_b, gain, shift = small
    return (
        act[None],
        dx[None],
        grad_qkv[None],
        qkv_b,
        grad_out[None],
        out_b,
        grad_up[None],
        up_b,
        grad_down[None],
        down_b,
        gain[None],
        shift[None],
    )


def solution(mesh):
    rows = P(("group", "replica"))
    stack = P("section")
    return jax.shard_map(
        shards,
        mesh=mesh,
        in_specs=(rows,) * 4 + (stack,) * 10,
        out_specs=(
            P("section", ("group", "replica"), None),
            P("section", ("group", "replica"), None),
            P("section", "group", None),
            P("section", "group"),
            P("section", "group", None),
            P("section", "group"),
            P("section", "group", None),
            P("section", "group"),
            P("section", "group", None),
            P("section", "group"),
            P("section", None, "group"),
            P("section", None, "group"),
        ),
        check_vma=False,
    )
```

```python
import jax
import jax.numpy as jnp
import numpy as np
from jax import lax
from jax.experimental import pallas as pl
from jax.experimental.pallas import tpu as pltpu
from jax.sharding import PartitionSpec as P

HEADS = 20
HEAD_DIM = 32
LEN = 256
MASK_MEAN = 38
CROP_DEV = 2
EPSILON = 1e-05
ROTARY_BASE = 10000.0

BF = jnp.bfloat16
F32 = jnp.float32
NN = (((1,), (0,)), ((), ()))
NT = (((1,), (1,)), ((), ()))
TN = (((0,), (0,)), ((), ()))

FIRST_LIMIT, FORWARD_LIMIT, DOWN_LIMIT, UP_LIMIT, ATTENTION_LIMIT = 40, 24, 12, 20, 24
GROUPS = 4
PAD = 16
ROW_QKV, ROW_OUT, ROW_UP, ROW_DOWN, ROW_GAIN, ROW_SHIFT = 0, 3, 4, 8, 9, 11

ANY = pl.BlockSpec(memory_space=pl.ANY)
HBM = pl.BlockSpec(memory_space=pltpu.HBM)
VMEM = pl.BlockSpec(memory_space=pltpu.VMEM)
SMEM = pl.BlockSpec(memory_space=pltpu.SMEM)


def shape(dims, dtype):
    return jax.ShapeDtypeStruct(dims, dtype)


def mm(left, right, dims=NN):
    return lax.dot_general(left, right, dims, preferred_element_type=F32)


def unit_rows_of(values):
    centred = values - jnp.mean(values, axis=-1, keepdims=True)
    inverse = lax.rsqrt(jnp.mean(centred * centred, axis=-1, keepdims=True) + EPSILON)
    return centred * inverse, inverse


def norm_back(grad, unit, inverse, gain):
    scaled = grad * gain
    return inverse * (
        scaled
        - jnp.mean(scaled, axis=-1, keepdims=True)
        - unit * jnp.mean(scaled * unit, axis=-1, keepdims=True)
    )


def rotary_tables():
    lane = np.arange(128) % HEAD_DIM
    half = HEAD_DIM // 2
    freq = ROTARY_BASE ** (-(lane % half).astype(np.float64) * (2.0 / HEAD_DIM))
    angles = np.arange(LEN)[:, None] * freq[None, :]
    sign = np.where(lane < half, -1.0, 1.0)[None, :]
    return np.stack([np.cos(angles), np.sin(angles) * sign]).astype(np.float32)


def rotary_columns():
    half = HEAD_DIM // 2
    freq = ROTARY_BASE ** (-np.arange(half, dtype=np.float64) * (2.0 / HEAD_DIM))
    angles = freq[:, None] * np.arange(LEN)[None, :]
    return np.stack([np.cos(angles), np.sin(angles)]).astype(np.float32)


def swap_halves(values):
    lane = lax.broadcasted_iota(jnp.int32, values.shape, 1) % HEAD_DIM
    half = HEAD_DIM // 2
    return jnp.where(
        lane < half,
        pltpu.roll(values, 128 - half, axis=1),
        pltpu.roll(values, half, axis=1),
    )


def head_stack(block, per):
    head = lax.broadcasted_iota(jnp.int32, block.shape, 1) // HEAD_DIM
    return jnp.concatenate(
        [jnp.where(head == h, block, jnp.zeros_like(block)) for h in range(per)], axis=0
    )


class Copies:
    def __init__(self, sems):
        self.sems = sems
        self.used = 0
        self.open = []

    def start(self, src, dst):
        copy = pltpu.make_async_copy(src, dst, self.sems.at[self.used])
        self.used += 1
        copy.start()
        return copy

    def save(self, src, dst):
        self.open.append(self.start(src, dst))

    def finish(self):
        for copy in self.open:
            copy.wait()


def call(kernel, outs, ins, scratch, sems, aliases, name, after=None, limit=16, spaces=None, out_spaces=None):
    count = len(ins)
    places = {"v": VMEM, "h": HBM, "a": ANY, "s": SMEM}
    spaces = spaces or "v" * count
    out_spaces = out_spaces or "v" * len(outs)
    in_specs = [SMEM if a.ndim == 1 else places[p] for a, p in zip(ins, spaces)]
    ins = [pltpu.with_memory_space_constraint(a, pltpu.HBM) if p == "h" else a for a, p in zip(ins, spaces)]
    body = kernel
    if after is not None:
        ins = list(ins) + [after]
        in_specs = in_specs + [ANY]

        def body(*refs):
            kernel(*refs[:count], *refs[count + 1 :])

    outs = [pltpu.HBM(o.shape, o.dtype) if p == "h" else o for o, p in zip(outs, out_spaces)]
    return pl.pallas_call(
        body,
        out_shape=outs,
        in_specs=in_specs,
        out_specs=[places[p] for p in out_spaces],
        scratch_shapes=scratch + ([pltpu.SemaphoreType.DMA((sems,))] if sems else []),
        input_output_aliases=aliases,
        compiler_params=pltpu.CompilerParams(vmem_limit_bytes=limit << 20),
        name=name,
    )(*ins)


TOKEN = jax.ShapeDtypeStruct((8, 128), F32)


def vmem_like(arr):
    return pltpu.VMEM(arr.shape, arr.dtype)


def forward(slot, info, live, own, arrived, params, tab, act, after=None):
    qkvw, qkvb, outw, outb, upw, upb, downw, downb, gain, shift = params
    dim = own.shape[1]
    blocks = dim // 128
    wide = upw.shape[1]
    parts = wide // dim
    per = 128 // HEAD_DIM
    manual = slot == 0
    saved = [
        shape((LEN, dim), BF),
        shape((LEN, 3 * dim), BF),
        shape((HEADS, LEN, LEN), BF),
        shape((dim, LEN), BF),
        shape((LEN, dim), F32),
        shape((LEN, wide), BF),
        shape((LEN, wide), BF),
    ]
    weights = [qkvb, outb, upb, downb, gain, shift, tab, qkvw, outw, upw, downw]
    sources = [own] if slot == 0 else [arrived] if slot == 2 else [own, arrived]
    before = [] if act is None else [act]
    ins = [info, live] + sources + weights + before
    count = len(sources)

    def kernel(info, live, *refs):
        xs = refs[:count]
        given = refs[count : count + 11]
        act_h, *outs = refs[count + 11 + len(before) : count + 19 + len(before)]
        scratch = refs[count + 19 + len(before) :]
        act_s, vt_s, score_s, up_s = scratch[:4]
        sems = scratch[-1]
        y_s, qkv_s, prob_s, mixt_s, mid_s, gp_s, hid_s = outs
        used = scratch[4:-1] if manual else xs[-1:] + given
        qkvb, outb, upb, downb, gain, shift, tab, qkvw, outw, upw, downw = used[1:]
        crop = slot - info[0]

        @pl.when(jnp.logical_and(crop >= 0, crop < CROP_DEV))
        def _():
            copies = Copies(sems)
            heavy = []
            if manual:
                rows = xs[0].at[pl.ds(0, LEN)]
                loads = [copies.start(h, s) for h, s in zip((rows,) + given, used)]
                heavy = loads[8:]
                wait_all(loads[:8])
                x = used[0][...].astype(F32)
            elif slot == 1:
                x = jnp.where(info[0] == 0, xs[0][LEN:, :], xs[1][...]).astype(F32)
            else:
                x = xs[0][...].astype(F32)

            def ready(index):
                if manual:
                    heavy[index].wait()

            unit, _ = unit_rows_of(x)
            normed = (unit * gain[0:1, :] + shift[0:1, :]).astype(BF)
            ready(0)
            third = mm(normed, qkvw[:, 2 * dim :]) + qkvb[:, 2 * dim :]
            low = third.astype(BF)
            qkv_s[:, 2 * dim :] = low
            vt_s[...] = low.T
            for part in range(2):
                third = mm(normed, qkvw[:, part * dim : (part + 1) * dim])
                third = third + qkvb[:, part * dim : (part + 1) * dim]
                for j in range(blocks):
                    b = third[:, 128 * j : 128 * j + 128]
                    b = b * tab[0] + swap_halves(b) * tab[1]
                    if part == 0:
                        b = b * HEAD_DIM**-0.5
                    at = part * dim + 128 * j
                    qkv_s[:, at : at + 128] = b.astype(BF)
            for j in range(blocks):
                q = qkv_s[:, 128 * j : 128 * j + 128]
                k = qkv_s[:, dim + 128 * j : dim + 128 * j + 128]
                score_s[per * LEN * j : per * LEN * (j + 1), :] = mm(head_stack(k, per), q, NT)

            def soft(h, _):
                s = score_s[pl.ds(pl.multiple_of(h * LEN, LEN), LEN), :]
                e = jnp.exp(s - jnp.max(s, axis=0, keepdims=True))
                prob_s[h] = (e * (1.0 / jnp.sum(e, axis=0, keepdims=True))).astype(BF)
                return 0

            lax.fori_loop(0, HEADS, soft, 0, unroll=2)
            for h in range(HEADS):
                at = slice(HEAD_DIM * h, HEAD_DIM * (h + 1))
                mixt_s[at, :] = mm(vt_s[at, :], prob_s[h]).astype(BF)
            ready(1)
            mid = x + mm(mixt_s[...], outw[...], TN) + outb[...]
            mid_s[...] = mid
            unit, _ = unit_rows_of(mid)
            normed = (unit * gain[1:2, :] + shift[1:2, :]).astype(BF)
            ready(2)
            up_s[...] = mm(normed, upw[...])
            for c in range(parts):
                cols = slice(c * dim, (c + 1) * dim)
                u = up_s[:, cols] + upb[:, cols]
                cdf = 0.5 + 0.5 * lax.erf(u * 0.5**0.5)
                hid_s[:, cols] = (u * cdf).astype(BF)
                gp_s[:, cols] = (
                    cdf + u * (jnp.exp(u * u * -0.5) * (2 * np.pi) ** -0.5)
                ).astype(BF)
            ready(3)
            low = (mid_s[...] + downb[...] + mm(hid_s[...], downw[...])).astype(BF)
            y_s[...] = low
            act_s[...] = jnp.where(crop < live[0], low, jnp.zeros_like(low))
            at = pl.multiple_of(crop * LEN, LEN)
            copies.save(act_s, act_h.at[pl.ds(at, LEN)])
            copies.finish()

    outs = [shape(own.shape, BF)] + saved
    scratch = [
        pltpu.VMEM((LEN, dim), BF),
        pltpu.VMEM((dim, LEN), BF),
        pltpu.VMEM((HEADS * LEN, LEN), F32),
        pltpu.VMEM((LEN, wide), F32),
    ]
    if manual:
        scratch += [pltpu.VMEM((LEN, dim), BF)] + [vmem_like(a) for a in weights]
    aliases = {} if act is None else {len(ins) - 1: 0}
    spaces = "ss" + ("h" if manual else "v") * (count + 11) + "h" * len(before)
    out = call(
        kernel,
        outs,
        ins,
        scratch,
        16,
        aliases,
        "layer_forward",
        after,
        FIRST_LIMIT if manual else FORWARD_LIMIT,
        spaces,
        "h" + "v" * 7,
    )
    return out[0], out[1:]


def gradient_rows(g, live, masks, section):
    grad = g.astype(F32)
    if section == 0:
        return grad
    crop = lax.broadcasted_iota(jnp.int32, (g.shape[0], 1), 0) // LEN
    weight = jnp.zeros_like(crop)
    for c in range(CROP_DEV):
        weight = jnp.where(crop == c, masks[c], weight)
    weight = jnp.where(crop < live[0], weight, 0)
    return grad * (weight.astype(F32) / MASK_MEAN)


def lay_out(info, bufs, block, pieces):
    send_a, keep_a, send_b, keep_b = bufs
    half_rows = send_b.shape[0] // 2
    for row, count, shard, is_b, at in pieces:
        x, y = shard % 2, shard // 2
        own, index, keep, send = (
            (info[2] == y, x, keep_b, send_b) if is_b else (info[1] == x, y, keep_a, send_a)
        )
        start = index * half_rows + at

        @pl.when(own)
        def _():
            keep[start : start + count, :] = block[row : row + count, :]

        @pl.when(jnp.logical_not(own))
        def _():
            send[start : start + count, :] = block[row : row + count, :]


def keep_given(active, given, bufs):
    @pl.when(jnp.logical_not(active))
    def _():
        for old, new in zip(given, bufs):
            new[...] = old[...]


def quarters(block, dim, parts):
    count = dim // parts
    return [(s * count, count, s, block >= 2, (block % 2) * count) for s in range(parts)]


def buffer_shapes(dim):
    return [shape((dim + PAD, dim), BF)] * 2 + [shape((dim, dim), BF)] * 2


def joined(refs, cols):
    return jnp.concatenate([r[:, cols] for r in refs], axis=0)


def wait_all(copies):
    for copy in copies:
        copy.wait()


def down_grad(section, info, live, masks, g, saved, before, after):
    hids = [s[6] for s in saved]
    rows, dim = g.shape
    parts = hids[0].shape[1] // dim
    given = [] if before is None else list(before)
    ins = [info, live, masks, g] + hids + given

    def kernel(info, live, masks, g_s, *refs):
        hid_s = refs[: len(hids)]
        old = refs[len(hids) : len(hids) + len(given)]
        bufs = refs[len(hids) + len(given) : len(hids) + len(given) + 4]
        (block_s,) = refs[len(hids) + len(given) + 5 :]
        keep_given(info[0] == section, old, bufs)

        @pl.when(info[0] == section)
        def _():
            low = gradient_rows(g_s[...], live, masks, section).astype(BF)
            for c in range(parts):
                cols = slice(c * dim, (c + 1) * dim)
                block_s[c] = mm(joined(hid_s, cols), low, TN).astype(BF)
            half = dim // 2
            for c in range(parts):
                pieces = [(0, half, c, False, 0), (half, half, c, True, 0)]
                lay_out(info, bufs, block_s.at[c], pieces)

    scratch = [pltpu.VMEM((parts, dim, dim), BF)]
    aliases = {len(ins) - 4 + i: i for i in range(4)} if given else {}
    outs = buffer_shapes(dim) + [TOKEN]
    out = call(kernel, outs, ins, scratch, 0, aliases, "down_grad", after, DOWN_LIMIT)
    return out[:4], out[4]


def up_grad(section, info, live, masks, g, saved, params, before, after):
    mids, gps = [s[4] for s in saved], [s[5] for s in saved]
    upw, downw, gain, shift = params[4], params[6], params[8], params[9]
    rows, dim = g.shape
    wide = upw.shape[1]
    parts = wide // dim
    crops = len(saved)
    given = [] if before is None else list(before)
    ins = [info, live, masks, g, gain, shift, downw, upw] + mids + gps + given

    def kernel(info, live, masks, g_s, gain, shift, downw, upw, *refs):
        mid_s, gp_s = refs[:crops], refs[crops : 2 * crops]
        old = refs[2 * crops : 2 * crops + len(given)]
        refs = refs[2 * crops + len(given) :]
        bufs, gmid_s, small_s = refs[:4], refs[4], refs[5]
        gu_s, block_s = refs[7:]
        keep_given(info[0] == section, old, bufs)

        @pl.when(info[0] == section)
        def _():
            grad = gradient_rows(g_s[...], live, masks, section)
            low = grad.astype(BF)
            small_s[...] = jnp.zeros_like(small_s)
            small_s[ROW_DOWN : ROW_DOWN + 1, :] = jnp.sum(low.astype(F32), axis=0, keepdims=True)
            unit, inverse = unit_rows_of(joined(mid_s, slice(None)))
            normed_t = (unit * gain[1:2, :] + shift[1:2, :]).astype(BF).T
            for c in range(parts):
                cols = slice(c * dim, (c + 1) * dim)
                grad_up = mm(low, downw[cols, :], NT) * joined(gp_s, cols).astype(F32)
                grad_up = grad_up.astype(BF)
                gu_s[:, cols] = grad_up
                small_s[ROW_UP + c : ROW_UP + c + 1, :] = jnp.sum(
                    grad_up.astype(F32), axis=0, keepdims=True
                )
            back = mm(gu_s[...], upw[...], NT)
            gmid_s[...] = grad + norm_back(back, unit, inverse, gain[1:2, :])
            small_s[ROW_GAIN + 1 : ROW_GAIN + 2, :] = jnp.sum(back * unit, axis=0, keepdims=True)
            small_s[ROW_SHIFT + 1 : ROW_SHIFT + 2, :] = jnp.sum(back, axis=0, keepdims=True)
            for c in range(parts):
                block_s[c] = mm(normed_t, gu_s[:, c * dim : (c + 1) * dim]).astype(BF)
            for c in range(parts):
                lay_out(info, bufs, block_s.at[c], quarters(c, dim, parts))

    scratch = [pltpu.VMEM((rows, wide), BF), pltpu.VMEM((parts, dim, dim), BF)]
    aliases = {len(ins) - 4 + i: i for i in range(4)} if given else {}
    outs = buffer_shapes(dim) + [shape((rows, dim), F32), shape((PAD, dim), F32), TOKEN]
    out = call(kernel, outs, ins, scratch, 0, aliases, "up_grad", after, UP_LIMIT)
    return out[:4], out[4], out[5], out[6]


def rotate_back(block, tab_t):
    half = HEAD_DIM // 2
    cos, sin = tab_t[0], tab_t[1]
    out = []
    for at in range(0, block.shape[0], HEAD_DIM):
        a, b = block[at : at + half], block[at + half : at + HEAD_DIM]
        out += [a * cos + b * sin, b * cos - a * sin]
    return jnp.concatenate(out, axis=0)


def attention_grad(section, info, gmid, small, xs, saved, params, tab_t, before, after):
    qkvs, probs, mixts = [s[1] for s in saved], [s[2] for s in saved], [s[3] for s in saved]
    qkvw, outw, gain, shift = params[0], params[2], params[8], params[9]
    rows, dim = gmid.shape
    blocks = dim // 128
    per = 128 // HEAD_DIM
    crops = len(saved)
    given = [] if before is None else [before]
    ins = [info, gmid, outw, small, gain, shift, tab_t, qkvw]
    ins += qkvs + probs + mixts + list(xs) + given

    def kernel(info, gmid_s, outw, small_s, gain, shift, tab_t, qkvw, *refs):
        qkv_s, prob_s, mixt_s = (refs[i * crops : (i + 1) * crops] for i in range(3))
        x_s = refs[3 * crops : 3 * crops + len(xs)]
        old = refs[3 * crops + len(xs) : 3 * crops + len(xs) + len(given)]
        refs = refs[3 * crops + len(xs) + len(given) :]
        keep_given(info[0] == section, old, refs[:1])
        dx_s, gqkv_s, normt_s, low_s, small_out = refs[:5]
        gmt_s, delta_s, da_s, ds_s, dt_s, kt_s = refs[6:]

        @pl.when(info[0] == section)
        def _():
            low = gmid_s[...].astype(BF)
            low_s[...] = low
            gmt_s[...] = mm(outw[...], low, NT).astype(BF)
            for c in range(crops):
                crop = slice(c * LEN, (c + 1) * LEN)
                qkv, prob = qkv_s[c], prob_s[c]
                product = gmt_s[:, crop].astype(F32) * mixt_s[c][...].astype(F32)
                delta_s[...] = jnp.sum(product.reshape(HEADS, HEAD_DIM, LEN), axis=1)[:, None, :]
                kt_s[0] = qkv[:, dim : 2 * dim].T
                kt_s[1] = qkv[:, :dim].T
                for j in range(blocks):
                    v = qkv[:, 2 * dim + 128 * j : 2 * dim + 128 * j + 128]
                    da_s[per * LEN * j : per * LEN * (j + 1), :] = mm(
                        head_stack(v, per), gmt_s[128 * j : 128 * j + 128, crop]
                    )

                def scores(h, _):
                    da = da_s[pl.ds(pl.multiple_of(h * LEN, LEN), LEN), :]
                    ds_s[h] = (prob[h].astype(F32) * (da - delta_s[h])).astype(BF)
                    return 0

                lax.fori_loop(0, HEADS, scores, 0, unroll=2)
                for h in range(HEADS):
                    at = slice(HEAD_DIM * h, HEAD_DIM * (h + 1))
                    dt_s[0, at, :] = mm(kt_s[0, at, :], ds_s[h])
                    dt_s[1, at, :] = mm(kt_s[1, at, :], ds_s[h], NT)
                    dt_s[2, at, :] = mm(gmt_s[at, crop], prob[h], NT)
                dq = rotate_back(dt_s[0] * HEAD_DIM**-0.5, tab_t)
                gqkv_s[crop, :dim] = dq.astype(BF).T
                gqkv_s[crop, dim : 2 * dim] = rotate_back(dt_s[1], tab_t).astype(BF).T
                gqkv_s[crop, 2 * dim :] = dt_s[2].astype(BF).T
            unit, inverse = unit_rows_of(joined(x_s, slice(None)).astype(F32))
            normt_s[...] = (unit * gain[0:1, :] + shift[0:1, :]).astype(BF).T
            back = mm(gqkv_s[...], qkvw[...], NT)
            dx_s[...] = (gmid_s[...] + norm_back(back, unit, inverse, gain[0:1, :])).astype(BF)
            small_out[...] = small_s[...]
            small_out[ROW_GAIN : ROW_GAIN + 1, :] = jnp.sum(back * unit, axis=0, keepdims=True)
            small_out[ROW_SHIFT : ROW_SHIFT + 1, :] = jnp.sum(back, axis=0, keepdims=True)

    outs = [
        shape((rows, dim), BF),
        shape((rows, 3 * dim), BF),
        shape((dim, rows), BF),
        shape((rows, dim), BF),
        shape(small.shape, F32),
        TOKEN,
    ]
    scratch = [
        pltpu.VMEM((dim, rows), BF),
        pltpu.VMEM((HEADS, 1, LEN), F32),
        pltpu.VMEM((HEADS * LEN, LEN), F32),
        pltpu.VMEM((HEADS, LEN, LEN), BF),
        pltpu.VMEM((3, dim, LEN), F32),
        pltpu.VMEM((2, dim, LEN), BF),
    ]
    aliases = {len(ins) - 1: 0} if given else {}
    out = call(kernel, outs, ins, scratch, 0, aliases, "attention_grad", after, ATTENTION_LIMIT)
    return out[0], out[1:5], out[5]


def qkv_grad(section, info, kept, saved, after):
    gqkv, normt, low, small = kept
    mixts = [s[3] for s in saved]
    rows, dim = low.shape
    parts = 4
    ins = [info, gqkv, normt, low, small] + mixts

    def kernel(info, gqkv_s, normt_s, low_s, small_s, *refs):
        mixt_s = refs[: len(mixts)]
        bufs = refs[len(mixts) : len(mixts) + 4]
        (block_s,) = refs[len(mixts) + 5 :]

        @pl.when(info[0] == section)
        def _():
            sums = [
                jnp.sum(gqkv_s[:, c * dim : (c + 1) * dim].astype(F32), axis=0, keepdims=True)
                for c in range(3)
            ]
            sums.append(jnp.sum(low_s[...].astype(F32), axis=0, keepdims=True))
            tail = jnp.concatenate(sums + [small_s[ROW_UP:, :]], axis=0).astype(BF)
            bufs[0][dim:, :] = tail
            bufs[1][dim:, :] = tail
            for c in range(3):
                block_s[c] = mm(normt_s[...], gqkv_s[:, c * dim : (c + 1) * dim]).astype(BF)
            mixt = jnp.concatenate([m[...] for m in mixt_s], axis=1)
            block_s[3] = mm(mixt, low_s[...]).astype(BF)
            for c in range(parts):
                lay_out(info, bufs, block_s.at[c], quarters(c, dim, parts))

    scratch = [pltpu.VMEM((parts, dim, dim), BF)]
    outs = buffer_shapes(dim) + [TOKEN]
    out = call(kernel, outs, ins, scratch, 0, {}, "qkv_grad", after, DOWN_LIMIT)
    return out[:4], out[4]


def plus(one, two):
    return (one.astype(F32) + two.astype(F32)).astype(BF)


def taking_part(info, sections, middle):
    check = None
    if len(sections) == 1:
        check = info[0] == sections[0]
    if middle:
        inner = jnp.logical_or(info[3] == 1, info[3] == 2)
        check = inner if check is None else jnp.logical_and(check, inner)
    return info[3] >= 0 if check is None else check


def vmem_call(kernel, outs, info, ins, name, after):
    return call(kernel, outs, [info] + ins, [], 0, {}, name, after, 8)


def first_sum(info, sections, keep_a, recv_a, keep_b, recv_b, after):
    dim = keep_b.shape[1]
    half = dim // 2

    def kernel(info, ka, ra, kb, rb, sa, na, sb, nb):
        @pl.when(taking_part(info, sections, False))
        def _():
            for own, one, two, new, out in ((info[2], ka, ra, na, sa), (info[1], kb, rb, nb, sb)):
                mine = pl.ds(pl.multiple_of(own * half, half), half)
                other = pl.ds(pl.multiple_of((1 - own) * half, half), half)
                out[:half, :] = plus(one[other, :], two[other, :])
                new[:half, :] = plus(one[mine, :], two[mine, :])
                if one.shape[0] > 2 * half:
                    tail = plus(one[2 * half :, :], two[2 * half :, :])
                    new[half:, :] = tail
                    out[half:, :] = tail

    outs = [shape((half + PAD, dim), BF)] * 2 + [shape((half, dim), BF)] * 2
    return vmem_call(kernel, outs, info, [keep_a, recv_a, keep_b, recv_b], "first_sum", after)


def second_sum(info, sections, keep_a, recv_a, keep_b, recv_b, after):
    dim = keep_b.shape[1]

    def kernel(info, ka, ra, kb, rb, out):
        @pl.when(taking_part(info, sections, False))
        def _():
            top = ka.shape[0]
            out[:top, :] = plus(ka[...], ra[...])
            out[top:, :] = plus(kb[...], rb[...])

    outs = [shape((dim + PAD, dim), BF)]
    return vmem_call(kernel, outs, info, [keep_a, recv_a, keep_b, recv_b], "second_sum", after)[0]


def pair_sum(info, sections, one, two, after):
    def kernel(info, one, two, out):
        @pl.when(taking_part(info, sections, True))
        def _():
            out[...] = plus(one[...], two[...])

    return vmem_call(kernel, [shape(one.shape, BF)], info, [one, two], "pair_sum", after)[0]


def own_pieces(row, count, width, group):
    share = count * width // GROUPS
    at, pieces = group * share, []
    while at < (group + 1) * share:
        size = min((group + 1) * share - at, width - at % width)
        pieces.append((row + at // width, at % width, size, at - group * share))
        at += size
    return pieces


def finish(info, sources, wide, after):
    (part0, got0), (part1, got1) = sources
    rows, dim = part0.shape
    half = dim // 2
    quarter = half // 2
    vectors = ((ROW_QKV, 3), (ROW_OUT, 1), (ROW_UP, 4), (ROW_DOWN, 1))
    if wide == 0:
        outs = [shape((dim, dim), F32)]
    elif wide == 4:
        outs = [shape((quarter, 4 * dim), F32)]
    else:
        outs = [shape((quarter, 3 * dim), F32), shape((quarter, dim), F32)]
    large = len(outs)
    if wide == 3:
        outs += [shape((1, count * dim // GROUPS), F32) for _, count in vectors]
        outs += [shape((2, dim // GROUPS), F32)] * 2

    def kernel(info, p0, g0, p1, g1, *refs):
        out_h = refs[:large]
        small = refs[large : len(outs)]
        src = refs[len(outs)]
        stage = refs[len(outs) + 1 : -1]
        sems = refs[-1]
        inner = jnp.logical_or(info[3] == 1, info[3] == 2)
        for section, part, got in ((0, p0, g0), (1, p1, g1)):
            mine = info[0] == section

            @pl.when(jnp.logical_and(mine, inner))
            def _():
                pltpu.make_async_copy(part, src, sems.at[0]).start()

            @pl.when(jnp.logical_and(mine, jnp.logical_not(inner)))
            def _():
                pltpu.make_async_copy(got, src, sems.at[0]).start()

        pltpu.make_async_copy(p0, src, sems.at[0]).wait()
        block_a = src[:half, :].astype(F32)
        block_b = src[half + PAD :, :].astype(F32)
        if wide == 0:
            stage[0][:half, :] = block_a
            stage[0][half:, :] = block_b
        else:
            pieces = (block_a[:quarter], block_a[quarter:], block_b[:quarter], block_b[quarter:])
            for i in range(wide):
                stage[0][:, i * dim : (i + 1) * dim] = pieces[i]
            if wide == 3:
                stage[1][...] = pieces[3]
        copies = [
            pltpu.make_async_copy(s, o, sems.at[1 + i]) for i, (s, o) in enumerate(zip(stage, out_h))
        ]
        for copy in copies:
            copy.start()
        if wide == 3:
            tail = src[half : half + PAD, :].astype(F32)
            for group in range(GROUPS):

                @pl.when(info[1] + 2 * info[2] == group)
                def _():
                    for out, (row, count) in zip(small, vectors):
                        for r, c, size, at in own_pieces(row, count, dim, group):
                            out[:, at : at + size] = tail[r : r + 1, c : c + size]
                    share = dim // GROUPS
                    for out, row in zip(small[4:], (ROW_GAIN, ROW_SHIFT)):
                        out[...] = tail[row : row + 2, group * share : (group + 1) * share]

        for copy in copies:
            copy.wait()

    scratch = [vmem_like(part0)] + [vmem_like(o) for o in outs[:large]]
    ins = [info, part0, got0, part1, got1]
    places = "h" * large + "v" * (len(outs) - large)
    return call(kernel, outs, ins, scratch, 4, {}, "finish", after, 12, "saaaa", places)


def flow(shard, axis, pairs, sections):
    if sections == (0, 1):
        return lax.ppermute(shard, axis, pairs)
    peers = lax.axis_size(axis)
    pairs = [(s * peers + i, s * peers + j) for s in sections for i, j in pairs]
    return lax.ppermute(shard, ("section", axis), pairs)


class Reduction:
    def __init__(self, info, sections, bufs):
        self.info, self.sections, self.bufs = info, sections, bufs
        groups = range(lax.axis_size("group"))
        self.across = [(g, g ^ 1) for g in groups]
        self.along = [(g, g ^ 2) for g in groups]
        self.line = lax.axis_size("replica") == 4
        self.got = (
            flow(bufs[0], "group", self.across, sections),
            flow(bufs[2], "group", self.along, sections),
        )

    def group_two(self, after):
        send_a, keep_a, send_b, keep_b = first_sum(
            self.info, self.sections, self.bufs[1], self.got[0], self.bufs[3], self.got[1], after
        )
        self.kept = (keep_a, keep_b)
        self.got = (
            flow(send_a, "group", self.along, self.sections),
            flow(send_b, "group", self.across, self.sections),
        )
        return keep_a

    def replica_one(self, after):
        self.part = second_sum(
            self.info, self.sections, self.kept[0], self.got[0], self.kept[1], self.got[1], after
        )
        if self.line:
            self.got = flow(self.part, "replica", [(0, 1), (3, 2)], self.sections)
        else:
            self.part = self.got = lax.psum(self.part, "replica")
        return self.part

    def replica_next(self, pairs, after):
        if self.line:
            self.part = pair_sum(self.info, self.sections, self.part, self.got, after)
            self.got = flow(self.part, "replica", pairs, self.sections)
        return self.part

    def replica_two(self, after):
        return self.replica_next([(1, 2), (2, 1)], after)

    def replica_three(self, after):
        return self.replica_next([(1, 0), (2, 3)], after)


def shards(
    block_input,
    cotangent,
    crop_count,
    mask_count,
    qkv_weight,
    qkv_bias,
    out_weight,
    out_bias,
    up_weight,
    up_bias,
    down_weight,
    down_bias,
    norm_gain,
    norm_shift,
):
    params = (
        qkv_weight[0],
        qkv_bias,
        out_weight[0],
        out_bias,
        up_weight[0],
        up_bias,
        down_weight[0],
        down_bias,
        norm_gain[0],
        norm_shift[0],
    )
    rows, dim = block_input.shape
    tab = jnp.asarray(rotary_tables())
    tab_t = jnp.asarray(rotary_columns())
    group = lax.axis_index("group")
    assert lax.axis_size("group") == GROUPS
    info = jnp.stack([lax.axis_index("section"), group % 2, group // 2, lax.axis_index("replica")])

    def to_other(shard, pairs):
        return lax.ppermute(shard, "section", pairs)

    act, first = forward(0, info, crop_count, block_input, None, params, tab, None)
    arrived = [to_other(first[0], [(0, 1)])]
    act, second = forward(1, info, crop_count, block_input, arrived[0], params, tab, act)
    arrived.append(to_other(second[0], [(0, 1)]))
    act, third = forward(2, info, crop_count, block_input, arrived[1], params, tab, act)
    kept_one, kept_zero = (second, third), (first, second)

    common = (info, crop_count, mask_count)
    bufs, last = down_grad(1, *common, cotangent, kept_one, None, None)
    one = Reduction(info, (1,), bufs)
    bufs, gmid, small, last = up_grad(1, *common, cotangent, kept_one, params, None, last)
    two = Reduction(info, (1,), bufs)
    dx, kept, last = attention_grad(
        1, info, gmid, small, arrived, kept_one, params, tab_t, None, last
    )
    grad_back = to_other(dx, [(1, 0)])
    bufs_three, last = qkv_grad(1, info, kept, kept_one, last)
    last = one.group_two(last)
    last = two.group_two(last)
    bufs, last = down_grad(0, *common, grad_back, kept_zero, bufs_three, last)
    three = Reduction(info, (0, 1), bufs)
    bufs, gmid, small, last = up_grad(0, *common, grad_back, kept_zero, params, None, last)
    four = Reduction(info, (0,), bufs)
    last = one.replica_one(last)
    last = two.replica_one(last)
    dx, kept, last = attention_grad(
        0, info, gmid, small, [block_input], kept_zero, params, tab_t, dx, last
    )
    last = one.replica_two(last)
    last = two.replica_two(last)
    last = three.group_two(last)
    last = four.group_two(last)
    bufs, last = qkv_grad(0, info, kept, kept_zero, last)
    five = Reduction(info, (0,), bufs)
    last = one.replica_three(last)
    last = two.replica_three(last)
    last = three.replica_one(last)
    last = four.replica_one(last)
    last = five.group_two(last)
    last = three.replica_two(last)
    last = four.replica_two(last)
    last = five.replica_one(last)
    last = three.replica_three(last)
    last = four.replica_three(last)
    last = five.replica_two(last)

    def both(zero, one):
        return ((zero.part, zero.got), (one.part, one.got))

    (grad_down,) = finish(info, both(three, one), 0, last)
    (grad_up,) = finish(info, both(four, two), 4, grad_down)
    last = five.replica_three(grad_up)
    grad_qkv, grad_out, *small = finish(info, both(five, three), 3, last)
    qkv_b, out_b, up_b, down_b, gain, shift = small
    return (
        act[None],
        dx[None],
        grad_qkv[None],
        qkv_b,
        grad_out[None],
        out_b,
        grad_up[None],
        up_b,
        grad_down[None],
        down_b,
        gain[None],
        shift[None],
    )


def solution(mesh):
    rows = P(("group", "replica"))
    stack = P("section")
    return jax.shard_map(
        shards,
        mesh=mesh,
        in_specs=(rows,) * 4 + (stack,) * 10,
        out_specs=(
            P("section", ("group", "replica"), None),
            P("section", ("group", "replica"), None),
            P("section", "group", None),
            P("section", "group"),
            P("section", "group", None),
            P("section", "group"),
            P("section", "group", None),
            P("section", "group"),
            P("section", "group", None),
            P("section", "group"),
            P("section", None, "group"),
            P("section", None, "group"),
        ),
        check_vma=False,
    )
```

```python
import jax
import jax.numpy as jnp
import numpy as np
from jax import lax
from jax.experimental import pallas as pl
from jax.experimental.pallas import tpu as pltpu
from jax.sharding import PartitionSpec as P

HEADS = 20
HEAD_DIM = 32
LEN = 256
MASK_MEAN = 38
CROP_DEV = 2
EPSILON = 1e-05
ROTARY_BASE = 10000.0

BF = jnp.bfloat16
F32 = jnp.float32
NN = (((1,), (0,)), ((), ()))
NT = (((1,), (1,)), ((), ()))
TN = (((0,), (0,)), ((), ()))

FIRST_LIMIT, FORWARD_LIMIT, MLP_LIMIT, ATTENTION_LIMIT, QKV_LIMIT = 40, 14, 16, 17, 8
ATTENTION_MICROS = 12
REPLICAS = 4
GROUPS = 4
PAD = 16
ROW_QKV, ROW_OUT, ROW_UP, ROW_DOWN, ROW_GAIN, ROW_SHIFT = 0, 3, 4, 8, 9, 11

ANY = pl.BlockSpec(memory_space=pl.ANY)
HBM = pl.BlockSpec(memory_space=pltpu.HBM)
VMEM = pl.BlockSpec(memory_space=pltpu.VMEM)
SMEM = pl.BlockSpec(memory_space=pltpu.SMEM)


def shape(dims, dtype):
    return jax.ShapeDtypeStruct(dims, dtype)


def mm(left, right, dims=NN):
    return lax.dot_general(left, right, dims, preferred_element_type=F32)


def unit_rows_of(values):
    centred = values - jnp.mean(values, axis=-1, keepdims=True)
    inverse = lax.rsqrt(jnp.mean(centred * centred, axis=-1, keepdims=True) + EPSILON)
    return centred * inverse, inverse


def norm_back(grad, unit, inverse, gain):
    scaled = grad * gain
    return inverse * (
        scaled
        - jnp.mean(scaled, axis=-1, keepdims=True)
        - unit * jnp.mean(scaled * unit, axis=-1, keepdims=True)
    )


def rotary_tables():
    lane = np.arange(128) % HEAD_DIM
    half = HEAD_DIM // 2
    freq = ROTARY_BASE ** (-(lane % half).astype(np.float64) * (2.0 / HEAD_DIM))
    angles = np.arange(LEN)[:, None] * freq[None, :]
    sign = np.where(lane < half, -1.0, 1.0)[None, :]
    return np.stack([np.cos(angles), np.sin(angles) * sign]).astype(np.float32)


def rotary_columns():
    half = HEAD_DIM // 2
    freq = ROTARY_BASE ** (-np.arange(half, dtype=np.float64) * (2.0 / HEAD_DIM))
    angles = freq[:, None] * np.arange(LEN)[None, :]
    return np.stack([np.cos(angles), np.sin(angles)]).astype(np.float32)


def swap_halves(values):
    lane = lax.broadcasted_iota(jnp.int32, values.shape, 1) % HEAD_DIM
    half = HEAD_DIM // 2
    return jnp.where(
        lane < half,
        pltpu.roll(values, 128 - half, axis=1),
        pltpu.roll(values, half, axis=1),
    )


def head_stack(block, per):
    head = lax.broadcasted_iota(jnp.int32, block.shape, 1) // HEAD_DIM
    return jnp.concatenate(
        [jnp.where(head == h, block, jnp.zeros_like(block)) for h in range(per)], axis=0
    )


class Copies:
    def __init__(self, sems):
        self.sems = sems
        self.used = 0
        self.open = []

    def start(self, src, dst):
        copy = pltpu.make_async_copy(src, dst, self.sems.at[self.used])
        self.used += 1
        copy.start()
        return copy

    def save(self, src, dst):
        self.open.append(self.start(src, dst))

    def finish(self):
        for copy in self.open:
            copy.wait()


def call(kernel, outs, ins, scratch, sems, aliases, name, after=None, limit=16, spaces=None, out_spaces=None, micros=0.1):
    count = len(ins)
    places = {"v": VMEM, "h": HBM, "a": ANY, "s": SMEM}
    spaces = spaces or "v" * count
    out_spaces = out_spaces or "v" * len(outs)
    in_specs = [SMEM if a.ndim == 1 else places[p] for a, p in zip(ins, spaces)]
    ins = [pltpu.with_memory_space_constraint(a, pltpu.HBM) if p == "h" else a for a, p in zip(ins, spaces)]
    body = kernel
    if after is not None:
        ins = list(ins) + [after]
        in_specs = in_specs + [ANY]

        def body(*refs):
            kernel(*refs[:count], *refs[count + 1 :])

    outs = [pltpu.HBM(o.shape, o.dtype) if p == "h" else o for o, p in zip(outs, out_spaces)]
    return pl.pallas_call(
        body,
        out_shape=outs,
        in_specs=in_specs,
        out_specs=[places[p] for p in out_spaces],
        scratch_shapes=scratch + ([pltpu.SemaphoreType.DMA((sems,))] if sems else []),
        input_output_aliases=aliases,
        compiler_params=pltpu.CompilerParams(vmem_limit_bytes=limit << 20),
        cost_estimate=pl.CostEstimate(
            flops=int(micros * 1.15e9), bytes_accessed=0, transcendentals=0
        ),
        name=name,
    )(*ins)


TOKEN = jax.ShapeDtypeStruct((8, 128), F32)


def vmem_like(arr):
    return pltpu.VMEM(arr.shape, arr.dtype)


def forward(slot, info, live, own, arrived, params, tab, act, after=None):
    qkvw, qkvb, outw, outb, upw, upb, downw, downb, gain, shift = params
    dim = own.shape[1]
    blocks = dim // 128
    wide = upw.shape[1]
    parts = wide // dim
    per = 128 // HEAD_DIM
    manual = slot == 0
    saved = [
        shape((LEN, dim), BF),
        shape((LEN, 3 * dim), BF),
        shape((HEADS, LEN, LEN), BF),
        shape((dim, LEN), BF),
        shape((LEN, dim), F32),
        shape((LEN, wide), BF),
        shape((LEN, wide), BF),
    ]
    weights = [qkvb, outb, upb, downb, gain, shift, tab, qkvw, outw, upw, downw]
    sources = [own] if slot == 0 else [arrived] if slot == 2 else [own, arrived]
    before = [] if act is None else [act]
    ins = [info, live] + sources + weights + before
    count = len(sources)

    def kernel(info, live, *refs):
        xs = refs[:count]
        given = refs[count : count + 11]
        act_h, *outs = refs[count + 11 + len(before) : count + 19 + len(before)]
        scratch = refs[count + 19 + len(before) :]
        act_s, vt_s, score_s, up_s = scratch[:4]
        sems = scratch[-1]
        y_s, qkv_s, prob_s, mixt_s, mid_s, gp_s, hid_s = outs
        used = scratch[4:-1] if manual else xs[-1:] + given
        qkvb, outb, upb, downb, gain, shift, tab, qkvw, outw, upw, downw = used[1:]
        crop = slot - info[0]

        @pl.when(jnp.logical_and(crop >= 0, crop < CROP_DEV))
        def _():
            copies = Copies(sems)
            heavy = []
            if manual:
                rows = xs[0].at[pl.ds(0, LEN)]
                loads = [copies.start(h, s) for h, s in zip((rows,) + given, used)]
                heavy = loads[8:]
                wait_all(loads[:8])
                x = used[0][...].astype(F32)
            elif slot == 1:
                x = jnp.where(info[0] == 0, xs[0][LEN:, :], xs[1][...]).astype(F32)
            else:
                x = xs[0][...].astype(F32)

            def ready(index):
                if manual:
                    heavy[index].wait()

            unit, _ = unit_rows_of(x)
            normed = (unit * gain[0:1, :] + shift[0:1, :]).astype(BF)
            ready(0)
            third = mm(normed, qkvw[:, 2 * dim :]) + qkvb[:, 2 * dim :]
            low = third.astype(BF)
            qkv_s[:, 2 * dim :] = low
            vt_s[...] = low.T
            for part in range(2):
                third = mm(normed, qkvw[:, part * dim : (part + 1) * dim])
                third = third + qkvb[:, part * dim : (part + 1) * dim]
                for j in range(blocks):
                    b = third[:, 128 * j : 128 * j + 128]
                    b = b * tab[0] + swap_halves(b) * tab[1]
                    if part == 0:
                        b = b * HEAD_DIM**-0.5
                    at = part * dim + 128 * j
                    qkv_s[:, at : at + 128] = b.astype(BF)
            for j in range(blocks):
                q = qkv_s[:, 128 * j : 128 * j + 128]
                k = qkv_s[:, dim + 128 * j : dim + 128 * j + 128]
                score_s[per * LEN * j : per * LEN * (j + 1), :] = mm(head_stack(k, per), q, NT)

            def soft(h, _):
                s = score_s[pl.ds(pl.multiple_of(h * LEN, LEN), LEN), :]
                e = jnp.exp(s - jnp.max(s, axis=0, keepdims=True))
                prob_s[h] = (e * (1.0 / jnp.sum(e, axis=0, keepdims=True))).astype(BF)
                return 0

            lax.fori_loop(0, HEADS, soft, 0, unroll=2)
            for h in range(HEADS):
                at = slice(HEAD_DIM * h, HEAD_DIM * (h + 1))
                mixt_s[at, :] = mm(vt_s[at, :], prob_s[h]).astype(BF)
            ready(1)
            mid = x + mm(mixt_s[...], outw[...], TN) + outb[...]
            mid_s[...] = mid
            unit, _ = unit_rows_of(mid)
            normed = (unit * gain[1:2, :] + shift[1:2, :]).astype(BF)
            ready(2)
            up_s[...] = mm(normed, upw[...])
            for c in range(parts):
                cols = slice(c * dim, (c + 1) * dim)
                u = up_s[:, cols] + upb[:, cols]
                cdf = 0.5 + 0.5 * lax.erf(u * 0.5**0.5)
                hid_s[:, cols] = (u * cdf).astype(BF)
                gp_s[:, cols] = (
                    cdf + u * (jnp.exp(u * u * -0.5) * (2 * np.pi) ** -0.5)
                ).astype(BF)
            ready(3)
            low = (mid_s[...] + downb[...] + mm(hid_s[...], downw[...])).astype(BF)
            y_s[...] = low
            act_s[...] = jnp.where(crop < live[0], low, jnp.zeros_like(low))
            at = pl.multiple_of(crop * LEN, LEN)
            copies.save(act_s, act_h.at[pl.ds(at, LEN)])
            copies.finish()

    outs = [shape(own.shape, BF)] + saved
    scratch = [
        pltpu.VMEM((LEN, dim), BF),
        pltpu.VMEM((dim, LEN), BF),
        pltpu.VMEM((HEADS * LEN, LEN), F32),
        pltpu.VMEM((LEN, wide), F32),
    ]
    if manual:
        scratch += [pltpu.VMEM((LEN, dim), BF)] + [vmem_like(a) for a in weights]
    aliases = {} if act is None else {len(ins) - 1: 0}
    spaces = "ss" + ("h" if manual else "v") * (count + 11) + "h" * len(before)
    out = call(
        kernel,
        outs,
        ins,
        scratch,
        16,
        aliases,
        "layer_forward",
        after,
        FIRST_LIMIT if manual else FORWARD_LIMIT,
        spaces,
        "h" + "v" * 7,
    )
    return out[0], out[1:]


def crop_weight(live, masks, crop, section):
    if section == 0:
        return 1.0
    count = jnp.where(live[0] > crop, masks[crop], 0)
    return jnp.full((1, 1), count, jnp.int32).astype(F32) / MASK_MEAN


def add_row(ref, row, values):
    ref[row : row + 1, :] = ref[row : row + 1, :] + jnp.sum(values, axis=0, keepdims=True)


def lay_out(own, bit, keep, send, block, index, row, count, at):
    src = pl.ds(row if isinstance(row, int) else pl.multiple_of(row, PAD), count)
    dst = pl.ds(at if isinstance(at, int) else pl.multiple_of(at, PAD), count)
    mine = own == bit

    @pl.when(mine)
    def _():
        keep[dst, :] = block[index, src, :]

    @pl.when(jnp.logical_not(mine))
    def _():
        send[dst, :] = block[index, src, :]


def keep_given(active, given, bufs):
    @pl.when(jnp.logical_not(active))
    def _():
        for old, new in zip(given, bufs):
            new[...] = old[...]


def pair_shapes(rows, dim):
    return [shape((rows, dim), BF)] * 2


def joined(refs, cols):
    return jnp.concatenate([r[:, cols] for r in refs], axis=0)


def wait_all(copies):
    for copy in copies:
        copy.wait()


def mlp_grad(section, info, live, masks, g, saved, params, after):
    mixts = [s[3] for s in saved]
    mids, gps, hids = ([s[k] for s in saved] for k in (4, 5, 6))
    upw, downw, gain, shift = params[4], params[6], params[8], params[9]
    rows, dim = g.shape
    wide = upw.shape[1]
    parts = wide // dim
    crops = len(saved)
    share = dim // GROUPS
    ins = [info, live, masks, g, gain, shift, downw, upw] + mids + gps + hids + mixts

    def kernel(info, live, masks, g_s, gain, shift, downw, upw, *refs):
        mid_s, gp_s, hid_s, mixt_s = (refs[i * crops : (i + 1) * crops] for i in range(4))
        refs = refs[4 * crops :]
        send_a, keep_a, send_b, keep_b, gmid_s, small_s = refs[:6]
        gu_s, block_s, low_s, normt_s, back_s = refs[7:]

        @pl.when(info[0] == section)
        def _():
            small_s[...] = jnp.zeros_like(small_s)
            for c in range(crops):
                crop = slice(c * LEN, (c + 1) * LEN)
                grad = g_s[crop, :].astype(F32) * crop_weight(live, masks, c, section)
                low = grad.astype(BF)
                low_s[crop, :] = low
                add_row(small_s, ROW_DOWN, low.astype(F32))
                unit, _ = unit_rows_of(mid_s[c][...])
                normt_s[:, crop] = (unit * gain[1:2, :] + shift[1:2, :]).astype(BF).T
            for c in range(parts):
                cols = slice(c * dim, (c + 1) * dim)
                block_s[c] = mm(joined(hid_s, cols), low_s[...], TN).astype(BF)

            @pl.loop(0, GROUPS * parts)
            def _(i):
                shard, row = i // parts, (i % parts) * share
                at = (shard // 2) * dim + row
                lay_out(info[1], shard % 2, keep_a, send_a, block_s, shard, row, share, at)

            for c in range(parts):
                cols = slice(c * dim, (c + 1) * dim)
                grad_up = mm(low_s[...], downw[cols, :], NT) * joined(gp_s, cols).astype(F32)
                grad_up = grad_up.astype(BF)
                gu_s[:, cols] = grad_up
                small_s[ROW_UP + c : ROW_UP + c + 1, :] = jnp.sum(
                    grad_up.astype(F32), axis=0, keepdims=True
                )
            back_s[...] = mm(gu_s[...], upw[...], NT)
            for c in range(crops):
                crop = slice(c * LEN, (c + 1) * LEN)
                grad = g_s[crop, :].astype(F32) * crop_weight(live, masks, c, section)
                unit, inverse = unit_rows_of(mid_s[c][...])
                back = back_s[crop, :]
                gmid = grad + norm_back(back, unit, inverse, gain[1:2, :])
                gmid_s[crop, :] = gmid
                low = gmid.astype(BF)
                low_s[crop, :] = low
                add_row(small_s, ROW_GAIN + 1, back * unit)
                add_row(small_s, ROW_SHIFT + 1, back)
                add_row(small_s, ROW_OUT, low.astype(F32))
            for c in range(parts):
                block_s[c] = mm(normt_s[...], gu_s[:, c * dim : (c + 1) * dim]).astype(BF)
            mixt = jnp.concatenate([m[...] for m in mixt_s], axis=1)
            block_s[parts] = mm(mixt, low_s[...]).astype(BF)

            @pl.loop(0, GROUPS * (parts + 1))
            def _(i):
                shard, c = i // (parts + 1), i % (parts + 1)
                at = ((shard % 2) * (parts + 1) + c) * share
                lay_out(info[2], shard // 2, keep_b, send_b, block_s, c, shard * share, share, at)

    scratch = [
        pltpu.VMEM((rows, wide), BF),
        pltpu.VMEM((parts + 1, dim, dim), BF),
        pltpu.VMEM((rows, dim), BF),
        pltpu.VMEM((dim, rows), BF),
        pltpu.VMEM((rows, dim), F32),
    ]
    outs = pair_shapes(2 * dim, dim) + pair_shapes(2 * (parts + 1) * share, dim)
    outs += [shape((rows, dim), F32), shape((PAD, dim), F32), TOKEN]
    out = call(kernel, outs, ins, scratch, 0, {}, "mlp_grad", after, MLP_LIMIT, micros=10)
    return out[:4], out[4], out[5], out[6]


def rotate_back(block, tab_t):
    half = HEAD_DIM // 2
    cos, sin = tab_t[0], tab_t[1]
    out = []
    for at in range(0, block.shape[0], HEAD_DIM):
        a, b = block[at : at + half], block[at + half : at + HEAD_DIM]
        out += [a * cos + b * sin, b * cos - a * sin]
    return jnp.concatenate(out, axis=0)


def attention_grad(section, info, gmid, small, xs, saved, params, tab_t, before, after):
    qkvs, probs, mixts = [s[1] for s in saved], [s[2] for s in saved], [s[3] for s in saved]
    qkvw, outw, gain, shift = params[0], params[2], params[8], params[9]
    rows, dim = gmid.shape
    blocks = dim // 128
    per = 128 // HEAD_DIM
    crops = len(saved)
    given = [] if before is None else [before]
    ins = [info, gmid, outw, small, gain, shift, tab_t, qkvw]
    ins += qkvs + probs + mixts + list(xs) + given

    def kernel(info, gmid_s, outw, small_s, gain, shift, tab_t, qkvw, *refs):
        qkv_s, prob_s, mixt_s = (refs[i * crops : (i + 1) * crops] for i in range(3))
        x_s = refs[3 * crops : 3 * crops + len(xs)]
        old = refs[3 * crops + len(xs) : 3 * crops + len(xs) + len(given)]
        refs = refs[3 * crops + len(xs) + len(given) :]
        keep_given(info[0] == section, old, refs[:1])
        dx_s, gqkv_s, normt_s, small_out = refs[:4]
        gmt_s, delta_s, da_s, ds_s, dt_s, kt_s = refs[5:]

        @pl.when(info[0] == section)
        def _():
            low = gmid_s[...].astype(BF)
            gmt_s[...] = mm(outw[...], low, NT).astype(BF)
            for c in range(crops):
                crop = slice(c * LEN, (c + 1) * LEN)
                qkv, prob = qkv_s[c], prob_s[c]
                product = gmt_s[:, crop].astype(F32) * mixt_s[c][...].astype(F32)
                delta_s[...] = jnp.sum(product.reshape(HEADS, HEAD_DIM, LEN), axis=1)[:, None, :]
                kt_s[0] = qkv[:, dim : 2 * dim].T
                kt_s[1] = qkv[:, :dim].T
                for j in range(blocks):
                    v = qkv[:, 2 * dim + 128 * j : 2 * dim + 128 * j + 128]
                    da_s[per * LEN * j : per * LEN * (j + 1), :] = mm(
                        head_stack(v, per), gmt_s[128 * j : 128 * j + 128, crop]
                    )

                def scores(h, _):
                    da = da_s[pl.ds(pl.multiple_of(h * LEN, LEN), LEN), :]
                    ds_s[h] = (prob[h].astype(F32) * (da - delta_s[h])).astype(BF)
                    return 0

                lax.fori_loop(0, HEADS, scores, 0, unroll=2)
                for h in range(HEADS):
                    at = slice(HEAD_DIM * h, HEAD_DIM * (h + 1))
                    dt_s[0, at, :] = mm(kt_s[0, at, :], ds_s[h])
                    dt_s[1, at, :] = mm(kt_s[1, at, :], ds_s[h], NT)
                    dt_s[2, at, :] = mm(gmt_s[at, crop], prob[h], NT)
                dq = rotate_back(dt_s[0] * HEAD_DIM**-0.5, tab_t)
                gqkv_s[crop, :dim] = dq.astype(BF).T
                gqkv_s[crop, dim : 2 * dim] = rotate_back(dt_s[1], tab_t).astype(BF).T
                gqkv_s[crop, 2 * dim :] = dt_s[2].astype(BF).T
            unit, inverse = unit_rows_of(joined(x_s, slice(None)).astype(F32))
            normt_s[...] = (unit * gain[0:1, :] + shift[0:1, :]).astype(BF).T
            back = mm(gqkv_s[...], qkvw[...], NT)
            dx_s[...] = (gmid_s[...] + norm_back(back, unit, inverse, gain[0:1, :])).astype(BF)
            small_out[...] = small_s[...]
            small_out[ROW_GAIN : ROW_GAIN + 1, :] = jnp.sum(back * unit, axis=0, keepdims=True)
            small_out[ROW_SHIFT : ROW_SHIFT + 1, :] = jnp.sum(back, axis=0, keepdims=True)

    outs = [
        shape((rows, dim), BF),
        shape((rows, 3 * dim), BF),
        shape((dim, rows), BF),
        shape(small.shape, F32),
        TOKEN,
    ]
    scratch = [
        pltpu.VMEM((dim, rows), BF),
        pltpu.VMEM((HEADS, 1, LEN), F32),
        pltpu.VMEM((HEADS * LEN, LEN), F32),
        pltpu.VMEM((HEADS, LEN, LEN), BF),
        pltpu.VMEM((3, dim, LEN), F32),
        pltpu.VMEM((2, dim, LEN), BF),
    ]
    aliases = {len(ins) - 1: 0} if given else {}
    out = call(kernel, outs, ins, scratch, 0, aliases, "attention_grad", after, ATTENTION_LIMIT, micros=ATTENTION_MICROS)
    return out[0], out[1:4], out[4]


def qkv_grad(section, info, kept, before, after):
    gqkv, normt, small = kept
    dim, rows = normt.shape
    share = dim // GROUPS
    half = 3 * share // 2
    given = [] if before is None else list(before)
    ins = [info, gqkv, normt, small] + given

    def kernel(info, gqkv_s, normt_s, small_s, *refs):
        old = refs[: len(given)]
        bufs = refs[len(given) : len(given) + 4]
        send_a, keep_a, send_b, keep_b = bufs
        (block_s,) = refs[len(given) + 5 :]
        keep_given(info[0] == section, old, bufs)

        @pl.when(info[0] == section)
        def _():
            sums = [
                jnp.sum(gqkv_s[:, c * dim : (c + 1) * dim].astype(F32), axis=0, keepdims=True)
                for c in range(3)
            ]
            tail = jnp.concatenate(sums + [small_s[ROW_OUT:, :]], axis=0).astype(BF)
            send_a[2 * half :, :] = tail
            keep_a[2 * half :, :] = tail
            for c in range(3):
                block_s[c] = mm(normt_s[...], gqkv_s[:, c * dim : (c + 1) * dim]).astype(BF)

            @pl.loop(0, GROUPS)
            def _(shard):
                x, y, base = shard % 2, shard // 2, shard * share
                for c in range(3):
                    row, at, left = 0, c * share, share
                    while left:
                        count = min(left, half - at % half)
                        if at < half:
                            own, bit, keep, send, to = info[1], x, keep_a, send_a, y * half + at
                        else:
                            own, bit, keep, send, to = info[2], y, keep_b, send_b, x * half + at - half
                        lay_out(own, bit, keep, send, block_s, c, base + row, count, to)
                        row, at, left = row + count, at + count, left - count

    scratch = [pltpu.VMEM((3, dim, dim), BF)]
    aliases = {len(ins) - 4 + i: i for i in range(4)} if given else {}
    outs = pair_shapes(2 * half + PAD, dim) + pair_shapes(2 * half, dim) + [TOKEN]
    out = call(kernel, outs, ins, scratch, 0, aliases, "qkv_grad", after, QKV_LIMIT)
    return out[:4], out[4]


STEP = 80


def plus(one, two):
    return (one.astype(F32) + two.astype(F32)).astype(BF)


def add_rows(out, at, one, two, start, count):
    whole = count // STEP * STEP

    @pl.loop(0, whole // STEP)
    def _(i):
        src = pl.ds(pl.multiple_of(start + i * STEP, PAD), STEP)
        dst = pl.ds(pl.multiple_of(at + i * STEP, PAD), STEP)
        out[dst, :] = plus(one[src, :], two[src, :])

    if count > whole:
        src = pl.ds(pl.multiple_of(start + whole, PAD), count - whole)
        out[pl.ds(at + whole, count - whole), :] = plus(one[src, :], two[src, :])


def vmem_call(kernel, outs, ins, name, after, scratch=()):
    return call(kernel, outs, ins, list(scratch), 0, {}, name, after, 8)


def copy_rows(out, at, src, start, count):
    whole = count // STEP * STEP

    @pl.loop(0, whole // STEP)
    def _(i):
        lines = pl.ds(pl.multiple_of(start + i * STEP, PAD), STEP)
        out[pl.ds(pl.multiple_of(at + i * STEP, PAD), STEP), :] = src[lines, :]

    if count > whole:
        lines = pl.ds(pl.multiple_of(start + whole, PAD), count - whole)
        out[pl.ds(pl.multiple_of(at + whole, PAD), count - whole), :] = src[lines, :]


def first_sum(section, info, held, came, third, after):
    dim = third[0].shape[1]
    halves = [k.shape[0] // 2 for k in (held[1], held[3])]
    riders = (third[2], third[0])

    def kernel(info, ka, ra, kb, rb, *refs):
        given = refs[:2]
        sa, na, sb, nb = refs[2:]

        @pl.when(info[0] == section)
        def _():
            for own, one, two, new, out, half, rider in (
                (info[2], ka, ra, na, sa, halves[0], given[0]),
                (info[1], kb, rb, nb, sb, halves[1], given[1]),
            ):
                add_rows(out, 0, one, two, (1 - own) * half, half)
                add_rows(new, 0, one, two, own * half, half)
                copy_rows(out, half, rider, 0, rider.shape[0])

    outs = []
    for half, rider in zip(halves, riders):
        outs += [shape((half + rider.shape[0], dim), BF), shape((half, dim), BF)]
    ins = [info, held[1], came[0], held[3], came[1]] + list(riders)
    return vmem_call(kernel, outs, ins, "first_sum", after)


def padded(rows):
    return -(-rows // (PAD * REPLICAS)) * PAD * REPLICAS


def split_shapes(rows, dim):
    return [shape((rows, dim), BF)]


def sum_pieces(info, outs, pieces, rows):
    for at, one, two, start_one, start_two, count in pieces:
        add_shifted(outs[0], at, one, start_one, two, start_two, count)


def add_shifted(out, at, one, start_one, two, start_two, count):
    whole = count // STEP * STEP

    @pl.loop(0, whole // STEP)
    def _(i):
        a = pl.ds(pl.multiple_of(start_one + i * STEP, PAD), STEP)
        b = pl.ds(pl.multiple_of(start_two + i * STEP, PAD), STEP)
        out[pl.ds(pl.multiple_of(at + i * STEP, PAD), STEP), :] = plus(one[a, :], two[b, :])

    if count > whole:
        a = pl.ds(pl.multiple_of(start_one + whole, PAD), count - whole)
        b = pl.ds(pl.multiple_of(start_two + whole, PAD), count - whole)
        out[pl.ds(pl.multiple_of(at + whole, PAD), count - whole), :] = plus(one[a, :], two[b, :])


def third_sum(info, flows, third, after):
    dim = third[1].shape[1]
    half_a, half_b = (third[1].shape[0] - PAD) // 2, third[3].shape[0] // 2
    top, rest = flows[0][0].shape[0] - 2 * half_b, flows[0][1].shape[0] - 2 * half_a - PAD

    def kernel(info, ka, kb, *refs):
        sa, ma, sb, mb = refs[4:]
        for section in range(2):
            along, across = refs[2 * section : 2 * section + 2]

            @pl.when(info[0] == section)
            def _():
                for own, one, two, base, new, out, half in (
                    (info[2], ka, across, rest, ma, sa, half_a),
                    (info[1], kb, along, top, mb, sb, half_b),
                ):
                    for target, part in ((new, own), (out, 1 - own)):
                        add_shifted(target, 0, one, part * half, two, base + part * half, half)
                    extra = one.shape[0] - 2 * half
                    if extra:
                        low = base + 2 * half
                        tail = plus(one[2 * half :, :], two[low : low + extra, :])
                        new[half:, :] = tail
                        out[half:, :] = tail

    outs = [shape((half_a + PAD, dim), BF)] * 2 + [shape((half_b, dim), BF)] * 2
    ins = [info, third[1], third[3]] + [a for f in flows for a in f]
    return vmem_call(kernel, outs, ins, "third_sum", after)


def group_sum(section, info, kept, came, given, after):
    rows = [a.shape[0] for a in kept]
    given = list(given or [])

    def kernel(info, ka, kb, ra, rb, *refs):
        outs = refs[len(given) :]
        keep_given(info[0] == section, refs[: len(given)], outs)

        @pl.when(info[0] == section)
        def _():
            pieces = [(0, ka, ra, 0, 0, rows[0]), (rows[0], kb, rb, 0, 0, rows[1])]
            sum_pieces(info, outs, pieces, sum(rows))

    outs = split_shapes(sum(rows), kept[0].shape[1])
    ins = [info] + list(kept) + list(came) + given
    aliases = {5 + i: i for i in range(len(given))}
    return call(kernel, outs, ins, [], 0, aliases, "group_sum", after, 10)


def last_sum(info, kept, came, after):
    rows = [a.shape[0] for a in kept]

    def kernel(info, ka, kb, ra, rb, *outs):
        pieces = [(0, ka, ra, 0, 0, rows[0]), (rows[0], kb, rb, 0, 0, rows[1])]
        sum_pieces(info, outs, pieces, sum(rows))

    outs = split_shapes(sum(rows), kept[0].shape[1])
    return vmem_call(kernel, outs, [info] + list(kept) + list(came), "last_sum", after)


class Line:
    def __init__(self, info, part):
        self.info, self.part = info, part
        self.four = lax.axis_size("replica") == REPLICAS
        if self.four:
            self.came = lax.ppermute(part, "replica", [(0, 1), (3, 2)])
        else:
            self.part = self.came = lax.psum(part, "replica")

    def hop(self, pairs, after):
        if not self.four:
            return after

        def kernel(info, one, two, out):
            @pl.when(jnp.logical_or(info[3] == 1, info[3] == 2))
            def _():
                add_rows(out, 0, one, two, 0, one.shape[0])

        outs = [shape(self.part.shape, BF)]
        ins = [self.info, self.part, self.came]
        self.part = vmem_call(kernel, outs, ins, "pair_sum", after)[0]
        self.came = lax.ppermute(self.part, "replica", pairs)
        return self.part

    def middle(self, after):
        return self.hop([(1, 2), (2, 1)], after)

    def back(self, after):
        return self.hop([(1, 0), (2, 3)], after)


def own_pieces(row, count, width, group):
    share = count * width // GROUPS
    at, pieces = group * share, []
    while at < (group + 1) * share:
        size = min((group + 1) * share - at, width - at % width)
        pieces.append((row + at // width, at % width, size, at - group * share))
        at += size
    return pieces


def finish(info, sets, after):
    dim = sets[0][0].shape[1]
    share = dim // GROUPS
    half = 3 * share // 2
    top = dim + 5 * share
    base = sets[0][0].shape[0]
    vectors = ((ROW_QKV, 3), (ROW_OUT, 1), (ROW_UP, 4), (ROW_DOWN, 1))
    outs = [
        shape((dim, dim), F32),
        shape((share, 4 * dim), F32),
        shape((share, dim), F32),
        shape((share, 3 * dim), F32),
    ]
    large = len(outs)
    outs += [shape((1, count * dim // GROUPS), F32) for _, count in vectors]
    outs += [shape((2, share), F32)] * 2

    def kernel(info, *refs):
        given, refs = refs[:4], refs[4:]
        out_h = refs[:large]
        small = refs[large : len(outs)]
        src = refs[len(outs)]
        stage = refs[len(outs) + 1 : -1]
        sems = refs[-1]
        inner = jnp.logical_or(info[3] == 1, info[3] == 2)
        lines = [src.at[pl.ds(0, base)], src.at[pl.ds(base, src.shape[0] - base)]]
        for k, dst in enumerate(lines):
            for side, check in enumerate((inner, jnp.logical_not(inner))):

                @pl.when(check)
                def _():
                    pltpu.make_async_copy(given[2 * k + side], dst, sems.at[k]).start()

        for k, dst in enumerate(lines):
            pltpu.make_async_copy(given[2 * k], dst, sems.at[k]).wait()
        copies = []

        def save(i):
            copy = pltpu.make_async_copy(stage[i], out_h[i], sems.at[4 + i])
            copy.start()
            copies.append(copy)

        stage[0][...] = src[:dim, :].astype(F32)
        save(0)
        for i in range(4):
            block = src[dim + i * share : dim + (i + 1) * share, :].astype(F32)
            stage[1][:, i * dim : (i + 1) * dim] = block
        save(1)
        for i in range(3):
            at, left, to = i * share, share, 0
            while left:
                count = min(left, half - at % half)
                row = base + (at if at < half else at + PAD)
                block = src[row : row + count, :].astype(F32)
                stage[3][to : to + count, i * dim : (i + 1) * dim] = block
                at, left, to = at + count, left - count, to + count
        save(3)
        stage[2][...] = src[dim + 4 * share : top, :].astype(F32)
        save(2)
        tail = src[base + half : base + half + PAD, :].astype(F32)
        for group in range(GROUPS):

            @pl.when(info[1] + 2 * info[2] == group)
            def _():
                for out, (row, count) in zip(small, vectors):
                    for r, c, size, at in own_pieces(row, count, dim, group):
                        out[:, at : at + size] = tail[r : r + 1, c : c + size]
                for out, row in zip(small[4:], (ROW_GAIN, ROW_SHIFT)):
                    out[...] = tail[row : row + 2, group * share : (group + 1) * share]

        for copy in copies:
            copy.wait()

    scratch = [pltpu.VMEM((base + sets[1][0].shape[0], dim), BF)]
    scratch += [vmem_like(o) for o in outs[:large]]
    places = "h" * large + "v" * (len(outs) - large)
    ins = [info] + [a for pair in sets for a in pair]
    return call(
        kernel, outs, ins, scratch, 8, {}, "finish", after, 16, "saaaa", places
    )


def flow(shard, axis, pairs, sections):
    if sections == (0, 1):
        return lax.ppermute(shard, axis, pairs)
    peers = lax.axis_size(axis)
    pairs = [(s * peers + i, s * peers + j) for s in sections for i, j in pairs]
    return lax.ppermute(shard, ("section", axis), pairs)


ACROSS = [(g, g ^ 1) for g in range(GROUPS)]
ALONG = [(g, g ^ 2) for g in range(GROUPS)]
BOTH = (0, 1)


def exchange(a, b, turned, sections):
    ways = (ALONG, ACROSS) if turned else (ACROSS, ALONG)
    return flow(a, "group", ways[0], sections), flow(b, "group", ways[1], sections)


def shards(
    block_input,
    cotangent,
    crop_count,
    mask_count,
    qkv_weight,
    qkv_bias,
    out_weight,
    out_bias,
    up_weight,
    up_bias,
    down_weight,
    down_bias,
    norm_gain,
    norm_shift,
):
    params = (
        qkv_weight[0],
        qkv_bias,
        out_weight[0],
        out_bias,
        up_weight[0],
        up_bias,
        down_weight[0],
        down_bias,
        norm_gain[0],
        norm_shift[0],
    )
    rows, dim = block_input.shape
    tab = jnp.asarray(rotary_tables())
    tab_t = jnp.asarray(rotary_columns())
    group = lax.axis_index("group")
    assert lax.axis_size("group") == GROUPS
    info = jnp.stack([lax.axis_index("section"), group % 2, group // 2, lax.axis_index("replica")])

    def to_other(shard, pairs):
        return lax.ppermute(shard, "section", pairs)

    act, first = forward(0, info, crop_count, block_input, None, params, tab, None)
    arrived = [to_other(first[0], [(0, 1)])]
    act, second = forward(1, info, crop_count, block_input, arrived[0], params, tab, act)
    arrived.append(to_other(second[0], [(0, 1)]))
    act, third = forward(2, info, crop_count, block_input, arrived[1], params, tab, act)
    kept_one, kept_zero = (second, third), (first, second)

    common = (info, crop_count, mask_count)
    one, gmid, small, last = mlp_grad(1, *common, cotangent, kept_one, params, None)
    came = exchange(one[0], one[2], False, (1,))
    dx, kept, last = attention_grad(
        1, info, gmid, small, arrived, kept_one, params, tab_t, None, last
    )
    grad_back = to_other(dx, [(1, 0)])
    third, last = qkv_grad(1, info, kept, None, last)
    one = first_sum(1, info, one, came, third, last)
    came_one = exchange(one[0], one[2], True, (1,))
    zero, gmid, small, last = mlp_grad(0, *common, grad_back, kept_zero, params, one[1])
    came = exchange(zero[0], zero[2], False, (0,))
    sums = group_sum(1, info, (one[1], one[3]), came_one, None, last)
    dx, kept, last = attention_grad(
        0, info, gmid, small, [block_input], kept_zero, params, tab_t, dx, sums[-1]
    )
    third, last = qkv_grad(0, info, kept, third, last)
    zero = first_sum(0, info, zero, came, third, last)
    came_zero = exchange(zero[0], zero[2], True, (0,))
    sums = group_sum(0, info, (zero[1], zero[3]), came_zero, sums, zero[1])
    mlp = Line(info, sums[0])
    send_a, keep_a, send_b, keep_b = third_sum(info, (came_zero, came_one), third, sums[0])
    came = exchange(send_a, send_b, True, BOTH)
    qkv = Line(info, last_sum(info, (keep_a, keep_b), came, keep_a)[0])
    last = mlp.middle(qkv.part)
    last = qkv.middle(last)
    last = mlp.back(last)
    last = qkv.back(last)
    sets = ((mlp.part, mlp.came), (qkv.part, qkv.came))
    grad_down, grad_up, grad_out, grad_qkv, *small = finish(info, sets, last)
    qkv_b, out_b, up_b, down_b, gain, shift = small
    return (
        act[None],
        dx[None],
        grad_qkv[None],
        qkv_b,
        grad_out[None],
        out_b,
        grad_up[None],
        up_b,
        grad_down[None],
        down_b,
        gain[None],
        shift[None],
    )


def solution(mesh):
    rows = P(("group", "replica"))
    stack = P("section")
    return jax.shard_map(
        shards,
        mesh=mesh,
        in_specs=(rows,) * 4 + (stack,) * 10,
        out_specs=(
            P("section", ("group", "replica"), None),
            P("section", ("group", "replica"), None),
            P("section", "group", None),
            P("section", "group"),
            P("section", "group", None),
            P("section", "group"),
            P("section", "group", None),
            P("section", "group"),
            P("section", "group", None),
            P("section", "group"),
            P("section", None, "group"),
            P("section", None, "group"),
        ),
        check_vma=False,
    )
```

```python
import jax
import jax.numpy as jnp
import numpy as np
from jax import lax
from jax.experimental import pallas as pl
from jax.experimental.pallas import tpu as pltpu
from jax.sharding import PartitionSpec as P

HEADS = 20
HEAD_DIM = 32
LEN = 256
MASK_MEAN = 38
CROP_DEV = 2
EPSILON = 1e-05
ROTARY_BASE = 10000.0

BF = jnp.bfloat16
F32 = jnp.float32
NN = (((1,), (0,)), ((), ()))
NT = (((1,), (1,)), ((), ()))
TN = (((0,), (0,)), ((), ()))

FIRST_LIMIT, FORWARD_LIMIT, MLP_LIMIT, ATTENTION_LIMIT, QKV_LIMIT = 40, 14, 13, 16, 7
ATTENTION_MICROS = 12
GROUPS = 4
PAD = 16
ROW_QKV, ROW_OUT, ROW_UP, ROW_DOWN, ROW_GAIN, ROW_SHIFT = 0, 3, 4, 8, 9, 11

ANY = pl.BlockSpec(memory_space=pl.ANY)
HBM = pl.BlockSpec(memory_space=pltpu.HBM)
VMEM = pl.BlockSpec(memory_space=pltpu.VMEM)
SMEM = pl.BlockSpec(memory_space=pltpu.SMEM)


def shape(dims, dtype):
    return jax.ShapeDtypeStruct(dims, dtype)


def mm(left, right, dims=NN):
    return lax.dot_general(left, right, dims, preferred_element_type=F32)


def unit_rows_of(values):
    centred = values - jnp.mean(values, axis=-1, keepdims=True)
    inverse = lax.rsqrt(jnp.mean(centred * centred, axis=-1, keepdims=True) + EPSILON)
    return centred * inverse, inverse


def norm_back(grad, unit, inverse, gain):
    scaled = grad * gain
    return inverse * (
        scaled
        - jnp.mean(scaled, axis=-1, keepdims=True)
        - unit * jnp.mean(scaled * unit, axis=-1, keepdims=True)
    )


def rotary_tables():
    lane = np.arange(128) % HEAD_DIM
    half = HEAD_DIM // 2
    freq = ROTARY_BASE ** (-(lane % half).astype(np.float64) * (2.0 / HEAD_DIM))
    angles = np.arange(LEN)[:, None] * freq[None, :]
    sign = np.where(lane < half, -1.0, 1.0)[None, :]
    return np.stack([np.cos(angles), np.sin(angles) * sign]).astype(np.float32)


def rotary_columns():
    half = HEAD_DIM // 2
    freq = ROTARY_BASE ** (-np.arange(half, dtype=np.float64) * (2.0 / HEAD_DIM))
    angles = freq[:, None] * np.arange(LEN)[None, :]
    return np.stack([np.cos(angles), np.sin(angles)]).astype(np.float32)


def swap_halves(values):
    lane = lax.broadcasted_iota(jnp.int32, values.shape, 1) % HEAD_DIM
    half = HEAD_DIM // 2
    return jnp.where(
        lane < half,
        pltpu.roll(values, 128 - half, axis=1),
        pltpu.roll(values, half, axis=1),
    )


def head_stack(block, per):
    head = lax.broadcasted_iota(jnp.int32, block.shape, 1) // HEAD_DIM
    return jnp.concatenate(
        [jnp.where(head == h, block, jnp.zeros_like(block)) for h in range(per)], axis=0
    )


class Copies:
    def __init__(self, sems):
        self.sems = sems
        self.used = 0
        self.open = []

    def start(self, src, dst):
        copy = pltpu.make_async_copy(src, dst, self.sems.at[self.used])
        self.used += 1
        copy.start()
        return copy

    def save(self, src, dst):
        self.open.append(self.start(src, dst))

    def finish(self):
        for copy in self.open:
            copy.wait()


def call(kernel, outs, ins, scratch, sems, aliases, name, after=None, limit=16, spaces=None, out_spaces=None, micros=0.1):
    count = len(ins)
    places = {"v": VMEM, "h": HBM, "a": ANY, "s": SMEM}
    spaces = spaces or "v" * count
    out_spaces = out_spaces or "v" * len(outs)
    in_specs = [SMEM if a.ndim == 1 else places[p] for a, p in zip(ins, spaces)]
    ins = [pltpu.with_memory_space_constraint(a, pltpu.HBM) if p == "h" else a for a, p in zip(ins, spaces)]
    body = kernel
    if after is not None:
        ins = list(ins) + [after]
        in_specs = in_specs + [ANY]

        def body(*refs):
            kernel(*refs[:count], *refs[count + 1 :])

    outs = [pltpu.HBM(o.shape, o.dtype) if p == "h" else o for o, p in zip(outs, out_spaces)]
    return pl.pallas_call(
        body,
        out_shape=outs,
        in_specs=in_specs,
        out_specs=[places[p] for p in out_spaces],
        scratch_shapes=scratch + ([pltpu.SemaphoreType.DMA((sems,))] if sems else []),
        input_output_aliases=aliases,
        compiler_params=pltpu.CompilerParams(vmem_limit_bytes=limit << 20),
        cost_estimate=pl.CostEstimate(
            flops=int(micros * 1.15e9), bytes_accessed=0, transcendentals=0
        ),
        name=name,
    )(*ins)


TOKEN = jax.ShapeDtypeStruct((8, 128), F32)


def vmem_like(arr):
    return pltpu.VMEM(arr.shape, arr.dtype)


def forward(slot, info, live, own, arrived, params, tab, act, after=None):
    qkvw, qkvb, outw, outb, upw, upb, downw, downb, gain, shift = params
    dim = own.shape[1]
    blocks = dim // 128
    wide = upw.shape[1]
    parts = wide // dim
    per = 128 // HEAD_DIM
    manual = slot == 0
    saved = [
        shape((LEN, dim), BF),
        shape((LEN, 3 * dim), BF),
        shape((HEADS, LEN, LEN), BF),
        shape((dim, LEN), BF),
        shape((LEN, dim), F32),
        shape((LEN, wide), BF),
        shape((LEN, wide), BF),
    ]
    weights = [qkvb, outb, upb, downb, gain, shift, tab, qkvw, outw, upw, downw]
    sources = [own] if slot == 0 else [arrived] if slot == 2 else [own, arrived]
    before = [] if act is None else [act]
    ins = [info, live] + sources + weights + before
    count = len(sources)

    def kernel(info, live, *refs):
        xs = refs[:count]
        given = refs[count : count + 11]
        act_h, *outs = refs[count + 11 + len(before) : count + 19 + len(before)]
        scratch = refs[count + 19 + len(before) :]
        act_s, vt_s, score_s, up_s = scratch[:4]
        sems = scratch[-1]
        y_s, qkv_s, prob_s, mixt_s, mid_s, gp_s, hid_s = outs
        used = scratch[4:-1] if manual else xs[-1:] + given
        qkvb, outb, upb, downb, gain, shift, tab, qkvw, outw, upw, downw = used[1:]
        crop = slot - info[0]

        @pl.when(jnp.logical_and(crop >= 0, crop < CROP_DEV))
        def _():
            copies = Copies(sems)
            heavy = []
            if manual:
                rows = xs[0].at[pl.ds(0, LEN)]
                loads = [copies.start(h, s) for h, s in zip((rows,) + given, used)]
                heavy = loads[8:]
                wait_all(loads[:8])
                x = used[0][...].astype(F32)
            elif slot == 1:
                x = jnp.where(info[0] == 0, xs[0][LEN:, :], xs[1][...]).astype(F32)
            else:
                x = xs[0][...].astype(F32)

            def ready(index):
                if manual:
                    heavy[index].wait()

            unit, _ = unit_rows_of(x)
            normed = (unit * gain[0:1, :] + shift[0:1, :]).astype(BF)
            ready(0)
            third = mm(normed, qkvw[:, 2 * dim :]) + qkvb[:, 2 * dim :]
            low = third.astype(BF)
            qkv_s[:, 2 * dim :] = low
            vt_s[...] = low.T
            for part in range(2):
                third = mm(normed, qkvw[:, part * dim : (part + 1) * dim])
                third = third + qkvb[:, part * dim : (part + 1) * dim]
                for j in range(blocks):
                    b = third[:, 128 * j : 128 * j + 128]
                    b = b * tab[0] + swap_halves(b) * tab[1]
                    if part == 0:
                        b = b * HEAD_DIM**-0.5
                    at = part * dim + 128 * j
                    qkv_s[:, at : at + 128] = b.astype(BF)
            for j in range(blocks):
                q = qkv_s[:, 128 * j : 128 * j + 128]
                k = qkv_s[:, dim + 128 * j : dim + 128 * j + 128]
                score_s[per * LEN * j : per * LEN * (j + 1), :] = mm(head_stack(k, per), q, NT)

            def soft(h, _):
                s = score_s[pl.ds(pl.multiple_of(h * LEN, LEN), LEN), :]
                e = jnp.exp(s - jnp.max(s, axis=0, keepdims=True))
                prob_s[h] = (e * (1.0 / jnp.sum(e, axis=0, keepdims=True))).astype(BF)
                return 0

            lax.fori_loop(0, HEADS, soft, 0, unroll=2)
            for h in range(HEADS):
                at = slice(HEAD_DIM * h, HEAD_DIM * (h + 1))
                mixt_s[at, :] = mm(vt_s[at, :], prob_s[h]).astype(BF)
            ready(1)
            mid = x + mm(mixt_s[...], outw[...], TN) + outb[...]
            mid_s[...] = mid
            unit, _ = unit_rows_of(mid)
            normed = (unit * gain[1:2, :] + shift[1:2, :]).astype(BF)
            ready(2)
            up_s[...] = mm(normed, upw[...])
            for c in range(parts):
                cols = slice(c * dim, (c + 1) * dim)
                u = up_s[:, cols] + upb[:, cols]
                cdf = 0.5 + 0.5 * lax.erf(u * 0.5**0.5)
                hid_s[:, cols] = (u * cdf).astype(BF)
                gp_s[:, cols] = (
                    cdf + u * (jnp.exp(u * u * -0.5) * (2 * np.pi) ** -0.5)
                ).astype(BF)
            ready(3)
            low = (mid_s[...] + downb[...] + mm(hid_s[...], downw[...])).astype(BF)
            y_s[...] = low
            act_s[...] = jnp.where(crop < live[0], low, jnp.zeros_like(low))
            at = pl.multiple_of(crop * LEN, LEN)
            copies.save(act_s, act_h.at[pl.ds(at, LEN)])
            copies.finish()

    outs = [shape(own.shape, BF)] + saved
    scratch = [
        pltpu.VMEM((LEN, dim), BF),
        pltpu.VMEM((dim, LEN), BF),
        pltpu.VMEM((HEADS * LEN, LEN), F32),
        pltpu.VMEM((LEN, wide), F32),
    ]
    if manual:
        scratch += [pltpu.VMEM((LEN, dim), BF)] + [vmem_like(a) for a in weights]
    aliases = {} if act is None else {len(ins) - 1: 0}
    spaces = "ss" + ("h" if manual else "v") * (count + 11) + "h" * len(before)
    out = call(
        kernel,
        outs,
        ins,
        scratch,
        16,
        aliases,
        "layer_forward",
        after,
        FIRST_LIMIT if manual else FORWARD_LIMIT,
        spaces,
        "h" + "v" * 7,
    )
    return out[0], out[1:]


def crop_weight(live, masks, crop, section):
    if section == 0:
        return 1.0
    count = jnp.where(live[0] > crop, masks[crop], 0)
    return jnp.full((1, 1), count, jnp.int32).astype(F32) / MASK_MEAN


def add_row(ref, row, values):
    ref[row : row + 1, :] = ref[row : row + 1, :] + jnp.sum(values, axis=0, keepdims=True)


def lay_out(own, bit, keep, send, block, index, row, count, at):
    src = pl.ds(row if isinstance(row, int) else pl.multiple_of(row, PAD), count)
    dst = pl.ds(at if isinstance(at, int) else pl.multiple_of(at, PAD), count)
    mine = own == bit

    @pl.when(mine)
    def _():
        keep[dst, :] = block[index, src, :]

    @pl.when(jnp.logical_not(mine))
    def _():
        send[dst, :] = block[index, src, :]


def keep_given(active, given, bufs):
    @pl.when(jnp.logical_not(active))
    def _():
        for old, new in zip(given, bufs):
            new[...] = old[...]


def pair_shapes(rows, dim):
    return [shape((rows, dim), BF)] * 2


def joined(refs, cols):
    return jnp.concatenate([r[:, cols] for r in refs], axis=0)


def wait_all(copies):
    for copy in copies:
        copy.wait()


def mlp_grad(section, info, live, masks, g, saved, params, after):
    mixts = [s[3] for s in saved]
    mids, gps, hids = ([s[k] for s in saved] for k in (4, 5, 6))
    upw, downw, gain, shift = params[4], params[6], params[8], params[9]
    rows, dim = g.shape
    wide = upw.shape[1]
    parts = wide // dim
    crops = len(saved)
    share = dim // GROUPS
    ins = [info, live, masks, g, gain, shift, downw, upw] + mids + gps + hids + mixts

    def kernel(info, live, masks, g_s, gain, shift, downw, upw, *refs):
        mid_s, gp_s, hid_s, mixt_s = (refs[i * crops : (i + 1) * crops] for i in range(4))
        refs = refs[4 * crops :]
        send_a, keep_a, send_b, keep_b, gmid_s, small_s = refs[:6]
        gu_s, block_s, low_s, normt_s, back_s = refs[7:]

        @pl.when(info[0] == section)
        def _():
            small_s[...] = jnp.zeros_like(small_s)
            for c in range(crops):
                crop = slice(c * LEN, (c + 1) * LEN)
                grad = g_s[crop, :].astype(F32) * crop_weight(live, masks, c, section)
                low = grad.astype(BF)
                low_s[crop, :] = low
                add_row(small_s, ROW_DOWN, low.astype(F32))
                unit, _ = unit_rows_of(mid_s[c][...])
                normt_s[:, crop] = (unit * gain[1:2, :] + shift[1:2, :]).astype(BF).T
            for c in range(parts):
                cols = slice(c * dim, (c + 1) * dim)
                block_s[c] = mm(joined(hid_s, cols), low_s[...], TN).astype(BF)

            @pl.loop(0, GROUPS * parts)
            def _(i):
                shard, row = i // parts, (i % parts) * share
                at = (shard // 2) * dim + row
                lay_out(info[1], shard % 2, keep_a, send_a, block_s, shard, row, share, at)

            for c in range(parts):
                cols = slice(c * dim, (c + 1) * dim)
                grad_up = mm(low_s[...], downw[cols, :], NT) * joined(gp_s, cols).astype(F32)
                grad_up = grad_up.astype(BF)
                gu_s[:, cols] = grad_up
                small_s[ROW_UP + c : ROW_UP + c + 1, :] = jnp.sum(
                    grad_up.astype(F32), axis=0, keepdims=True
                )
            back_s[...] = mm(gu_s[...], upw[...], NT)
            for c in range(crops):
                crop = slice(c * LEN, (c + 1) * LEN)
                grad = g_s[crop, :].astype(F32) * crop_weight(live, masks, c, section)
                unit, inverse = unit_rows_of(mid_s[c][...])
                back = back_s[crop, :]
                gmid = grad + norm_back(back, unit, inverse, gain[1:2, :])
                gmid_s[crop, :] = gmid
                low = gmid.astype(BF)
                low_s[crop, :] = low
                add_row(small_s, ROW_GAIN + 1, back * unit)
                add_row(small_s, ROW_SHIFT + 1, back)
                add_row(small_s, ROW_OUT, low.astype(F32))
            for c in range(parts):
                block_s[c] = mm(normt_s[...], gu_s[:, c * dim : (c + 1) * dim]).astype(BF)
            mixt = jnp.concatenate([m[...] for m in mixt_s], axis=1)
            block_s[parts] = mm(mixt, low_s[...]).astype(BF)

            @pl.loop(0, GROUPS * (parts + 1))
            def _(i):
                shard, c = i // (parts + 1), i % (parts + 1)
                at = ((shard % 2) * (parts + 1) + c) * share
                lay_out(info[2], shard // 2, keep_b, send_b, block_s, c, shard * share, share, at)

    scratch = [
        pltpu.VMEM((rows, wide), BF),
        pltpu.VMEM((parts + 1, dim, dim), BF),
        pltpu.VMEM((rows, dim), BF),
        pltpu.VMEM((dim, rows), BF),
        pltpu.VMEM((rows, dim), F32),
    ]
    outs = pair_shapes(2 * dim, dim) + pair_shapes(2 * (parts + 1) * share, dim)
    outs += [shape((rows, dim), F32), shape((PAD, dim), F32), TOKEN]
    out = call(kernel, outs, ins, scratch, 0, {}, "mlp_grad", after, MLP_LIMIT, micros=10)
    return out[:4], out[4], out[5], out[6]


def rotate_back(block, tab_t):
    half = HEAD_DIM // 2
    cos, sin = tab_t[0], tab_t[1]
    out = []
    for at in range(0, block.shape[0], HEAD_DIM):
        a, b = block[at : at + half], block[at + half : at + HEAD_DIM]
        out += [a * cos + b * sin, b * cos - a * sin]
    return jnp.concatenate(out, axis=0)


def attention_grad(section, info, gmid, small, xs, saved, params, tab_t, before, after):
    qkvs, probs, mixts = [s[1] for s in saved], [s[2] for s in saved], [s[3] for s in saved]
    qkvw, outw, gain, shift = params[0], params[2], params[8], params[9]
    rows, dim = gmid.shape
    blocks = dim // 128
    per = 128 // HEAD_DIM
    crops = len(saved)
    given = [] if before is None else [before]
    ins = [info, gmid, outw, small, gain, shift, tab_t, qkvw]
    ins += qkvs + probs + mixts + list(xs) + given

    def kernel(info, gmid_s, outw, small_s, gain, shift, tab_t, qkvw, *refs):
        qkv_s, prob_s, mixt_s = (refs[i * crops : (i + 1) * crops] for i in range(3))
        x_s = refs[3 * crops : 3 * crops + len(xs)]
        old = refs[3 * crops + len(xs) : 3 * crops + len(xs) + len(given)]
        refs = refs[3 * crops + len(xs) + len(given) :]
        keep_given(info[0] == section, old, refs[:1])
        dx_s, gqkv_s, normt_s, small_out = refs[:4]
        gmt_s, delta_s, da_s, ds_s, dt_s, kt_s = refs[5:]

        @pl.when(info[0] == section)
        def _():
            low = gmid_s[...].astype(BF)
            gmt_s[...] = mm(outw[...], low, NT).astype(BF)
            for c in range(crops):
                crop = slice(c * LEN, (c + 1) * LEN)
                qkv, prob = qkv_s[c], prob_s[c]
                product = gmt_s[:, crop].astype(F32) * mixt_s[c][...].astype(F32)
                delta_s[...] = jnp.sum(product.reshape(HEADS, HEAD_DIM, LEN), axis=1)[:, None, :]
                kt_s[0] = qkv[:, dim : 2 * dim].T
                kt_s[1] = qkv[:, :dim].T
                for j in range(blocks):
                    v = qkv[:, 2 * dim + 128 * j : 2 * dim + 128 * j + 128]
                    da_s[per * LEN * j : per * LEN * (j + 1), :] = mm(
                        head_stack(v, per), gmt_s[128 * j : 128 * j + 128, crop]
                    )

                def scores(h, _):
                    da = da_s[pl.ds(pl.multiple_of(h * LEN, LEN), LEN), :]
                    ds_s[h] = (prob[h].astype(F32) * (da - delta_s[h])).astype(BF)
                    return 0

                lax.fori_loop(0, HEADS, scores, 0, unroll=2)
                for h in range(HEADS):
                    at = slice(HEAD_DIM * h, HEAD_DIM * (h + 1))
                    dt_s[0, at, :] = mm(kt_s[0, at, :], ds_s[h])
                    dt_s[1, at, :] = mm(kt_s[1, at, :], ds_s[h], NT)
                    dt_s[2, at, :] = mm(gmt_s[at, crop], prob[h], NT)
                dq = rotate_back(dt_s[0] * HEAD_DIM**-0.5, tab_t)
                gqkv_s[crop, :dim] = dq.astype(BF).T
                gqkv_s[crop, dim : 2 * dim] = rotate_back(dt_s[1], tab_t).astype(BF).T
                gqkv_s[crop, 2 * dim :] = dt_s[2].astype(BF).T
            unit, inverse = unit_rows_of(joined(x_s, slice(None)).astype(F32))
            normt_s[...] = (unit * gain[0:1, :] + shift[0:1, :]).astype(BF).T
            back = mm(gqkv_s[...], qkvw[...], NT)
            dx_s[...] = (gmid_s[...] + norm_back(back, unit, inverse, gain[0:1, :])).astype(BF)
            small_out[...] = small_s[...]
            small_out[ROW_GAIN : ROW_GAIN + 1, :] = jnp.sum(back * unit, axis=0, keepdims=True)
            small_out[ROW_SHIFT : ROW_SHIFT + 1, :] = jnp.sum(back, axis=0, keepdims=True)

    outs = [
        shape((rows, dim), BF),
        shape((rows, 3 * dim), BF),
        shape((dim, rows), BF),
        shape(small.shape, F32),
        TOKEN,
    ]
    scratch = [
        pltpu.VMEM((dim, rows), BF),
        pltpu.VMEM((HEADS, 1, LEN), F32),
        pltpu.VMEM((HEADS * LEN, LEN), F32),
        pltpu.VMEM((HEADS, LEN, LEN), BF),
        pltpu.VMEM((3, dim, LEN), F32),
        pltpu.VMEM((2, dim, LEN), BF),
    ]
    aliases = {len(ins) - 1: 0} if given else {}
    out = call(kernel, outs, ins, scratch, 0, aliases, "attention_grad", after, ATTENTION_LIMIT, micros=ATTENTION_MICROS)
    return out[0], out[1:4], out[4]


def qkv_grad(section, info, kept, before, after):
    gqkv, normt, small = kept
    dim, rows = normt.shape
    share = dim // GROUPS
    half = 3 * share // 2
    given = [] if before is None else list(before)
    ins = [info, gqkv, normt, small] + given

    def kernel(info, gqkv_s, normt_s, small_s, *refs):
        old = refs[: len(given)]
        bufs = refs[len(given) : len(given) + 4]
        send_a, keep_a, send_b, keep_b = bufs
        (block_s,) = refs[len(given) + 5 :]
        keep_given(info[0] == section, old, bufs)

        @pl.when(info[0] == section)
        def _():
            sums = [
                jnp.sum(gqkv_s[:, c * dim : (c + 1) * dim].astype(F32), axis=0, keepdims=True)
                for c in range(3)
            ]
            tail = jnp.concatenate(sums + [small_s[ROW_OUT:, :]], axis=0).astype(BF)
            send_a[2 * half :, :] = tail
            keep_a[2 * half :, :] = tail
            for c in range(3):
                block_s[c] = mm(normt_s[...], gqkv_s[:, c * dim : (c + 1) * dim]).astype(BF)

            @pl.loop(0, GROUPS)
            def _(shard):
                x, y, base = shard % 2, shard // 2, shard * share
                for c in range(3):
                    row, at, left = 0, c * share, share
                    while left:
                        count = min(left, half - at % half)
                        if at < half:
                            own, bit, keep, send, to = info[1], x, keep_a, send_a, y * half + at
                        else:
                            own, bit, keep, send, to = info[2], y, keep_b, send_b, x * half + at - half
                        lay_out(own, bit, keep, send, block_s, c, base + row, count, to)
                        row, at, left = row + count, at + count, left - count

    scratch = [pltpu.VMEM((3, dim, dim), BF)]
    aliases = {len(ins) - 4 + i: i for i in range(4)} if given else {}
    outs = pair_shapes(2 * half + PAD, dim) + pair_shapes(2 * half, dim) + [TOKEN]
    out = call(kernel, outs, ins, scratch, 0, aliases, "qkv_grad", after, QKV_LIMIT)
    return out[:4], out[4]


STEP = 80


def plus(one, two):
    return (one.astype(F32) + two.astype(F32)).astype(BF)


def add_rows(out, at, one, two, start, count):
    whole = count // STEP * STEP

    @pl.loop(0, whole // STEP)
    def _(i):
        src = pl.ds(pl.multiple_of(start + i * STEP, PAD), STEP)
        dst = pl.ds(pl.multiple_of(at + i * STEP, PAD), STEP)
        out[dst, :] = plus(one[src, :], two[src, :])

    if count > whole:
        src = pl.ds(pl.multiple_of(start + whole, PAD), count - whole)
        out[pl.ds(at + whole, count - whole), :] = plus(one[src, :], two[src, :])


def taking_part(info, sections, middle):
    check = None
    if len(sections) == 1:
        check = info[0] == sections[0]
    if middle:
        inner = jnp.logical_or(info[3] == 1, info[3] == 2)
        check = inner if check is None else jnp.logical_and(check, inner)
    return info[3] >= 0 if check is None else check


def vmem_call(kernel, outs, info, ins, name, after):
    return call(kernel, outs, [info] + ins, [], 0, {}, name, after, 8)


def first_sum(info, sections, keep_a, recv_a, keep_b, recv_b, after):
    dim = keep_b.shape[1]
    sizes = [(k.shape[0] // (2 * PAD) * PAD, k.shape[0] % (2 * PAD)) for k in (keep_a, keep_b)]

    def kernel(info, ka, ra, kb, rb, sa, na, sb, nb):
        @pl.when(taking_part(info, sections, False))
        def _():
            for own, one, two, new, out, (half, extra) in (
                (info[2], ka, ra, na, sa, sizes[0]),
                (info[1], kb, rb, nb, sb, sizes[1]),
            ):
                add_rows(out, 0, one, two, (1 - own) * half, half)
                add_rows(new, 0, one, two, own * half, half)
                if extra:
                    tail = plus(one[2 * half :, :], two[2 * half :, :])
                    new[half:, :] = tail
                    out[half:, :] = tail

    outs = [shape((sum(size), dim), BF) for size in sizes for _ in range(2)]
    return vmem_call(kernel, outs, info, [keep_a, recv_a, keep_b, recv_b], "first_sum", after)


def second_sum(info, sections, keep_a, recv_a, keep_b, recv_b, joint, after):
    dim = keep_b.shape[1]
    top, rest = keep_a.shape[0], keep_b.shape[0]

    def kernel(info, ka, ra, kb, rb, *out):
        @pl.when(taking_part(info, sections, False))
        def _():
            add_rows(out[0], 0, ka, ra, 0, top)
            add_rows(out[-1], out[-1].shape[0] - rest, kb, rb, 0, rest)

    outs = [shape((top + rest, dim), BF)]
    if not joint:
        outs = [shape((top, dim), BF), shape((rest, dim), BF)]
    return vmem_call(kernel, outs, info, [keep_a, recv_a, keep_b, recv_b], "second_sum", after)


def pair_sum(info, sections, one, two, after):
    def kernel(info, one, two, out):
        @pl.when(taking_part(info, sections, True))
        def _():
            add_rows(out, 0, one, two, 0, one.shape[0])

    return vmem_call(kernel, [shape(one.shape, BF)], info, [one, two], "pair_sum", after)[0]


def own_pieces(row, count, width, group):
    share = count * width // GROUPS
    at, pieces = group * share, []
    while at < (group + 1) * share:
        size = min((group + 1) * share - at, width - at % width)
        pieces.append((row + at // width, at % width, size, at - group * share))
        at += size
    return pieces


def finish(info, sources, kind, after):
    dim = sources[0][0].shape[1]
    share = dim // GROUPS
    half = 3 * share // 2
    vectors = ((ROW_QKV, 3), (ROW_OUT, 1), (ROW_UP, 4), (ROW_DOWN, 1))
    if kind == "down":
        rows, outs = dim, [shape((dim, dim), F32)]
    elif kind == "up":
        rows, outs = 5 * share, [shape((share, 4 * dim), F32), shape((share, dim), F32)]
    else:
        rows, outs = 3 * share + PAD, [shape((share, 3 * dim), F32)]
    large = len(outs)
    if kind == "qkv":
        outs += [shape((1, count * dim // GROUPS), F32) for _, count in vectors]
        outs += [shape((2, share), F32)] * 2

    def kernel(info, p0, g0, p1, g1, *refs):
        out_h = refs[:large]
        small = refs[large : len(outs)]
        src = refs[len(outs)]
        stage = refs[len(outs) + 1 : -1]
        sems = refs[-1]
        inner = jnp.logical_or(info[3] == 1, info[3] == 2)
        for section, part, got in ((0, p0, g0), (1, p1, g1)):
            mine = info[0] == section
            lines = pl.ds(sources[section][2], rows)

            @pl.when(jnp.logical_and(mine, inner))
            def _():
                pltpu.make_async_copy(part.at[lines], src, sems.at[0]).start()

            @pl.when(jnp.logical_and(mine, jnp.logical_not(inner)))
            def _():
                pltpu.make_async_copy(got.at[lines], src, sems.at[0]).start()

        pltpu.make_async_copy(p0.at[pl.ds(sources[0][2], rows)], src, sems.at[0]).wait()
        if kind == "down":
            stage[0][...] = src[...].astype(F32)
        elif kind == "up":
            for i in range(4):
                block = src[i * share : (i + 1) * share, :].astype(F32)
                stage[0][:, i * dim : (i + 1) * dim] = block
            stage[1][...] = src[4 * share :, :].astype(F32)
        else:
            for i in range(3):
                at, left, to = i * share, share, 0
                while left:
                    count = min(left, half - at % half)
                    row = at if at < half else at + PAD
                    block = src[row : row + count, :].astype(F32)
                    stage[0][to : to + count, i * dim : (i + 1) * dim] = block
                    at, left, to = at + count, left - count, to + count
        copies = [
            pltpu.make_async_copy(s, o, sems.at[1 + i]) for i, (s, o) in enumerate(zip(stage, out_h))
        ]
        for copy in copies:
            copy.start()
        if kind == "qkv":
            tail = src[half : half + PAD, :].astype(F32)
            for group in range(GROUPS):

                @pl.when(info[1] + 2 * info[2] == group)
                def _():
                    for out, (row, count) in zip(small, vectors):
                        for r, c, size, at in own_pieces(row, count, dim, group):
                            out[:, at : at + size] = tail[r : r + 1, c : c + size]
                    for out, row in zip(small[4:], (ROW_GAIN, ROW_SHIFT)):
                        out[...] = tail[row : row + 2, group * share : (group + 1) * share]

        for copy in copies:
            copy.wait()

    scratch = [pltpu.VMEM((rows, dim), BF)] + [vmem_like(o) for o in outs[:large]]
    ins = [info] + [a for source in sources for a in source[:2]]
    places = "h" * large + "v" * (len(outs) - large)
    return call(kernel, outs, ins, scratch, 4, {}, "finish", after, 12, "saaaa", places)


def flow(shard, axis, pairs, sections):
    if sections == (0, 1):
        return lax.ppermute(shard, axis, pairs)
    peers = lax.axis_size(axis)
    pairs = [(s * peers + i, s * peers + j) for s in sections for i, j in pairs]
    return lax.ppermute(shard, ("section", axis), pairs)


class Reduction:
    def __init__(self, info, sections, bufs, joint):
        self.info, self.sections, self.joint = info, sections, joint
        groups = range(GROUPS)
        self.across = [(g, g ^ 1) for g in groups]
        self.along = [(g, g ^ 2) for g in groups]
        self.line = lax.axis_size("replica") == 4
        send_a, keep_a, send_b, keep_b = bufs
        self.kept = (keep_a, keep_b)
        self.got = (
            flow(send_a, "group", self.across, sections),
            flow(send_b, "group", self.along, sections),
        )

    def group_two(self, after):
        send_a, keep_a, send_b, keep_b = first_sum(
            self.info, self.sections, self.kept[0], self.got[0], self.kept[1], self.got[1], after
        )
        self.kept = (keep_a, keep_b)
        self.got = (
            flow(send_a, "group", self.along, self.sections),
            flow(send_b, "group", self.across, self.sections),
        )
        return keep_a

    def replica_one(self, after):
        self.parts = list(
            second_sum(
                self.info,
                self.sections,
                self.kept[0],
                self.got[0],
                self.kept[1],
                self.got[1],
                self.joint,
                after,
            )
        )
        if self.line:
            self.got = [
                flow(part, "replica", [(0, 1), (3, 2)], self.sections) for part in self.parts
            ]
        else:
            self.parts = [lax.psum(part, "replica") for part in self.parts]
            self.got = list(self.parts)
        return self.parts[0]

    def replica_next(self, pairs, after):
        for i in range(len(self.parts)):
            if self.line:
                self.parts[i] = after = pair_sum(
                    self.info, self.sections, self.parts[i], self.got[i], after
                )
                self.got[i] = flow(self.parts[i], "replica", pairs, self.sections)
        return after

    def replica_two(self, after):
        return self.replica_next([(1, 2), (2, 1)], after)

    def replica_three(self, after):
        return self.replica_next([(1, 0), (2, 3)], after)

    def source(self, half, row):
        index = 0 if self.joint else half
        return self.parts[index], self.got[index], row


def shards(
    block_input,
    cotangent,
    crop_count,
    mask_count,
    qkv_weight,
    qkv_bias,
    out_weight,
    out_bias,
    up_weight,
    up_bias,
    down_weight,
    down_bias,
    norm_gain,
    norm_shift,
):
    params = (
        qkv_weight[0],
        qkv_bias,
        out_weight[0],
        out_bias,
        up_weight[0],
        up_bias,
        down_weight[0],
        down_bias,
        norm_gain[0],
        norm_shift[0],
    )
    rows, dim = block_input.shape
    tab = jnp.asarray(rotary_tables())
    tab_t = jnp.asarray(rotary_columns())
    group = lax.axis_index("group")
    assert lax.axis_size("group") == GROUPS
    info = jnp.stack([lax.axis_index("section"), group % 2, group // 2, lax.axis_index("replica")])

    def to_other(shard, pairs):
        return lax.ppermute(shard, "section", pairs)

    act, first = forward(0, info, crop_count, block_input, None, params, tab, None)
    arrived = [to_other(first[0], [(0, 1)])]
    act, second = forward(1, info, crop_count, block_input, arrived[0], params, tab, act)
    arrived.append(to_other(second[0], [(0, 1)]))
    act, third = forward(2, info, crop_count, block_input, arrived[1], params, tab, act)
    kept_one, kept_zero = (second, third), (first, second)

    common = (info, crop_count, mask_count)
    bufs, gmid, small, last = mlp_grad(1, *common, cotangent, kept_one, params, None)
    one = Reduction(info, (1,), bufs, True)
    dx, kept, last = attention_grad(
        1, info, gmid, small, arrived, kept_one, params, tab_t, None, last
    )
    grad_back = to_other(dx, [(1, 0)])
    bufs_three, last = qkv_grad(1, info, kept, None, last)
    last = one.group_two(last)
    bufs, gmid, small, last = mlp_grad(0, *common, grad_back, kept_zero, params, last)
    two = Reduction(info, (0,), bufs, False)
    last = one.replica_one(last)
    dx, kept, last = attention_grad(
        0, info, gmid, small, [block_input], kept_zero, params, tab_t, dx, last
    )
    bufs, last = qkv_grad(0, info, kept, bufs_three, last)
    three = Reduction(info, (0, 1), bufs, True)
    last = two.group_two(last)
    last = three.group_two(last)
    last = one.replica_two(last)
    last = two.replica_one(last)
    last = two.replica_two(last)
    last = three.replica_one(last)
    last = one.replica_three(last)
    last = two.replica_three(last)
    last = three.replica_two(last)
    (grad_down,) = finish(info, (two.source(0, 0), one.source(0, 0)), "down", last)
    last = three.replica_three(grad_down)
    grad_up, grad_out = finish(info, (two.source(1, 0), one.source(1, dim)), "up", last)
    grad_qkv, *small = finish(info, (three.source(0, 0), three.source(0, 0)), "qkv", grad_out)
    qkv_b, out_b, up_b, down_b, gain, shift = small
    return (
        act[None],
        dx[None],
        grad_qkv[None],
        qkv_b,
        grad_out[None],
        out_b,
        grad_up[None],
        up_b,
        grad_down[None],
        down_b,
        gain[None],
        shift[None],
    )


def solution(mesh):
    rows = P(("group", "replica"))
    stack = P("section")
    return jax.shard_map(
        shards,
        mesh=mesh,
        in_specs=(rows,) * 4 + (stack,) * 10,
        out_specs=(
            P("section", ("group", "replica"), None),
            P("section", ("group", "replica"), None),
            P("section", "group", None),
            P("section", "group"),
            P("section", "group", None),
            P("section", "group"),
            P("section", "group", None),
            P("section", "group"),
            P("section", "group", None),
            P("section", "group"),
            P("section", None, "group"),
            P("section", None, "group"),
        ),
        check_vma=False,
    )
```

```python
import jax
import jax.numpy as jnp
import numpy as np
from jax import lax
from jax.experimental import pallas as pl
from jax.experimental.pallas import tpu as pltpu
from jax.sharding import PartitionSpec as P

HEADS = 20
HEAD_DIM = 32
LEN = 256
MASK_MEAN = 38
CROP_DEV = 2
EPSILON = 1e-05
ROTARY_BASE = 10000.0

BF = jnp.bfloat16
F32 = jnp.float32
NN = (((1,), (0,)), ((), ()))
NT = (((1,), (1,)), ((), ()))
TN = (((0,), (0,)), ((), ()))

FIRST_LIMIT, FORWARD_LIMIT, MLP_LIMIT, ATTENTION_LIMIT, QKV_LIMIT = 40, 14, 13, 16, 7
ATTENTION_MICROS = 12
GROUPS = 4
PAD = 16
ROW_QKV, ROW_OUT, ROW_UP, ROW_DOWN, ROW_GAIN, ROW_SHIFT = 0, 3, 4, 8, 9, 11

ANY = pl.BlockSpec(memory_space=pl.ANY)
HBM = pl.BlockSpec(memory_space=pltpu.HBM)
VMEM = pl.BlockSpec(memory_space=pltpu.VMEM)
SMEM = pl.BlockSpec(memory_space=pltpu.SMEM)


def shape(dims, dtype):
    return jax.ShapeDtypeStruct(dims, dtype)


def mm(left, right, dims=NN):
    return lax.dot_general(left, right, dims, preferred_element_type=F32)


def unit_rows_of(values):
    centred = values - jnp.mean(values, axis=-1, keepdims=True)
    inverse = lax.rsqrt(jnp.mean(centred * centred, axis=-1, keepdims=True) + EPSILON)
    return centred * inverse, inverse


def norm_back(grad, unit, inverse, gain):
    scaled = grad * gain
    return inverse * (
        scaled
        - jnp.mean(scaled, axis=-1, keepdims=True)
        - unit * jnp.mean(scaled * unit, axis=-1, keepdims=True)
    )


def rotary_tables():
    lane = np.arange(128) % HEAD_DIM
    half = HEAD_DIM // 2
    freq = ROTARY_BASE ** (-(lane % half).astype(np.float64) * (2.0 / HEAD_DIM))
    angles = np.arange(LEN)[:, None] * freq[None, :]
    sign = np.where(lane < half, -1.0, 1.0)[None, :]
    return np.stack([np.cos(angles), np.sin(angles) * sign]).astype(np.float32)


def rotary_columns():
    half = HEAD_DIM // 2
    freq = ROTARY_BASE ** (-np.arange(half, dtype=np.float64) * (2.0 / HEAD_DIM))
    angles = freq[:, None] * np.arange(LEN)[None, :]
    return np.stack([np.cos(angles), np.sin(angles)]).astype(np.float32)


def swap_halves(values):
    lane = lax.broadcasted_iota(jnp.int32, values.shape, 1) % HEAD_DIM
    half = HEAD_DIM // 2
    return jnp.where(
        lane < half,
        pltpu.roll(values, 128 - half, axis=1),
        pltpu.roll(values, half, axis=1),
    )


def head_stack(block, per):
    head = lax.broadcasted_iota(jnp.int32, block.shape, 1) // HEAD_DIM
    return jnp.concatenate(
        [jnp.where(head == h, block, jnp.zeros_like(block)) for h in range(per)], axis=0
    )


class Copies:
    def __init__(self, sems):
        self.sems = sems
        self.used = 0
        self.open = []

    def start(self, src, dst):
        copy = pltpu.make_async_copy(src, dst, self.sems.at[self.used])
        self.used += 1
        copy.start()
        return copy

    def save(self, src, dst):
        self.open.append(self.start(src, dst))

    def finish(self):
        for copy in self.open:
            copy.wait()


def call(kernel, outs, ins, scratch, sems, aliases, name, after=None, limit=16, spaces=None, out_spaces=None, micros=0.1):
    count = len(ins)
    places = {"v": VMEM, "h": HBM, "a": ANY, "s": SMEM}
    spaces = spaces or "v" * count
    out_spaces = out_spaces or "v" * len(outs)
    in_specs = [SMEM if a.ndim == 1 else places[p] for a, p in zip(ins, spaces)]
    ins = [pltpu.with_memory_space_constraint(a, pltpu.HBM) if p == "h" else a for a, p in zip(ins, spaces)]
    body = kernel
    if after is not None:
        ins = list(ins) + [after]
        in_specs = in_specs + [ANY]

        def body(*refs):
            kernel(*refs[:count], *refs[count + 1 :])

    outs = [pltpu.HBM(o.shape, o.dtype) if p == "h" else o for o, p in zip(outs, out_spaces)]
    return pl.pallas_call(
        body,
        out_shape=outs,
        in_specs=in_specs,
        out_specs=[places[p] for p in out_spaces],
        scratch_shapes=scratch + ([pltpu.SemaphoreType.DMA((sems,))] if sems else []),
        input_output_aliases=aliases,
        compiler_params=pltpu.CompilerParams(vmem_limit_bytes=limit << 20),
        cost_estimate=pl.CostEstimate(
            flops=int(micros * 1.15e9), bytes_accessed=0, transcendentals=0
        ),
        name=name,
    )(*ins)


TOKEN = jax.ShapeDtypeStruct((8, 128), F32)


def vmem_like(arr):
    return pltpu.VMEM(arr.shape, arr.dtype)


def forward(slot, info, live, own, arrived, params, tab, act, after=None):
    qkvw, qkvb, outw, outb, upw, upb, downw, downb, gain, shift = params
    dim = own.shape[1]
    blocks = dim // 128
    wide = upw.shape[1]
    parts = wide // dim
    per = 128 // HEAD_DIM
    manual = slot == 0
    saved = [
        shape((LEN, dim), BF),
        shape((LEN, 3 * dim), BF),
        shape((HEADS, LEN, LEN), BF),
        shape((dim, LEN), BF),
        shape((LEN, dim), F32),
        shape((LEN, wide), BF),
        shape((LEN, wide), BF),
    ]
    weights = [qkvb, outb, upb, downb, gain, shift, tab, qkvw, outw, upw, downw]
    sources = [own] if slot == 0 else [arrived] if slot == 2 else [own, arrived]
    before = [] if act is None else [act]
    ins = [info, live] + sources + weights + before
    count = len(sources)

    def kernel(info, live, *refs):
        xs = refs[:count]
        given = refs[count : count + 11]
        act_h, *outs = refs[count + 11 + len(before) : count + 19 + len(before)]
        scratch = refs[count + 19 + len(before) :]
        act_s, vt_s, score_s, up_s = scratch[:4]
        sems = scratch[-1]
        y_s, qkv_s, prob_s, mixt_s, mid_s, gp_s, hid_s = outs
        used = scratch[4:-1] if manual else xs[-1:] + given
        qkvb, outb, upb, downb, gain, shift, tab, qkvw, outw, upw, downw = used[1:]
        crop = slot - info[0]

        @pl.when(jnp.logical_and(crop >= 0, crop < CROP_DEV))
        def _():
            copies = Copies(sems)
            heavy = []
            if manual:
                rows = xs[0].at[pl.ds(0, LEN)]
                loads = [copies.start(h, s) for h, s in zip((rows,) + given, used)]
                heavy = loads[8:]
                wait_all(loads[:8])
                x = used[0][...].astype(F32)
            elif slot == 1:
                x = jnp.where(info[0] == 0, xs[0][LEN:, :], xs[1][...]).astype(F32)
            else:
                x = xs[0][...].astype(F32)

            def ready(index):
                if manual:
                    heavy[index].wait()

            unit, _ = unit_rows_of(x)
            normed = (unit * gain[0:1, :] + shift[0:1, :]).astype(BF)
            ready(0)
            third = mm(normed, qkvw[:, 2 * dim :]) + qkvb[:, 2 * dim :]
            low = third.astype(BF)
            qkv_s[:, 2 * dim :] = low
            vt_s[...] = low.T
            for part in range(2):
                third = mm(normed, qkvw[:, part * dim : (part + 1) * dim])
                third = third + qkvb[:, part * dim : (part + 1) * dim]
                for j in range(blocks):
                    b = third[:, 128 * j : 128 * j + 128]
                    b = b * tab[0] + swap_halves(b) * tab[1]
                    if part == 0:
                        b = b * HEAD_DIM**-0.5
                    at = part * dim + 128 * j
                    qkv_s[:, at : at + 128] = b.astype(BF)
            for j in range(blocks):
                q = qkv_s[:, 128 * j : 128 * j + 128]
                k = qkv_s[:, dim + 128 * j : dim + 128 * j + 128]
                score_s[per * LEN * j : per * LEN * (j + 1), :] = mm(head_stack(k, per), q, NT)

            def soft(h, _):
                s = score_s[pl.ds(pl.multiple_of(h * LEN, LEN), LEN), :]
                e = jnp.exp(s - jnp.max(s, axis=0, keepdims=True))
                prob_s[h] = (e * (1.0 / jnp.sum(e, axis=0, keepdims=True))).astype(BF)
                return 0

            lax.fori_loop(0, HEADS, soft, 0, unroll=2)
            for h in range(HEADS):
                at = slice(HEAD_DIM * h, HEAD_DIM * (h + 1))
                mixt_s[at, :] = mm(vt_s[at, :], prob_s[h]).astype(BF)
            ready(1)
            mid = x + mm(mixt_s[...], outw[...], TN) + outb[...]
            mid_s[...] = mid
            unit, _ = unit_rows_of(mid)
            normed = (unit * gain[1:2, :] + shift[1:2, :]).astype(BF)
            ready(2)
            up_s[...] = mm(normed, upw[...])
            for c in range(parts):
                cols = slice(c * dim, (c + 1) * dim)
                u = up_s[:, cols] + upb[:, cols]
                cdf = 0.5 + 0.5 * lax.erf(u * 0.5**0.5)
                hid_s[:, cols] = (u * cdf).astype(BF)
                gp_s[:, cols] = (
                    cdf + u * (jnp.exp(u * u * -0.5) * (2 * np.pi) ** -0.5)
                ).astype(BF)
            ready(3)
            low = (mid_s[...] + downb[...] + mm(hid_s[...], downw[...])).astype(BF)
            y_s[...] = low
            act_s[...] = jnp.where(crop < live[0], low, jnp.zeros_like(low))
            at = pl.multiple_of(crop * LEN, LEN)
            copies.save(act_s, act_h.at[pl.ds(at, LEN)])
            copies.finish()

    outs = [shape(own.shape, BF)] + saved
    scratch = [
        pltpu.VMEM((LEN, dim), BF),
        pltpu.VMEM((dim, LEN), BF),
        pltpu.VMEM((HEADS * LEN, LEN), F32),
        pltpu.VMEM((LEN, wide), F32),
    ]
    if manual:
        scratch += [pltpu.VMEM((LEN, dim), BF)] + [vmem_like(a) for a in weights]
    aliases = {} if act is None else {len(ins) - 1: 0}
    spaces = "ss" + ("h" if manual else "v") * (count + 11) + "h" * len(before)
    out = call(
        kernel,
        outs,
        ins,
        scratch,
        16,
        aliases,
        "layer_forward",
        after,
        FIRST_LIMIT if manual else FORWARD_LIMIT,
        spaces,
        "h" + "v" * 7,
    )
    return out[0], out[1:]


def crop_weight(live, masks, crop, section):
    if section == 0:
        return 1.0
    count = jnp.where(live[0] > crop, masks[crop], 0)
    return jnp.full((1, 1), count, jnp.int32).astype(F32) / MASK_MEAN


def add_row(ref, row, values):
    ref[row : row + 1, :] = ref[row : row + 1, :] + jnp.sum(values, axis=0, keepdims=True)


def lay_out(own, bit, keep, send, block, index, row, count, at):
    src = pl.ds(row if isinstance(row, int) else pl.multiple_of(row, PAD), count)
    dst = pl.ds(at if isinstance(at, int) else pl.multiple_of(at, PAD), count)
    mine = own == bit

    @pl.when(mine)
    def _():
        keep[dst, :] = block[index, src, :]

    @pl.when(jnp.logical_not(mine))
    def _():
        send[dst, :] = block[index, src, :]


def keep_given(active, given, bufs):
    @pl.when(jnp.logical_not(active))
    def _():
        for old, new in zip(given, bufs):
            new[...] = old[...]


def pair_shapes(rows, dim):
    return [shape((rows, dim), BF)] * 2


def joined(refs, cols):
    return jnp.concatenate([r[:, cols] for r in refs], axis=0)


def wait_all(copies):
    for copy in copies:
        copy.wait()


def mlp_grad(section, info, live, masks, g, saved, params, after):
    mixts = [s[3] for s in saved]
    mids, gps, hids = ([s[k] for s in saved] for k in (4, 5, 6))
    upw, downw, gain, shift = params[4], params[6], params[8], params[9]
    rows, dim = g.shape
    wide = upw.shape[1]
    parts = wide // dim
    crops = len(saved)
    share = dim // GROUPS
    ins = [info, live, masks, g, gain, shift, downw, upw] + mids + gps + hids + mixts

    def kernel(info, live, masks, g_s, gain, shift, downw, upw, *refs):
        mid_s, gp_s, hid_s, mixt_s = (refs[i * crops : (i + 1) * crops] for i in range(4))
        refs = refs[4 * crops :]
        send_a, keep_a, send_b, keep_b, gmid_s, small_s = refs[:6]
        gu_s, block_s, low_s, normt_s, back_s = refs[7:]

        @pl.when(info[0] == section)
        def _():
            small_s[...] = jnp.zeros_like(small_s)
            for c in range(crops):
                crop = slice(c * LEN, (c + 1) * LEN)
                grad = g_s[crop, :].astype(F32) * crop_weight(live, masks, c, section)
                low = grad.astype(BF)
                low_s[crop, :] = low
                add_row(small_s, ROW_DOWN, low.astype(F32))
                unit, _ = unit_rows_of(mid_s[c][...])
                normt_s[:, crop] = (unit * gain[1:2, :] + shift[1:2, :]).astype(BF).T
            for c in range(parts):
                cols = slice(c * dim, (c + 1) * dim)
                block_s[c] = mm(joined(hid_s, cols), low_s[...], TN).astype(BF)

            @pl.loop(0, GROUPS * parts)
            def _(i):
                shard, row = i // parts, (i % parts) * share
                at = (shard // 2) * dim + row
                lay_out(info[1], shard % 2, keep_a, send_a, block_s, shard, row, share, at)

            for c in range(parts):
                cols = slice(c * dim, (c + 1) * dim)
                grad_up = mm(low_s[...], downw[cols, :], NT) * joined(gp_s, cols).astype(F32)
                grad_up = grad_up.astype(BF)
                gu_s[:, cols] = grad_up
                small_s[ROW_UP + c : ROW_UP + c + 1, :] = jnp.sum(
                    grad_up.astype(F32), axis=0, keepdims=True
                )
            back_s[...] = mm(gu_s[...], upw[...], NT)
            for c in range(crops):
                crop = slice(c * LEN, (c + 1) * LEN)
                grad = g_s[crop, :].astype(F32) * crop_weight(live, masks, c, section)
                unit, inverse = unit_rows_of(mid_s[c][...])
                back = back_s[crop, :]
                gmid = grad + norm_back(back, unit, inverse, gain[1:2, :])
                gmid_s[crop, :] = gmid
                low = gmid.astype(BF)
                low_s[crop, :] = low
                add_row(small_s, ROW_GAIN + 1, back * unit)
                add_row(small_s, ROW_SHIFT + 1, back)
                add_row(small_s, ROW_OUT, low.astype(F32))
            for c in range(parts):
                block_s[c] = mm(normt_s[...], gu_s[:, c * dim : (c + 1) * dim]).astype(BF)
            mixt = jnp.concatenate([m[...] for m in mixt_s], axis=1)
            block_s[parts] = mm(mixt, low_s[...]).astype(BF)

            @pl.loop(0, GROUPS * (parts + 1))
            def _(i):
                shard, c = i // (parts + 1), i % (parts + 1)
                at = ((shard % 2) * (parts + 1) + c) * share
                lay_out(info[2], shard // 2, keep_b, send_b, block_s, c, shard * share, share, at)

    scratch = [
        pltpu.VMEM((rows, wide), BF),
        pltpu.VMEM((parts + 1, dim, dim), BF),
        pltpu.VMEM((rows, dim), BF),
        pltpu.VMEM((dim, rows), BF),
        pltpu.VMEM((rows, dim), F32),
    ]
    outs = pair_shapes(2 * dim, dim) + pair_shapes(2 * (parts + 1) * share, dim)
    outs += [shape((rows, dim), F32), shape((PAD, dim), F32), TOKEN]
    out = call(kernel, outs, ins, scratch, 0, {}, "mlp_grad", after, MLP_LIMIT, micros=10)
    return out[:4], out[4], out[5], out[6]


def rotate_back(block, tab_t):
    half = HEAD_DIM // 2
    cos, sin = tab_t[0], tab_t[1]
    out = []
    for at in range(0, block.shape[0], HEAD_DIM):
        a, b = block[at : at + half], block[at + half : at + HEAD_DIM]
        out += [a * cos + b * sin, b * cos - a * sin]
    return jnp.concatenate(out, axis=0)


def attention_grad(section, info, gmid, small, xs, saved, params, tab_t, before, after):
    qkvs, probs, mixts = [s[1] for s in saved], [s[2] for s in saved], [s[3] for s in saved]
    qkvw, outw, gain, shift = params[0], params[2], params[8], params[9]
    rows, dim = gmid.shape
    blocks = dim // 128
    per = 128 // HEAD_DIM
    crops = len(saved)
    given = [] if before is None else [before]
    ins = [info, gmid, outw, small, gain, shift, tab_t, qkvw]
    ins += qkvs + probs + mixts + list(xs) + given

    def kernel(info, gmid_s, outw, small_s, gain, shift, tab_t, qkvw, *refs):
        qkv_s, prob_s, mixt_s = (refs[i * crops : (i + 1) * crops] for i in range(3))
        x_s = refs[3 * crops : 3 * crops + len(xs)]
        old = refs[3 * crops + len(xs) : 3 * crops + len(xs) + len(given)]
        refs = refs[3 * crops + len(xs) + len(given) :]
        keep_given(info[0] == section, old, refs[:1])
        dx_s, gqkv_s, normt_s, small_out = refs[:4]
        gmt_s, delta_s, da_s, ds_s, dt_s, kt_s = refs[5:]

        @pl.when(info[0] == section)
        def _():
            low = gmid_s[...].astype(BF)
            gmt_s[...] = mm(outw[...], low, NT).astype(BF)
            for c in range(crops):
                crop = slice(c * LEN, (c + 1) * LEN)
                qkv, prob = qkv_s[c], prob_s[c]
                product = gmt_s[:, crop].astype(F32) * mixt_s[c][...].astype(F32)
                delta_s[...] = jnp.sum(product.reshape(HEADS, HEAD_DIM, LEN), axis=1)[:, None, :]
                kt_s[0] = qkv[:, dim : 2 * dim].T
                kt_s[1] = qkv[:, :dim].T
                for j in range(blocks):
                    v = qkv[:, 2 * dim + 128 * j : 2 * dim + 128 * j + 128]
                    da_s[per * LEN * j : per * LEN * (j + 1), :] = mm(
                        head_stack(v, per), gmt_s[128 * j : 128 * j + 128, crop]
                    )

                def scores(h, _):
                    da = da_s[pl.ds(pl.multiple_of(h * LEN, LEN), LEN), :]
                    ds_s[h] = (prob[h].astype(F32) * (da - delta_s[h])).astype(BF)
                    return 0

                lax.fori_loop(0, HEADS, scores, 0, unroll=2)
                for h in range(HEADS):
                    at = slice(HEAD_DIM * h, HEAD_DIM * (h + 1))
                    dt_s[0, at, :] = mm(kt_s[0, at, :], ds_s[h])
                    dt_s[1, at, :] = mm(kt_s[1, at, :], ds_s[h], NT)
                    dt_s[2, at, :] = mm(gmt_s[at, crop], prob[h], NT)
                dq = rotate_back(dt_s[0] * HEAD_DIM**-0.5, tab_t)
                gqkv_s[crop, :dim] = dq.astype(BF).T
                gqkv_s[crop, dim : 2 * dim] = rotate_back(dt_s[1], tab_t).astype(BF).T
                gqkv_s[crop, 2 * dim :] = dt_s[2].astype(BF).T
            unit, inverse = unit_rows_of(joined(x_s, slice(None)).astype(F32))
            normt_s[...] = (unit * gain[0:1, :] + shift[0:1, :]).astype(BF).T
            back = mm(gqkv_s[...], qkvw[...], NT)
            dx_s[...] = (gmid_s[...] + norm_back(back, unit, inverse, gain[0:1, :])).astype(BF)
            small_out[...] = small_s[...]
            small_out[ROW_GAIN : ROW_GAIN + 1, :] = jnp.sum(back * unit, axis=0, keepdims=True)
            small_out[ROW_SHIFT : ROW_SHIFT + 1, :] = jnp.sum(back, axis=0, keepdims=True)

    outs = [
        shape((rows, dim), BF),
        shape((rows, 3 * dim), BF),
        shape((dim, rows), BF),
        shape(small.shape, F32),
        TOKEN,
    ]
    scratch = [
        pltpu.VMEM((dim, rows), BF),
        pltpu.VMEM((HEADS, 1, LEN), F32),
        pltpu.VMEM((HEADS * LEN, LEN), F32),
        pltpu.VMEM((HEADS, LEN, LEN), BF),
        pltpu.VMEM((3, dim, LEN), F32),
        pltpu.VMEM((2, dim, LEN), BF),
    ]
    aliases = {len(ins) - 1: 0} if given else {}
    out = call(kernel, outs, ins, scratch, 0, aliases, "attention_grad", after, ATTENTION_LIMIT, micros=ATTENTION_MICROS)
    return out[0], out[1:4], out[4]


def qkv_grad(section, info, kept, before, after):
    gqkv, normt, small = kept
    dim, rows = normt.shape
    share = dim // GROUPS
    half = 3 * share // 2
    given = [] if before is None else list(before)
    ins = [info, gqkv, normt, small] + given

    def kernel(info, gqkv_s, normt_s, small_s, *refs):
        old = refs[: len(given)]
        bufs = refs[len(given) : len(given) + 4]
        send_a, keep_a, send_b, keep_b = bufs
        (block_s,) = refs[len(given) + 5 :]
        keep_given(info[0] == section, old, bufs)

        @pl.when(info[0] == section)
        def _():
            sums = [
                jnp.sum(gqkv_s[:, c * dim : (c + 1) * dim].astype(F32), axis=0, keepdims=True)
                for c in range(3)
            ]
            tail = jnp.concatenate(sums + [small_s[ROW_OUT:, :]], axis=0).astype(BF)
            send_a[2 * half :, :] = tail
            keep_a[2 * half :, :] = tail
            for c in range(3):
                block_s[c] = mm(normt_s[...], gqkv_s[:, c * dim : (c + 1) * dim]).astype(BF)

            @pl.loop(0, GROUPS)
            def _(shard):
                x, y, base = shard % 2, shard // 2, shard * share
                for c in range(3):
                    row, at, left = 0, c * share, share
                    while left:
                        count = min(left, half - at % half)
                        if at < half:
                            own, bit, keep, send, to = info[1], x, keep_a, send_a, y * half + at
                        else:
                            own, bit, keep, send, to = info[2], y, keep_b, send_b, x * half + at - half
                        lay_out(own, bit, keep, send, block_s, c, base + row, count, to)
                        row, at, left = row + count, at + count, left - count

    scratch = [pltpu.VMEM((3, dim, dim), BF)]
    aliases = {len(ins) - 4 + i: i for i in range(4)} if given else {}
    outs = pair_shapes(2 * half + PAD, dim) + pair_shapes(2 * half, dim) + [TOKEN]
    out = call(kernel, outs, ins, scratch, 0, aliases, "qkv_grad", after, QKV_LIMIT)
    return out[:4], out[4]


STEP = 80


def plus(one, two):
    return (one.astype(F32) + two.astype(F32)).astype(BF)


def add_rows(out, at, one, two, start, count):
    whole = count // STEP * STEP

    @pl.loop(0, whole // STEP)
    def _(i):
        src = pl.ds(pl.multiple_of(start + i * STEP, PAD), STEP)
        dst = pl.ds(pl.multiple_of(at + i * STEP, PAD), STEP)
        out[dst, :] = plus(one[src, :], two[src, :])

    if count > whole:
        src = pl.ds(pl.multiple_of(start + whole, PAD), count - whole)
        out[pl.ds(at + whole, count - whole), :] = plus(one[src, :], two[src, :])


def taking_part(info, sections, middle):
    check = None
    if len(sections) == 1:
        check = info[0] == sections[0]
    if middle:
        inner = jnp.logical_or(info[3] == 1, info[3] == 2)
        check = inner if check is None else jnp.logical_and(check, inner)
    return info[3] >= 0 if check is None else check


def vmem_call(kernel, outs, info, ins, name, after):
    return call(kernel, outs, [info] + ins, [], 0, {}, name, after, 8)


def first_sum(info, sections, keep_a, recv_a, keep_b, recv_b, after):
    dim = keep_b.shape[1]
    sizes = [(k.shape[0] // (2 * PAD) * PAD, k.shape[0] % (2 * PAD)) for k in (keep_a, keep_b)]

    def kernel(info, ka, ra, kb, rb, sa, na, sb, nb):
        @pl.when(taking_part(info, sections, False))
        def _():
            for own, one, two, new, out, (half, extra) in (
                (info[2], ka, ra, na, sa, sizes[0]),
                (info[1], kb, rb, nb, sb, sizes[1]),
            ):
                add_rows(out, 0, one, two, (1 - own) * half, half)
                add_rows(new, 0, one, two, own * half, half)
                if extra:
                    tail = plus(one[2 * half :, :], two[2 * half :, :])
                    new[half:, :] = tail
                    out[half:, :] = tail

    outs = [shape((sum(size), dim), BF) for size in sizes for _ in range(2)]
    return vmem_call(kernel, outs, info, [keep_a, recv_a, keep_b, recv_b], "first_sum", after)


def second_sum(info, sections, keep_a, recv_a, keep_b, recv_b, joint, after):
    dim = keep_b.shape[1]
    top, rest = keep_a.shape[0], keep_b.shape[0]

    def kernel(info, ka, ra, kb, rb, *out):
        @pl.when(taking_part(info, sections, False))
        def _():
            add_rows(out[0], 0, ka, ra, 0, top)
            add_rows(out[-1], out[-1].shape[0] - rest, kb, rb, 0, rest)

    outs = [shape((top + rest, dim), BF)]
    if not joint:
        outs = [shape((top, dim), BF), shape((rest, dim), BF)]
    return vmem_call(kernel, outs, info, [keep_a, recv_a, keep_b, recv_b], "second_sum", after)


def pair_sum(info, sections, one, two, after):
    def kernel(info, one, two, out):
        @pl.when(taking_part(info, sections, True))
        def _():
            add_rows(out, 0, one, two, 0, one.shape[0])

    return vmem_call(kernel, [shape(one.shape, BF)], info, [one, two], "pair_sum", after)[0]


def own_pieces(row, count, width, group):
    share = count * width // GROUPS
    at, pieces = group * share, []
    while at < (group + 1) * share:
        size = min((group + 1) * share - at, width - at % width)
        pieces.append((row + at // width, at % width, size, at - group * share))
        at += size
    return pieces


def finish(info, sources, kind, after):
    dim = sources[0][0].shape[1]
    share = dim // GROUPS
    half = 3 * share // 2
    vectors = ((ROW_QKV, 3), (ROW_OUT, 1), (ROW_UP, 4), (ROW_DOWN, 1))
    if kind == "down":
        rows, outs = dim, [shape((dim, dim), F32)]
    elif kind == "up":
        rows, outs = 5 * share, [shape((share, 4 * dim), F32), shape((share, dim), F32)]
    else:
        rows, outs = 3 * share + PAD, [shape((share, 3 * dim), F32)]
    large = len(outs)
    if kind == "qkv":
        outs += [shape((1, count * dim // GROUPS), F32) for _, count in vectors]
        outs += [shape((2, share), F32)] * 2

    def kernel(info, p0, g0, p1, g1, *refs):
        out_h = refs[:large]
        small = refs[large : len(outs)]
        src = refs[len(outs)]
        stage = refs[len(outs) + 1 : -1]
        sems = refs[-1]
        inner = jnp.logical_or(info[3] == 1, info[3] == 2)
        for section, part, got in ((0, p0, g0), (1, p1, g1)):
            mine = info[0] == section
            lines = pl.ds(sources[section][2], rows)

            @pl.when(jnp.logical_and(mine, inner))
            def _():
                pltpu.make_async_copy(part.at[lines], src, sems.at[0]).start()

            @pl.when(jnp.logical_and(mine, jnp.logical_not(inner)))
            def _():
                pltpu.make_async_copy(got.at[lines], src, sems.at[0]).start()

        pltpu.make_async_copy(p0.at[pl.ds(sources[0][2], rows)], src, sems.at[0]).wait()
        if kind == "down":
            stage[0][...] = src[...].astype(F32)
        elif kind == "up":
            for i in range(4):
                block = src[i * share : (i + 1) * share, :].astype(F32)
                stage[0][:, i * dim : (i + 1) * dim] = block
            stage[1][...] = src[4 * share :, :].astype(F32)
        else:
            for i in range(3):
                at, left, to = i * share, share, 0
                while left:
                    count = min(left, half - at % half)
                    row = at if at < half else at + PAD
                    block = src[row : row + count, :].astype(F32)
                    stage[0][to : to + count, i * dim : (i + 1) * dim] = block
                    at, left, to = at + count, left - count, to + count
        copies = [
            pltpu.make_async_copy(s, o, sems.at[1 + i]) for i, (s, o) in enumerate(zip(stage, out_h))
        ]
        for copy in copies:
            copy.start()
        if kind == "qkv":
            tail = src[half : half + PAD, :].astype(F32)
            for group in range(GROUPS):

                @pl.when(info[1] + 2 * info[2] == group)
                def _():
                    for out, (row, count) in zip(small, vectors):
                        for r, c, size, at in own_pieces(row, count, dim, group):
                            out[:, at : at + size] = tail[r : r + 1, c : c + size]
                    for out, row in zip(small[4:], (ROW_GAIN, ROW_SHIFT)):
                        out[...] = tail[row : row + 2, group * share : (group + 1) * share]

        for copy in copies:
            copy.wait()

    scratch = [pltpu.VMEM((rows, dim), BF)] + [vmem_like(o) for o in outs[:large]]
    ins = [info] + [a for source in sources for a in source[:2]]
    places = "h" * large + "v" * (len(outs) - large)
    return call(kernel, outs, ins, scratch, 4, {}, "finish", after, 12, "saaaa", places)


def flow(shard, axis, pairs, sections):
    if sections == (0, 1):
        return lax.ppermute(shard, axis, pairs)
    peers = lax.axis_size(axis)
    pairs = [(s * peers + i, s * peers + j) for s in sections for i, j in pairs]
    return lax.ppermute(shard, ("section", axis), pairs)


class Reduction:
    def __init__(self, info, sections, bufs, joint):
        self.info, self.sections, self.joint = info, sections, joint
        groups = range(GROUPS)
        self.across = [(g, g ^ 1) for g in groups]
        self.along = [(g, g ^ 2) for g in groups]
        self.line = lax.axis_size("replica") == 4
        send_a, keep_a, send_b, keep_b = bufs
        self.kept = (keep_a, keep_b)
        self.got = (
            flow(send_a, "group", self.across, sections),
            flow(send_b, "group", self.along, sections),
        )

    def group_two(self, after):
        send_a, keep_a, send_b, keep_b = first_sum(
            self.info, self.sections, self.kept[0], self.got[0], self.kept[1], self.got[1], after
        )
        self.kept = (keep_a, keep_b)
        self.got = (
            flow(send_a, "group", self.along, self.sections),
            flow(send_b, "group", self.across, self.sections),
        )
        return keep_a

    def replica_one(self, after):
        self.parts = list(
            second_sum(
                self.info,
                self.sections,
                self.kept[0],
                self.got[0],
                self.kept[1],
                self.got[1],
                self.joint,
                after,
            )
        )
        if self.line:
            self.got = [
                flow(part, "replica", [(0, 1), (3, 2)], self.sections) for part in self.parts
            ]
        else:
            self.parts = [lax.psum(part, "replica") for part in self.parts]
            self.got = list(self.parts)
        return self.parts[0]

    def replica_next(self, pairs, after):
        for i in range(len(self.parts)):
            if self.line:
                self.parts[i] = after = pair_sum(
                    self.info, self.sections, self.parts[i], self.got[i], after
                )
                self.got[i] = flow(self.parts[i], "replica", pairs, self.sections)
        return after

    def replica_two(self, after):
        return self.replica_next([(1, 2), (2, 1)], after)

    def replica_three(self, after):
        return self.replica_next([(1, 0), (2, 3)], after)

    def source(self, half, row):
        index = 0 if self.joint else half
        return self.parts[index], self.got[index], row


def shards(
    block_input,
    cotangent,
    crop_count,
    mask_count,
    qkv_weight,
    qkv_bias,
    out_weight,
    out_bias,
    up_weight,
    up_bias,
    down_weight,
    down_bias,
    norm_gain,
    norm_shift,
):
    params = (
        qkv_weight[0],
        qkv_bias,
        out_weight[0],
        out_bias,
        up_weight[0],
        up_bias,
        down_weight[0],
        down_bias,
        norm_gain[0],
        norm_shift[0],
    )
    rows, dim = block_input.shape
    tab = jnp.asarray(rotary_tables())
    tab_t = jnp.asarray(rotary_columns())
    group = lax.axis_index("group")
    assert lax.axis_size("group") == GROUPS
    info = jnp.stack([lax.axis_index("section"), group % 2, group // 2, lax.axis_index("replica")])

    def to_other(shard, pairs):
        return lax.ppermute(shard, "section", pairs)

    act, first = forward(0, info, crop_count, block_input, None, params, tab, None)
    arrived = [to_other(first[0], [(0, 1)])]
    act, second = forward(1, info, crop_count, block_input, arrived[0], params, tab, act)
    arrived.append(to_other(second[0], [(0, 1)]))
    act, third = forward(2, info, crop_count, block_input, arrived[1], params, tab, act)
    kept_one, kept_zero = (second, third), (first, second)

    common = (info, crop_count, mask_count)
    bufs, gmid, small, last = mlp_grad(1, *common, cotangent, kept_one, params, None)
    one = Reduction(info, (1,), bufs, True)
    dx, kept, last = attention_grad(
        1, info, gmid, small, arrived, kept_one, params, tab_t, None, last
    )
    grad_back = to_other(dx, [(1, 0)])
    bufs_three, last = qkv_grad(1, info, kept, None, last)
    last = one.group_two(last)
    bufs, gmid, small, last = mlp_grad(0, *common, grad_back, kept_zero, params, last)
    two = Reduction(info, (0,), bufs, False)
    last = one.replica_one(last)
    dx, kept, last = attention_grad(
        0, info, gmid, small, [block_input], kept_zero, params, tab_t, dx, last
    )
    bufs, last = qkv_grad(0, info, kept, bufs_three, last)
    three = Reduction(info, (0, 1), bufs, True)
    last = two.group_two(last)
    last = one.replica_two(last)
    last = two.replica_one(last)
    last = three.group_two(last)
    last = two.replica_two(last)
    last = three.replica_one(last)
    last = one.replica_three(last)
    last = two.replica_three(last)
    last = three.replica_two(last)
    last = three.replica_three(last)
    (grad_down,) = finish(info, (two.source(0, 0), one.source(0, 0)), "down", last)
    grad_up, grad_out = finish(info, (two.source(1, 0), one.source(1, dim)), "up", grad_down)
    grad_qkv, *small = finish(info, (three.source(0, 0), three.source(0, 0)), "qkv", grad_out)
    qkv_b, out_b, up_b, down_b, gain, shift = small
    return (
        act[None],
        dx[None],
        grad_qkv[None],
        qkv_b,
        grad_out[None],
        out_b,
        grad_up[None],
        up_b,
        grad_down[None],
        down_b,
        gain[None],
        shift[None],
    )


def solution(mesh):
    rows = P(("group", "replica"))
    stack = P("section")
    return jax.shard_map(
        shards,
        mesh=mesh,
        in_specs=(rows,) * 4 + (stack,) * 10,
        out_specs=(
            P("section", ("group", "replica"), None),
            P("section", ("group", "replica"), None),
            P("section", "group", None),
            P("section", "group"),
            P("section", "group", None),
            P("section", "group"),
            P("section", "group", None),
            P("section", "group"),
            P("section", "group", None),
            P("section", "group"),
            P("section", None, "group"),
            P("section", None, "group"),
        ),
        check_vma=False,
    )
```

```python
import jax
import jax.numpy as jnp
import numpy as np
from jax import lax
from jax.experimental import pallas as pl
from jax.experimental.pallas import tpu as pltpu
from jax.sharding import PartitionSpec as P

HEADS = 20
HEAD_DIM = 32
LEN = 256
MASK_MEAN = 38
CROP_DEV = 2
EPSILON = 1e-05
ROTARY_BASE = 10000.0

BF = jnp.bfloat16
F32 = jnp.float32
NN = (((1,), (0,)), ((), ()))
NT = (((1,), (1,)), ((), ()))
TN = (((0,), (0,)), ((), ()))

FIRST_LIMIT, FORWARD_LIMIT, MLP_LIMIT, ATTENTION_LIMIT, QKV_LIMIT = 40, 14, 13, 16, 7
ATTENTION_MICROS = 12
GROUPS = 4
PAD = 16
ROW_QKV, ROW_OUT, ROW_UP, ROW_DOWN, ROW_GAIN, ROW_SHIFT = 0, 3, 4, 8, 9, 11

ANY = pl.BlockSpec(memory_space=pl.ANY)
HBM = pl.BlockSpec(memory_space=pltpu.HBM)
VMEM = pl.BlockSpec(memory_space=pltpu.VMEM)
SMEM = pl.BlockSpec(memory_space=pltpu.SMEM)


def shape(dims, dtype):
    return jax.ShapeDtypeStruct(dims, dtype)


def mm(left, right, dims=NN):
    return lax.dot_general(left, right, dims, preferred_element_type=F32)


def unit_rows_of(values):
    centred = values - jnp.mean(values, axis=-1, keepdims=True)
    inverse = lax.rsqrt(jnp.mean(centred * centred, axis=-1, keepdims=True) + EPSILON)
    return centred * inverse, inverse


def norm_back(grad, unit, inverse, gain):
    scaled = grad * gain
    return inverse * (
        scaled
        - jnp.mean(scaled, axis=-1, keepdims=True)
        - unit * jnp.mean(scaled * unit, axis=-1, keepdims=True)
    )


def rotary_tables():
    lane = np.arange(128) % HEAD_DIM
    half = HEAD_DIM // 2
    freq = ROTARY_BASE ** (-(lane % half).astype(np.float64) * (2.0 / HEAD_DIM))
    angles = np.arange(LEN)[:, None] * freq[None, :]
    sign = np.where(lane < half, -1.0, 1.0)[None, :]
    return np.stack([np.cos(angles), np.sin(angles) * sign]).astype(np.float32)


def rotary_columns():
    half = HEAD_DIM // 2
    freq = ROTARY_BASE ** (-np.arange(half, dtype=np.float64) * (2.0 / HEAD_DIM))
    angles = freq[:, None] * np.arange(LEN)[None, :]
    return np.stack([np.cos(angles), np.sin(angles)]).astype(np.float32)


def swap_halves(values):
    lane = lax.broadcasted_iota(jnp.int32, values.shape, 1) % HEAD_DIM
    half = HEAD_DIM // 2
    return jnp.where(
        lane < half,
        pltpu.roll(values, 128 - half, axis=1),
        pltpu.roll(values, half, axis=1),
    )


def head_stack(block, per):
    head = lax.broadcasted_iota(jnp.int32, block.shape, 1) // HEAD_DIM
    return jnp.concatenate(
        [jnp.where(head == h, block, jnp.zeros_like(block)) for h in range(per)], axis=0
    )


class Copies:
    def __init__(self, sems):
        self.sems = sems
        self.used = 0
        self.open = []

    def start(self, src, dst):
        copy = pltpu.make_async_copy(src, dst, self.sems.at[self.used])
        self.used += 1
        copy.start()
        return copy

    def save(self, src, dst):
        self.open.append(self.start(src, dst))

    def finish(self):
        for copy in self.open:
            copy.wait()


def call(kernel, outs, ins, scratch, sems, aliases, name, after=None, limit=16, spaces=None, out_spaces=None, micros=0.1):
    count = len(ins)
    places = {"v": VMEM, "h": HBM, "a": ANY, "s": SMEM}
    spaces = spaces or "v" * count
    out_spaces = out_spaces or "v" * len(outs)
    in_specs = [SMEM if a.ndim == 1 else places[p] for a, p in zip(ins, spaces)]
    ins = [pltpu.with_memory_space_constraint(a, pltpu.HBM) if p == "h" else a for a, p in zip(ins, spaces)]
    body = kernel
    if after is not None:
        ins = list(ins) + [after]
        in_specs = in_specs + [ANY]

        def body(*refs):
            kernel(*refs[:count], *refs[count + 1 :])

    outs = [pltpu.HBM(o.shape, o.dtype) if p == "h" else o for o, p in zip(outs, out_spaces)]
    return pl.pallas_call(
        body,
        out_shape=outs,
        in_specs=in_specs,
        out_specs=[places[p] for p in out_spaces],
        scratch_shapes=scratch + ([pltpu.SemaphoreType.DMA((sems,))] if sems else []),
        input_output_aliases=aliases,
        compiler_params=pltpu.CompilerParams(vmem_limit_bytes=limit << 20),
        cost_estimate=pl.CostEstimate(
            flops=int(micros * 1.15e9), bytes_accessed=0, transcendentals=0
        ),
        name=name,
    )(*ins)


TOKEN = jax.ShapeDtypeStruct((8, 128), F32)


def vmem_like(arr):
    return pltpu.VMEM(arr.shape, arr.dtype)


def forward(slot, info, live, own, arrived, params, tab, act, after=None):
    qkvw, qkvb, outw, outb, upw, upb, downw, downb, gain, shift = params
    dim = own.shape[1]
    blocks = dim // 128
    wide = upw.shape[1]
    parts = wide // dim
    per = 128 // HEAD_DIM
    manual = slot == 0
    saved = [
        shape((LEN, dim), BF),
        shape((LEN, 3 * dim), BF),
        shape((HEADS, LEN, LEN), BF),
        shape((dim, LEN), BF),
        shape((LEN, dim), F32),
        shape((LEN, wide), BF),
        shape((LEN, wide), BF),
    ]
    weights = [qkvb, outb, upb, downb, gain, shift, tab, qkvw, outw, upw, downw]
    sources = [own] if slot == 0 else [arrived] if slot == 2 else [own, arrived]
    before = [] if act is None else [act]
    ins = [info, live] + sources + weights + before
    count = len(sources)

    def kernel(info, live, *refs):
        xs = refs[:count]
        given = refs[count : count + 11]
        act_h, *outs = refs[count + 11 + len(before) : count + 19 + len(before)]
        scratch = refs[count + 19 + len(before) :]
        act_s, vt_s, score_s, up_s = scratch[:4]
        sems = scratch[-1]
        y_s, qkv_s, prob_s, mixt_s, mid_s, gp_s, hid_s = outs
        used = scratch[4:-1] if manual else xs[-1:] + given
        qkvb, outb, upb, downb, gain, shift, tab, qkvw, outw, upw, downw = used[1:]
        crop = slot - info[0]

        @pl.when(jnp.logical_and(crop >= 0, crop < CROP_DEV))
        def _():
            copies = Copies(sems)
            heavy = []
            if manual:
                rows = xs[0].at[pl.ds(0, LEN)]
                pairs = list(zip((rows,) + given, used))
                loads = {i: copies.start(*pairs[i]) for i in (0, 8, *range(1, 8), 9, 10, 11)}
                heavy = [loads[i] for i in range(8, 12)]
                wait_all([loads[i] for i in range(8)])
                x = used[0][...].astype(F32)
            elif slot == 1:
                x = jnp.where(info[0] == 0, xs[0][LEN:, :], xs[1][...]).astype(F32)
            else:
                x = xs[0][...].astype(F32)

            def ready(index):
                if manual:
                    heavy[index].wait()

            unit, _ = unit_rows_of(x)
            normed = (unit * gain[0:1, :] + shift[0:1, :]).astype(BF)
            ready(0)
            third = mm(normed, qkvw[:, 2 * dim :]) + qkvb[:, 2 * dim :]
            low = third.astype(BF)
            qkv_s[:, 2 * dim :] = low
            vt_s[...] = low.T
            for part in range(2):
                third = mm(normed, qkvw[:, part * dim : (part + 1) * dim])
                third = third + qkvb[:, part * dim : (part + 1) * dim]
                for j in range(blocks):
                    b = third[:, 128 * j : 128 * j + 128]
                    b = b * tab[0] + swap_halves(b) * tab[1]
                    if part == 0:
                        b = b * HEAD_DIM**-0.5
                    at = part * dim + 128 * j
                    qkv_s[:, at : at + 128] = b.astype(BF)
            for j in range(blocks):
                q = qkv_s[:, 128 * j : 128 * j + 128]
                k = qkv_s[:, dim + 128 * j : dim + 128 * j + 128]
                score_s[per * LEN * j : per * LEN * (j + 1), :] = mm(head_stack(k, per), q, NT)

            def soft(h, _):
                s = score_s[pl.ds(pl.multiple_of(h * LEN, LEN), LEN), :]
                e = jnp.exp(s - jnp.max(s, axis=0, keepdims=True))
                prob_s[h] = (e * (1.0 / jnp.sum(e, axis=0, keepdims=True))).astype(BF)
                return 0

            lax.fori_loop(0, HEADS, soft, 0, unroll=2)
            for h in range(HEADS):
                at = slice(HEAD_DIM * h, HEAD_DIM * (h + 1))
                mixt_s[at, :] = mm(vt_s[at, :], prob_s[h]).astype(BF)
            ready(1)
            mid = x + mm(mixt_s[...], outw[...], TN) + outb[...]
            mid_s[...] = mid
            unit, _ = unit_rows_of(mid)
            normed = (unit * gain[1:2, :] + shift[1:2, :]).astype(BF)
            ready(2)
            up_s[...] = mm(normed, upw[...])
            for c in range(parts):
                cols = slice(c * dim, (c + 1) * dim)
                u = up_s[:, cols] + upb[:, cols]
                cdf = 0.5 + 0.5 * lax.erf(u * 0.5**0.5)
                hid_s[:, cols] = (u * cdf).astype(BF)
                gp_s[:, cols] = (
                    cdf + u * (jnp.exp(u * u * -0.5) * (2 * np.pi) ** -0.5)
                ).astype(BF)
            ready(3)
            low = (mid_s[...] + downb[...] + mm(hid_s[...], downw[...])).astype(BF)
            y_s[...] = low
            act_s[...] = jnp.where(crop < live[0], low, jnp.zeros_like(low))
            at = pl.multiple_of(crop * LEN, LEN)
            copies.save(act_s, act_h.at[pl.ds(at, LEN)])
            copies.finish()

    outs = [shape(own.shape, BF)] + saved
    scratch = [
        pltpu.VMEM((LEN, dim), BF),
        pltpu.VMEM((dim, LEN), BF),
        pltpu.VMEM((HEADS * LEN, LEN), F32),
        pltpu.VMEM((LEN, wide), F32),
    ]
    if manual:
        scratch += [pltpu.VMEM((LEN, dim), BF)] + [vmem_like(a) for a in weights]
    aliases = {} if act is None else {len(ins) - 1: 0}
    spaces = "ss" + ("h" if manual else "v") * (count + 11) + "h" * len(before)
    out = call(
        kernel,
        outs,
        ins,
        scratch,
        16,
        aliases,
        "layer_forward",
        after,
        FIRST_LIMIT if manual else FORWARD_LIMIT,
        spaces,
        "h" + "v" * 7,
    )
    return out[0], out[1:]


def crop_weight(live, masks, crop, section):
    if section == 0:
        return 1.0
    count = jnp.where(live[0] > crop, masks[crop], 0)
    return jnp.full((1, 1), count, jnp.int32).astype(F32) / MASK_MEAN


def add_row(ref, row, values):
    ref[row : row + 1, :] = ref[row : row + 1, :] + jnp.sum(values, axis=0, keepdims=True)


def lay_out(own, bit, keep, send, block, index, row, count, at):
    src = pl.ds(row if isinstance(row, int) else pl.multiple_of(row, PAD), count)
    dst = pl.ds(at if isinstance(at, int) else pl.multiple_of(at, PAD), count)
    mine = own == bit

    @pl.when(mine)
    def _():
        keep[dst, :] = block[index, src, :]

    @pl.when(jnp.logical_not(mine))
    def _():
        send[dst, :] = block[index, src, :]


def keep_given(active, given, bufs):
    @pl.when(jnp.logical_not(active))
    def _():
        for old, new in zip(given, bufs):
            new[...] = old[...]


def pair_shapes(rows, dim):
    return [shape((rows, dim), BF)] * 2


def joined(refs, cols):
    return jnp.concatenate([r[:, cols] for r in refs], axis=0)


def wait_all(copies):
    for copy in copies:
        copy.wait()


def mlp_grad(section, info, live, masks, g, saved, params, after):
    mixts = [s[3] for s in saved]
    mids, gps, hids = ([s[k] for s in saved] for k in (4, 5, 6))
    upw, downw, gain, shift = params[4], params[6], params[8], params[9]
    rows, dim = g.shape
    wide = upw.shape[1]
    parts = wide // dim
    crops = len(saved)
    share = dim // GROUPS
    ins = [info, live, masks, g, gain, shift, downw, upw] + mids + gps + hids + mixts

    def kernel(info, live, masks, g_s, gain, shift, downw, upw, *refs):
        mid_s, gp_s, hid_s, mixt_s = (refs[i * crops : (i + 1) * crops] for i in range(4))
        refs = refs[4 * crops :]
        send_a, keep_a, send_b, keep_b, gmid_s, small_s = refs[:6]
        gu_s, block_s, low_s, normt_s, back_s = refs[7:]

        @pl.when(info[0] == section)
        def _():
            small_s[...] = jnp.zeros_like(small_s)
            for c in range(crops):
                crop = slice(c * LEN, (c + 1) * LEN)
                grad = g_s[crop, :].astype(F32) * crop_weight(live, masks, c, section)
                low = grad.astype(BF)
                low_s[crop, :] = low
                add_row(small_s, ROW_DOWN, low.astype(F32))
                unit, _ = unit_rows_of(mid_s[c][...])
                normt_s[:, crop] = (unit * gain[1:2, :] + shift[1:2, :]).astype(BF).T
            for c in range(parts):
                cols = slice(c * dim, (c + 1) * dim)
                block_s[c] = mm(joined(hid_s, cols), low_s[...], TN).astype(BF)

            @pl.loop(0, GROUPS * parts)
            def _(i):
                shard, row = i // parts, (i % parts) * share
                at = (shard // 2) * dim + row
                lay_out(info[1], shard % 2, keep_a, send_a, block_s, shard, row, share, at)

            for c in range(parts):
                cols = slice(c * dim, (c + 1) * dim)
                grad_up = mm(low_s[...], downw[cols, :], NT) * joined(gp_s, cols).astype(F32)
                grad_up = grad_up.astype(BF)
                gu_s[:, cols] = grad_up
                small_s[ROW_UP + c : ROW_UP + c + 1, :] = jnp.sum(
                    grad_up.astype(F32), axis=0, keepdims=True
                )
            back_s[...] = mm(gu_s[...], upw[...], NT)
            for c in range(crops):
                crop = slice(c * LEN, (c + 1) * LEN)
                grad = g_s[crop, :].astype(F32) * crop_weight(live, masks, c, section)
                unit, inverse = unit_rows_of(mid_s[c][...])
                back = back_s[crop, :]
                gmid = grad + norm_back(back, unit, inverse, gain[1:2, :])
                gmid_s[crop, :] = gmid
                low = gmid.astype(BF)
                low_s[crop, :] = low
                add_row(small_s, ROW_GAIN + 1, back * unit)
                add_row(small_s, ROW_SHIFT + 1, back)
                add_row(small_s, ROW_OUT, low.astype(F32))
            for c in range(parts):
                block_s[c] = mm(normt_s[...], gu_s[:, c * dim : (c + 1) * dim]).astype(BF)
            mixt = jnp.concatenate([m[...] for m in mixt_s], axis=1)
            block_s[parts] = mm(mixt, low_s[...]).astype(BF)

            @pl.loop(0, GROUPS * (parts + 1))
            def _(i):
                shard, c = i // (parts + 1), i % (parts + 1)
                at = ((shard % 2) * (parts + 1) + c) * share
                lay_out(info[2], shard // 2, keep_b, send_b, block_s, c, shard * share, share, at)

    scratch = [
        pltpu.VMEM((rows, wide), BF),
        pltpu.VMEM((parts + 1, dim, dim), BF),
        pltpu.VMEM((rows, dim), BF),
        pltpu.VMEM((dim, rows), BF),
        pltpu.VMEM((rows, dim), F32),
    ]
    outs = pair_shapes(2 * dim, dim) + pair_shapes(2 * (parts + 1) * share, dim)
    outs += [shape((rows, dim), F32), shape((PAD, dim), F32), TOKEN]
    out = call(kernel, outs, ins, scratch, 0, {}, "mlp_grad", after, MLP_LIMIT, micros=10)
    return out[:4], out[4], out[5], out[6]


def rotate_back(block, tab_t):
    half = HEAD_DIM // 2
    cos, sin = tab_t[0], tab_t[1]
    out = []
    for at in range(0, block.shape[0], HEAD_DIM):
        a, b = block[at : at + half], block[at + half : at + HEAD_DIM]
        out += [a * cos + b * sin, b * cos - a * sin]
    return jnp.concatenate(out, axis=0)


def attention_grad(section, info, gmid, small, xs, saved, params, tab_t, before, after):
    qkvs, probs, mixts = [s[1] for s in saved], [s[2] for s in saved], [s[3] for s in saved]
    qkvw, outw, gain, shift = params[0], params[2], params[8], params[9]
    rows, dim = gmid.shape
    blocks = dim // 128
    per = 128 // HEAD_DIM
    crops = len(saved)
    given = [] if before is None else [before]
    ins = [info, gmid, outw, small, gain, shift, tab_t, qkvw]
    ins += qkvs + probs + mixts + list(xs) + given

    def kernel(info, gmid_s, outw, small_s, gain, shift, tab_t, qkvw, *refs):
        qkv_s, prob_s, mixt_s = (refs[i * crops : (i + 1) * crops] for i in range(3))
        x_s = refs[3 * crops : 3 * crops + len(xs)]
        old = refs[3 * crops + len(xs) : 3 * crops + len(xs) + len(given)]
        refs = refs[3 * crops + len(xs) + len(given) :]
        keep_given(info[0] == section, old, refs[:1])
        dx_s, gqkv_s, normt_s, small_out = refs[:4]
        gmt_s, delta_s, da_s, ds_s, dt_s, kt_s = refs[5:]

        @pl.when(info[0] == section)
        def _():
            low = gmid_s[...].astype(BF)
            gmt_s[...] = mm(outw[...], low, NT).astype(BF)
            for c in range(crops):
                crop = slice(c * LEN, (c + 1) * LEN)
                qkv, prob = qkv_s[c], prob_s[c]
                product = gmt_s[:, crop].astype(F32) * mixt_s[c][...].astype(F32)
                delta_s[...] = jnp.sum(product.reshape(HEADS, HEAD_DIM, LEN), axis=1)[:, None, :]
                kt_s[0] = qkv[:, dim : 2 * dim].T
                kt_s[1] = qkv[:, :dim].T
                for j in range(blocks):
                    v = qkv[:, 2 * dim + 128 * j : 2 * dim + 128 * j + 128]
                    da_s[per * LEN * j : per * LEN * (j + 1), :] = mm(
                        head_stack(v, per), gmt_s[128 * j : 128 * j + 128, crop]
                    )

                def scores(h, _):
                    da = da_s[pl.ds(pl.multiple_of(h * LEN, LEN), LEN), :]
                    ds_s[h] = (prob[h].astype(F32) * (da - delta_s[h])).astype(BF)
                    return 0

                lax.fori_loop(0, HEADS, scores, 0, unroll=2)
                for h in range(HEADS):
                    at = slice(HEAD_DIM * h, HEAD_DIM * (h + 1))
                    dt_s[0, at, :] = mm(kt_s[0, at, :], ds_s[h])
                    dt_s[1, at, :] = mm(kt_s[1, at, :], ds_s[h], NT)
                    dt_s[2, at, :] = mm(gmt_s[at, crop], prob[h], NT)
                dq = rotate_back(dt_s[0] * HEAD_DIM**-0.5, tab_t)
                gqkv_s[crop, :dim] = dq.astype(BF).T
                gqkv_s[crop, dim : 2 * dim] = rotate_back(dt_s[1], tab_t).astype(BF).T
                gqkv_s[crop, 2 * dim :] = dt_s[2].astype(BF).T
            unit, inverse = unit_rows_of(joined(x_s, slice(None)).astype(F32))
            normt_s[...] = (unit * gain[0:1, :] + shift[0:1, :]).astype(BF).T
            back = mm(gqkv_s[...], qkvw[...], NT)
            dx_s[...] = (gmid_s[...] + norm_back(back, unit, inverse, gain[0:1, :])).astype(BF)
            small_out[...] = small_s[...]
            small_out[ROW_GAIN : ROW_GAIN + 1, :] = jnp.sum(back * unit, axis=0, keepdims=True)
            small_out[ROW_SHIFT : ROW_SHIFT + 1, :] = jnp.sum(back, axis=0, keepdims=True)

    outs = [
        shape((rows, dim), BF),
        shape((rows, 3 * dim), BF),
        shape((dim, rows), BF),
        shape(small.shape, F32),
        TOKEN,
    ]
    scratch = [
        pltpu.VMEM((dim, rows), BF),
        pltpu.VMEM((HEADS, 1, LEN), F32),
        pltpu.VMEM((HEADS * LEN, LEN), F32),
        pltpu.VMEM((HEADS, LEN, LEN), BF),
        pltpu.VMEM((3, dim, LEN), F32),
        pltpu.VMEM((2, dim, LEN), BF),
    ]
    aliases = {len(ins) - 1: 0} if given else {}
    out = call(kernel, outs, ins, scratch, 0, aliases, "attention_grad", after, ATTENTION_LIMIT, micros=ATTENTION_MICROS)
    return out[0], out[1:4], out[4]


def qkv_grad(section, info, kept, before, after):
    gqkv, normt, small = kept
    dim, rows = normt.shape
    share = dim // GROUPS
    half = 3 * share // 2
    given = [] if before is None else list(before)
    ins = [info, gqkv, normt, small] + given

    def kernel(info, gqkv_s, normt_s, small_s, *refs):
        old = refs[: len(given)]
        bufs = refs[len(given) : len(given) + 4]
        send_a, keep_a, send_b, keep_b = bufs
        (block_s,) = refs[len(given) + 5 :]
        keep_given(info[0] == section, old, bufs)

        @pl.when(info[0] == section)
        def _():
            sums = [
                jnp.sum(gqkv_s[:, c * dim : (c + 1) * dim].astype(F32), axis=0, keepdims=True)
                for c in range(3)
            ]
            tail = jnp.concatenate(sums + [small_s[ROW_OUT:, :]], axis=0).astype(BF)
            send_a[2 * half :, :] = tail
            keep_a[2 * half :, :] = tail
            for c in range(3):
                block_s[c] = mm(normt_s[...], gqkv_s[:, c * dim : (c + 1) * dim]).astype(BF)

            @pl.loop(0, GROUPS)
            def _(shard):
                x, y, base = shard % 2, shard // 2, shard * share
                for c in range(3):
                    row, at, left = 0, c * share, share
                    while left:
                        count = min(left, half - at % half)
                        if at < half:
                            own, bit, keep, send, to = info[1], x, keep_a, send_a, y * half + at
                        else:
                            own, bit, keep, send, to = info[2], y, keep_b, send_b, x * half + at - half
                        lay_out(own, bit, keep, send, block_s, c, base + row, count, to)
                        row, at, left = row + count, at + count, left - count

    scratch = [pltpu.VMEM((3, dim, dim), BF)]
    aliases = {len(ins) - 4 + i: i for i in range(4)} if given else {}
    outs = pair_shapes(2 * half + PAD, dim) + pair_shapes(2 * half, dim) + [TOKEN]
    out = call(kernel, outs, ins, scratch, 0, aliases, "qkv_grad", after, QKV_LIMIT)
    return out[:4], out[4]


STEP = 80


def plus(one, two):
    return (one.astype(F32) + two.astype(F32)).astype(BF)


def add_rows(out, at, one, two, start, count):
    whole = count // STEP * STEP

    @pl.loop(0, whole // STEP)
    def _(i):
        src = pl.ds(pl.multiple_of(start + i * STEP, PAD), STEP)
        dst = pl.ds(pl.multiple_of(at + i * STEP, PAD), STEP)
        out[dst, :] = plus(one[src, :], two[src, :])

    if count > whole:
        src = pl.ds(pl.multiple_of(start + whole, PAD), count - whole)
        out[pl.ds(at + whole, count - whole), :] = plus(one[src, :], two[src, :])


def taking_part(info, sections, middle):
    check = None
    if len(sections) == 1:
        check = info[0] == sections[0]
    if middle:
        inner = jnp.logical_or(info[3] == 1, info[3] == 2)
        check = inner if check is None else jnp.logical_and(check, inner)
    return info[3] >= 0 if check is None else check


def vmem_call(kernel, outs, info, ins, name, after):
    return call(kernel, outs, [info] + ins, [], 0, {}, name, after, 8)


def first_sum(info, sections, keep_a, recv_a, keep_b, recv_b, after):
    dim = keep_b.shape[1]
    sizes = [(k.shape[0] // (2 * PAD) * PAD, k.shape[0] % (2 * PAD)) for k in (keep_a, keep_b)]

    def kernel(info, ka, ra, kb, rb, sa, na, sb, nb):
        @pl.when(taking_part(info, sections, False))
        def _():
            for own, one, two, new, out, (half, extra) in (
                (info[2], ka, ra, na, sa, sizes[0]),
                (info[1], kb, rb, nb, sb, sizes[1]),
            ):
                add_rows(out, 0, one, two, (1 - own) * half, half)
                add_rows(new, 0, one, two, own * half, half)
                if extra:
                    tail = plus(one[2 * half :, :], two[2 * half :, :])
                    new[half:, :] = tail
                    out[half:, :] = tail

    outs = [shape((sum(size), dim), BF) for size in sizes for _ in range(2)]
    return vmem_call(kernel, outs, info, [keep_a, recv_a, keep_b, recv_b], "first_sum", after)


def second_sum(info, sections, keep_a, recv_a, keep_b, recv_b, joint, after):
    dim = keep_b.shape[1]
    top, rest = keep_a.shape[0], keep_b.shape[0]

    def kernel(info, ka, ra, kb, rb, *out):
        @pl.when(taking_part(info, sections, False))
        def _():
            add_rows(out[0], 0, ka, ra, 0, top)
            add_rows(out[-1], out[-1].shape[0] - rest, kb, rb, 0, rest)

    outs = [shape((top + rest, dim), BF)]
    if not joint:
        outs = [shape((top, dim), BF), shape((rest, dim), BF)]
    return vmem_call(kernel, outs, info, [keep_a, recv_a, keep_b, recv_b], "second_sum", after)


def pair_sum(info, sections, one, two, after):
    def kernel(info, one, two, out):
        @pl.when(taking_part(info, sections, True))
        def _():
            add_rows(out, 0, one, two, 0, one.shape[0])

    return vmem_call(kernel, [shape(one.shape, BF)], info, [one, two], "pair_sum", after)[0]


def own_pieces(row, count, width, group):
    share = count * width // GROUPS
    at, pieces = group * share, []
    while at < (group + 1) * share:
        size = min((group + 1) * share - at, width - at % width)
        pieces.append((row + at // width, at % width, size, at - group * share))
        at += size
    return pieces


def finish(info, sources, kind, after):
    dim = sources[0][0].shape[1]
    share = dim // GROUPS
    half = 3 * share // 2
    vectors = ((ROW_QKV, 3), (ROW_OUT, 1), (ROW_UP, 4), (ROW_DOWN, 1))
    if kind == "down":
        rows, outs = dim, [shape((dim, dim), F32)]
    elif kind == "up":
        rows, outs = 5 * share, [shape((share, 4 * dim), F32), shape((share, dim), F32)]
    else:
        rows, outs = 3 * share + PAD, [shape((share, 3 * dim), F32)]
    large = len(outs)
    if kind == "qkv":
        outs += [shape((1, count * dim // GROUPS), F32) for _, count in vectors]
        outs += [shape((2, share), F32)] * 2

    def kernel(info, p0, g0, p1, g1, *refs):
        out_h = refs[:large]
        small = refs[large : len(outs)]
        src = refs[len(outs)]
        stage = refs[len(outs) + 1 : -1]
        sems = refs[-1]
        inner = jnp.logical_or(info[3] == 1, info[3] == 2)
        for section, part, got in ((0, p0, g0), (1, p1, g1)):
            mine = info[0] == section
            lines = pl.ds(sources[section][2], rows)

            @pl.when(jnp.logical_and(mine, inner))
            def _():
                pltpu.make_async_copy(part.at[lines], src, sems.at[0]).start()

            @pl.when(jnp.logical_and(mine, jnp.logical_not(inner)))
            def _():
                pltpu.make_async_copy(got.at[lines], src, sems.at[0]).start()

        pltpu.make_async_copy(p0.at[pl.ds(sources[0][2], rows)], src, sems.at[0]).wait()
        if kind == "down":
            stage[0][...] = src[...].astype(F32)
        elif kind == "up":
            for i in range(4):
                block = src[i * share : (i + 1) * share, :].astype(F32)
                stage[0][:, i * dim : (i + 1) * dim] = block
            stage[1][...] = src[4 * share :, :].astype(F32)
        else:
            for i in range(3):
                at, left, to = i * share, share, 0
                while left:
                    count = min(left, half - at % half)
                    row = at if at < half else at + PAD
                    block = src[row : row + count, :].astype(F32)
                    stage[0][to : to + count, i * dim : (i + 1) * dim] = block
                    at, left, to = at + count, left - count, to + count
        copies = [
            pltpu.make_async_copy(s, o, sems.at[1 + i]) for i, (s, o) in enumerate(zip(stage, out_h))
        ]
        for copy in copies:
            copy.start()
        if kind == "qkv":
            tail = src[half : half + PAD, :].astype(F32)
            for group in range(GROUPS):

                @pl.when(info[1] + 2 * info[2] == group)
                def _():
                    for out, (row, count) in zip(small, vectors):
                        for r, c, size, at in own_pieces(row, count, dim, group):
                            out[:, at : at + size] = tail[r : r + 1, c : c + size]
                    for out, row in zip(small[4:], (ROW_GAIN, ROW_SHIFT)):
                        out[...] = tail[row : row + 2, group * share : (group + 1) * share]

        for copy in copies:
            copy.wait()

    scratch = [pltpu.VMEM((rows, dim), BF)] + [vmem_like(o) for o in outs[:large]]
    ins = [info] + [a for source in sources for a in source[:2]]
    places = "h" * large + "v" * (len(outs) - large)
    return call(kernel, outs, ins, scratch, 4, {}, "finish", after, 12, "saaaa", places)


def flow(shard, axis, pairs, sections):
    if sections == (0, 1):
        return lax.ppermute(shard, axis, pairs)
    peers = lax.axis_size(axis)
    pairs = [(s * peers + i, s * peers + j) for s in sections for i, j in pairs]
    return lax.ppermute(shard, ("section", axis), pairs)


class Reduction:
    def __init__(self, info, sections, bufs, joint):
        self.info, self.sections, self.joint = info, sections, joint
        groups = range(GROUPS)
        self.across = [(g, g ^ 1) for g in groups]
        self.along = [(g, g ^ 2) for g in groups]
        self.line = lax.axis_size("replica") == 4
        send_a, keep_a, send_b, keep_b = bufs
        self.kept = (keep_a, keep_b)
        self.got = (
            flow(send_a, "group", self.across, sections),
            flow(send_b, "group", self.along, sections),
        )

    def group_two(self, after):
        send_a, keep_a, send_b, keep_b = first_sum(
            self.info, self.sections, self.kept[0], self.got[0], self.kept[1], self.got[1], after
        )
        self.kept = (keep_a, keep_b)
        self.got = (
            flow(send_a, "group", self.along, self.sections),
            flow(send_b, "group", self.across, self.sections),
        )
        return keep_a

    def replica_one(self, after):
        self.parts = list(
            second_sum(
                self.info,
                self.sections,
                self.kept[0],
                self.got[0],
                self.kept[1],
                self.got[1],
                self.joint,
                after,
            )
        )
        if self.line:
            self.got = [
                flow(part, "replica", [(0, 1), (3, 2)], self.sections) for part in self.parts
            ]
        else:
            self.parts = [lax.psum(part, "replica") for part in self.parts]
            self.got = list(self.parts)
        return self.parts[0]

    def replica_next(self, pairs, after):
        for i in range(len(self.parts)):
            if self.line:
                self.parts[i] = after = pair_sum(
                    self.info, self.sections, self.parts[i], self.got[i], after
                )
                self.got[i] = flow(self.parts[i], "replica", pairs, self.sections)
        return after

    def replica_two(self, after):
        return self.replica_next([(1, 2), (2, 1)], after)

    def replica_three(self, after):
        return self.replica_next([(1, 0), (2, 3)], after)

    def source(self, half, row):
        index = 0 if self.joint else half
        return self.parts[index], self.got[index], row


def shards(
    block_input,
    cotangent,
    crop_count,
    mask_count,
    qkv_weight,
    qkv_bias,
    out_weight,
    out_bias,
    up_weight,
    up_bias,
    down_weight,
    down_bias,
    norm_gain,
    norm_shift,
):
    params = (
        qkv_weight[0],
        qkv_bias,
        out_weight[0],
        out_bias,
        up_weight[0],
        up_bias,
        down_weight[0],
        down_bias,
        norm_gain[0],
        norm_shift[0],
    )
    rows, dim = block_input.shape
    tab = jnp.asarray(rotary_tables())
    tab_t = jnp.asarray(rotary_columns())
    group = lax.axis_index("group")
    assert lax.axis_size("group") == GROUPS
    info = jnp.stack([lax.axis_index("section"), group % 2, group // 2, lax.axis_index("replica")])

    def to_other(shard, pairs):
        return lax.ppermute(shard, "section", pairs)

    act, first = forward(0, info, crop_count, block_input, None, params, tab, None)
    arrived = [to_other(first[0], [(0, 1)])]
    act, second = forward(1, info, crop_count, block_input, arrived[0], params, tab, act)
    arrived.append(to_other(second[0], [(0, 1)]))
    act, third = forward(2, info, crop_count, block_input, arrived[1], params, tab, act)
    kept_one, kept_zero = (second, third), (first, second)

    common = (info, crop_count, mask_count)
    bufs, gmid, small, last = mlp_grad(1, *common, cotangent, kept_one, params, None)
    one = Reduction(info, (1,), bufs, True)
    dx, kept, last = attention_grad(
        1, info, gmid, small, arrived, kept_one, params, tab_t, None, last
    )
    grad_back = to_other(dx, [(1, 0)])
    bufs_three, last = qkv_grad(1, info, kept, None, last)
    last = one.group_two(last)
    bufs, gmid, small, last = mlp_grad(0, *common, grad_back, kept_zero, params, last)
    two = Reduction(info, (0,), bufs, False)
    last = one.replica_one(last)
    dx, kept, last = attention_grad(
        0, info, gmid, small, [block_input], kept_zero, params, tab_t, dx, last
    )
    bufs, last = qkv_grad(0, info, kept, bufs_three, last)
    three = Reduction(info, (0, 1), bufs, True)
    last = two.group_two(last)
    last = one.replica_two(last)
    last = two.replica_one(last)
    last = three.group_two(last)
    last = two.replica_two(last)
    last = three.replica_one(last)
    last = one.replica_three(last)
    last = two.replica_three(last)
    last = three.replica_two(last)
    (grad_down,) = finish(info, (two.source(0, 0), one.source(0, 0)), "down", last)
    last = three.replica_three(grad_down)
    grad_up, grad_out = finish(info, (two.source(1, 0), one.source(1, dim)), "up", last)
    grad_qkv, *small = finish(info, (three.source(0, 0), three.source(0, 0)), "qkv", grad_out)
    qkv_b, out_b, up_b, down_b, gain, shift = small
    return (
        act[None],
        dx[None],
        grad_qkv[None],
        qkv_b,
        grad_out[None],
        out_b,
        grad_up[None],
        up_b,
        grad_down[None],
        down_b,
        gain[None],
        shift[None],
    )


def solution(mesh):
    rows = P(("group", "replica"))
    stack = P("section")
    return jax.shard_map(
        shards,
        mesh=mesh,
        in_specs=(rows,) * 4 + (stack,) * 10,
        out_specs=(
            P("section", ("group", "replica"), None),
            P("section", ("group", "replica"), None),
            P("section", "group", None),
            P("section", "group"),
            P("section", "group", None),
            P("section", "group"),
            P("section", "group", None),
            P("section", "group"),
            P("section", "group", None),
            P("section", "group"),
            P("section", None, "group"),
            P("section", None, "group"),
        ),
        check_vma=False,
    )
```
